32 devices in a mesh: dp: 8 (over y, x, core), seq: 4 (over z).
Axes of the slice: x: 2, y: 2, z: 4, core: 2. Of those that a mesh axis runs over, the one named last changes fastest.
Arguments:
- tokens: bfloat16 [12288, 1024], P(('dp', 'seq')), may hold values from -6 to 6
- query_weight: bfloat16 [1024, 1024], replicated, may hold values from -0.046875 to 0.046875
- key_weight: bfloat16 [1024, 1024], replicated, may hold values from -0.1875 to 0.1875
- value_weight: bfloat16 [1024, 1024], replicated, may hold values from -0.1875 to 0.1875
- out_weight: bfloat16 [1024, 1024], replicated, may hold values from -0.75 to 0.75
- gate_weight: bfloat16 [1024, 2816], replicated, may hold values from -0.1875 to 0.1875
- up_weight: bfloat16 [1024, 2816], replicated, may hold values from -0.1875 to 0.1875
- down_weight: bfloat16 [2816, 1024], replicated, may hold values from -0.109375 to 0.109375
- attention_gain: float32 [1024], replicated, may hold values from 0.5 to 1.5
- feedforward_gain: float32 [1024], replicated, may hold values from 0.5 to 1.5
- pair_lengths: int32 [8, 4], P('dp'), may hold values from 1 to 1153, 1536 in all within a row
- live_mask: int32 [12288], P(('dp', 'seq')), may hold values 0 or 1
- out_grad: bfloat16 [12288, 1024], P(('dp', 'seq')), may hold values from -6 to 6
Outputs:
- layer_out: bfloat16 [12288, 1024], P(('dp', 'seq'))
- grad_tokens: float32 [12288, 1024], P(('dp', 'seq'))
- grad_query: float32 [1024, 1024], P('dp')
- grad_key: float32 [1024, 1024], P('dp')
- grad_value: float32 [1024, 1024], P('dp')
- grad_output: float32 [1024, 1024], P('dp')
- grad_gate: float32 [1024, 2816], P('dp')
- grad_upward: float32 [1024, 2816], P('dp')
- grad_down: float32 [2816, 1024], P('dp')
- grad_attention_gain: float32 [1024], P('dp')
- grad_feedforward_gain: float32 [1024], P('dp')
The draws below stay inside these ranges and needn't reach their ends.
Inputs may be any that keep to these rules, and one draw needn't show every extreme that they name: `pair_lengths`: each row's 4 lengths sum to 1536; pairs lie one after another in their row; in each row exactly one pair has 1153 tokens.
All inputs are finite; a program needn't handle non-finite values. No bound on the sum of `live_mask` on one device may be relied on, other than what follows from the above.
Results may differ from the reference program's by a relative error of at most 0.02.
Values may be sent and summed in bfloat16 or wider, within the bound.
A program may use at most 320 MiB of HBM per device.

```python
import math
import jax
import jax.numpy as jnp
import numpy as np
from jax import lax

D = 1024
HEADS = 16
HEAD_DIM = 64
FF = 2816
PAIRS = 4
ROW_LEN = 1536
ROWS = 8
TOKENS = 12288
LONGEST = 1153


def touch_ends(values, stream_key, least, largest):
    longest = values.shape.index(max(values.shape))
    spots = []
    for shift in (0, 1):
        where = [jax.random.randint(jax.random.fold_in(stream_key, axis), (), 0, length) for axis, length in enumerate(values.shape)]
        where[longest] = (where[longest] + shift) % values.shape[longest]
        spots.append(tuple(where))
    return values.at[spots[0]].set(least).at[spots[1]].set(largest)


def strengthened(values, stream_key, source, target, blocks, factor):
    owner, partner = [(jnp.arange(values.shape[axis_at]) // (values.shape[axis_at] // blocks)).reshape([-1 if axis == axis_at else 1 for axis in range(values.ndim)]) for axis_at in (source, target)]
    chosen = jax.random.permutation(stream_key, blocks)[partner]
    strong = (owner == chosen) | (owner == (partner + blocks // 2) % blocks)
    return jnp.where(strong, factor * values, values)


def steps_of(key, extent, split, least, top_value):
    def one(position, parts):
        draws = jax.random.uniform(jax.random.fold_in(jax.random.fold_in(key, 6), position), (parts,), jnp.float32, least / len(split), top_value / len(split))
        return jnp.repeat(jnp.exp(draws), extent[position] // parts).reshape((-1,) + (1,) * (len(extent) - position - 1))

    factor_of = one(*split[0])
    for cut in split[1:]:
        factor_of = factor_of * one(*cut)
    return factor_of


def profile(number_of, total, most, skew):
    loads = [(1 << 20) // math.isqrt(grade ** skew) + 1 for grade in range(2, number_of + 1)]
    surplus, holding = total - most - (number_of - 1), [1] * (number_of - 1)
    while surplus > 0:
        free = [i for i in range(number_of - 1) if holding[i] < most]
        pool, budget = sum([loads[i] for i in free]), surplus
        for i in free:
            more = min(most - holding[i], max(1, budget * loads[i] // pool), surplus)
            holding[i] = holding[i] + more
            surplus = surplus - more
    return np.array([most] + holding)


def ragged_sizes(stream_key, number_of, total, reach, skew):
    if number_of == 2:
        one = jax.random.randint(stream_key, (), max(1, total - reach), min(reach, total - 1) + 1)
        return jnp.stack([one, total - one])
    tallies = jnp.asarray(profile(number_of, total, reach, skew), jnp.int32)
    couples = (number_of - 1) // 2
    donor, sink = tallies[1:1 + 2 * couples:2], tallies[2:2 + 2 * couples:2]
    slack = jnp.minimum(donor - 1, reach - sink)
    moved = jax.random.randint(jax.random.fold_in(stream_key, 1), (couples,), 0, 1 << 20) % (slack + 1)
    tallies = tallies.at[1:1 + 2 * couples:2].set(donor - moved).at[2:2 + 2 * couples:2].set(sink + moved)
    return tallies[jax.random.permutation(jax.random.fold_in(stream_key, 2), number_of)]


def gaussian(rng, dims, width, most, cuts=(), held_as=jnp.bfloat16):
    values = width * jax.random.normal(rng, dims, jnp.float32)
    if cuts:
        values = values * steps_of(rng, dims, cuts, -0.22, 0.18)
    return jnp.clip(values, -most, most).astype(held_as)


def bell_draw_with(own_key, dims, width, limit, shards, heavy, held_as=jnp.bfloat16):
    array = width * jax.random.normal(own_key, dims, jnp.float32)
    if shards:
        array = array * steps_of(own_key, dims, shards, -0.22, 0.18)
    return jnp.clip(strengthened(array, jax.random.fold_in(own_key, 3), *heavy), -limit, limit).astype(held_as)


def setup_inputs(seed: int = 0) -> dict:
    splits = jax.random.split(jax.random.key(seed), 14)
    return {
        "tokens": bell_draw_with(splits[0], (TOKENS, D), 1.0, 6.0, ((0, 32),), (0, 1, 32, 2.75)),
        "query_weight": gaussian(splits[1], (D, D), (16 * D) ** -0.5, 0.046875),
        "key_weight": gaussian(splits[2], (D, D), D ** -0.5, 0.1875),
        "value_weight": gaussian(splits[3], (D, D), D ** -0.5, 0.1875),
        "out_weight": gaussian(splits[4], (D, D), (D // 16) ** -0.5, 0.75),
        "gate_weight": gaussian(splits[5], (D, FF), D ** -0.5, 0.1875),
        "up_weight": gaussian(splits[6], (D, FF), D ** -0.5, 0.1875),
        "down_weight": gaussian(splits[7], (FF, D), FF ** -0.5, 0.109375),
        "attention_gain": jnp.clip(1.0 + 0.1 * jax.random.normal(splits[8], (D,), jnp.float32), 0.5, 1.5),
        "feedforward_gain": jnp.clip(1.0 + 0.1 * jax.random.normal(splits[9], (D,), jnp.float32), 0.5, 1.5),
        "pair_lengths": jax.vmap(lambda own: ragged_sizes(own, PAIRS, ROW_LEN, LONGEST, 2))(jax.random.split(splits[10], ROWS)).reshape((ROWS, PAIRS)).astype(jnp.int32),
        "live_mask": touch_ends((jax.random.randint(splits[11], (TOKENS,), 0, 8) < 7).astype(jnp.int32), jax.random.fold_in(splits[11], 1), 0, 1),
        "out_grad": gaussian(splits[12], (TOKENS, D), 1.0, 6.0, ((0, 32),)),
    }


EPS = 1e-06
HIGH = lax.Precision.HIGHEST

@jax.custom_vjp
def low(v):
    return lax.optimization_barrier(v.astype(jnp.bfloat16)).astype(jnp.float32)

@jax.custom_vjp
def low_back(v):
    return v

def low_keep(v):
    return (low(v), None)

def low_pass(kept, grad):
    return (grad,)

def back_keep(v):
    return (v, None)

def back_low(kept, grad):
    return (low(grad),)
low.defvjp(low_keep, low_pass)
low_back.defvjp(back_keep, back_low)

def matmul(former, latter):
    return jnp.dot(former, latter, precision=HIGH)

def rms_scale(values, gain_row):
    return values * lax.rsqrt(lax.optimization_barrier(jnp.mean(values * values, axis=-1, keepdims=True)) + EPS) * gain_row

def segment_of(lengths, positions):
    bounds = jnp.cumsum(lengths)[:-1]
    return lax.optimization_barrier(jnp.sum((positions[:, None] >= bounds[None, :]).astype(jnp.int32), axis=1))

def split_heads(values):
    return values.reshape(values.shape[0], HEADS, HEAD_DIM).transpose(1, 0, 2)

def join_heads(values):
    return values.transpose(1, 0, 2).reshape(values.shape[1], HEADS * HEAD_DIM)

def attend(query_row, key_row, value_row, lengths, live_row):
    positions = jnp.arange(ROW_LEN, dtype=jnp.int32)
    segments = segment_of(lengths, positions)
    allowed = (segments[:, None] == segments[None, :]) & ((live_row[None, :] > 0) | (positions[:, None] == positions[None, :]))

    def one_head(pieces):
        query_head, key_head, value_head = pieces
        scores = low_back(matmul(query_head, key_head.T))
        scores = jnp.where(allowed, scores, -1e+30)
        row_max = lax.optimization_barrier(jnp.max(scores, axis=1, keepdims=True))
        weights = jnp.exp(scores - row_max)
        probs = low(weights / lax.optimization_barrier(jnp.sum(weights, axis=1, keepdims=True)))
        return matmul(probs, value_head)
    heads = lax.map(jax.checkpoint(one_head), (split_heads(query_row), split_heads(key_row), split_heads(value_row)))
    return join_heads(heads)

def forward(inputs, query_weight, key_weight, value_weight, out_weight, gate_weight, up_weight, down_weight, attention_gain, feedforward_gain, pair_lengths, live_mask):
    normed_one = low(rms_scale(inputs, attention_gain))
    queries = low(low_back(matmul(normed_one, query_weight)))
    keys_all = low(low_back(matmul(normed_one, key_weight)))
    values_all = low(low_back(matmul(normed_one, value_weight)))

    def one_row(carry, pieces):
        query_row, key_row, value_row, lengths, live_row = pieces
        return (carry, attend(query_row, key_row, value_row, lengths, live_row))
    _, mixed = lax.scan(one_row, jnp.zeros((), jnp.float32), (queries.reshape(ROWS, ROW_LEN, D), keys_all.reshape(ROWS, ROW_LEN, D), values_all.reshape(ROWS, ROW_LEN, D), pair_lengths, live_mask.reshape(ROWS, ROW_LEN)))
    heads_out = low(low_back(mixed.reshape(TOKENS, D)))
    hidden = inputs + low_back(matmul(heads_out, out_weight))
    normed_two = low(rms_scale(hidden, feedforward_gain))
    gates = low_back(matmul(normed_two, gate_weight))
    upward = low_back(matmul(normed_two, up_weight))
    inner = low(jax.nn.gelu(gates, approximate=True) * upward)
    return hidden + low_back(matmul(inner, down_weight))

def reference(tokens, query_weight, key_weight, value_weight, out_weight, gate_weight, up_weight, down_weight, attention_gain, feedforward_gain, pair_lengths, live_mask, out_grad):
    floats = (tokens.astype(jnp.float32), query_weight.astype(jnp.float32), key_weight.astype(jnp.float32), value_weight.astype(jnp.float32), out_weight.astype(jnp.float32), gate_weight.astype(jnp.float32), up_weight.astype(jnp.float32), down_weight.astype(jnp.float32), attention_gain.astype(jnp.float32), feedforward_gain.astype(jnp.float32))

    def layer(inputs, w_one, w_two, w_three, w_four, w_five, w_six, w_seven, gain_one, gain_two):
        return forward(inputs, w_one, w_two, w_three, w_four, w_five, w_six, w_seven, gain_one, gain_two, pair_lengths, live_mask)
    result, layer_back = jax.vjp(layer, floats[0], floats[1], floats[2], floats[3], floats[4], floats[5], floats[6], floats[7], floats[8], floats[9])
    grads = layer_back(out_grad.astype(jnp.float32))
    return (result.astype(jnp.bfloat16), grads[0], grads[1], grads[2], grads[3], grads[4], grads[5], grads[6], grads[7], grads[8], grads[9])
```

```python
import functools

import jax
import jax.numpy as jnp
from jax import lax
from jax.experimental import pallas as pl
from jax.experimental.pallas import tpu as pltpu
from jax.sharding import PartitionSpec as P

HEADS = 16
HEAD_DIM = 64
EPS = 1e-06
BIG = float(2.0**40)
F32 = jnp.float32
BF16 = jnp.bfloat16
AXES = ("dp", "seq")


def dot_nn(a, b):
    return lax.dot_general(a, b, (((1,), (0,)), ((), ())), preferred_element_type=F32)


def dot_nt(a, b):
    return lax.dot_general(a, b, (((1,), (1,)), ((), ())), preferred_element_type=F32)


def dot_tn(a, b):
    return lax.dot_general(a, b, (((0,), (0,)), ((), ())), preferred_element_type=F32)


def three_parts(v):
    high = v.astype(BF16).astype(F32)
    mid = (v - high).astype(BF16).astype(F32)
    low = (v - high - mid).astype(BF16).astype(F32)
    return high, mid, low


def forward_kernel(q_ref, k_ref, v_ref, mq_ref, mk_ref, dead_ref, kd_ref, vd_ref, o_ref, l_ref):
    lane = lax.broadcasted_iota(jnp.int32, q_ref.shape, 1)
    klane = lax.broadcasted_iota(jnp.int32, k_ref.shape, 1)
    q = q_ref[...]
    dead = dead_ref[...]
    qk = q.astype(F32) * kd_ref[...].astype(F32)
    outs, logs = [], []
    for h in range(2):
        mine = (lane < HEAD_DIM) if h == 0 else (lane >= HEAD_DIM)
        kmine = (klane < HEAD_DIM) if h == 0 else (klane >= HEAD_DIM)
        qa = jnp.where(mine, q, mq_ref[...])
        ka = jnp.where(kmine, k_ref[...], mk_ref[...])
        s = dot_nt(qa, ka)
        own = jnp.sum(jnp.where(mine, qk, 0.0), axis=1, keepdims=True)
        own = jnp.where(dead > 0, own, -BIG)
        top = jnp.maximum(jnp.max(s, axis=1, keepdims=True), own)
        p = jnp.exp(s - top).astype(BF16)
        va = jnp.where(kmine, v_ref[...], jnp.ones_like(v_ref[...]))
        r = dot_nn(p, va)
        own_p = jnp.exp(own - top)
        total = (r[:, HEAD_DIM : HEAD_DIM + 1] if h == 0 else r[:, 0:1]) + own_p
        outs.append((r + own_p * vd_ref[...].astype(F32)) * (1.0 / total))
        logs.append(top + jnp.log(total))
    o_ref[...] = jnp.where(lane < HEAD_DIM, outs[0], outs[1])
    l_ref[...] = jnp.where(lane < HEAD_DIM, logs[0], logs[1])


def rows_per_step(tokens):
    for rows in (512, 384, 256, 128):
        if tokens % rows == 0 and rows * tokens <= 800000:
            return rows
    return 128


def attention_forward(q, k, v, mq, mk, dead):
    tokens, width = q.shape
    rows = rows_per_step(tokens)
    part = pl.BlockSpec((rows, 128), lambda h, i: (i, h))
    full = pl.BlockSpec((tokens, 128), lambda h, i: (0, h))
    return pl.pallas_call(
        forward_kernel,
        grid=(width // 128, tokens // rows),
        in_specs=[
            part,
            full,
            full,
            pl.BlockSpec((rows, 128), lambda h, i: (i, 0)),
            pl.BlockSpec((tokens, 128), lambda h, i: (0, 0)),
            pl.BlockSpec((rows, 1), lambda h, i: (i, 0)),
            part,
            part,
        ],
        out_specs=[part, part],
        out_shape=[jax.ShapeDtypeStruct((tokens, width), F32)] * 2,
        compiler_params=pltpu.CompilerParams(vmem_limit_bytes=56 << 20),
        cost_estimate=pl.CostEstimate(
            flops=16 * tokens * tokens * width, bytes_accessed=16 * tokens * width, transcendentals=tokens * tokens * width // HEAD_DIM
        ),
        name="attention_forward",
    )(q, k, v, mq, mk, dead, k, v)


def backward_kernel(
    q_ref, k_ref, v_ref, do_ref, o_ref, l_ref, mq_ref, mk_ref, dead_ref, dq_ref, dk_ref, dv_ref, qa_s, doa_s, dq_s
):
    j = pl.program_id(1)
    tokens = q_ref.shape[0]
    rows = k_ref.shape[0]
    lane = lax.broadcasted_iota(jnp.int32, (tokens, 128), 1)
    klane = lax.broadcasted_iota(jnp.int32, (rows, 128), 1)

    @pl.when(j == 0)
    def _():
        do = do_ref[...].astype(F32)
        prod = do * o_ref[...]
        q = q_ref[...].astype(F32)
        logs = l_ref[...]
        for h in range(2):
            mine = (lane < HEAD_DIM) if h == 0 else (lane >= HEAD_DIM)
            other = lane - (HEAD_DIM if h == 0 else 0)
            delta = jnp.sum(jnp.where(mine, prod, 0.0), axis=1, keepdims=True)
            log = logs[:, 0:1] if h == 0 else logs[:, HEAD_DIM : HEAD_DIM + 1]
            a, b, c = three_parts(log)
            aug = mq_ref[...].astype(F32)
            aug = jnp.where(other == 5, -a, jnp.where(other == 6, -b, jnp.where(other == 7, -c, aug)))
            qa_s[h] = jnp.where(mine, q, aug).astype(BF16)
            a, b, c = three_parts(delta)
            aug = jnp.where(other == 5, -a, jnp.where(other == 6, -b, jnp.where(other == 7, -c, 0.0)))
            doa_s[h] = jnp.where(mine, do, aug).astype(BF16)
        dq_s[...] = jnp.zeros_like(dq_s)

    k = k_ref[...]
    v = v_ref[...]
    here = pl.ds(pl.multiple_of(j * rows, rows), rows)
    kf = k.astype(F32)
    vf = v.astype(F32)
    dead = dead_ref[...]
    dks, dvs = [], []
    for h in range(2):
        kmine = (klane < HEAD_DIM) if h == 0 else (klane >= HEAD_DIM)
        other = klane - (HEAD_DIM if h == 0 else 0)
        one = (other >= 5) & (other < 8)
        ka = jnp.where(kmine, k, mk_ref[...])
        va = jnp.where(kmine, v, jnp.where(one, jnp.ones_like(v), jnp.zeros_like(v)))
        p = jnp.exp(dot_nt(ka, qa_s[h]))
        ds = (p * dot_nt(va, doa_s[h])).astype(BF16)
        dk = dot_nn(ds, qa_s[h])
        dv = dot_nn(p.astype(BF16), doa_s[h])
        dq_s[h] += dot_tn(ds, ka)
        qd = qa_s[h, here, :].astype(F32)
        dod = doa_s[h, here, :].astype(F32)
        own = jnp.sum(jnp.where(kmine | one, qd * jnp.where(kmine, kf, 1.0), 0.0), axis=1, keepdims=True)
        own_p = jnp.where(dead > 0, jnp.exp(jnp.where(dead > 0, own, 0.0)), 0.0)
        own_d = jnp.sum(jnp.where(kmine | one, dod * jnp.where(kmine, vf, 1.0), 0.0), axis=1, keepdims=True)
        own_ds = own_p * own_d
        dks.append(dk + own_ds * qd)
        dvs.append(dv + own_p * dod)
        dq_s[h, here, :] += jnp.where(kmine, own_ds * kf, 0.0)
    dk_ref[...] = jnp.where(klane < HEAD_DIM, dks[0], dks[1]).astype(BF16)
    dv_ref[...] = jnp.where(klane < HEAD_DIM, dvs[0], dvs[1]).astype(BF16)

    @pl.when(j == pl.num_programs(1) - 1)
    def _():
        dq_ref[...] = jnp.where(lane < HEAD_DIM, dq_s[0], dq_s[1]).astype(BF16)


def attention_backward(q, k, v, do, o, logs, mq, mk, dead):
    tokens, width = q.shape
    rows = rows_per_step(tokens)
    part = pl.BlockSpec((rows, 128), lambda h, i: (i, h))
    full = pl.BlockSpec((tokens, 128), lambda h, i: (0, h))
    return pl.pallas_call(
        backward_kernel,
        grid=(width // 128, tokens // rows),
        in_specs=[
            full,
            part,
            part,
            full,
            full,
            full,
            pl.BlockSpec((tokens, 128), lambda h, i: (0, 0)),
            pl.BlockSpec((rows, 128), lambda h, i: (i, 0)),
            pl.BlockSpec((rows, 1), lambda h, i: (i, 0)),
        ],
        out_specs=[full, part, part],
        out_shape=[jax.ShapeDtypeStruct((tokens, width), BF16)] * 3,
        scratch_shapes=[
            pltpu.VMEM((2, tokens, 128), BF16),
            pltpu.VMEM((2, tokens, 128), BF16),
            pltpu.VMEM((2, tokens, 128), F32),
        ],
        compiler_params=pltpu.CompilerParams(vmem_limit_bytes=56 << 20),
        cost_estimate=pl.CostEstimate(
            flops=40 * tokens * tokens * width, bytes_accessed=24 * tokens * width, transcendentals=tokens * tokens * width // HEAD_DIM
        ),
        name="attention_backward",
    )(q, k, v, do, o, logs, mq, mk, dead)


def mask_terms(pair, live):
    lane = jnp.arange(128, dtype=jnp.int32)[None, :] % HEAD_DIM
    same = lane == pair[:, None]
    query = jnp.where(lane < 4, same, lane == 4).astype(BF16)
    key = jnp.where(
        lane < 4,
        jnp.where(same, 0.0, -BIG),
        jnp.where(lane == 4, jnp.where(live[:, None], 0.0, -BIG), ((lane >= 5) & (lane < 8)).astype(F32)),
    ).astype(BF16)
    return query, key, 1.0 - live.astype(F32)[:, None]


def gelu_parts(g):
    c = 0.7978845608028654
    t = jnp.tanh(c * (g + 0.044715 * g * g * g))
    act = 0.5 * g * (1.0 + t)
    slope = 0.5 * (1.0 + t) + 0.5 * g * (1.0 - t * t) * c * (1.0 + 3 * 0.044715 * g * g)
    return act, slope


def local(
    dps,
    seqs,
    tokens,
    query_weight,
    key_weight,
    value_weight,
    out_weight,
    gate_weight,
    up_weight,
    down_weight,
    attention_gain,
    feedforward_gain,
    pair_lengths,
    live_mask,
    out_grad,
):
    mine, dim = tokens.shape
    units = gate_weight.shape[1]
    half = seqs // 2
    width = dim // seqs
    chips = dps // 2
    d = lax.axis_index("dp")
    s = lax.axis_index("seq")
    core = d % 2
    high = (s >= half).astype(jnp.int32)
    low = s % half
    member = core * half + low
    moved = core != high

    def move(value, target):
        pairs = []
        for i in range(dps * seqs):
            to = target(i // seqs, i % seqs)
            if to is not None:
                pairs.append((i, to[0] * seqs + to[1]))
        return lax.ppermute(value, AXES, pairs)

    def trade(value):
        def target(dd, ss):
            return (dd ^ 1, (ss + half) % seqs) if dd % 2 != ss // half else None

        return move(value, target)

    def with_core(value):
        return move(value, lambda dd, ss: (dd ^ 1, ss))

    def with_chip(value, bit):
        return move(value, lambda dd, ss: (dd ^ bit, ss))

    def with_seq(value, bit):
        return move(value, lambda dd, ss: (dd, ss ^ bit))

    def with_member(value, bit):
        return with_core(value) if bit == half else with_seq(value, bit)

    bits = []
    while (1 << len(bits)) < seqs:
        bits.append(1 << len(bits))
    chip_bits = []
    while (2 << len(chip_bits)) < dps:
        chip_bits.append(2 << len(chip_bits))

    def gather_row(value):
        value = value[None]
        for bit in bits:
            value = jnp.concatenate([value, with_member(value, bit)], axis=0)
        return value

    def to_tokens(value):
        value = value.reshape(seqs, mine, width)
        for bit in bits:
            value = value.reshape(value.shape[0] // 2, 2, mine, value.shape[2])
            keep, come = value[:, 0], with_member(value[:, 1], bit)
            upper = (member & bit) != 0
            value = jnp.concatenate([jnp.where(upper, come, keep), jnp.where(upper, keep, come)], axis=2)
        return value[0]

    def to_heads(value):
        value = value[None]
        for bit in reversed(bits):
            first, second = jnp.split(value, 2, axis=2)
            upper = (member & bit) != 0
            come = with_member(jnp.where(upper, first, second), bit)
            value = jnp.stack([jnp.where(upper, second, first), come], axis=1)
            value = value.reshape(-1, mine, value.shape[3])
        return value.reshape(seqs * mine, width)

    def row_sum(value):
        value = value.reshape(seqs, mine, dim)
        for bit in reversed(bits):
            keep, give = value[: value.shape[0] // 2], value[value.shape[0] // 2 :]
            value = keep + with_member(give.astype(BF16), bit).astype(F32)
        return value[0]

    def over_chips(value, order):
        cols = value.shape[1]
        rows = value.shape[0] // chips
        value = value.reshape((2,) * len(chip_bits) + (rows, cols))
        left = list(reversed(chip_bits))
        for bit in order:
            axis = left.index(bit)
            left.pop(axis)
            upper = ((d & bit) != 0).astype(jnp.int32)
            give = lax.dynamic_index_in_dim(value, 1 - upper, axis, keepdims=False)
            keep = lax.dynamic_index_in_dim(value, upper, axis, keepdims=False)
            come = with_chip(give, bit)
            value = (keep.astype(F32) + come.astype(F32)).astype(BF16)
        return value.reshape(rows, cols)

    def over_seq(value):
        for i in range(half - 1):
            come = move(
                value,
                lambda dd, ss: (dd, i + 1) if ss == i else ((dd, seqs - 2 - i) if ss == seqs - 1 - i else None),
            )
            value = (value.astype(F32) + come.astype(F32)).astype(BF16)
        come = move(value, lambda dd, ss: (dd, seqs - 1 - ss) if ss in (half - 1, half) else None)
        value = (value.astype(F32) + come.astype(F32)).astype(BF16)
        for i in reversed(range(half - 1)):
            come = move(
                value,
                lambda dd, ss: (dd, i) if ss == i + 1 else ((dd, seqs - 1 - i) if ss == seqs - 2 - i else None),
            )
            value = jnp.where((s == i) | (s == seqs - 1 - i), come, value)
        return value

    def my_core(value, axis, other=False):
        shape = value.shape
        size = shape[axis] // dps
        value = value.reshape(shape[:axis] + (chips, 2, size) + shape[axis + 1 :])
        value = lax.dynamic_index_in_dim(value, (1 - core) if other else core, axis + 1, keepdims=False)
        return value.reshape(shape[:axis] + (chips * size,) + shape[axis + 1 :])

    bounds = jnp.cumsum(pair_lengths[0])[:-1]
    place = s * mine + jnp.arange(mine, dtype=jnp.int32)
    pair = jnp.sum((place[:, None] >= bounds[None, :]).astype(jnp.int32), axis=1)
    code = (2 * pair + (live_mask > 0)).astype(BF16)
    lines = -(-mine // dim)
    code = jnp.pad(code, (0, 16 * dim * (-(-lines // 16)) - mine)).reshape(-1, dim)
    packed = jnp.concatenate([tokens, code], axis=0)
    packed = jnp.where(moved, trade(packed), packed)
    row = gather_row(packed)
    x_row = row[:, :mine].reshape(seqs * mine, dim)
    code_row = row[:, mine:].reshape(seqs, -1)[:, :mine].reshape(-1).astype(jnp.int32)
    mask_query, mask_key, dead = mask_terms(code_row // 2, code_row % 2 == 1)
    x = packed[:mine].astype(F32)
    dy = jnp.where(moved, trade(out_grad), out_grad)

    def scaled(v, gain):
        return v * lax.rsqrt(jnp.mean(v * v, axis=1, keepdims=True) + EPS) * gain[None, :]

    def heads_of(weight):
        return lax.dynamic_slice_in_dim(weight, member * width, width, axis=1)

    n1_row = scaled(x_row.astype(F32), attention_gain).astype(BF16)
    wq, wk, wv = heads_of(query_weight), heads_of(key_weight), heads_of(value_weight)
    lanes = -(-width // 128) * 128
    widen = (lambda v: jnp.pad(v, ((0, 0), (0, lanes - width)))) if lanes != width else (lambda v: v)
    q, k, v = [widen(dot_nn(n1_row, w).astype(BF16)) for w in (wq, wk, wv)]
    o_heads, logs = attention_forward(q, k, v, mask_query, mask_key, dead)
    o = to_tokens(o_heads[:, :width].astype(BF16))

    h = x + dot_nn(o, out_weight)
    h_scale = lax.rsqrt(jnp.mean(h * h, axis=1, keepdims=True) + EPS)
    n2 = (h * h_scale * feedforward_gain[None, :]).astype(BF16)
    n2_both = jnp.concatenate([n2, with_core(n2)], axis=0)
    dy_both = jnp.concatenate([dy, with_core(dy)], axis=0)
    wg, wu, wd = my_core(gate_weight, 1), my_core(up_weight, 1), my_core(down_weight, 0)
    g = dot_nn(n2_both, wg)
    u = dot_nn(n2_both, wu)
    act, slope = gelu_parts(g)
    z = (act * u).astype(BF16)
    f = dot_nn(z, wd)
    layer_out = (h + f[:mine] + with_core(f[mine:].astype(BF16)).astype(F32)).astype(BF16)
    layer_out = jnp.where(moved, trade(layer_out), layer_out)

    grad_down = dot_tn(z, dy_both).astype(BF16)
    dz = dot_nt(dy_both, wd)
    dg = (dz * u * slope).astype(BF16)
    du = (dz * act).astype(BF16)
    grad_gate = dot_tn(n2_both, dg).astype(BF16)
    grad_upward = dot_tn(n2_both, du).astype(BF16)
    dn2_both = dot_nt(dg, wg) + dot_nt(du, wu)
    dn2 = dn2_both[:mine] + with_core(dn2_both[mine:].astype(BF16)).astype(F32)

    ghd = dn2 * feedforward_gain[None, :]
    dh = dy.astype(F32) + h_scale * ghd - h * (h_scale**3 * jnp.mean(h * ghd, axis=1, keepdims=True))
    gain_two = jnp.sum(dn2 * h * h_scale, axis=0)
    da = dh.astype(BF16)
    do = to_heads(dot_nt(da, out_weight).astype(BF16))
    o_both = jnp.concatenate([my_core(o, 1), with_core(my_core(o, 1, other=True))], axis=0)
    da_both = jnp.concatenate([da, with_core(da)], axis=0)
    grad_output = dot_tn(o_both, da_both).astype(BF16)

    dq, dk, dv = attention_backward(q, k, v, widen(do), o_heads, logs, mask_query, mask_key, dead)
    dq, dk, dv = dq[:, :width], dk[:, :width], dv[:, :width]
    dn1_row = dot_nt(dq, wq) + dot_nt(dk, wk) + dot_nt(dv, wv)
    x_row_scale = lax.rsqrt(jnp.mean(jnp.square(x_row.astype(F32)), axis=1, keepdims=True) + EPS)
    gain_one = jnp.sum(dn1_row * (x_row.astype(F32) * x_row_scale), axis=0)
    grad_heads = dot_tn(n1_row, jnp.concatenate([dq, dk, dv], axis=1)).astype(BF16)
    gains = jnp.pad(jnp.stack([gain_one, gain_two], axis=1), ((0, 0), (0, 126))).astype(BF16)
    dn1 = row_sum(dn1_row)

    x_scale = lax.rsqrt(jnp.mean(x * x, axis=1, keepdims=True) + EPS)
    gxd = dn1 * attention_gain[None, :]
    grad_tokens = dh + x_scale * gxd - x * (x_scale**3 * jnp.mean(x * gxd, axis=1, keepdims=True))
    grad_tokens = jnp.where(moved, trade(grad_tokens.astype(BF16)).astype(F32), grad_tokens)

    ahead, back = chip_bits, chip_bits[::-1]
    down_out = over_seq(over_chips(grad_down, ahead)).astype(F32)

    def both_cores(value):
        n = value.shape[0] // 2
        first, second = value[:n], value[n:]
        upper = core == 1
        come = with_core(jnp.where(upper, first, second))
        keep = jnp.where(upper, second, first)
        return jnp.stack([jnp.where(upper, come, keep), jnp.where(upper, keep, come)], axis=1)

    def unit_columns(value):
        n = value.shape[0]
        return value.reshape(n, 2, chips, units // dps).transpose(0, 2, 1, 3).reshape(n, units)

    gate_out = unit_columns(over_seq(both_cores(over_chips(grad_gate, back)))).astype(F32)
    upward_out = unit_columns(over_seq(both_cores(over_chips(grad_upward, ahead)))).astype(F32)
    output_out = over_seq(over_chips(grad_output, back)).astype(F32)

    heads_part = over_chips(jnp.concatenate([grad_heads, gains], axis=1), back)
    heads_part = both_cores(heads_part)
    heads_part = (heads_part.astype(F32) + with_seq(heads_part, half).astype(F32)).astype(BF16)
    heads_part = heads_part[None]
    for bit in bits[:-1]:
        come = with_seq(heads_part, bit)
        upper = (member & bit) != 0
        heads_part = jnp.concatenate([jnp.where(upper, come, heads_part), jnp.where(upper, heads_part, come)], axis=0)
    heads_part = heads_part.transpose(1, 2, 0, 3).reshape(-1, seqs, 3 * width + 128)
    query_out, key_out, value_out = [
        heads_part[:, :, i * width : (i + 1) * width].reshape(-1, dim).astype(F32) for i in range(3)
    ]
    gains_out = jnp.sum(heads_part[:, :, 3 * width : 3 * width + 2].astype(F32), axis=1)
    return (
        layer_out,
        grad_tokens,
        query_out,
        key_out,
        value_out,
        output_out,
        gate_out,
        upward_out,
        down_out,
        gains_out[:, 0],
        gains_out[:, 1],
    )


def solution(mesh):
    both = P(("dp", "seq"), None)
    rows = P("dp", None)
    return jax.shard_map(
        functools.partial(local, mesh.shape["dp"], mesh.shape["seq"]),
        mesh=mesh,
        in_specs=(both, P(), P(), P(), P(), P(), P(), P(), P(), P(), rows, P(("dp", "seq")), both),
        out_specs=(both, both, rows, rows, rows, rows, rows, rows, rows, P("dp"), P("dp")),
        check_vma=False,
    )
```

```python
import functools

import jax
import jax.numpy as jnp
from jax import lax
from jax.experimental import pallas as pl
from jax.experimental.pallas import tpu as pltpu
from jax.sharding import PartitionSpec as P

HEADS = 16
HEAD_DIM = 64
EPS = 1e-06
BIG = float(2.0**40)
F32 = jnp.float32
BF16 = jnp.bfloat16
AXES = ("dp", "seq")
MESH = pl.DeviceIdType.MESH
VMEM_BYTES = 62 << 20


def dot_nn(a, b):
    return lax.dot_general(a, b, (((1,), (0,)), ((), ())), preferred_element_type=F32)


def dot_nt(a, b):
    return lax.dot_general(a, b, (((1,), (1,)), ((), ())), preferred_element_type=F32)


def dot_tn(a, b):
    return lax.dot_general(a, b, (((0,), (0,)), ((), ())), preferred_element_type=F32)


def three_parts(v):
    high = v.astype(BF16).astype(F32)
    mid = (v - high).astype(BF16).astype(F32)
    low = (v - high - mid).astype(BF16).astype(F32)
    return high, mid, low


def forward_kernel(q_ref, k_ref, v_ref, mq_ref, mk_ref, dead_ref, kd_ref, vd_ref, o_ref, l_ref):
    lane = lax.broadcasted_iota(jnp.int32, q_ref.shape, 1)
    klane = lax.broadcasted_iota(jnp.int32, k_ref.shape, 1)
    q = q_ref[...]
    dead = dead_ref[...]
    qk = q.astype(F32) * kd_ref[...].astype(F32)
    outs, logs = [], []
    for h in range(2):
        mine = (lane < HEAD_DIM) if h == 0 else (lane >= HEAD_DIM)
        kmine = (klane < HEAD_DIM) if h == 0 else (klane >= HEAD_DIM)
        qa = jnp.where(mine, q, mq_ref[...])
        ka = jnp.where(kmine, k_ref[...], mk_ref[...])
        s = dot_nt(qa, ka)
        own = jnp.sum(jnp.where(mine, qk, 0.0), axis=1, keepdims=True)
        own = jnp.where(dead > 0, own, -BIG)
        top = jnp.maximum(jnp.max(s, axis=1, keepdims=True), own)
        p = jnp.exp(s - top).astype(BF16)
        va = jnp.where(kmine, v_ref[...], jnp.ones_like(v_ref[...]))
        r = dot_nn(p, va)
        own_p = jnp.exp(own - top)
        total = (r[:, HEAD_DIM : HEAD_DIM + 1] if h == 0 else r[:, 0:1]) + own_p
        outs.append((r + own_p * vd_ref[...].astype(F32)) * (1.0 / total))
        logs.append(top + jnp.log(total))
    o_ref[...] = jnp.where(lane < HEAD_DIM, outs[0], outs[1])
    l_ref[...] = jnp.where(lane < HEAD_DIM, logs[0], logs[1])


def rows_per_step(tokens):
    for rows in (512, 384, 256, 128):
        if tokens % rows == 0 and rows * tokens <= 800000:
            return rows
    return 128


def attention_forward(q, k, v, mq, mk, dead, group=None):
    tokens, width = q.shape
    rows = rows_per_step(tokens)
    first, count = (0, width // 128) if group is None else (group, 1)
    part = pl.BlockSpec((rows, 128), lambda h, i: (i, h + first))
    full = pl.BlockSpec((tokens, 128), lambda h, i: (0, h + first))
    out = pl.BlockSpec((rows, 128), lambda h, i: (i, h))
    return pl.pallas_call(
        forward_kernel,
        grid=(count, tokens // rows),
        in_specs=[
            part,
            full,
            full,
            pl.BlockSpec((rows, 128), lambda h, i: (i, 0)),
            pl.BlockSpec((tokens, 128), lambda h, i: (0, 0)),
            pl.BlockSpec((rows, 1), lambda h, i: (i, 0)),
            part,
            part,
        ],
        out_specs=[out, out],
        out_shape=[jax.ShapeDtypeStruct((tokens, 128 * count), F32)] * 2,
        compiler_params=pltpu.CompilerParams(vmem_limit_bytes=56 << 20),
        cost_estimate=pl.CostEstimate(
            flops=16 * tokens * tokens * 128 * count, bytes_accessed=16 * tokens * width, transcendentals=2 * tokens * tokens * count
        ),
        name="attention_forward",
    )(q, k, v, mq, mk, dead, k, v)


def backward_kernel(
    q_ref, k_ref, v_ref, do_ref, o_ref, l_ref, mq_ref, mk_ref, dead_ref, dq_ref, dk_ref, dv_ref, qa_s, doa_s, dq_s
):
    j = pl.program_id(1)
    tokens = q_ref.shape[0]
    rows = k_ref.shape[0]
    lane = lax.broadcasted_iota(jnp.int32, (tokens, 128), 1)
    klane = lax.broadcasted_iota(jnp.int32, (rows, 128), 1)

    @pl.when(j == 0)
    def _():
        do = do_ref[...].astype(F32)
        prod = do * o_ref[...]
        q = q_ref[...].astype(F32)
        logs = l_ref[...]
        for h in range(2):
            mine = (lane < HEAD_DIM) if h == 0 else (lane >= HEAD_DIM)
            other = lane - (HEAD_DIM if h == 0 else 0)
            delta = jnp.sum(jnp.where(mine, prod, 0.0), axis=1, keepdims=True)
            log = logs[:, 0:1] if h == 0 else logs[:, HEAD_DIM : HEAD_DIM + 1]
            a, b, c = three_parts(log)
            aug = mq_ref[...].astype(F32)
            aug = jnp.where(other == 5, -a, jnp.where(other == 6, -b, jnp.where(other == 7, -c, aug)))
            qa_s[h] = jnp.where(mine, q, aug).astype(BF16)
            a, b, c = three_parts(delta)
            aug = jnp.where(other == 5, -a, jnp.where(other == 6, -b, jnp.where(other == 7, -c, 0.0)))
            doa_s[h] = jnp.where(mine, do, aug).astype(BF16)
        dq_s[...] = jnp.zeros_like(dq_s)

    k = k_ref[...]
    v = v_ref[...]
    here = pl.ds(pl.multiple_of(j * rows, rows), rows)
    kf = k.astype(F32)
    vf = v.astype(F32)
    dead = dead_ref[...]
    dks, dvs = [], []
    for h in range(2):
        kmine = (klane < HEAD_DIM) if h == 0 else (klane >= HEAD_DIM)
        other = klane - (HEAD_DIM if h == 0 else 0)
        one = (other >= 5) & (other < 8)
        ka = jnp.where(kmine, k, mk_ref[...])
        va = jnp.where(kmine, v, jnp.where(one, jnp.ones_like(v), jnp.zeros_like(v)))
        p = jnp.exp(dot_nt(ka, qa_s[h]))
        ds = (p * dot_nt(va, doa_s[h])).astype(BF16)
        dk = dot_nn(ds, qa_s[h])
        dv = dot_nn(p.astype(BF16), doa_s[h])
        dq_s[h] += dot_tn(ds, ka)
        qd = qa_s[h, here, :].astype(F32)
        dod = doa_s[h, here, :].astype(F32)
        own = jnp.sum(jnp.where(kmine | one, qd * jnp.where(kmine, kf, 1.0), 0.0), axis=1, keepdims=True)
        own_p = jnp.where(dead > 0, jnp.exp(jnp.where(dead > 0, own, 0.0)), 0.0)
        own_d = jnp.sum(jnp.where(kmine | one, dod * jnp.where(kmine, vf, 1.0), 0.0), axis=1, keepdims=True)
        own_ds = own_p * own_d
        dks.append(dk + own_ds * qd)
        dvs.append(dv + own_p * dod)
        dq_s[h, here, :] += jnp.where(kmine, own_ds * kf, 0.0)
    dk_ref[...] = jnp.where(klane < HEAD_DIM, dks[0], dks[1]).astype(BF16)
    dv_ref[...] = jnp.where(klane < HEAD_DIM, dvs[0], dvs[1]).astype(BF16)

    @pl.when(j == pl.num_programs(1) - 1)
    def _():
        dq_ref[...] = jnp.where(lane < HEAD_DIM, dq_s[0], dq_s[1]).astype(BF16)


def attention_backward(q, k, v, do, o, logs, mq, mk, dead):
    tokens, width = q.shape
    rows = rows_per_step(tokens)
    part = pl.BlockSpec((rows, 128), lambda h, i: (i, h))
    full = pl.BlockSpec((tokens, 128), lambda h, i: (0, h))
    return pl.pallas_call(
        backward_kernel,
        grid=(width // 128, tokens // rows),
        in_specs=[
            full,
            part,
            part,
            full,
            full,
            full,
            pl.BlockSpec((tokens, 128), lambda h, i: (0, 0)),
            pl.BlockSpec((rows, 128), lambda h, i: (i, 0)),
            pl.BlockSpec((rows, 1), lambda h, i: (i, 0)),
        ],
        out_specs=[full, part, part],
        out_shape=[jax.ShapeDtypeStruct((tokens, width), BF16)] * 3,
        scratch_shapes=[
            pltpu.VMEM((2, tokens, 128), BF16),
            pltpu.VMEM((2, tokens, 128), BF16),
            pltpu.VMEM((2, tokens, 128), F32),
        ],
        compiler_params=pltpu.CompilerParams(vmem_limit_bytes=56 << 20),
        cost_estimate=pl.CostEstimate(
            flops=40 * tokens * tokens * width, bytes_accessed=24 * tokens * width, transcendentals=tokens * tokens * width // HEAD_DIM
        ),
        name="attention_backward",
    )(q, k, v, do, o, logs, mq, mk, dead)


def mask_terms(pair, live):
    lane = jnp.arange(128, dtype=jnp.int32)[None, :] % HEAD_DIM
    same = lane == pair[:, None]
    query = jnp.where(lane < 4, same, lane == 4).astype(BF16)
    key = jnp.where(
        lane < 4,
        jnp.where(same, 0.0, -BIG),
        jnp.where(lane == 4, jnp.where(live[:, None], 0.0, -BIG), ((lane >= 5) & (lane < 8)).astype(F32)),
    ).astype(BF16)
    return query, key, 1.0 - live.astype(F32)[:, None]


def gelu_parts(g):
    c = 0.7978845608028654
    t = jnp.tanh(c * (g + 0.044715 * g * g * g))
    act = 0.5 * g * (1.0 + t)
    slope = 0.5 * (1.0 + t) + 0.5 * g * (1.0 - t * t) * c * (1.0 + 3 * 0.044715 * g * g)
    return act, slope


def local_plain(
    dps,
    seqs,
    tokens,
    query_weight,
    key_weight,
    value_weight,
    out_weight,
    gate_weight,
    up_weight,
    down_weight,
    attention_gain,
    feedforward_gain,
    pair_lengths,
    live_mask,
    out_grad,
):
    mine, dim = tokens.shape
    units = gate_weight.shape[1]
    half = seqs // 2
    width = dim // seqs
    chips = dps // 2
    d = lax.axis_index("dp")
    s = lax.axis_index("seq")
    core = d % 2
    high = (s >= half).astype(jnp.int32)
    low = s % half
    member = core * half + low
    moved = core != high

    def move(value, target):
        pairs = []
        for i in range(dps * seqs):
            to = target(i // seqs, i % seqs)
            if to is not None:
                pairs.append((i, to[0] * seqs + to[1]))
        return lax.ppermute(value, AXES, pairs)

    def trade(value):
        def target(dd, ss):
            return (dd ^ 1, (ss + half) % seqs) if dd % 2 != ss // half else None

        return move(value, target)

    def with_core(value):
        return move(value, lambda dd, ss: (dd ^ 1, ss))

    def with_chip(value, bit):
        return move(value, lambda dd, ss: (dd ^ bit, ss))

    def with_seq(value, bit):
        return move(value, lambda dd, ss: (dd, ss ^ bit))

    def with_member(value, bit):
        return with_core(value) if bit == half else with_seq(value, bit)

    bits = []
    while (1 << len(bits)) < seqs:
        bits.append(1 << len(bits))
    chip_bits = []
    while (2 << len(chip_bits)) < dps:
        chip_bits.append(2 << len(chip_bits))

    def gather_row(value):
        value = value[None]
        for bit in bits:
            value = jnp.concatenate([value, with_member(value, bit)], axis=0)
        return value

    def to_tokens(value):
        value = value.reshape(seqs, mine, width)
        for bit in bits:
            value = value.reshape(value.shape[0] // 2, 2, mine, value.shape[2])
            keep, come = value[:, 0], with_member(value[:, 1], bit)
            upper = (member & bit) != 0
            value = jnp.concatenate([jnp.where(upper, come, keep), jnp.where(upper, keep, come)], axis=2)
        return value[0]

    def to_heads(value):
        value = value[None]
        for bit in reversed(bits):
            first, second = jnp.split(value, 2, axis=2)
            upper = (member & bit) != 0
            come = with_member(jnp.where(upper, first, second), bit)
            value = jnp.stack([jnp.where(upper, second, first), come], axis=1)
            value = value.reshape(-1, mine, value.shape[3])
        return value.reshape(seqs * mine, width)

    def row_sum(value):
        value = value.reshape(seqs, mine, dim)
        for bit in reversed(bits):
            keep, give = value[: value.shape[0] // 2], value[value.shape[0] // 2 :]
            value = keep + with_member(give.astype(BF16), bit).astype(F32)
        return value[0]

    def over_chips(value, order):
        cols = value.shape[1]
        rows = value.shape[0] // chips
        value = value.reshape((2,) * len(chip_bits) + (rows, cols))
        left = list(reversed(chip_bits))
        for bit in order:
            axis = left.index(bit)
            left.pop(axis)
            upper = ((d & bit) != 0).astype(jnp.int32)
            give = lax.dynamic_index_in_dim(value, 1 - upper, axis, keepdims=False)
            keep = lax.dynamic_index_in_dim(value, upper, axis, keepdims=False)
            come = with_chip(give, bit)
            value = (keep.astype(F32) + come.astype(F32)).astype(BF16)
        return value.reshape(rows, cols)

    def over_seq(value):
        for i in range(half - 1):
            come = move(
                value,
                lambda dd, ss: (dd, i + 1) if ss == i else ((dd, seqs - 2 - i) if ss == seqs - 1 - i else None),
            )
            value = (value.astype(F32) + come.astype(F32)).astype(BF16)
        come = move(value, lambda dd, ss: (dd, seqs - 1 - ss) if ss in (half - 1, half) else None)
        value = (value.astype(F32) + come.astype(F32)).astype(BF16)
        for i in reversed(range(half - 1)):
            come = move(
                value,
                lambda dd, ss: (dd, i) if ss == i + 1 else ((dd, seqs - 1 - i) if ss == seqs - 2 - i else None),
            )
            value = jnp.where((s == i) | (s == seqs - 1 - i), come, value)
        return value

    def my_core(value, axis, other=False):
        shape = value.shape
        size = shape[axis] // dps
        value = value.reshape(shape[:axis] + (chips, 2, size) + shape[axis + 1 :])
        value = lax.dynamic_index_in_dim(value, (1 - core) if other else core, axis + 1, keepdims=False)
        return value.reshape(shape[:axis] + (chips * size,) + shape[axis + 1 :])

    bounds = jnp.cumsum(pair_lengths[0])[:-1]
    place = s * mine + jnp.arange(mine, dtype=jnp.int32)
    pair = jnp.sum((place[:, None] >= bounds[None, :]).astype(jnp.int32), axis=1)
    code = (2 * pair + (live_mask > 0)).astype(BF16)
    lines = -(-mine // dim)
    code = jnp.pad(code, (0, 16 * dim * (-(-lines // 16)) - mine)).reshape(-1, dim)
    packed = jnp.concatenate([tokens, code], axis=0)
    packed = jnp.where(moved, trade(packed), packed)
    row = gather_row(packed)
    x_row = row[:, :mine].reshape(seqs * mine, dim)
    code_row = row[:, mine:].reshape(seqs, -1)[:, :mine].reshape(-1).astype(jnp.int32)
    mask_query, mask_key, dead = mask_terms(code_row // 2, code_row % 2 == 1)
    x = packed[:mine].astype(F32)
    dy = jnp.where(moved, trade(out_grad), out_grad)

    def scaled(v, gain):
        return v * lax.rsqrt(jnp.mean(v * v, axis=1, keepdims=True) + EPS) * gain[None, :]

    def heads_of(weight):
        return lax.dynamic_slice_in_dim(weight, member * width, width, axis=1)

    n1_row = scaled(x_row.astype(F32), attention_gain).astype(BF16)
    wq, wk, wv = heads_of(query_weight), heads_of(key_weight), heads_of(value_weight)
    lanes = -(-width // 128) * 128
    widen = (lambda v: jnp.pad(v, ((0, 0), (0, lanes - width)))) if lanes != width else (lambda v: v)
    q, k, v = [widen(dot_nn(n1_row, w).astype(BF16)) for w in (wq, wk, wv)]
    o_heads, logs = attention_forward(q, k, v, mask_query, mask_key, dead)
    o = to_tokens(o_heads[:, :width].astype(BF16))

    h = x + dot_nn(o, out_weight)
    h_scale = lax.rsqrt(jnp.mean(h * h, axis=1, keepdims=True) + EPS)
    n2 = (h * h_scale * feedforward_gain[None, :]).astype(BF16)
    n2_both = jnp.concatenate([n2, with_core(n2)], axis=0)
    dy_both = jnp.concatenate([dy, with_core(dy)], axis=0)
    wg, wu, wd = my_core(gate_weight, 1), my_core(up_weight, 1), my_core(down_weight, 0)
    g = dot_nn(n2_both, wg)
    u = dot_nn(n2_both, wu)
    act, slope = gelu_parts(g)
    z = (act * u).astype(BF16)
    f = dot_nn(z, wd)
    layer_out = (h + f[:mine] + with_core(f[mine:].astype(BF16)).astype(F32)).astype(BF16)
    layer_out = jnp.where(moved, trade(layer_out), layer_out)

    grad_down = dot_tn(z, dy_both).astype(BF16)
    dz = dot_nt(dy_both, wd)
    dg = (dz * u * slope).astype(BF16)
    du = (dz * act).astype(BF16)
    grad_gate = dot_tn(n2_both, dg).astype(BF16)
    grad_upward = dot_tn(n2_both, du).astype(BF16)
    dn2_both = dot_nt(dg, wg) + dot_nt(du, wu)
    dn2 = dn2_both[:mine] + with_core(dn2_both[mine:].astype(BF16)).astype(F32)

    ghd = dn2 * feedforward_gain[None, :]
    dh = dy.astype(F32) + h_scale * ghd - h * (h_scale**3 * jnp.mean(h * ghd, axis=1, keepdims=True))
    gain_two = jnp.sum(dn2 * h * h_scale, axis=0)
    da = dh.astype(BF16)
    do = to_heads(dot_nt(da, out_weight).astype(BF16))
    o_both = jnp.concatenate([my_core(o, 1), with_core(my_core(o, 1, other=True))], axis=0)
    da_both = jnp.concatenate([da, with_core(da)], axis=0)
    grad_output = dot_tn(o_both, da_both).astype(BF16)

    dq, dk, dv = attention_backward(q, k, v, widen(do), o_heads, logs, mask_query, mask_key, dead)
    dq, dk, dv = dq[:, :width], dk[:, :width], dv[:, :width]
    dn1_row = dot_nt(dq, wq) + dot_nt(dk, wk) + dot_nt(dv, wv)
    x_row_scale = lax.rsqrt(jnp.mean(jnp.square(x_row.astype(F32)), axis=1, keepdims=True) + EPS)
    gain_one = jnp.sum(dn1_row * (x_row.astype(F32) * x_row_scale), axis=0)
    grad_heads = dot_tn(n1_row, jnp.concatenate([dq, dk, dv], axis=1)).astype(BF16)
    gains = jnp.pad(jnp.stack([gain_one, gain_two], axis=1), ((0, 0), (0, 126))).astype(BF16)
    dn1 = row_sum(dn1_row)

    x_scale = lax.rsqrt(jnp.mean(x * x, axis=1, keepdims=True) + EPS)
    gxd = dn1 * attention_gain[None, :]
    grad_tokens = dh + x_scale * gxd - x * (x_scale**3 * jnp.mean(x * gxd, axis=1, keepdims=True))
    grad_tokens = jnp.where(moved, trade(grad_tokens.astype(BF16)).astype(F32), grad_tokens)

    ahead, back = chip_bits, chip_bits[::-1]
    down_out = over_seq(over_chips(grad_down, ahead)).astype(F32)

    def both_cores(value):
        n = value.shape[0] // 2
        first, second = value[:n], value[n:]
        upper = core == 1
        come = with_core(jnp.where(upper, first, second))
        keep = jnp.where(upper, second, first)
        return jnp.stack([jnp.where(upper, come, keep), jnp.where(upper, keep, come)], axis=1)

    def unit_columns(value):
        n = value.shape[0]
        return value.reshape(n, 2, chips, units // dps).transpose(0, 2, 1, 3).reshape(n, units)

    gate_out = unit_columns(over_seq(both_cores(over_chips(grad_gate, back)))).astype(F32)
    upward_out = unit_columns(over_seq(both_cores(over_chips(grad_upward, ahead)))).astype(F32)
    output_out = over_seq(over_chips(grad_output, back)).astype(F32)

    heads_part = over_chips(jnp.concatenate([grad_heads, gains], axis=1), back)
    heads_part = both_cores(heads_part)
    heads_part = (heads_part.astype(F32) + with_seq(heads_part, half).astype(F32)).astype(BF16)
    heads_part = heads_part[None]
    for bit in bits[:-1]:
        come = with_seq(heads_part, bit)
        upper = (member & bit) != 0
        heads_part = jnp.concatenate([jnp.where(upper, come, heads_part), jnp.where(upper, heads_part, come)], axis=0)
    heads_part = heads_part.transpose(1, 2, 0, 3).reshape(-1, seqs, 3 * width + 128)
    query_out, key_out, value_out = [
        heads_part[:, :, i * width : (i + 1) * width].reshape(-1, dim).astype(F32) for i in range(3)
    ]
    gains_out = jnp.sum(heads_part[:, :, 3 * width : 3 * width + 2].astype(F32), axis=1)
    return (
        layer_out,
        grad_tokens,
        query_out,
        key_out,
        value_out,
        output_out,
        gate_out,
        upward_out,
        down_out,
        gains_out[:, 0],
        gains_out[:, 1],
    )


def closing_kernel(
    dps,
    seqs,
    q_ref,
    k_ref,
    v_ref,
    do_ref,
    o0_ref,
    o1_ref,
    log0_ref,
    log1_ref,
    mq_ref,
    mk_ref,
    dead_ref,
    n1t_ref,
    wt_ref,
    x_ref,
    dh_ref,
    gain_ref,
    gate_ref,
    up_ref,
    da_ref,
    db_ref,
    out_ref,
    gt_o,
    gate_o,
    up_o,
    da_o,
    db_o,
    out_o,
    heads_o,
    gate_r,
    up_r,
    da_r,
    db_r,
    out_r,
    gate_c,
    up_c,
    da_c,
    db_c,
    out_c,
    gate_a,
    up_a,
    da_a,
    db_a,
    out_a,
    gate_z,
    up_z,
    da_z,
    db_z,
    out_z,
    qa_s,
    doa_s,
    dq_s,
    dqkv_s,
    hs_s,
    h1_r,
    h2_s,
    h2_r,
    hk_s,
    hc_s,
    hh_s,
    hh_r,
    cs_s,
    cr_r,
    zs_s,
    zr_r,
    gs_s,
    dn_s,
    send_sem,
    recv_sem,
):
    d = lax.axis_index("dp")
    s = lax.axis_index("seq")
    core = d % 2
    xb = (d // 2) % 2
    yb = (d // 4) % 2
    low = s % 2
    high = s // 2
    sibling = (d + 1 - 2 * core, s)
    over_x = (d + 2 - 4 * xb, s)
    over_y = (d + 4 - 8 * yb, s)
    over_z = (d, s + 1 - 2 * low)
    over_high = (d, s + 2 - 4 * high)
    swapped = (d + 1 - 2 * core, s + 2 - 4 * high)
    third = (d, 3 - s)
    inner = (s == 1) | (s == 2)
    outer = (s == 0) | (s == 3)
    moved = core != high

    barrier = pltpu.get_barrier_semaphore()
    for other in (sibling, over_x, over_y, over_z, over_high, swapped, third):
        pl.semaphore_signal(barrier, inc=1, device_id=other, device_id_type=MESH)
    pl.semaphore_wait(barrier, 7)

    used = []

    class Copy:
        def __init__(self, src, dst, target):
            self.parts = (src, dst, target, len(used))
            used.append(self)

        def made(self):
            src, dst, target, i = self.parts
            return pltpu.make_async_remote_copy(
                src_ref=src, dst_ref=dst, send_sem=send_sem.at[i], recv_sem=recv_sem.at[i], device_id=target, device_id_type=MESH
            )

        def start(self):
            self.made().start()

        def wait_recv(self):
            self.made().wait_recv()

        def wait_send(self):
            self.made().wait_send()

    copy = Copy

    def rows_at(start, size):
        return pl.ds(pl.multiple_of(start * size, size), size)

    class Item:
        pass

    items = []
    for src, second, bit, r, c, a, z, o in (
        (da_ref, over_x, xb, da_r, da_c, da_a, da_z, da_o),
        (db_ref, over_y, yb, db_r, db_c, db_a, db_z, db_o),
        (out_ref, over_y, yb, out_r, out_c, out_a, out_z, out_o),
        (gate_ref, over_x, xb, gate_r, gate_c, gate_a, gate_z, gate_o),
        (up_ref, over_y, yb, up_r, up_c, up_a, up_z, up_o),
    ):
        it = Item()
        it.src, it.bit, it.r, it.c, it.a, it.z, it.o = src, bit, r, c, a, z, o
        n = r.shape[0] // 2
        it.n = n
        it.chip = copy(src.at[rows_at(1 - bit, 2 * n)], r, second)
        it.core = copy(c, a.at[core], sibling)
        it.in1 = copy(a, z.at[0], (d, jnp.where(s == 0, 1, 2)))
        it.in2 = copy(a, z.at[1], third)
        it.out = copy(o, o, (d, jnp.where(s == 1, 0, 3)))
        items.append(it)

    def step0(it):
        it.chip.start()

    def step1(it):
        it.chip.wait_recv()
        n = it.n
        base = it.bit * (2 * n)

        def summed(which):
            mine = it.src[pl.ds(pl.multiple_of(base + which * n, n), n), :].astype(F32)
            return (mine + it.r[rows_at(which, n), :].astype(F32)).astype(BF16)

        it.c[...] = summed(1 - core)
        it.core.start()
        it.a[core] = summed(core)

    def step2(it):
        it.core.wait_recv()

        @pl.when(outer)
        def _():
            it.in1.start()

    def step3(it):
        @pl.when(inner)
        def _():
            it.in1.wait_recv()
            it.a[...] = (it.a[...].astype(F32) + it.z[0].astype(F32)).astype(BF16)
            it.in2.start()

    def step4(it):
        @pl.when(inner)
        def _():
            it.in2.wait_recv()
            it.o[...] = (it.a[...].astype(F32) + it.z[1].astype(F32)).astype(BF16)
            it.out.start()

    def step5(it):
        @pl.when(outer)
        def _():
            it.out.wait_recv()

    def finish(it):
        it.chip.wait_send()
        it.core.wait_send()

        @pl.when(outer)
        def _():
            it.in1.wait_send()

        @pl.when(inner)
        def _():
            it.in2.wait_send()
            it.out.wait_send()

    for it in items:
        step0(it)
    down_a, down_b, outp, gate, upw = items

    block = hk_s.shape[1]
    half = block // 2
    firsts = ((over_x, over_y), (over_y, over_x))
    heads = []
    for p in range(2):
        h = Item()
        h.p1 = [copy(hs_s.at[p, i], h1_r.at[p, i], firsts[p][0]) for i in range(2)]
        h.p2 = copy(h2_s.at[p], h2_r.at[p], firsts[p][1])
        h.core = copy(hk_s.at[p, rows_at(1 - core, half)], hc_s.at[p, core], sibling)
        h.high = copy(hh_s.at[p], hh_r.at[p], over_high)
        h.z = copy(heads_o.at[low, p], heads_o.at[low, p], over_z)
        heads.append(h)

    def product(p, yy, xx):
        left = n1t_ref[rows_at(2 * yy + xx, block), :]
        return dot_nn(left, dqkv_s[p])

    def heads0(p):
        h = heads[p]
        for turn in range(2):
            if p == 0:
                i = (1 - yb) if turn == 0 else yb
                hs_s[p, turn] = product(p, i, 1 - xb).astype(BF16)
            else:
                i = (1 - xb) if turn == 0 else xb
                hs_s[p, turn] = product(p, 1 - yb, i).astype(BF16)
            h.p1[turn].start()

    def heads1(p):
        h = heads[p]
        part = product(p, 1 - yb, xb) if p == 0 else product(p, yb, 1 - xb)
        h.p1[0].wait_recv()
        h2_s[p] = (part + h1_r[p, 0].astype(F32)).astype(BF16)
        h.p2.start()

    def heads2(p):
        h = heads[p]
        part = product(p, yb, xb)
        h.p1[1].wait_recv()
        part = part + h1_r[p, 1].astype(F32)
        h.p2.wait_recv()
        hk_s[p] = (part + h2_r[p].astype(F32)).astype(BF16)
        h.core.start()
        hc_s[p, core] = hk_s[p, rows_at(core, half), :]

    def heads3(p):
        h = heads[p]
        h.core.wait_recv()
        hh_s[p] = hc_s[p]
        h.high.start()

    def heads4(p):
        h = heads[p]
        h.high.wait_recv()
        heads_o[low, p] = (hh_s[p].astype(F32) + hh_r[p].astype(F32)).astype(BF16)
        h.z.start()

    def heads5(p):
        heads[p].z.wait_recv()

    def finish_heads(p):
        h = heads[p]
        for made in h.p1 + [h.p2, h.core, h.high, h.z]:
            made.wait_send()

    tokens = q_ref.shape[0]
    rows = 256
    steps = tokens // rows
    lane = lax.broadcasted_iota(jnp.int32, (tokens, 128), 1)
    klane = lax.broadcasted_iota(jnp.int32, (rows, 128), 1)

    def prepare(p):
        cols = slice(128 * p, 128 * p + 128)
        do = do_ref[:, cols].astype(F32)
        prod = do * (o0_ref, o1_ref)[p][...]
        qq = q_ref[:, cols].astype(F32)
        logs = (log0_ref, log1_ref)[p][...]
        for h in range(2):
            mine = (lane < HEAD_DIM) if h == 0 else (lane >= HEAD_DIM)
            other = lane - (HEAD_DIM if h == 0 else 0)
            delta = jnp.sum(jnp.where(mine, prod, 0.0), axis=1, keepdims=True)
            log = logs[:, 0:1] if h == 0 else logs[:, HEAD_DIM : HEAD_DIM + 1]
            a, b, c = three_parts(log)
            aug = mq_ref[...].astype(F32)
            aug = jnp.where(other == 5, -a, jnp.where(other == 6, -b, jnp.where(other == 7, -c, aug)))
            qa_s[h] = jnp.where(mine, qq, aug).astype(BF16)
            a, b, c = three_parts(delta)
            aug = jnp.where(other == 5, -a, jnp.where(other == 6, -b, jnp.where(other == 7, -c, 0.0)))
            doa_s[h] = jnp.where(mine, do, aug).astype(BF16)
        dq_s[...] = jnp.zeros_like(dq_s)

    def attend(p, j):
        cols = slice(128 * p, 128 * p + 128)
        here = pl.ds(pl.multiple_of(j * rows, rows), rows)
        k = k_ref[here, cols]
        v = v_ref[here, cols]
        kf = k.astype(F32)
        vf = v.astype(F32)
        dead = dead_ref[here, :]
        mk = mk_ref[here, :]
        dks, dvs = [], []
        for h in range(2):
            kmine = (klane < HEAD_DIM) if h == 0 else (klane >= HEAD_DIM)
            other = klane - (HEAD_DIM if h == 0 else 0)
            one = (other >= 5) & (other < 8)
            ka = jnp.where(kmine, k, mk)
            va = jnp.where(kmine, v, jnp.where(one, jnp.ones_like(v), jnp.zeros_like(v)))
            pr = jnp.exp(dot_nt(ka, qa_s[h]))
            ds = (pr * dot_nt(va, doa_s[h])).astype(BF16)
            dk = dot_nn(ds, qa_s[h])
            dv = dot_nn(pr.astype(BF16), doa_s[h])
            dq_s[h] += dot_tn(ds, ka)
            qd = qa_s[h, here, :].astype(F32)
            dod = doa_s[h, here, :].astype(F32)
            own = jnp.sum(jnp.where(kmine | one, qd * jnp.where(kmine, kf, 1.0), 0.0), axis=1, keepdims=True)
            own_p = jnp.where(dead > 0, jnp.exp(jnp.where(dead > 0, own, 0.0)), 0.0)
            own_d = jnp.sum(jnp.where(kmine | one, dod * jnp.where(kmine, vf, 1.0), 0.0), axis=1, keepdims=True)
            own_ds = own_p * own_d
            dks.append(dk + own_ds * qd)
            dvs.append(dv + own_p * dod)
            dq_s[h, here, :] += jnp.where(kmine, own_ds * kf, 0.0)
        dqkv_s[p, here, 128:256] = jnp.where(klane < HEAD_DIM, dks[0], dks[1]).astype(BF16)
        dqkv_s[p, here, 256:384] = jnp.where(klane < HEAD_DIM, dvs[0], dvs[1]).astype(BF16)

    after = (
        {
            1: lambda: (step1(down_a), step1(down_b)),
            2: lambda: (step2(down_a), step2(down_b)),
            3: lambda: step1(outp),
            4: lambda: (step3(down_a), step3(down_b), step2(outp)),
            5: lambda: (step1(gate), step1(upw)),
        },
        {
            0: lambda: (step2(gate), step2(upw), step3(outp), heads1(0)),
            1: lambda: (step4(down_a), step4(down_b), heads2(0)),
            2: lambda: (step4(outp), heads3(0)),
            3: lambda: (step3(gate), step5(down_a), step5(down_b)),
            4: lambda: (step3(upw), heads4(0)),
            5: lambda: (step4(gate), step5(outp)),
        },
    )
    for p in range(2):
        prepare(p)

        @pl.loop(0, steps)
        def _(j, p=p):
            attend(p, j)
            for i, work in after[p].items():

                @pl.when(j == i)
                def _(work=work):
                    work()

        dqkv_s[p, :, 0:128] = jnp.where(lane < HEAD_DIM, dq_s[0], dq_s[1]).astype(BF16)
        heads0(p)

    mine = x_ref.shape[0]
    cut = mine // 3

    def dn1_of(i):
        at = pl.ds(i * mine, mine)
        width = dqkv_s.shape[2]
        return dot_nn(dqkv_s[0, at, :], wt_ref[0:width, :]) + dot_nn(dqkv_s[1, at, :], wt_ref[width : 2 * width, :])

    to_core = [copy(cs_s.at[i], cr_r.at[i], sibling) for i in range(2)]
    to_z = [copy(zs_s.at[pl.ds(i * cut, cut)], zr_r.at[pl.ds(i * cut, cut)], over_z) for i in range(3)]
    to_home = [copy(gs_s.at[pl.ds(i * cut, cut)], gt_o.at[pl.ds(i * cut, cut)], swapped) for i in range(3)]
    for i in (1, 0):
        cs_s[i] = dn1_of(2 + i).astype(BF16)
        to_core[i].start()
    dn = dn1_of(1)
    to_core[1].wait_recv()
    zs_s[...] = (dn + cr_r[1].astype(F32)).astype(BF16)
    for made in to_z:
        made.start()
    heads1(1)
    dn_s[...] = dn1_of(0)
    step4(upw)
    to_core[0].wait_recv()
    heads2(1)
    heads3(1)
    for i in range(3):
        at = pl.ds(i * cut, cut)
        to_z[i].wait_recv()
        dn = dn_s[at, :] + cr_r[0, at, :].astype(F32) + zr_r[at, :].astype(F32)
        x = x_ref[at, :].astype(F32)
        scale = lax.rsqrt(jnp.mean(x * x, axis=1, keepdims=True) + EPS)
        dn = dn * gain_ref[...]
        grad = dh_ref[at, :] + scale * dn - x * (scale * scale * scale * jnp.mean(x * dn, axis=1, keepdims=True))
        gs_s[at, :] = grad.astype(BF16)

        @pl.when(moved)
        def _():
            to_home[i].start()

        @pl.when(jnp.logical_not(moved))
        def _():
            gt_o[at, :] = gs_s[at, :]

    step5(gate)
    step5(upw)
    heads4(1)
    heads5(0)
    heads5(1)
    for it in items:
        finish(it)
    for p in range(2):
        finish_heads(p)
    for made in to_core + to_z:
        made.wait_send()

    @pl.when(moved)
    def _():
        for made in to_home:
            made.wait_recv()
            made.wait_send()


def closing(dps, seqs, q, k, v, do, o0, o1, log0, log1, mq, mk, dead, n1t, wt, x, dh, gain, gate, up, down_a, down_b, outp):
    tokens = q.shape[0]
    mine, dim = x.shape
    vmem = pl.BlockSpec(memory_space=pltpu.VMEM)
    weights = (gate, up, down_a, down_b, outp)

    def shard(w):
        return (w.shape[0] // 4, w.shape[1])

    finals = [jax.ShapeDtypeStruct((2,) + shard(w), BF16) for w in weights]
    block = dim // (dps // 2)
    wide = 3 * 128
    scratch = [pltpu.VMEM((2 * shard(w)[0], shard(w)[1]), BF16) for w in weights]
    scratch += [pltpu.VMEM(shard(w), BF16) for w in weights]
    scratch += [pltpu.VMEM((2,) + shard(w), BF16) for w in weights]
    scratch += [pltpu.VMEM((2, 2) + shard(w), BF16) for w in weights]
    scratch += [
        pltpu.VMEM((2, tokens, 128), BF16),
        pltpu.VMEM((2, tokens, 128), BF16),
        pltpu.VMEM((2, tokens, 128), F32),
        pltpu.VMEM((2, tokens, wide), BF16),
        pltpu.VMEM((2, 2, block, wide), BF16),
        pltpu.VMEM((2, 2, block, wide), BF16),
        pltpu.VMEM((2, block, wide), BF16),
        pltpu.VMEM((2, block, wide), BF16),
        pltpu.VMEM((2, block, wide), BF16),
        pltpu.VMEM((2, 2, block // 2, wide), BF16),
        pltpu.VMEM((2, 2, block // 2, wide), BF16),
        pltpu.VMEM((2, 2, block // 2, wide), BF16),
        pltpu.VMEM((2, mine, dim), BF16),
        pltpu.VMEM((2, mine, dim), BF16),
        pltpu.VMEM((mine, dim), BF16),
        pltpu.VMEM((mine, dim), BF16),
        pltpu.VMEM((mine, dim), BF16),
        pltpu.VMEM((mine, dim), F32),
    ]
    copies = 5 * 5 + 2 * 6 + 2 + 3 + 3
    return pl.pallas_call(
        functools.partial(closing_kernel, dps, seqs),
        in_specs=[vmem] * 21,
        out_specs=[vmem] * 7,
        out_shape=[jax.ShapeDtypeStruct((mine, dim), BF16)]
        + finals
        + [jax.ShapeDtypeStruct((2, 2, 2, block // 2, wide), BF16)],
        scratch_shapes=scratch + [pltpu.SemaphoreType.DMA((copies,)), pltpu.SemaphoreType.DMA((copies,))],
        compiler_params=pltpu.CompilerParams(collective_id=0, has_side_effects=True, vmem_limit_bytes=VMEM_BYTES),
        cost_estimate=pl.CostEstimate(
            flops=40 * tokens * tokens * 256, bytes_accessed=40 << 20, transcendentals=4 * tokens * tokens
        ),
        name="closing",
    )(q, k, v, do, o0, o1, log0, log1, mq, mk, dead, n1t, wt, x, dh, gain, gate, up, down_a, down_b, outp)


def local_fused(
    dps,
    seqs,
    tokens,
    query_weight,
    key_weight,
    value_weight,
    out_weight,
    gate_weight,
    up_weight,
    down_weight,
    attention_gain,
    feedforward_gain,
    pair_lengths,
    live_mask,
    out_grad,
):
    mine, dim = tokens.shape
    width = dim // seqs
    d = lax.axis_index("dp")
    s = lax.axis_index("seq")
    core = d % 2
    x_bit = (d // 2) % 2
    y_bit = (d // 4) % 2
    member = core * 2 + s % 2
    moved = core != s // 2

    def move(value, target):
        pairs = []
        for i in range(dps * seqs):
            to = target(i // seqs, i % seqs)
            if to is not None:
                pairs.append((i, to[0] * seqs + to[1]))
        return lax.ppermute(value, AXES, pairs)

    def trade(value):
        return move(value, lambda dd, ss: (dd ^ 1, ss ^ 2) if dd % 2 != ss // 2 else None)

    def with_core(value):
        return move(value, lambda dd, ss: (dd ^ 1, ss))

    def with_chip(value, bit):
        return move(value, lambda dd, ss: (dd ^ bit, ss))

    def with_member(value, bit):
        return with_core(value) if bit == 2 else move(value, lambda dd, ss: (dd, ss ^ 1))

    def half_of(value, which, axis):
        size = value.shape[axis] // 2
        return lax.dynamic_slice_in_dim(value, which * size, size, axis=axis)

    def with_sibling(value):
        return jnp.concatenate([value, with_core(value)], axis=0)

    def to_tokens(value):
        value = value.reshape(seqs, mine, -1)
        for bit in (1, 2):
            value = value.reshape(value.shape[0] // 2, 2, mine, value.shape[2])
            keep, come = value[:, 0], with_member(value[:, 1], bit)
            upper = (member & bit) != 0
            value = jnp.concatenate([jnp.where(upper, come, keep), jnp.where(upper, keep, come)], axis=2)
        return value[0]

    def to_heads(value):
        value = value[None]
        for bit in (2, 1):
            first, second = jnp.split(value, 2, axis=2)
            upper = (member & bit) != 0
            come = with_member(jnp.where(upper, first, second), bit)
            value = jnp.stack([jnp.where(upper, second, first), come], axis=1)
            value = value.reshape(-1, mine, value.shape[3])
        return value.reshape(seqs * mine, -1)

    def rms(v):
        return lax.rsqrt(jnp.mean(v * v, axis=1, keepdims=True) + EPS)

    bounds = jnp.cumsum(pair_lengths[0])[:-1]
    place = s * mine + jnp.arange(mine, dtype=jnp.int32)
    pair = jnp.sum((place[:, None] >= bounds[None, :]).astype(jnp.int32), axis=1)
    code = (2 * pair + (live_mask > 0)).astype(BF16)
    lines = 16 * -(-mine // (16 * dim))
    code = jnp.pad(code, (0, lines * dim - mine)).reshape(lines, dim)
    packed = jnp.concatenate([tokens, code], axis=0)
    come = move(packed, lambda dd, ss: (dd ^ 1, ss ^ 2) if dd % 2 != ss // 2 else (dd, ss ^ 1))
    late = move(come, lambda dd, ss: (dd, ss ^ 1) if dd % 2 != ss // 2 else None)
    row = jnp.stack([jnp.where(moved, come, packed), jnp.where(moved, late, come)])
    row = jnp.concatenate([row, with_core(row)], axis=0)
    x_row = row[:, :mine].reshape(seqs * mine, dim)
    code_row = row[:, mine:].reshape(seqs, -1)[:, :mine].reshape(-1).astype(jnp.int32)
    mask_query, mask_key, dead = mask_terms(code_row // 2, code_row % 2 == 1)
    x_low = row[0, :mine]
    x = x_low.astype(F32)
    out_grad, _ = lax.optimization_barrier((out_grad, row))
    dy = jnp.where(moved, trade(out_grad), out_grad)
    dy_both = with_sibling(dy)

    def heads_of(weight):
        return lax.dynamic_slice_in_dim(weight, member * width, width, axis=1)

    xf = x_row.astype(F32)
    n1_row = (xf * rms(xf) * attention_gain[None, :]).astype(BF16)
    wqkv = [heads_of(query_weight), heads_of(key_weight), heads_of(value_weight)]
    q, k, v = [dot_nn(n1_row, w).astype(BF16) for w in wqkv]
    o_parts, log_parts, o_tokens = [], [], []
    for i in range(2):
        o_part, log_part = attention_forward(q, k, v, mask_query, mask_key, dead, i)
        o_parts.append(o_part)
        log_parts.append(log_part)
        o_tokens.append(to_tokens(o_part.astype(BF16)))
    by_pair = out_weight.reshape(seqs, 2, 128, dim)

    h = x + dot_nn(o_tokens[0], by_pair[:, 0].reshape(-1, dim)) + dot_nn(o_tokens[1], by_pair[:, 1].reshape(-1, dim))
    h_scale = rms(h)
    n2 = (h * h_scale * feedforward_gain[None, :]).astype(BF16)
    n2_both = with_sibling(n2)
    wg, wu, wd = half_of(gate_weight, core, 1), half_of(up_weight, core, 1), half_of(down_weight, core, 0)
    g = dot_nn(n2_both, wg)
    u = dot_nn(n2_both, wu)
    act, slope = gelu_parts(g)
    z = (act * u).astype(BF16)
    z_come = with_core(z)
    z_come = jnp.concatenate([z_come[mine:], z_come[:mine]], axis=0)
    dz = dot_nt(dy_both, wd)
    dg = (dz * u * slope).astype(BF16)
    du = (dz * act).astype(BF16)

    def blocks(parts):
        return jnp.concatenate(parts, axis=1)

    def half_sum(left, right, which, bit):
        come = with_chip(dot_tn(half_of(left, 1 - which, 1), right).astype(BF16), bit)
        return (dot_tn(half_of(left, which, 1), right) + come.astype(F32)).astype(BF16)

    chip = dim // (dps // 2)
    n2_x = blocks([n2_both[:, (2 * yy + xx) * chip : (2 * yy + xx + 1) * chip] for xx in range(2) for yy in range(2)])
    gate_sum = half_sum(n2_both, dg, y_bit, 4)
    up_sum = half_sum(n2_x, du, x_bit, 2)
    dy_part = half_of(dy_both, core, 1)
    down_own = dot_tn(z, dy_part).astype(BF16)
    down_far = dot_tn(z_come, dy_part).astype(BF16)
    cut = dy_part.shape[1] // 2
    own_y = y_bit == core
    come = with_chip(jnp.where(own_y, down_far[:, :cut], down_own[:, :cut]), 4)
    down_a = (jnp.where(own_y, down_own[:, :cut], down_far[:, :cut]).astype(F32) + come.astype(F32)).astype(BF16)

    def of_x(which):
        one = half_of(down_own[:, cut:], which, 0)
        two = half_of(down_far[:, cut:], which, 0)
        return jnp.concatenate([jnp.where(core == 0, one, two), jnp.where(core == 0, two, one)], axis=0)

    come = with_chip(of_x(1 - x_bit), 2)
    down_b = (of_x(x_bit).astype(F32) + come.astype(F32)).astype(BF16)

    f = dot_nn(z, wd)
    layer_out = (h + f[:mine] + with_core(f[mine:].astype(BF16)).astype(F32)).astype(BF16)
    layer_out = jnp.where(moved, trade(layer_out), layer_out)

    dn2_both = dot_nt(dg, wg) + dot_nt(du, wu)
    dn2 = dn2_both[:mine] + with_core(dn2_both[mine:].astype(BF16)).astype(F32)
    ghd = dn2 * feedforward_gain[None, :]
    dh = dy.astype(F32) + h_scale * ghd - h * (h_scale**3 * jnp.mean(h * ghd, axis=1, keepdims=True))
    da = dh.astype(BF16)
    do = to_heads(dot_nt(da, out_weight).astype(BF16))

    o_x = blocks([o_tokens[i][:, (2 * yy + xx) * 128 : (2 * yy + xx + 1) * 128] for xx in range(2) for yy in range(2) for i in range(2)])
    o_x = with_sibling(o_x)
    da_part = jnp.concatenate([half_of(da, core, 1), with_core(half_of(da, 1 - core, 1))], axis=0)
    out_sum = half_sum(o_x, da_part, x_bit, 2)

    wt = jnp.concatenate([w[:, i * 128 : (i + 1) * 128].T for i in range(2) for w in wqkv], axis=0)
    grad_tokens, gate_out, up_out, down_a, down_b, out_out, heads_out = closing(
        dps, seqs, q, k, v, do, o_parts[0], o_parts[1], log_parts[0], log_parts[1], mask_query, mask_key, dead,
        n1_row.T, wt, x_low, dh, attention_gain[None, :], gate_sum, up_sum, down_a, down_b, out_sum,
    )

    def columns(value):
        return jnp.concatenate([value[0], value[1]], axis=1)

    gate_out, up_out, out_out = [columns(w).astype(F32) for w in (gate_out, up_out, out_out)]
    down_out = jnp.concatenate([down_a[0], down_b[0], down_a[1], down_b[1]], axis=1).astype(F32)
    projections = [
        jnp.concatenate(
            [heads_out[m % 2, i, m // 2, :, t * 128 : (t + 1) * 128] for m in range(seqs) for i in range(2)], axis=1
        ).astype(F32)
        for t in range(3)
    ]

    def shard(weight):
        size = weight.shape[0] // dps
        return lax.dynamic_slice_in_dim(weight, d * size, size, axis=0).astype(F32)

    gain_one = sum(jnp.sum(g_out * shard(w), axis=1) for g_out, w in zip(projections, (query_weight, key_weight, value_weight)))
    gain_two = jnp.sum(gate_out * shard(gate_weight), axis=1) + jnp.sum(up_out * shard(up_weight), axis=1)
    gain_one = gain_one / shard(attention_gain)
    gain_two = gain_two / shard(feedforward_gain)
    return (layer_out, grad_tokens.astype(F32), *projections, out_out, gate_out, up_out, down_out, gain_one, gain_two)


def solution(mesh):
    both = P(("dp", "seq"), None)
    rows = P("dp", None)
    dps, seqs = mesh.shape["dp"], mesh.shape["seq"]
    local = local_fused if (dps, seqs) == (8, 4) else local_plain
    return jax.shard_map(
        functools.partial(local, dps, seqs),
        mesh=mesh,
        in_specs=(both, P(), P(), P(), P(), P(), P(), P(), P(), P(), rows, P(("dp", "seq")), both),
        out_specs=(both, both, rows, rows, rows, rows, rows, rows, rows, P("dp"), P("dp")),
        check_vma=False,
    )
```

```python
import functools

import jax
import jax.numpy as jnp
from jax import lax
from jax.experimental import pallas as pl
from jax.experimental.pallas import tpu as pltpu
from jax.sharding import PartitionSpec as P

HEADS = 16
HEAD_DIM = 64
EPS = 1e-06
BIG = float(2.0**40)
F32 = jnp.float32
BF16 = jnp.bfloat16
AXES = ("dp", "seq")
MESH = pl.DeviceIdType.MESH
VMEM_BYTES = 62 << 20
ITEMS, FETCHED = 7, 11


def dot_nn(a, b):
    return lax.dot_general(a, b, (((1,), (0,)), ((), ())), preferred_element_type=F32)


def dot_nt(a, b):
    return lax.dot_general(a, b, (((1,), (1,)), ((), ())), preferred_element_type=F32)


def dot_tn(a, b):
    return lax.dot_general(a, b, (((0,), (0,)), ((), ())), preferred_element_type=F32)


def three_parts(v):
    high = v.astype(BF16).astype(F32)
    mid = (v - high).astype(BF16).astype(F32)
    low = (v - high - mid).astype(BF16).astype(F32)
    return high, mid, low


def forward_kernel(keep_queries, q_ref, k_ref, v_ref, mq_ref, mk_ref, dead_ref, kd_ref, vd_ref, o_ref, l_ref):
    lane = lax.broadcasted_iota(jnp.int32, q_ref.shape, 1)
    klane = lax.broadcasted_iota(jnp.int32, k_ref.shape, 1)
    q = q_ref[...]
    dead = dead_ref[...]
    qk = q.astype(F32) * kd_ref[...].astype(F32)
    outs, logs = [], []
    for h in range(2):
        mine = (lane < HEAD_DIM) if h == 0 else (lane >= HEAD_DIM)
        kmine = (klane < HEAD_DIM) if h == 0 else (klane >= HEAD_DIM)
        qa = jnp.where(mine, q, mq_ref[...])
        ka = jnp.where(kmine, k_ref[...], mk_ref[...])
        s = dot_nt(qa, ka)
        own = jnp.sum(jnp.where(mine, qk, 0.0), axis=1, keepdims=True)
        own = jnp.where(dead > 0, own, -BIG)
        top = jnp.maximum(jnp.max(s, axis=1, keepdims=True), own)
        p = jnp.exp(s - top).astype(BF16)
        va = jnp.where(kmine, v_ref[...], jnp.ones_like(v_ref[...]))
        r = dot_nn(p, va)
        own_p = jnp.exp(own - top)
        total = (r[:, HEAD_DIM : HEAD_DIM + 1] if h == 0 else r[:, 0:1]) + own_p
        outs.append((r + own_p * vd_ref[...].astype(F32)) * (1.0 / total))
        log = top + jnp.log(total)
        if keep_queries:
            other = lane - (HEAD_DIM if h == 0 else 0)
            a, b, c = three_parts(log)
            aug = mq_ref[...].astype(F32)
            aug = jnp.where(other == 5, -a, jnp.where(other == 6, -b, jnp.where(other == 7, -c, aug)))
            l_ref[h] = jnp.where(mine, q.astype(F32), aug).astype(BF16)
        logs.append(log)
    o_ref[...] = jnp.where(lane < HEAD_DIM, outs[0], outs[1])
    if not keep_queries:
        l_ref[...] = jnp.where(lane < HEAD_DIM, logs[0], logs[1])


def rows_per_step(tokens):
    for rows in (512, 384, 256, 128):
        if tokens % rows == 0 and rows * tokens <= 800000:
            return rows
    return 128


def attention_forward(q, k, v, mq, mk, dead, group=None):
    tokens, width = q.shape
    rows = rows_per_step(tokens)
    first, count = (0, width // 128) if group is None else (group, 1)
    part = pl.BlockSpec((rows, 128), lambda h, i: (i, h + first))
    full = pl.BlockSpec((tokens, 128), lambda h, i: (0, h + first))
    out = pl.BlockSpec((rows, 128), lambda h, i: (i, h))
    keep = group is not None
    log_out, log_shape = out, jax.ShapeDtypeStruct((tokens, 128 * count), F32)
    if keep:
        log_out = pl.BlockSpec((2, rows, 128), lambda h, i: (0, i, 0))
        log_shape = jax.ShapeDtypeStruct((2, tokens, 128), BF16)
    return pl.pallas_call(
        functools.partial(forward_kernel, keep),
        grid=(count, tokens // rows),
        in_specs=[
            part,
            full,
            full,
            pl.BlockSpec((rows, 128), lambda h, i: (i, 0)),
            pl.BlockSpec((tokens, 128), lambda h, i: (0, 0)),
            pl.BlockSpec((rows, 1), lambda h, i: (i, 0)),
            part,
            part,
        ],
        out_specs=[out, log_out],
        out_shape=[jax.ShapeDtypeStruct((tokens, 128 * count), F32), log_shape],
        compiler_params=pltpu.CompilerParams(vmem_limit_bytes=56 << 20),
        cost_estimate=pl.CostEstimate(
            flops=16 * tokens * tokens * 128 * count, bytes_accessed=16 * tokens * width, transcendentals=2 * tokens * tokens * count
        ),
        name="attention_forward",
    )(q, k, v, mq, mk, dead, k, v)


def backward_kernel(
    q_ref, k_ref, v_ref, do_ref, o_ref, l_ref, mq_ref, mk_ref, dead_ref, dq_ref, dk_ref, dv_ref, qa_s, doa_s, dq_s
):
    j = pl.program_id(1)
    tokens = q_ref.shape[0]
    rows = k_ref.shape[0]
    lane = lax.broadcasted_iota(jnp.int32, (tokens, 128), 1)
    klane = lax.broadcasted_iota(jnp.int32, (rows, 128), 1)

    @pl.when(j == 0)
    def _():
        do = do_ref[...].astype(F32)
        prod = do * o_ref[...]
        q = q_ref[...].astype(F32)
        logs = l_ref[...]
        for h in range(2):
            mine = (lane < HEAD_DIM) if h == 0 else (lane >= HEAD_DIM)
            other = lane - (HEAD_DIM if h == 0 else 0)
            delta = jnp.sum(jnp.where(mine, prod, 0.0), axis=1, keepdims=True)
            log = logs[:, 0:1] if h == 0 else logs[:, HEAD_DIM : HEAD_DIM + 1]
            a, b, c = three_parts(log)
            aug = mq_ref[...].astype(F32)
            aug = jnp.where(other == 5, -a, jnp.where(other == 6, -b, jnp.where(other == 7, -c, aug)))
            qa_s[h] = jnp.where(mine, q, aug).astype(BF16)
            a, b, c = three_parts(delta)
            aug = jnp.where(other == 5, -a, jnp.where(other == 6, -b, jnp.where(other == 7, -c, 0.0)))
            doa_s[h] = jnp.where(mine, do, aug).astype(BF16)
        dq_s[...] = jnp.zeros_like(dq_s)

    k = k_ref[...]
    v = v_ref[...]
    here = pl.ds(pl.multiple_of(j * rows, rows), rows)
    kf = k.astype(F32)
    vf = v.astype(F32)
    dead = dead_ref[...]
    dks, dvs = [], []
    for h in range(2):
        kmine = (klane < HEAD_DIM) if h == 0 else (klane >= HEAD_DIM)
        other = klane - (HEAD_DIM if h == 0 else 0)
        one = (other >= 5) & (other < 8)
        ka = jnp.where(kmine, k, mk_ref[...])
        va = jnp.where(kmine, v, jnp.where(one, jnp.ones_like(v), jnp.zeros_like(v)))
        p = jnp.exp(dot_nt(ka, qa_s[h]))
        ds = (p * dot_nt(va, doa_s[h])).astype(BF16)
        dk = dot_nn(ds, qa_s[h])
        dv = dot_nn(p.astype(BF16), doa_s[h])
        dq_s[h] += dot_tn(ds, ka)
        qd = qa_s[h, here, :].astype(F32)
        dod = doa_s[h, here, :].astype(F32)
        own = jnp.sum(jnp.where(kmine | one, qd * jnp.where(kmine, kf, 1.0), 0.0), axis=1, keepdims=True)
        own_p = jnp.where(dead > 0, jnp.exp(jnp.where(dead > 0, own, 0.0)), 0.0)
        own_d = jnp.sum(jnp.where(kmine | one, dod * jnp.where(kmine, vf, 1.0), 0.0), axis=1, keepdims=True)
        own_ds = own_p * own_d
        dks.append(dk + own_ds * qd)
        dvs.append(dv + own_p * dod)
        dq_s[h, here, :] += jnp.where(kmine, own_ds * kf, 0.0)
    dk_ref[...] = jnp.where(klane < HEAD_DIM, dks[0], dks[1]).astype(BF16)
    dv_ref[...] = jnp.where(klane < HEAD_DIM, dvs[0], dvs[1]).astype(BF16)

    @pl.when(j == pl.num_programs(1) - 1)
    def _():
        dq_ref[...] = jnp.where(lane < HEAD_DIM, dq_s[0], dq_s[1]).astype(BF16)


def attention_backward(q, k, v, do, o, logs, mq, mk, dead):
    tokens, width = q.shape
    rows = rows_per_step(tokens)
    part = pl.BlockSpec((rows, 128), lambda h, i: (i, h))
    full = pl.BlockSpec((tokens, 128), lambda h, i: (0, h))
    return pl.pallas_call(
        backward_kernel,
        grid=(width // 128, tokens // rows),
        in_specs=[
            full,
            part,
            part,
            full,
            full,
            full,
            pl.BlockSpec((tokens, 128), lambda h, i: (0, 0)),
            pl.BlockSpec((rows, 128), lambda h, i: (i, 0)),
            pl.BlockSpec((rows, 1), lambda h, i: (i, 0)),
        ],
        out_specs=[full, part, part],
        out_shape=[jax.ShapeDtypeStruct((tokens, width), BF16)] * 3,
        scratch_shapes=[
            pltpu.VMEM((2, tokens, 128), BF16),
            pltpu.VMEM((2, tokens, 128), BF16),
            pltpu.VMEM((2, tokens, 128), F32),
        ],
        compiler_params=pltpu.CompilerParams(vmem_limit_bytes=56 << 20),
        cost_estimate=pl.CostEstimate(
            flops=40 * tokens * tokens * width, bytes_accessed=24 * tokens * width, transcendentals=tokens * tokens * width // HEAD_DIM
        ),
        name="attention_backward",
    )(q, k, v, do, o, logs, mq, mk, dead)


def mask_terms(pair, live):
    lane = jnp.arange(128, dtype=jnp.int32)[None, :] % HEAD_DIM
    same = lane == pair[:, None]
    query = jnp.where(lane < 4, same, lane == 4).astype(BF16)
    key = jnp.where(
        lane < 4,
        jnp.where(same, 0.0, -BIG),
        jnp.where(lane == 4, jnp.where(live[:, None], 0.0, -BIG), ((lane >= 5) & (lane < 8)).astype(F32)),
    ).astype(BF16)
    return query, key, 1.0 - live.astype(F32)[:, None]


def gelu_parts(g):
    c = 0.7978845608028654
    t = jnp.tanh(c * (g + 0.044715 * g * g * g))
    act = 0.5 * g * (1.0 + t)
    slope = 0.5 * (1.0 + t) + 0.5 * g * (1.0 - t * t) * c * (1.0 + 3 * 0.044715 * g * g)
    return act, slope


def local_plain(
    dps,
    seqs,
    tokens,
    query_weight,
    key_weight,
    value_weight,
    out_weight,
    gate_weight,
    up_weight,
    down_weight,
    attention_gain,
    feedforward_gain,
    pair_lengths,
    live_mask,
    out_grad,
):
    mine, dim = tokens.shape
    units = gate_weight.shape[1]
    half = seqs // 2
    width = dim // seqs
    chips = dps // 2
    d = lax.axis_index("dp")
    s = lax.axis_index("seq")
    core = d % 2
    high = (s >= half).astype(jnp.int32)
    low = s % half
    member = core * half + low
    moved = core != high

    def move(value, target):
        pairs = []
        for i in range(dps * seqs):
            to = target(i // seqs, i % seqs)
            if to is not None:
                pairs.append((i, to[0] * seqs + to[1]))
        return lax.ppermute(value, AXES, pairs)

    def trade(value):
        def target(dd, ss):
            return (dd ^ 1, (ss + half) % seqs) if dd % 2 != ss // half else None

        return move(value, target)

    def with_core(value):
        return move(value, lambda dd, ss: (dd ^ 1, ss))

    def with_chip(value, bit):
        return move(value, lambda dd, ss: (dd ^ bit, ss))

    def with_seq(value, bit):
        return move(value, lambda dd, ss: (dd, ss ^ bit))

    def with_member(value, bit):
        return with_core(value) if bit == half else with_seq(value, bit)

    bits = []
    while (1 << len(bits)) < seqs:
        bits.append(1 << len(bits))
    chip_bits = []
    while (2 << len(chip_bits)) < dps:
        chip_bits.append(2 << len(chip_bits))

    def gather_row(value):
        value = value[None]
        for bit in bits:
            value = jnp.concatenate([value, with_member(value, bit)], axis=0)
        return value

    def to_tokens(value):
        value = value.reshape(seqs, mine, width)
        for bit in bits:
            value = value.reshape(value.shape[0] // 2, 2, mine, value.shape[2])
            keep, come = value[:, 0], with_member(value[:, 1], bit)
            upper = (member & bit) != 0
            value = jnp.concatenate([jnp.where(upper, come, keep), jnp.where(upper, keep, come)], axis=2)
        return value[0]

    def to_heads(value):
        value = value[None]
        for bit in reversed(bits):
            first, second = jnp.split(value, 2, axis=2)
            upper = (member & bit) != 0
            come = with_member(jnp.where(upper, first, second), bit)
            value = jnp.stack([jnp.where(upper, second, first), come], axis=1)
            value = value.reshape(-1, mine, value.shape[3])
        return value.reshape(seqs * mine, width)

    def row_sum(value):
        value = value.reshape(seqs, mine, dim)
        for bit in reversed(bits):
            keep, give = value[: value.shape[0] // 2], value[value.shape[0] // 2 :]
            value = keep + with_member(give.astype(BF16), bit).astype(F32)
        return value[0]

    def over_chips(value, order):
        cols = value.shape[1]
        rows = value.shape[0] // chips
        value = value.reshape((2,) * len(chip_bits) + (rows, cols))
        left = list(reversed(chip_bits))
        for bit in order:
            axis = left.index(bit)
            left.pop(axis)
            upper = ((d & bit) != 0).astype(jnp.int32)
            give = lax.dynamic_index_in_dim(value, 1 - upper, axis, keepdims=False)
            keep = lax.dynamic_index_in_dim(value, upper, axis, keepdims=False)
            come = with_chip(give, bit)
            value = (keep.astype(F32) + come.astype(F32)).astype(BF16)
        return value.reshape(rows, cols)

    def over_seq(value):
        for i in range(half - 1):
            come = move(
                value,
                lambda dd, ss: (dd, i + 1) if ss == i else ((dd, seqs - 2 - i) if ss == seqs - 1 - i else None),
            )
            value = (value.astype(F32) + come.astype(F32)).astype(BF16)
        come = move(value, lambda dd, ss: (dd, seqs - 1 - ss) if ss in (half - 1, half) else None)
        value = (value.astype(F32) + come.astype(F32)).astype(BF16)
        for i in reversed(range(half - 1)):
            come = move(
                value,
                lambda dd, ss: (dd, i) if ss == i + 1 else ((dd, seqs - 1 - i) if ss == seqs - 2 - i else None),
            )
            value = jnp.where((s == i) | (s == seqs - 1 - i), come, value)
        return value

    def my_core(value, axis, other=False):
        shape = value.shape
        size = shape[axis] // dps
        value = value.reshape(shape[:axis] + (chips, 2, size) + shape[axis + 1 :])
        value = lax.dynamic_index_in_dim(value, (1 - core) if other else core, axis + 1, keepdims=False)
        return value.reshape(shape[:axis] + (chips * size,) + shape[axis + 1 :])

    bounds = jnp.cumsum(pair_lengths[0])[:-1]
    place = s * mine + jnp.arange(mine, dtype=jnp.int32)
    pair = jnp.sum((place[:, None] >= bounds[None, :]).astype(jnp.int32), axis=1)
    code = (2 * pair + (live_mask > 0)).astype(BF16)
    lines = -(-mine // dim)
    code = jnp.pad(code, (0, 16 * dim * (-(-lines // 16)) - mine)).reshape(-1, dim)
    packed = jnp.concatenate([tokens, code], axis=0)
    packed = jnp.where(moved, trade(packed), packed)
    row = gather_row(packed)
    x_row = row[:, :mine].reshape(seqs * mine, dim)
    code_row = row[:, mine:].reshape(seqs, -1)[:, :mine].reshape(-1).astype(jnp.int32)
    mask_query, mask_key, dead = mask_terms(code_row // 2, code_row % 2 == 1)
    x = packed[:mine].astype(F32)
    dy = jnp.where(moved, trade(out_grad), out_grad)

    def scaled(v, gain):
        return v * lax.rsqrt(jnp.mean(v * v, axis=1, keepdims=True) + EPS) * gain[None, :]

    def heads_of(weight):
        return lax.dynamic_slice_in_dim(weight, member * width, width, axis=1)

    n1_row = scaled(x_row.astype(F32), attention_gain).astype(BF16)
    wq, wk, wv = heads_of(query_weight), heads_of(key_weight), heads_of(value_weight)
    lanes = -(-width // 128) * 128
    widen = (lambda v: jnp.pad(v, ((0, 0), (0, lanes - width)))) if lanes != width else (lambda v: v)
    q, k, v = [widen(dot_nn(n1_row, w).astype(BF16)) for w in (wq, wk, wv)]
    o_heads, logs = attention_forward(q, k, v, mask_query, mask_key, dead)
    o = to_tokens(o_heads[:, :width].astype(BF16))

    h = x + dot_nn(o, out_weight)
    h_scale = lax.rsqrt(jnp.mean(h * h, axis=1, keepdims=True) + EPS)
    n2 = (h * h_scale * feedforward_gain[None, :]).astype(BF16)
    n2_both = jnp.concatenate([n2, with_core(n2)], axis=0)
    dy_both = jnp.concatenate([dy, with_core(dy)], axis=0)
    wg, wu, wd = my_core(gate_weight, 1), my_core(up_weight, 1), my_core(down_weight, 0)
    g = dot_nn(n2_both, wg)
    u = dot_nn(n2_both, wu)
    act, slope = gelu_parts(g)
    z = (act * u).astype(BF16)
    f = dot_nn(z, wd)
    layer_out = (h + f[:mine] + with_core(f[mine:].astype(BF16)).astype(F32)).astype(BF16)
    layer_out = jnp.where(moved, trade(layer_out), layer_out)

    grad_down = dot_tn(z, dy_both).astype(BF16)
    dz = dot_nt(dy_both, wd)
    dg = (dz * u * slope).astype(BF16)
    du = (dz * act).astype(BF16)
    grad_gate = dot_tn(n2_both, dg).astype(BF16)
    grad_upward = dot_tn(n2_both, du).astype(BF16)
    dn2_both = dot_nt(dg, wg) + dot_nt(du, wu)
    dn2 = dn2_both[:mine] + with_core(dn2_both[mine:].astype(BF16)).astype(F32)

    ghd = dn2 * feedforward_gain[None, :]
    dh = dy.astype(F32) + h_scale * ghd - h * (h_scale**3 * jnp.mean(h * ghd, axis=1, keepdims=True))
    gain_two = jnp.sum(dn2 * h * h_scale, axis=0)
    da = dh.astype(BF16)
    do = to_heads(dot_nt(da, out_weight).astype(BF16))
    o_both = jnp.concatenate([my_core(o, 1), with_core(my_core(o, 1, other=True))], axis=0)
    da_both = jnp.concatenate([da, with_core(da)], axis=0)
    grad_output = dot_tn(o_both, da_both).astype(BF16)

    dq, dk, dv = attention_backward(q, k, v, widen(do), o_heads, logs, mask_query, mask_key, dead)
    dq, dk, dv = dq[:, :width], dk[:, :width], dv[:, :width]
    dn1_row = dot_nt(dq, wq) + dot_nt(dk, wk) + dot_nt(dv, wv)
    x_row_scale = lax.rsqrt(jnp.mean(jnp.square(x_row.astype(F32)), axis=1, keepdims=True) + EPS)
    gain_one = jnp.sum(dn1_row * (x_row.astype(F32) * x_row_scale), axis=0)
    grad_heads = dot_tn(n1_row, jnp.concatenate([dq, dk, dv], axis=1)).astype(BF16)
    gains = jnp.pad(jnp.stack([gain_one, gain_two], axis=1), ((0, 0), (0, 126))).astype(BF16)
    dn1 = row_sum(dn1_row)

    x_scale = lax.rsqrt(jnp.mean(x * x, axis=1, keepdims=True) + EPS)
    gxd = dn1 * attention_gain[None, :]
    grad_tokens = dh + x_scale * gxd - x * (x_scale**3 * jnp.mean(x * gxd, axis=1, keepdims=True))
    grad_tokens = jnp.where(moved, trade(grad_tokens.astype(BF16)).astype(F32), grad_tokens)

    ahead, back = chip_bits, chip_bits[::-1]
    down_out = over_seq(over_chips(grad_down, ahead)).astype(F32)

    def both_cores(value):
        n = value.shape[0] // 2
        first, second = value[:n], value[n:]
        upper = core == 1
        come = with_core(jnp.where(upper, first, second))
        keep = jnp.where(upper, second, first)
        return jnp.stack([jnp.where(upper, come, keep), jnp.where(upper, keep, come)], axis=1)

    def unit_columns(value):
        n = value.shape[0]
        return value.reshape(n, 2, chips, units // dps).transpose(0, 2, 1, 3).reshape(n, units)

    gate_out = unit_columns(over_seq(both_cores(over_chips(grad_gate, back)))).astype(F32)
    upward_out = unit_columns(over_seq(both_cores(over_chips(grad_upward, ahead)))).astype(F32)
    output_out = over_seq(over_chips(grad_output, back)).astype(F32)

    heads_part = over_chips(jnp.concatenate([grad_heads, gains], axis=1), back)
    heads_part = both_cores(heads_part)
    heads_part = (heads_part.astype(F32) + with_seq(heads_part, half).astype(F32)).astype(BF16)
    heads_part = heads_part[None]
    for bit in bits[:-1]:
        come = with_seq(heads_part, bit)
        upper = (member & bit) != 0
        heads_part = jnp.concatenate([jnp.where(upper, come, heads_part), jnp.where(upper, heads_part, come)], axis=0)
    heads_part = heads_part.transpose(1, 2, 0, 3).reshape(-1, seqs, 3 * width + 128)
    query_out, key_out, value_out = [
        heads_part[:, :, i * width : (i + 1) * width].reshape(-1, dim).astype(F32) for i in range(3)
    ]
    gains_out = jnp.sum(heads_part[:, :, 3 * width : 3 * width + 2].astype(F32), axis=1)
    return (
        layer_out,
        grad_tokens,
        query_out,
        key_out,
        value_out,
        output_out,
        gate_out,
        upward_out,
        down_out,
        gains_out[:, 0],
        gains_out[:, 1],
    )


def closing_kernel(mask_k_ref, gain_one_ref, gain_two_ref, *refs):
    refs = list(refs)

    def take(n):
        taken, refs[:n] = refs[:n], []
        return taken

    fetched = take(FETCHED)
    dn2_give, ot_ref, wt_ref, x_ref = take(4)
    gives, keeps = take(ITEMS - 1), take(ITEMS - 1)
    (gt_o,) = take(1)
    finals = take(ITEMS)
    (heads_o,) = take(1)
    fetched_s = take(FETCHED)
    (dn2_s, h_s, dy_s, wo_s, qa0_s, qa1_s, k_s, v_s, o0_s, o1_s, n1t_s) = fetched_s
    out_give, out_keep = take(2)
    firsts_r, seconds_s, seconds_r, cores_s, accs, lines = [take(ITEMS) for _ in range(6)]
    doa_s, dq_s, dqkv_s, hs_s, h1_r, h2_s, h2_r, hk_s, hc_s, hh_s, hh_r = take(11)
    dn2_r, da_s, dap_s, dcr_s, dorow_s = take(5)
    dh_s, do_s = h_s, dn2_r
    cs_s, cr_r, zr_r, send_sem, recv_sem, local_sem = take(6)

    d = lax.axis_index("dp")
    s = lax.axis_index("seq")
    core = d % 2
    xb = (d // 2) % 2
    yb = (d // 4) % 2
    low = s % 2
    high = s // 2
    sibling = (d + 1 - 2 * core, s)
    over_x = (d + 2 - 4 * xb, s)
    over_y = (d + 4 - 8 * yb, s)
    over_z = (d, s + 1 - 2 * low)
    over_high = (d, s + 2 - 4 * high)
    swapped = (d + 1 - 2 * core, s + 2 - 4 * high)
    third = (d, 3 - s)
    inner = (s == 1) | (s == 2)
    outer = (s == 0) | (s == 3)
    moved = core != high

    barrier = pltpu.get_barrier_semaphore()
    for other in (sibling, over_x, over_y, over_z, over_high, swapped, third):
        pl.semaphore_signal(barrier, inc=1, device_id=other, device_id_type=MESH)
    pl.semaphore_wait(barrier, 7)

    counts = {"remote": 0, "local": 0}

    class Copy:
        def __init__(self, src, dst, target):
            self.parts = (src, dst, target, counts["remote"])
            counts["remote"] += 1

        def made(self):
            src, dst, target, i = self.parts
            return pltpu.make_async_remote_copy(
                src_ref=src, dst_ref=dst, send_sem=send_sem.at[i], recv_sem=recv_sem.at[i], device_id=target, device_id_type=MESH
            )

        def start(self):
            self.made().start()

        def wait_recv(self):
            self.made().wait_recv()

        def wait_send(self):
            self.made().wait_send()

    copy = Copy

    class Fetch:
        def __init__(self, src, dst):
            self.parts = (src, dst, counts["local"])
            counts["local"] += 1

        def made(self):
            src, dst, i = self.parts
            return pltpu.make_async_copy(src, dst, local_sem.at[i])

        def start(self):
            self.made().start()

        def wait(self):
            self.made().wait()

    def rows_at(start, size):
        return pl.ds(pl.multiple_of(start * size, size), size)

    def lanes_at(start, size):
        return pl.ds(pl.multiple_of(start * size, size), size)

    class Item:
        pass

    items = []
    along_x, along_y = (over_x, xb), (over_y, yb)
    for i in range(ITEMS):
        it = Item()
        first, second = (along_x, along_y) if i % 2 or i == ITEMS - 1 else (along_y, along_x)
        it.r1, it.t, it.r, it.c, it.a, it.z, it.o = [
            group[i] for group in (firsts_r, seconds_s, seconds_r, cores_s, accs, lines, finals)
        ]
        n = it.n = it.c.shape[0]
        target, it.bit = second
        give, keep = (gives[i], keeps[i]) if i < ITEMS - 1 else (out_give, out_keep)
        it.first = copy(give, it.r1, first[0])
        base = it.bit * (2 * n)
        it.parts = [
            Fetch(keep.at[rows_at(1 - it.bit, 2 * n)], it.t),
            Fetch(keep.at[pl.ds(pl.multiple_of(base + (1 - core) * n, n), n)], it.c),
            Fetch(keep.at[pl.ds(pl.multiple_of(base + core * n, n), n)], it.a.at[core]),
        ]
        it.chip = copy(it.t, it.r, target)
        it.core = copy(it.c, it.a.at[core], sibling)
        it.in1 = copy(it.a, it.z, (d, jnp.where(s == 0, 1, 2)))
        it.in2 = copy(it.a, it.o, third)
        it.out = copy(it.o, it.o, (d, jnp.where(s == 1, 0, 3)))
        items.append(it)

    def start(it):
        it.first.start()
        for part in it.parts:
            part.start()

    def step0(it):
        at = rows_at(1 - it.bit, 2 * it.n)
        it.parts[0].wait()
        it.first.wait_recv()
        it.t[...] = (it.t[...].astype(F32) + it.r1[at, :].astype(F32)).astype(BF16)
        it.chip.start()

    def step1(it):
        n = it.n
        it.parts[1].wait()
        it.parts[2].wait()
        it.chip.wait_recv()

        def come(which):
            at = pl.ds(pl.multiple_of(it.bit * (2 * n) + which * n, n), n)
            return it.r1[at, :].astype(F32) + it.r[rows_at(which, n), :].astype(F32)

        it.c[...] = (it.c[...].astype(F32) + come(1 - core)).astype(BF16)
        it.core.start()
        it.a[core] = (it.a[core].astype(F32) + come(core)).astype(BF16)

    def step2(it):
        it.core.wait_recv()

        @pl.when(outer)
        def _():
            it.in1.start()

    def step3(it):
        @pl.when(inner)
        def _():
            it.in1.wait_recv()
            it.a[...] = (it.a[...].astype(F32) + it.z[...].astype(F32)).astype(BF16)
            it.in2.start()

    def step4(it):
        @pl.when(inner)
        def _():
            it.in2.wait_recv()
            it.o[...] = (it.a[...].astype(F32) + it.o[...].astype(F32)).astype(BF16)
            it.out.start()

    def step5(it):
        @pl.when(outer)
        def _():
            it.out.wait_recv()

    def finish(it):
        it.first.wait_send()
        it.chip.wait_send()
        it.core.wait_send()

        @pl.when(outer)
        def _():
            it.in1.wait_send()

        @pl.when(inner)
        def _():
            it.in2.wait_send()
            it.out.wait_send()

    down_a, down_b, gate_a, up_a, gate_b, up_b, outp = items

    mine, dim = dh_s.shape
    half_dim = dim // 2
    dn2_copy = copy(dn2_give, dn2_r, sibling)
    dn2_copy.start()
    loads = [Fetch(src, dst) for src, dst in zip(fetched, fetched_s)]
    ot_s = wo_s.at[:, pl.ds(0, ot_ref.shape[1])]
    ot_load = Fetch(ot_ref, ot_s)
    wt_s = wo_s.at[pl.ds(0, wt_ref.shape[0])]
    wt_load = Fetch(wt_ref, wt_s)
    x_s = dy_s
    x_load = Fetch(x_ref, x_s)
    for load in loads[:4]:
        load.start()
    start(down_a)
    start(down_b)
    for load in loads[4:]:
        load.start()
    for load in loads[:3]:
        load.wait()
    dn2_copy.wait_recv()
    dn2 = (dn2_s[...] + dn2_r[...].astype(F32)) * gain_two_ref[...]
    h = h_s[...]
    h_scale = lax.rsqrt(jnp.mean(h * h, axis=1, keepdims=True) + EPS)
    dh = dy_s[...].astype(F32) + h_scale * dn2 - h * (h_scale * h_scale * h_scale * jnp.mean(h * dn2, axis=1, keepdims=True))
    dh_s[...] = dh
    da_s[...] = dh.astype(BF16)
    da_copy = copy(da_s.at[:, lanes_at(1 - core, half_dim)], dap_s.at[pl.ds(mine, mine)], sibling)
    loads[3].wait()
    do_s[...] = dot_nt(da_s[...], wo_s[...]).astype(BF16)
    ot_load.start()
    x_load.start()
    do_core = copy(do_s.at[:, lanes_at(1 - core, half_dim)], dcr_s, sibling)
    do_core.start()
    da_copy.start()
    dap_s[0:mine, :] = da_s[:, lanes_at(core, half_dim)]
    do_z = []
    for p in range(2):
        far = (2 * core + 1 - low) * 2 + p
        do_z.append(
            (
                copy(do_s.at[:, lanes_at(far, 128)], dorow_s.at[p, pl.ds(mine, mine)], over_z),
                copy(dcr_s.at[:, lanes_at(2 * (1 - low) + p, 128)], dorow_s.at[p, pl.ds(3 * mine, mine)], over_z),
            )
        )
    do_z[0][0].start()
    do_core.wait_recv()
    do_z[0][1].start()
    do_z[1][0].start()
    do_z[1][1].start()
    for p in range(2):
        dorow_s[p, 0:mine, :] = do_s[:, lanes_at((2 * core + low) * 2 + p, 128)]
        dorow_s[p, 2 * mine : 3 * mine, :] = dcr_s[:, lanes_at(2 * low + p, 128)]

    def get_do(p):
        for made in do_z[p]:
            made.wait_recv()

    def out_parts():
        ot_load.wait()
        da_copy.wait_recv()
        part = ot_s.shape[0] // 2
        out_give[...] = dot_nn(ot_s[rows_at(1 - xb, part), :], dap_s[...]).astype(BF16)
        out_keep[...] = dot_nn(ot_s[rows_at(xb, part), :], dap_s[...]).astype(BF16)
        wt_load.start()

    block = hk_s.shape[1]
    half = block // 2
    firsts = ((over_x, over_y), (over_y, over_x))
    heads = []
    for p in range(2):
        h = Item()
        h.p1 = [copy(hs_s.at[p, i], h1_r.at[p, i], firsts[p][0]) for i in range(2)]
        h.p2 = copy(h2_s.at[p], h2_r.at[p], firsts[p][1])
        h.core = copy(hk_s.at[p, rows_at(1 - core, half)], hc_s.at[p, core], sibling)
        h.high = copy(hh_s.at[p], hh_r.at[p], over_high)
        h.z = copy(heads_o.at[low, p], heads_o.at[low, p], over_z)
        heads.append(h)

    def product(p, yy, xx):
        left = n1t_s[rows_at(2 * yy + xx, block), :]
        return dot_nn(left, dqkv_s[p])

    def heads0(p):
        h = heads[p]
        for turn in range(2):
            if p == 0:
                i = (1 - yb) if turn == 0 else yb
                hs_s[p, turn] = product(p, i, 1 - xb).astype(BF16)
            else:
                i = (1 - xb) if turn == 0 else xb
                hs_s[p, turn] = product(p, 1 - yb, i).astype(BF16)
            h.p1[turn].start()

    def heads1(p):
        h = heads[p]
        part = product(p, 1 - yb, xb) if p == 0 else product(p, yb, 1 - xb)
        h.p1[0].wait_recv()
        h2_s[p] = (part + h1_r[p, 0].astype(F32)).astype(BF16)
        h.p2.start()

    def heads2(p):
        h = heads[p]
        part = product(p, yb, xb)
        h.p1[1].wait_recv()
        part = part + h1_r[p, 1].astype(F32)
        h.p2.wait_recv()
        hk_s[p] = (part + h2_r[p].astype(F32)).astype(BF16)
        h.core.start()
        hc_s[p, core] = hk_s[p, rows_at(core, half), :]

    def heads3(p):
        h = heads[p]
        h.core.wait_recv()
        hh_s[p] = hc_s[p]
        h.high.start()

    def heads4(p):
        h = heads[p]
        h.high.wait_recv()
        heads_o[low, p] = (hh_s[p].astype(F32) + hh_r[p].astype(F32)).astype(BF16)
        h.z.start()

    def heads5(p):
        heads[p].z.wait_recv()

    def finish_heads(p):
        h = heads[p]
        for made in h.p1 + [h.p2, h.core, h.high, h.z]:
            made.wait_send()

    tokens = k_s.shape[0]
    rows = 256
    steps = tokens // rows
    lane = lax.broadcasted_iota(jnp.int32, (tokens, 128), 1)
    klane = lax.broadcasted_iota(jnp.int32, (rows, 128), 1)

    def prepare(p):
        do = dorow_s[p].astype(F32)
        prod = do * (o0_s, o1_s)[p][...]
        for h in range(2):
            mine = (lane < HEAD_DIM) if h == 0 else (lane >= HEAD_DIM)
            other = lane - (HEAD_DIM if h == 0 else 0)
            delta = jnp.sum(jnp.where(mine, prod, 0.0), axis=1, keepdims=True)
            a, b, c = three_parts(delta)
            aug = jnp.where(other == 5, -a, jnp.where(other == 6, -b, jnp.where(other == 7, -c, 0.0)))
            doa_s[h] = jnp.where(mine, do, aug).astype(BF16)
        dq_s[...] = jnp.zeros_like(dq_s)

    def attend(p, j):
        qa_s = (qa0_s, qa1_s)[p]
        cols = slice(128 * p, 128 * p + 128)
        here = pl.ds(pl.multiple_of(j * rows, rows), rows)
        k = k_s[here, cols]
        v = v_s[here, cols]
        kf = k.astype(F32)
        vf = v.astype(F32)
        mk = mask_k_ref[here, :]
        dead = jnp.where(mk[:, 4:5].astype(F32) < 0, 1.0, 0.0)
        dks, dvs = [], []
        for h in range(2):
            kmine = (klane < HEAD_DIM) if h == 0 else (klane >= HEAD_DIM)
            other = klane - (HEAD_DIM if h == 0 else 0)
            one = (other >= 5) & (other < 8)
            ka = jnp.where(kmine, k, mk)
            va = jnp.where(kmine, v, jnp.where(one, jnp.ones_like(v), jnp.zeros_like(v)))
            pr = jnp.exp(dot_nt(ka, qa_s[h]))
            ds = (pr * dot_nt(va, doa_s[h])).astype(BF16)
            dk = dot_nn(ds, qa_s[h])
            dv = dot_nn(pr.astype(BF16), doa_s[h])
            dq_s[h] += dot_tn(ds, ka)
            qd = qa_s[h, here, :].astype(F32)
            dod = doa_s[h, here, :].astype(F32)
            own = jnp.sum(jnp.where(kmine | one, qd * jnp.where(kmine, kf, 1.0), 0.0), axis=1, keepdims=True)
            own_p = jnp.where(dead > 0, jnp.exp(jnp.where(dead > 0, own, 0.0)), 0.0)
            own_d = jnp.sum(jnp.where(kmine | one, dod * jnp.where(kmine, vf, 1.0), 0.0), axis=1, keepdims=True)
            own_ds = own_p * own_d
            dks.append(dk + own_ds * qd)
            dvs.append(dv + own_p * dod)
            dq_s[h, here, :] += jnp.where(kmine, own_ds * kf, 0.0)
        dqkv_s[p, here, 128:256] = jnp.where(klane < HEAD_DIM, dks[0], dks[1]).astype(BF16)
        dqkv_s[p, here, 256:384] = jnp.where(klane < HEAD_DIM, dvs[0], dvs[1]).astype(BF16)

    after = (
        {
            0: lambda: (step0(down_a), step0(down_b), start(gate_a), start(up_a)),
            3: lambda: (step1(down_a), step1(down_b)),
            4: lambda: (step2(down_a), step2(down_b)),
        },
        {
            0: lambda: step3(down_a),
            1: lambda: out_parts(),
            2: lambda: (step0(gate_a), step0(up_a), start(gate_b), start(up_b)),
            3: lambda: step3(down_b),
            4: lambda: step4(down_a),
            5: lambda: (step1(gate_a), step1(up_a)),
        },
    )
    for load in loads[4:10]:
        load.wait()
    for p in range(2):
        get_do(p)
        prepare(p)

        @pl.loop(0, steps)
        def _(j, p=p):
            attend(p, j)
            for i, work in after[p].items():

                @pl.when(j == i)
                def _(work=work):
                    work()

        dqkv_s[p, :, 0:128] = jnp.where(lane < HEAD_DIM, dq_s[0], dq_s[1]).astype(BF16)
        if p == 0:
            loads[10].wait()
        heads0(p)

    cut = mine // 3
    width = dqkv_s.shape[2]
    wt_load.wait()
    x_load.wait()

    def dn1_of(i):
        at = pl.ds(i * mine, mine)
        return dot_nn(dqkv_s[0, at, :], wt_s[0:width, :]) + dot_nn(dqkv_s[1, at, :], wt_s[width : 2 * width, :])

    to_core = [copy(cs_s.at[i], cr_r.at[i], sibling) for i in range(2)]
    to_z = [copy(cs_s.at[1, pl.ds(i * cut, cut)], zr_r.at[pl.ds(i * cut, cut)], over_z) for i in range(3)]
    to_home = [copy(cs_s.at[0, pl.ds(i * cut, cut)], gt_o.at[pl.ds(i * cut, cut)], swapped) for i in range(3)]
    for i in (1, 0):
        cs_s[i] = dn1_of(2 + i).astype(BF16)
        to_core[i].start()
    step4(down_b)
    step2(gate_a)
    step2(up_a)
    dn = dn1_of(1)
    to_core[1].wait_recv()
    to_core[1].wait_send()
    cs_s[1] = (dn + cr_r[1].astype(F32)).astype(BF16)
    for made in to_z:
        made.start()
    heads1(0)
    step3(gate_a)
    dn2_s[...] = dn1_of(0)
    heads2(0)
    to_core[0].wait_recv()
    to_core[0].wait_send()
    step0(gate_b)
    step0(up_b)
    start(outp)
    heads1(1)
    heads3(0)
    step3(up_a)
    heads2(1)
    step4(gate_a)
    heads4(0)
    heads3(1)
    for i in range(3):
        at = pl.ds(i * cut, cut)
        to_z[i].wait_recv()
        dn = dn2_s[at, :] + cr_r[0, at, :].astype(F32) + zr_r[at, :].astype(F32)
        x = x_s[at, :].astype(F32)
        scale = lax.rsqrt(jnp.mean(x * x, axis=1, keepdims=True) + EPS)
        dn = dn * gain_one_ref[...]
        grad = dh_s[at, :] + scale * dn - x * (scale * scale * scale * jnp.mean(x * dn, axis=1, keepdims=True))
        cs_s[0, at, :] = grad.astype(BF16)

        @pl.when(moved)
        def _():
            to_home[i].start()

        @pl.when(jnp.logical_not(moved))
        def _():
            gt_o[at, :] = cs_s[0, at, :]

    step1(gate_b)
    step1(up_b)
    step4(up_a)
    step2(gate_b)
    step2(up_b)
    step0(outp)
    heads4(1)
    step3(gate_b)
    step3(up_b)
    step1(outp)
    step2(outp)
    step4(gate_b)
    step4(up_b)
    step3(outp)
    step4(outp)
    for it in items:
        step5(it)
    heads5(0)
    heads5(1)
    for it in items:
        finish(it)
    for p in range(2):
        finish_heads(p)
        for made in do_z[p]:
            made.wait_send()
    for made in to_z + [dn2_copy, do_core, da_copy]:
        made.wait_send()

    @pl.when(moved)
    def _():
        for made in to_home:
            made.wait_recv()
            made.wait_send()


def closing(mask_key, gains, fetched, dn2_give, o_x, wt, x, gives, keeps):
    tokens = mask_key.shape[0]
    mine, dim = fetched[0].shape
    vmem = pl.BlockSpec(memory_space=pltpu.VMEM)
    anywhere = pl.BlockSpec(memory_space=pl.ANY)
    outp = (dim // 2, dim // 2)
    weights = [w.shape for w in gives] + [outp]
    shards = [(rows // 4, cols) for rows, cols in weights]
    block = dim // 4
    wide = 3 * 128
    scratch = [pltpu.VMEM(v.shape, v.dtype) for v in fetched]
    scratch += [pltpu.VMEM(outp, BF16)] * 2
    scratch += [pltpu.VMEM(w, BF16) for w in weights]
    scratch += [pltpu.VMEM((rows // 2, cols), BF16) for rows, cols in weights] * 2
    scratch += [pltpu.VMEM(w, BF16) for w in shards]
    scratch += [pltpu.VMEM((2,) + w, BF16) for w in shards] * 2
    scratch += [
        pltpu.VMEM((2, tokens, 128), BF16),
        pltpu.VMEM((2, tokens, 128), F32),
        pltpu.VMEM((2, tokens, wide), BF16),
        pltpu.VMEM((2, 2, block, wide), BF16),
        pltpu.VMEM((2, 2, block, wide), BF16),
        pltpu.VMEM((2, block, wide), BF16),
        pltpu.VMEM((2, block, wide), BF16),
        pltpu.VMEM((2, block, wide), BF16),
        pltpu.VMEM((2, 2, block // 2, wide), BF16),
        pltpu.VMEM((2, 2, block // 2, wide), BF16),
        pltpu.VMEM((2, 2, block // 2, wide), BF16),
        pltpu.VMEM((mine, dim), BF16),
        pltpu.VMEM((mine, dim), BF16),
        pltpu.VMEM((2 * mine, dim // 2), BF16),
        pltpu.VMEM((mine, dim // 2), BF16),
        pltpu.VMEM((2, tokens, 128), BF16),
        pltpu.VMEM((2, mine, dim), BF16),
        pltpu.VMEM((2, mine, dim), BF16),
        pltpu.VMEM((mine, dim), BF16),
    ]
    remote = 6 * ITEMS + 2 * 6 + 2 + 3 + 3 + 3 + 4
    local = FETCHED + 3 + 3 * ITEMS
    semaphores = [pltpu.SemaphoreType.DMA((count,)) for count in (remote, remote, local)]
    return pl.pallas_call(
        closing_kernel,
        in_specs=[vmem] * 3 + [anywhere] * (FETCHED + 4 + 2 * (ITEMS - 1)),
        out_specs=[vmem] * (2 + ITEMS),
        out_shape=[jax.ShapeDtypeStruct((mine, dim), BF16)]
        + [jax.ShapeDtypeStruct((2,) + w, BF16) for w in shards]
        + [jax.ShapeDtypeStruct((2, 2, 2, block // 2, wide), BF16)],
        scratch_shapes=scratch + semaphores,
        compiler_params=pltpu.CompilerParams(collective_id=0, has_side_effects=True, vmem_limit_bytes=VMEM_BYTES),
        cost_estimate=pl.CostEstimate(
            flops=40 * tokens * tokens * 256, bytes_accessed=40 << 20, transcendentals=4 * tokens * tokens
        ),
        name="closing",
    )(mask_key, *gains, *fetched, dn2_give, o_x, wt, x, *gives, *keeps)


def placing_kernel(gt, da, db, ga, ua, gb, ub, out, heads, wq, wk, wv, wg, wu, g1, g2, *outs):
    gt_o, q_o, k_o, v_o, out_o, gate_o, up_o, down_o, g1_o, g2_o = outs
    gt_o[...] = gt[...].astype(F32)
    wide = ga.shape[2]
    size = wide + gb.shape[2]
    cut = da.shape[2]
    for c in range(2):
        for to, one, two in ((gate_o, ga, gb), (up_o, ua, ub)):
            to[:, c * size : c * size + wide] = one[c].astype(F32)
            to[:, c * size + wide : (c + 1) * size] = two[c].astype(F32)
        down_o[:, 2 * c * cut : (2 * c + 1) * cut] = da[c].astype(F32)
        down_o[:, (2 * c + 1) * cut : (2 * c + 2) * cut] = db[c].astype(F32)
        out_o[:, 2 * c * cut : (2 * c + 2) * cut] = out[c].astype(F32)
    for m in range(4):
        for p in range(2):
            at = slice((2 * m + p) * 128, (2 * m + p + 1) * 128)
            for t, to in enumerate((q_o, k_o, v_o)):
                to[:, at] = heads[m % 2, p, m // 2, :, t * 128 : (t + 1) * 128].astype(F32)

    def along(pairs):
        return sum(jnp.sum(grad[...] * w[...].astype(F32), axis=1, keepdims=True) for grad, w in pairs)

    g1_o[...] = along(((q_o, wq), (k_o, wk), (v_o, wv))) / g1[...]
    g2_o[...] = along(((gate_o, wg), (up_o, wu))) / g2[...]


def placing(grads, heads, shards):
    gt, da, _, ga, _, gb, _, out = grads
    n, dim = out.shape[1], 2 * out.shape[2]
    units = 2 * (ga.shape[2] + gb.shape[2])
    shapes = [gt.shape] + [(n, dim)] * 4 + [(n, units)] * 2 + [(da.shape[1], dim)] + [(n, 1)] * 2
    vmem = pl.BlockSpec(memory_space=pltpu.VMEM)
    return pl.pallas_call(
        placing_kernel,
        in_specs=[vmem] * 16,
        out_specs=[vmem] * 10,
        out_shape=[jax.ShapeDtypeStruct(v, F32) for v in shapes],
        compiler_params=pltpu.CompilerParams(vmem_limit_bytes=40 << 20),
        cost_estimate=pl.CostEstimate(flops=1 << 22, bytes_accessed=14 << 20, transcendentals=0),
        name="placing",
    )(*grads, heads, *shards)


def local_fused(
    dps,
    seqs,
    tokens,
    query_weight,
    key_weight,
    value_weight,
    out_weight,
    gate_weight,
    up_weight,
    down_weight,
    attention_gain,
    feedforward_gain,
    pair_lengths,
    live_mask,
    out_grad,
):
    mine, dim = tokens.shape
    width = dim // seqs
    d = lax.axis_index("dp")
    s = lax.axis_index("seq")
    core = d % 2
    x_bit = (d // 2) % 2
    y_bit = (d // 4) % 2
    member = core * 2 + s % 2
    moved = core != s // 2

    def move(value, target):
        pairs = []
        for i in range(dps * seqs):
            to = target(i // seqs, i % seqs)
            if to is not None:
                pairs.append((i, to[0] * seqs + to[1]))
        return lax.ppermute(value, AXES, pairs)

    def trade(value):
        return move(value, lambda dd, ss: (dd ^ 1, ss ^ 2) if dd % 2 != ss // 2 else None)

    def with_core(value):
        return move(value, lambda dd, ss: (dd ^ 1, ss))

    def with_member(value, bit):
        return with_core(value) if bit == 2 else move(value, lambda dd, ss: (dd, ss ^ 1))

    def half_of(value, which, axis):
        size = value.shape[axis] // 2
        return lax.dynamic_slice_in_dim(value, which * size, size, axis=axis)

    def with_sibling(value):
        return jnp.concatenate([value, with_core(value)], axis=0)

    def to_tokens(value):
        value = value.reshape(seqs, mine, -1)
        for bit in (1, 2):
            value = value.reshape(value.shape[0] // 2, 2, mine, value.shape[2])
            keep, come = value[:, 0], with_member(value[:, 1], bit)
            upper = (member & bit) != 0
            value = jnp.concatenate([jnp.where(upper, come, keep), jnp.where(upper, keep, come)], axis=2)
        return value[0]

    def rms(v):
        return lax.rsqrt(jnp.mean(v * v, axis=1, keepdims=True) + EPS)

    bounds = jnp.cumsum(pair_lengths[0])[:-1]
    place = s * mine + jnp.arange(mine, dtype=jnp.int32)
    pair = jnp.sum((place[:, None] >= bounds[None, :]).astype(jnp.int32), axis=1)
    code = (2 * pair + (live_mask > 0)).astype(BF16)
    lines = 16 * -(-mine // (16 * dim))
    code = jnp.pad(code, (0, lines * dim - mine)).reshape(lines, dim)
    packed = jnp.concatenate([tokens, code], axis=0)
    come = move(packed, lambda dd, ss: (dd ^ 1, ss ^ 2) if dd % 2 != ss // 2 else (dd, ss ^ 1))
    late = move(come, lambda dd, ss: (dd, ss ^ 1) if dd % 2 != ss // 2 else None)
    row = jnp.stack([jnp.where(moved, come, packed), jnp.where(moved, late, come)])
    row = jnp.concatenate([row, with_core(row)], axis=0)
    x_row = row[:, :mine].reshape(seqs * mine, dim)
    code_row = row[:, mine:].reshape(seqs, -1)[:, :mine].reshape(-1).astype(jnp.int32)
    mask_query, mask_key, dead = mask_terms(code_row // 2, code_row % 2 == 1)
    x_low = row[0, :mine]
    x = x_low.astype(F32)
    out_grad, _ = lax.optimization_barrier((out_grad, row))
    dy = jnp.where(moved, trade(out_grad), out_grad)
    dy_both = with_sibling(dy)

    def heads_of(weight):
        return lax.dynamic_slice_in_dim(weight, member * width, width, axis=1)

    xf = x_row.astype(F32)
    n1_row = (xf * rms(xf) * attention_gain[None, :]).astype(BF16)
    wqkv = [heads_of(query_weight), heads_of(key_weight), heads_of(value_weight)]
    q, k, v = [dot_nn(n1_row, w).astype(BF16) for w in wqkv]
    o_parts, qa_parts, o_tokens = [], [], []
    for i in range(2):
        o_part, qa_part = attention_forward(q, k, v, mask_query, mask_key, dead, i)
        o_parts.append(o_part)
        qa_parts.append(qa_part)
        o_tokens.append(to_tokens(o_part.astype(BF16)))
    by_pair = out_weight.reshape(seqs, 2, 128, dim)

    h = x + dot_nn(o_tokens[0], by_pair[:, 0].reshape(-1, dim)) + dot_nn(o_tokens[1], by_pair[:, 1].reshape(-1, dim))
    h_scale = rms(h)
    n2 = (h * h_scale * feedforward_gain[None, :]).astype(BF16)
    n2_both = with_sibling(n2)
    wg, wu, wd = half_of(gate_weight, core, 1), half_of(up_weight, core, 1), half_of(down_weight, core, 0)
    g = dot_nn(n2_both, wg)
    u = dot_nn(n2_both, wu)
    act, slope = gelu_parts(g)
    z = (act * u).astype(BF16)
    z_come = with_core(z)
    z_come = jnp.concatenate([z_come[mine:], z_come[:mine]], axis=0)
    dz = dot_nt(dy_both, wd)
    dg = (dz * u * slope).astype(BF16)
    du = (dz * act).astype(BF16)

    def blocks(parts):
        return jnp.concatenate(parts, axis=1)

    chip = dim // (dps // 2)
    n2_x = blocks([n2_both[:, (2 * yy + xx) * chip : (2 * yy + xx + 1) * chip] for xx in range(2) for yy in range(2)])
    wide = 128 * -(-(dg.shape[1] // 2) // 128)

    def two_halves(left, right, which):
        give = dot_tn(half_of(left, 1 - which, 1), right).astype(BF16)
        keep = dot_tn(half_of(left, which, 1), right).astype(BF16)
        return give[:, :wide], give[:, wide:], keep[:, :wide], keep[:, wide:]

    gate = two_halves(n2_both, dg, y_bit)
    up = two_halves(n2_x, du, x_bit)
    dy_part = half_of(dy_both, core, 1)
    down_own = dot_tn(z, dy_part).astype(BF16)
    down_far = dot_tn(z_come, dy_part).astype(BF16)
    cut = dy_part.shape[1] // 2
    own_y = y_bit == core
    down_a = (
        jnp.where(own_y, down_far[:, :cut], down_own[:, :cut]),
        jnp.where(own_y, down_own[:, :cut], down_far[:, :cut]),
    )

    def of_x(which):
        one = half_of(down_own[:, cut:], which, 0)
        two = half_of(down_far[:, cut:], which, 0)
        return jnp.concatenate([jnp.where(core == 0, one, two), jnp.where(core == 0, two, one)], axis=0)

    down_b = (of_x(1 - x_bit), of_x(x_bit))
    f = dot_nn(z, wd)
    layer_out = (h + f[:mine] + with_core(f[mine:].astype(BF16)).astype(F32)).astype(BF16)
    layer_out = jnp.where(moved, trade(layer_out), layer_out)

    dn2_both = dot_nt(dg, wg) + dot_nt(du, wu)
    o_x = blocks([o_tokens[i][:, (2 * yy + xx) * 128 : (2 * yy + xx + 1) * 128] for xx in range(2) for yy in range(2) for i in range(2)])
    o_x = with_sibling(o_x)
    wt = jnp.concatenate([w[:, i * 128 : (i + 1) * 128].T for i in range(2) for w in wqkv], axis=0)
    *grads, heads_grads = closing(
        mask_key,
        (attention_gain[None, :], feedforward_gain[None, :]),
        (dn2_both[:mine], h, dy, out_weight, *qa_parts, k, v, *o_parts, n1_row.T),
        dn2_both[mine:].astype(BF16),
        o_x.T,
        wt,
        x_low,
        (down_a[0], down_b[0], gate[0], up[0], gate[1], up[1]),
        (down_a[1], down_b[1], gate[2], up[2], gate[3], up[3]),
    )

    def shard(weight):
        size = weight.shape[0] // dps
        return lax.dynamic_slice_in_dim(weight, d * size, size, axis=0)

    shards = [shard(w) for w in (query_weight, key_weight, value_weight, gate_weight, up_weight)]
    shards += [shard(w)[:, None] for w in (attention_gain, feedforward_gain)]
    *results, gain_one, gain_two = placing(grads, heads_grads, shards)
    return (layer_out, *results, gain_one[:, 0], gain_two[:, 0])


def solution(mesh):
    both = P(("dp", "seq"), None)
    rows = P("dp", None)
    dps, seqs = mesh.shape["dp"], mesh.shape["seq"]
    local = local_fused if (dps, seqs) == (8, 4) else local_plain
    return jax.shard_map(
        functools.partial(local, dps, seqs),
        mesh=mesh,
        in_specs=(both, P(), P(), P(), P(), P(), P(), P(), P(), P(), rows, P(("dp", "seq")), both),
        out_specs=(both, both, rows, rows, rows, rows, rows, rows, rows, P("dp"), P("dp")),
        check_vma=False,
    )
```

```python
import functools

import jax
import jax.numpy as jnp
from jax import lax
from jax.experimental import pallas as pl
from jax.experimental.pallas import tpu as pltpu
from jax.sharding import PartitionSpec as P

HEADS = 16
HEAD_DIM = 64
EPS = 1e-06
BIG = float(2.0**40)
F32 = jnp.float32
BF16 = jnp.bfloat16
AXES = ("dp", "seq")
MESH = pl.DeviceIdType.MESH
VMEM_BYTES = 62 << 20
ITEMS, FETCHED, OPENED = 7, 9, 13


def dot_nn(a, b):
    return lax.dot_general(a, b, (((1,), (0,)), ((), ())), preferred_element_type=F32)


def dot_nt(a, b):
    return lax.dot_general(a, b, (((1,), (1,)), ((), ())), preferred_element_type=F32)


def dot_tn(a, b):
    return lax.dot_general(a, b, (((0,), (0,)), ((), ())), preferred_element_type=F32)


def three_parts(v):
    high = v.astype(BF16).astype(F32)
    mid = (v - high).astype(BF16).astype(F32)
    low = (v - high - mid).astype(BF16).astype(F32)
    return high, mid, low


def forward_kernel(keep_queries, q_ref, k_ref, v_ref, mq_ref, mk_ref, dead_ref, kd_ref, vd_ref, o_ref, l_ref):
    lane = lax.broadcasted_iota(jnp.int32, q_ref.shape, 1)
    klane = lax.broadcasted_iota(jnp.int32, k_ref.shape, 1)
    q = q_ref[...]
    dead = dead_ref[...]
    qk = q.astype(F32) * kd_ref[...].astype(F32)
    outs, logs = [], []
    for h in range(2):
        mine = (lane < HEAD_DIM) if h == 0 else (lane >= HEAD_DIM)
        kmine = (klane < HEAD_DIM) if h == 0 else (klane >= HEAD_DIM)
        qa = jnp.where(mine, q, mq_ref[...])
        ka = jnp.where(kmine, k_ref[...], mk_ref[...])
        s = dot_nt(qa, ka)
        own = jnp.sum(jnp.where(mine, qk, 0.0), axis=1, keepdims=True)
        own = jnp.where(dead > 0, own, -BIG)
        top = jnp.maximum(jnp.max(s, axis=1, keepdims=True), own)
        p = jnp.exp(s - top).astype(BF16)
        va = jnp.where(kmine, v_ref[...], jnp.ones_like(v_ref[...]))
        r = dot_nn(p, va)
        own_p = jnp.exp(own - top)
        total = (r[:, HEAD_DIM : HEAD_DIM + 1] if h == 0 else r[:, 0:1]) + own_p
        outs.append((r + own_p * vd_ref[...].astype(F32)) * (1.0 / total))
        log = top + jnp.log(total)
        if keep_queries:
            other = lane - (HEAD_DIM if h == 0 else 0)
            a, b, c = three_parts(log)
            aug = mq_ref[...].astype(F32)
            aug = jnp.where(other == 5, -a, jnp.where(other == 6, -b, jnp.where(other == 7, -c, aug)))
            l_ref[h] = jnp.where(mine, q.astype(F32), aug).astype(BF16)
        logs.append(log)
    o_ref[...] = jnp.where(lane < HEAD_DIM, outs[0], outs[1])
    if not keep_queries:
        l_ref[...] = jnp.where(lane < HEAD_DIM, logs[0], logs[1])


def rows_per_step(tokens):
    for rows in (512, 384, 256, 128):
        if tokens % rows == 0 and rows * tokens <= 800000:
            return rows
    return 128


def attention_forward(q, k, v, mq, mk, dead, group=None):
    tokens, width = q.shape
    rows = rows_per_step(tokens)
    first, count = (0, width // 128) if group is None else (group, 1)
    part = pl.BlockSpec((rows, 128), lambda h, i: (i, h + first))
    full = pl.BlockSpec((tokens, 128), lambda h, i: (0, h + first))
    out = pl.BlockSpec((rows, 128), lambda h, i: (i, h))
    keep = group is not None
    log_out, log_shape = out, jax.ShapeDtypeStruct((tokens, 128 * count), F32)
    if keep:
        log_out = pl.BlockSpec((2, rows, 128), lambda h, i: (0, i, 0))
        log_shape = jax.ShapeDtypeStruct((2, tokens, 128), BF16)
    return pl.pallas_call(
        functools.partial(forward_kernel, keep),
        grid=(count, tokens // rows),
        in_specs=[
            part,
            full,
            full,
            pl.BlockSpec((rows, 128), lambda h, i: (i, 0)),
            pl.BlockSpec((tokens, 128), lambda h, i: (0, 0)),
            pl.BlockSpec((rows, 1), lambda h, i: (i, 0)),
            part,
            part,
        ],
        out_specs=[out, log_out],
        out_shape=[jax.ShapeDtypeStruct((tokens, 128 * count), F32), log_shape],
        compiler_params=pltpu.CompilerParams(vmem_limit_bytes=56 << 20),
        cost_estimate=pl.CostEstimate(
            flops=16 * tokens * tokens * 128 * count, bytes_accessed=16 * tokens * width, transcendentals=2 * tokens * tokens * count
        ),
        name="attention_forward",
    )(q, k, v, mq, mk, dead, k, v)


def backward_kernel(
    q_ref, k_ref, v_ref, do_ref, o_ref, l_ref, mq_ref, mk_ref, dead_ref, dq_ref, dk_ref, dv_ref, qa_s, doa_s, dq_s
):
    j = pl.program_id(1)
    tokens = q_ref.shape[0]
    rows = k_ref.shape[0]
    lane = lax.broadcasted_iota(jnp.int32, (tokens, 128), 1)
    klane = lax.broadcasted_iota(jnp.int32, (rows, 128), 1)

    @pl.when(j == 0)
    def _():
        do = do_ref[...].astype(F32)
        prod = do * o_ref[...]
        q = q_ref[...].astype(F32)
        logs = l_ref[...]
        for h in range(2):
            mine = (lane < HEAD_DIM) if h == 0 else (lane >= HEAD_DIM)
            other = lane - (HEAD_DIM if h == 0 else 0)
            delta = jnp.sum(jnp.where(mine, prod, 0.0), axis=1, keepdims=True)
            log = logs[:, 0:1] if h == 0 else logs[:, HEAD_DIM : HEAD_DIM + 1]
            a, b, c = three_parts(log)
            aug = mq_ref[...].astype(F32)
            aug = jnp.where(other == 5, -a, jnp.where(other == 6, -b, jnp.where(other == 7, -c, aug)))
            qa_s[h] = jnp.where(mine, q, aug).astype(BF16)
            a, b, c = three_parts(delta)
            aug = jnp.where(other == 5, -a, jnp.where(other == 6, -b, jnp.where(other == 7, -c, 0.0)))
            doa_s[h] = jnp.where(mine, do, aug).astype(BF16)
        dq_s[...] = jnp.zeros_like(dq_s)

    k = k_ref[...]
    v = v_ref[...]
    here = pl.ds(pl.multiple_of(j * rows, rows), rows)
    kf = k.astype(F32)
    vf = v.astype(F32)
    dead = dead_ref[...]
    dks, dvs = [], []
    for h in range(2):
        kmine = (klane < HEAD_DIM) if h == 0 else (klane >= HEAD_DIM)
        other = klane - (HEAD_DIM if h == 0 else 0)
        one = (other >= 5) & (other < 8)
        ka = jnp.where(kmine, k, mk_ref[...])
        va = jnp.where(kmine, v, jnp.where(one, jnp.ones_like(v), jnp.zeros_like(v)))
        p = jnp.exp(dot_nt(ka, qa_s[h]))
        ds = (p * dot_nt(va, doa_s[h])).astype(BF16)
        dk = dot_nn(ds, qa_s[h])
        dv = dot_nn(p.astype(BF16), doa_s[h])
        dq_s[h] += dot_tn(ds, ka)
        qd = qa_s[h, here, :].astype(F32)
        dod = doa_s[h, here, :].astype(F32)
        own = jnp.sum(jnp.where(kmine | one, qd * jnp.where(kmine, kf, 1.0), 0.0), axis=1, keepdims=True)
        own_p = jnp.where(dead > 0, jnp.exp(jnp.where(dead > 0, own, 0.0)), 0.0)
        own_d = jnp.sum(jnp.where(kmine | one, dod * jnp.where(kmine, vf, 1.0), 0.0), axis=1, keepdims=True)
        own_ds = own_p * own_d
        dks.append(dk + own_ds * qd)
        dvs.append(dv + own_p * dod)
        dq_s[h, here, :] += jnp.where(kmine, own_ds * kf, 0.0)
    dk_ref[...] = jnp.where(klane < HEAD_DIM, dks[0], dks[1]).astype(BF16)
    dv_ref[...] = jnp.where(klane < HEAD_DIM, dvs[0], dvs[1]).astype(BF16)

    @pl.when(j == pl.num_programs(1) - 1)
    def _():
        dq_ref[...] = jnp.where(lane < HEAD_DIM, dq_s[0], dq_s[1]).astype(BF16)


def attention_backward(q, k, v, do, o, logs, mq, mk, dead):
    tokens, width = q.shape
    rows = rows_per_step(tokens)
    part = pl.BlockSpec((rows, 128), lambda h, i: (i, h))
    full = pl.BlockSpec((tokens, 128), lambda h, i: (0, h))
    return pl.pallas_call(
        backward_kernel,
        grid=(width // 128, tokens // rows),
        in_specs=[
            full,
            part,
            part,
            full,
            full,
            full,
            pl.BlockSpec((tokens, 128), lambda h, i: (0, 0)),
            pl.BlockSpec((rows, 128), lambda h, i: (i, 0)),
            pl.BlockSpec((rows, 1), lambda h, i: (i, 0)),
        ],
        out_specs=[full, part, part],
        out_shape=[jax.ShapeDtypeStruct((tokens, width), BF16)] * 3,
        scratch_shapes=[
            pltpu.VMEM((2, tokens, 128), BF16),
            pltpu.VMEM((2, tokens, 128), BF16),
            pltpu.VMEM((2, tokens, 128), F32),
        ],
        compiler_params=pltpu.CompilerParams(vmem_limit_bytes=56 << 20),
        cost_estimate=pl.CostEstimate(
            flops=40 * tokens * tokens * width, bytes_accessed=24 * tokens * width, transcendentals=tokens * tokens * width // HEAD_DIM
        ),
        name="attention_backward",
    )(q, k, v, do, o, logs, mq, mk, dead)


def mask_terms(pair, live):
    lane = jnp.arange(128, dtype=jnp.int32)[None, :] % HEAD_DIM
    same = lane == pair[:, None]
    query = jnp.where(lane < 4, same, lane == 4).astype(BF16)
    key = jnp.where(
        lane < 4,
        jnp.where(same, 0.0, -BIG),
        jnp.where(lane == 4, jnp.where(live[:, None], 0.0, -BIG), ((lane >= 5) & (lane < 8)).astype(F32)),
    ).astype(BF16)
    return query, key, 1.0 - live.astype(F32)[:, None]


def gelu_parts(g):
    c = 0.7978845608028654
    t = jnp.tanh(c * (g + 0.044715 * g * g * g))
    act = 0.5 * g * (1.0 + t)
    slope = 0.5 * (1.0 + t) + 0.5 * g * (1.0 - t * t) * c * (1.0 + 3 * 0.044715 * g * g)
    return act, slope


def local_plain(
    dps,
    seqs,
    tokens,
    query_weight,
    key_weight,
    value_weight,
    out_weight,
    gate_weight,
    up_weight,
    down_weight,
    attention_gain,
    feedforward_gain,
    pair_lengths,
    live_mask,
    out_grad,
):
    mine, dim = tokens.shape
    units = gate_weight.shape[1]
    half = seqs // 2
    width = dim // seqs
    chips = dps // 2
    d = lax.axis_index("dp")
    s = lax.axis_index("seq")
    core = d % 2
    high = (s >= half).astype(jnp.int32)
    low = s % half
    member = core * half + low
    moved = core != high

    def move(value, target):
        pairs = []
        for i in range(dps * seqs):
            to = target(i // seqs, i % seqs)
            if to is not None:
                pairs.append((i, to[0] * seqs + to[1]))
        return lax.ppermute(value, AXES, pairs)

    def trade(value):
        def target(dd, ss):
            return (dd ^ 1, (ss + half) % seqs) if dd % 2 != ss // half else None

        return move(value, target)

    def with_core(value):
        return move(value, lambda dd, ss: (dd ^ 1, ss))

    def with_chip(value, bit):
        return move(value, lambda dd, ss: (dd ^ bit, ss))

    def with_seq(value, bit):
        return move(value, lambda dd, ss: (dd, ss ^ bit))

    def with_member(value, bit):
        return with_core(value) if bit == half else with_seq(value, bit)

    bits = []
    while (1 << len(bits)) < seqs:
        bits.append(1 << len(bits))
    chip_bits = []
    while (2 << len(chip_bits)) < dps:
        chip_bits.append(2 << len(chip_bits))

    def gather_row(value):
        value = value[None]
        for bit in bits:
            value = jnp.concatenate([value, with_member(value, bit)], axis=0)
        return value

    def to_tokens(value):
        value = value.reshape(seqs, mine, width)
        for bit in bits:
            value = value.reshape(value.shape[0] // 2, 2, mine, value.shape[2])
            keep, come = value[:, 0], with_member(value[:, 1], bit)
            upper = (member & bit) != 0
            value = jnp.concatenate([jnp.where(upper, come, keep), jnp.where(upper, keep, come)], axis=2)
        return value[0]

    def to_heads(value):
        value = value[None]
        for bit in reversed(bits):
            first, second = jnp.split(value, 2, axis=2)
            upper = (member & bit) != 0
            come = with_member(jnp.where(upper, first, second), bit)
            value = jnp.stack([jnp.where(upper, second, first), come], axis=1)
            value = value.reshape(-1, mine, value.shape[3])
        return value.reshape(seqs * mine, width)

    def row_sum(value):
        value = value.reshape(seqs, mine, dim)
        for bit in reversed(bits):
            keep, give = value[: value.shape[0] // 2], value[value.shape[0] // 2 :]
            value = keep + with_member(give.astype(BF16), bit).astype(F32)
        return value[0]

    def over_chips(value, order):
        cols = value.shape[1]
        rows = value.shape[0] // chips
        value = value.reshape((2,) * len(chip_bits) + (rows, cols))
        left = list(reversed(chip_bits))
        for bit in order:
            axis = left.index(bit)
            left.pop(axis)
            upper = ((d & bit) != 0).astype(jnp.int32)
            give = lax.dynamic_index_in_dim(value, 1 - upper, axis, keepdims=False)
            keep = lax.dynamic_index_in_dim(value, upper, axis, keepdims=False)
            come = with_chip(give, bit)
            value = (keep.astype(F32) + come.astype(F32)).astype(BF16)
        return value.reshape(rows, cols)

    def over_seq(value):
        for i in range(half - 1):
            come = move(
                value,
                lambda dd, ss: (dd, i + 1) if ss == i else ((dd, seqs - 2 - i) if ss == seqs - 1 - i else None),
            )
            value = (value.astype(F32) + come.astype(F32)).astype(BF16)
        come = move(value, lambda dd, ss: (dd, seqs - 1 - ss) if ss in (half - 1, half) else None)
        value = (value.astype(F32) + come.astype(F32)).astype(BF16)
        for i in reversed(range(half - 1)):
            come = move(
                value,
                lambda dd, ss: (dd, i) if ss == i + 1 else ((dd, seqs - 1 - i) if ss == seqs - 2 - i else None),
            )
            value = jnp.where((s == i) | (s == seqs - 1 - i), come, value)
        return value

    def my_core(value, axis, other=False):
        shape = value.shape
        size = shape[axis] // dps
        value = value.reshape(shape[:axis] + (chips, 2, size) + shape[axis + 1 :])
        value = lax.dynamic_index_in_dim(value, (1 - core) if other else core, axis + 1, keepdims=False)
        return value.reshape(shape[:axis] + (chips * size,) + shape[axis + 1 :])

    bounds = jnp.cumsum(pair_lengths[0])[:-1]
    place = s * mine + jnp.arange(mine, dtype=jnp.int32)
    pair = jnp.sum((place[:, None] >= bounds[None, :]).astype(jnp.int32), axis=1)
    code = (2 * pair + (live_mask > 0)).astype(BF16)
    lines = -(-mine // dim)
    code = jnp.pad(code, (0, 16 * dim * (-(-lines // 16)) - mine)).reshape(-1, dim)
    packed = jnp.concatenate([tokens, code], axis=0)
    packed = jnp.where(moved, trade(packed), packed)
    row = gather_row(packed)
    x_row = row[:, :mine].reshape(seqs * mine, dim)
    code_row = row[:, mine:].reshape(seqs, -1)[:, :mine].reshape(-1).astype(jnp.int32)
    mask_query, mask_key, dead = mask_terms(code_row // 2, code_row % 2 == 1)
    x = packed[:mine].astype(F32)
    dy = jnp.where(moved, trade(out_grad), out_grad)

    def scaled(v, gain):
        return v * lax.rsqrt(jnp.mean(v * v, axis=1, keepdims=True) + EPS) * gain[None, :]

    def heads_of(weight):
        return lax.dynamic_slice_in_dim(weight, member * width, width, axis=1)

    n1_row = scaled(x_row.astype(F32), attention_gain).astype(BF16)
    wq, wk, wv = heads_of(query_weight), heads_of(key_weight), heads_of(value_weight)
    lanes = -(-width // 128) * 128
    widen = (lambda v: jnp.pad(v, ((0, 0), (0, lanes - width)))) if lanes != width else (lambda v: v)
    q, k, v = [widen(dot_nn(n1_row, w).astype(BF16)) for w in (wq, wk, wv)]
    o_heads, logs = attention_forward(q, k, v, mask_query, mask_key, dead)
    o = to_tokens(o_heads[:, :width].astype(BF16))

    h = x + dot_nn(o, out_weight)
    h_scale = lax.rsqrt(jnp.mean(h * h, axis=1, keepdims=True) + EPS)
    n2 = (h * h_scale * feedforward_gain[None, :]).astype(BF16)
    n2_both = jnp.concatenate([n2, with_core(n2)], axis=0)
    dy_both = jnp.concatenate([dy, with_core(dy)], axis=0)
    wg, wu, wd = my_core(gate_weight, 1), my_core(up_weight, 1), my_core(down_weight, 0)
    g = dot_nn(n2_both, wg)
    u = dot_nn(n2_both, wu)
    act, slope = gelu_parts(g)
    z = (act * u).astype(BF16)
    f = dot_nn(z, wd)
    layer_out = (h + f[:mine] + with_core(f[mine:].astype(BF16)).astype(F32)).astype(BF16)
    layer_out = jnp.where(moved, trade(layer_out), layer_out)

    grad_down = dot_tn(z, dy_both).astype(BF16)
    dz = dot_nt(dy_both, wd)
    dg = (dz * u * slope).astype(BF16)
    du = (dz * act).astype(BF16)
    grad_gate = dot_tn(n2_both, dg).astype(BF16)
    grad_upward = dot_tn(n2_both, du).astype(BF16)
    dn2_both = dot_nt(dg, wg) + dot_nt(du, wu)
    dn2 = dn2_both[:mine] + with_core(dn2_both[mine:].astype(BF16)).astype(F32)

    ghd = dn2 * feedforward_gain[None, :]
    dh = dy.astype(F32) + h_scale * ghd - h * (h_scale**3 * jnp.mean(h * ghd, axis=1, keepdims=True))
    gain_two = jnp.sum(dn2 * h * h_scale, axis=0)
    da = dh.astype(BF16)
    do = to_heads(dot_nt(da, out_weight).astype(BF16))
    o_both = jnp.concatenate([my_core(o, 1), with_core(my_core(o, 1, other=True))], axis=0)
    da_both = jnp.concatenate([da, with_core(da)], axis=0)
    grad_output = dot_tn(o_both, da_both).astype(BF16)

    dq, dk, dv = attention_backward(q, k, v, widen(do), o_heads, logs, mask_query, mask_key, dead)
    dq, dk, dv = dq[:, :width], dk[:, :width], dv[:, :width]
    dn1_row = dot_nt(dq, wq) + dot_nt(dk, wk) + dot_nt(dv, wv)
    x_row_scale = lax.rsqrt(jnp.mean(jnp.square(x_row.astype(F32)), axis=1, keepdims=True) + EPS)
    gain_one = jnp.sum(dn1_row * (x_row.astype(F32) * x_row_scale), axis=0)
    grad_heads = dot_tn(n1_row, jnp.concatenate([dq, dk, dv], axis=1)).astype(BF16)
    gains = jnp.pad(jnp.stack([gain_one, gain_two], axis=1), ((0, 0), (0, 126))).astype(BF16)
    dn1 = row_sum(dn1_row)

    x_scale = lax.rsqrt(jnp.mean(x * x, axis=1, keepdims=True) + EPS)
    gxd = dn1 * attention_gain[None, :]
    grad_tokens = dh + x_scale * gxd - x * (x_scale**3 * jnp.mean(x * gxd, axis=1, keepdims=True))
    grad_tokens = jnp.where(moved, trade(grad_tokens.astype(BF16)).astype(F32), grad_tokens)

    ahead, back = chip_bits, chip_bits[::-1]
    down_out = over_seq(over_chips(grad_down, ahead)).astype(F32)

    def both_cores(value):
        n = value.shape[0] // 2
        first, second = value[:n], value[n:]
        upper = core == 1
        come = with_core(jnp.where(upper, first, second))
        keep = jnp.where(upper, second, first)
        return jnp.stack([jnp.where(upper, come, keep), jnp.where(upper, keep, come)], axis=1)

    def unit_columns(value):
        n = value.shape[0]
        return value.reshape(n, 2, chips, units // dps).transpose(0, 2, 1, 3).reshape(n, units)

    gate_out = unit_columns(over_seq(both_cores(over_chips(grad_gate, back)))).astype(F32)
    upward_out = unit_columns(over_seq(both_cores(over_chips(grad_upward, ahead)))).astype(F32)
    output_out = over_seq(over_chips(grad_output, back)).astype(F32)

    heads_part = over_chips(jnp.concatenate([grad_heads, gains], axis=1), back)
    heads_part = both_cores(heads_part)
    heads_part = (heads_part.astype(F32) + with_seq(heads_part, half).astype(F32)).astype(BF16)
    heads_part = heads_part[None]
    for bit in bits[:-1]:
        come = with_seq(heads_part, bit)
        upper = (member & bit) != 0
        heads_part = jnp.concatenate([jnp.where(upper, come, heads_part), jnp.where(upper, heads_part, come)], axis=0)
    heads_part = heads_part.transpose(1, 2, 0, 3).reshape(-1, seqs, 3 * width + 128)
    query_out, key_out, value_out = [
        heads_part[:, :, i * width : (i + 1) * width].reshape(-1, dim).astype(F32) for i in range(3)
    ]
    gains_out = jnp.sum(heads_part[:, :, 3 * width : 3 * width + 2].astype(F32), axis=1)
    return (
        layer_out,
        grad_tokens,
        query_out,
        key_out,
        value_out,
        output_out,
        gate_out,
        upward_out,
        down_out,
        gains_out[:, 0],
        gains_out[:, 1],
    )


def opening_kernel(tokens_ref, live_ref, lengths_ref, gain_one_ref, gain_two_ref, *refs):
    refs = list(refs)

    def take(n):
        taken, refs[:n] = refs[:n], []
        return taken

    wq_ref, wk_ref, wv_ref, wo_ref, dy_ref = take(5)
    outs = take(OPENED)
    kept = take(OPENED)
    n1_s, k_s, v_s, qa0_s, qa1_s, o0_s, o1_s, mk_s, h_s, n2_s, o_s, dy_s, x_s = kept
    xs, codes, w_s, wo_s, q_s, mq_s, ka_s, va_s, ob_s, send_sem, recv_sem, local_sem = take(12)

    d = lax.axis_index("dp")
    s = lax.axis_index("seq")
    core = d % 2
    low = s % 2
    high = s // 2
    member = 2 * core + low
    sibling = (d + 1 - 2 * core, s)
    over_z = (d, s + 1 - 2 * low)
    across = (d + 1 - 2 * core, s + 1 - 2 * low)
    swapped = (d + 1 - 2 * core, s + 2 - 4 * high)
    moved = core != high
    stays = core == high

    barrier = pltpu.get_barrier_semaphore()
    for other in (sibling, over_z, across, swapped):
        pl.semaphore_signal(barrier, inc=1, device_id=other, device_id_type=MESH)

    counts = {"remote": 0, "local": 0}

    class Copy:
        def __init__(self, src, dst, target):
            self.parts = (src, dst, target, counts["remote"])
            counts["remote"] += 1

        def made(self):
            src, dst, target, i = self.parts
            return pltpu.make_async_remote_copy(
                src_ref=src, dst_ref=dst, send_sem=send_sem.at[i], recv_sem=recv_sem.at[i], device_id=target, device_id_type=MESH
            )

        def start(self):
            self.made().start()

        def wait_recv(self):
            self.made().wait_recv()

        def wait_send(self):
            self.made().wait_send()

    class Fetch:
        def __init__(self, src, dst):
            self.parts = (src, dst, counts["local"])
            counts["local"] += 1

        def made(self):
            src, dst, i = self.parts
            return pltpu.make_async_copy(src, dst, local_sem.at[i])

        def start(self):
            self.made().start()

        def wait(self):
            self.made().wait()

    def lanes_at(start, size):
        return pl.ds(pl.multiple_of(start * size, size), size)

    mine, dim = tokens_ref.shape
    third = mine // 3
    pieces = [pl.ds(i * third, third) for i in range(3)]
    place = s * mine + lax.broadcasted_iota(jnp.int32, codes.shape[1:], 1)
    ends = [lengths_ref[0, 0]]
    for i in (1, 2):
        ends.append(ends[-1] + lengths_ref[0, i])
    pair = sum([jnp.where(place >= end, 1.0, 0.0) for end in ends])
    code = (2.0 * pair + jnp.where(live_ref[...] > 0, 1.0, 0.0)).astype(BF16)

    w_loads = []
    for p in range(2):
        for t, w in enumerate((wq_ref, wk_ref, wv_ref)):
            w_loads.append(Fetch(w.at[:, lanes_at(2 * member + p, 128)], w_s.at[:, pl.ds((3 * p + t) * 128, 128)]))
    wo_loads = [
        Fetch(wo_ref.at[pl.ds((2 * m + p) * 128, 128)], wo_s.at[pl.ds((4 * p + m) * 128, 128)]) for m in range(4) for p in range(2)
    ]

    trade = [Copy(tokens_ref.at[at], xs.at[0, at], swapped) for at in pieces]
    to_z = [Copy(xs.at[0, at], xs.at[1, at], over_z) for at in pieces]
    to_core = [Copy(xs.at[0, at], xs.at[2, at], sibling) for at in pieces]
    on_core = [Copy(xs.at[1, at], xs.at[3, at], sibling) for at in pieces]
    code_s = x_s.at[pl.ds(0, 16), pl.ds(0, mine)]
    code_trade = Copy(code_s, codes.at[0], swapped)
    code_z = Copy(codes.at[0], codes.at[1], over_z)
    code_core = Copy(codes.at[0], codes.at[2], sibling)
    code_on = Copy(codes.at[1], codes.at[3], sibling)
    dy_trade = Copy(dy_ref, dy_s.at[pl.ds(0, mine)], swapped)
    dy_local = Fetch(dy_ref, dy_s.at[pl.ds(0, mine)])
    dy_core = Copy(dy_s.at[pl.ds(0, mine)], dy_s.at[pl.ds(mine, mine)], sibling)

    code_s[...] = code
    pl.semaphore_wait(barrier, 4)

    @pl.when(moved)
    def _():
        code_trade.start()
        for made in trade:
            made.start()

    @pl.when(stays)
    def _():
        xs[0] = tokens_ref[...]
        codes[0] = code
        code_z.start()
        code_core.start()
        for a, b in zip(to_z, to_core):
            a.start()
            b.start()

    for load in w_loads + wo_loads:
        load.start()

    tokens = k_s.shape[0]
    lane = lax.broadcasted_iota(jnp.int32, (third, 128), 1)
    inside = lane % HEAD_DIM
    for load in w_loads:
        load.wait()

    def project(b):
        for i in range(3):
            at = pl.ds(i * third, third)
            x = xs[b, at, :].astype(F32)
            n1 = (x * lax.rsqrt(jnp.mean(x * x, axis=1, keepdims=True) + EPS) * gain_one_ref[...]).astype(BF16)
            to = pl.ds(pl.multiple_of(b * mine + i * third, 128), third)
            n1_s[to, :] = n1
            qkv = dot_nn(n1, w_s[...]).astype(BF16)
            for p in range(2):
                for t, out in enumerate((q_s, k_s, v_s)):
                    out[to, 128 * p : 128 * p + 128] = qkv[:, (3 * p + t) * 128 : (3 * p + t + 1) * 128]
            number = codes[b, 0:8, i * third : (i + 1) * third].astype(F32).T[:, 0:1]
            whose = jnp.floor(number * 0.5)
            dead = number - 2.0 * whose < 0.5
            same = inside.astype(F32) == whose
            mq_s[to, :] = jnp.where(inside < 4, jnp.where(same, 1.0, 0.0), jnp.where(inside == 4, 1.0, 0.0)).astype(BF16)
            key = jnp.where(inside == 4, jnp.where(dead, -BIG, 0.0), jnp.where((inside >= 5) & (inside < 8), 1.0, 0.0))
            mk_s[to, :] = jnp.where(inside < 4, jnp.where(same, 0.0, -BIG), key).astype(BF16)

    def block(i):
        return (i + 2 * moved.astype(jnp.int32)) % 4

    def relay():
        code_z.wait_recv()
        code_on.start()
        for a, b in zip(to_z, on_core):
            a.wait_recv()
            b.start()

    def from_core():
        code_core.wait_recv()
        for made in to_core:
            made.wait_recv()

    def from_core_on():
        code_on.wait_recv()
        for made in on_core:
            made.wait_recv()

    pl.when(moved)(from_core)
    project(block(0))

    @pl.when(moved)
    def _():
        code_trade.wait_recv()
        code_z.start()
        code_core.start()
        for made, a, b in zip(trade, to_z, to_core):
            made.wait_recv()
            a.start()
            b.start()
        dy_trade.start()
        from_core_on()

    pl.when(stays)(relay)
    project(block(1))
    pl.when(stays)(from_core)
    project(block(2))
    pl.when(moved)(relay)

    @pl.when(stays)
    def _():
        dy_local.start()
        from_core_on()

    project(block(3))
    code_trade_done = [code_trade] + trade

    @pl.when(moved)
    def _():
        for made in code_trade_done:
            made.wait_send()

    x_s[...] = xs[0]

    stores = [Fetch(src, dst) for src, dst in zip(kept, outs)]
    for i in (0, 1, 2, 7, 12):
        stores[i].start()

    rows = 256
    steps = tokens // rows
    lane = lax.broadcasted_iota(jnp.int32, (rows, 128), 1)
    klane = lax.broadcasted_iota(jnp.int32, (tokens, 128), 1)

    def attend(p, j):
        cols = slice(128 * p, 128 * p + 128)
        at = pl.ds(pl.multiple_of(j * rows, rows), rows)
        q = q_s[at, cols]
        mq = mq_s[at, :]
        qf = q.astype(F32)
        dead = mk_s[at, 4:5].astype(F32) < 0
        qk = qf * k_s[at, cols].astype(F32)
        v_own = v_s[at, cols].astype(F32)
        results = []
        for h in range(2):
            own_lanes = (lane < HEAD_DIM) if h == 0 else (lane >= HEAD_DIM)
            sc = dot_nt(jnp.where(own_lanes, q, mq), ka_s[h])
            own = jnp.sum(jnp.where(own_lanes, qk, 0.0), axis=1, keepdims=True)
            own = jnp.where(dead, own, -BIG)
            top = jnp.maximum(jnp.max(sc, axis=1, keepdims=True), own)
            pr = jnp.exp(sc - top).astype(BF16)
            r = dot_nn(pr, va_s[h])
            own_p = jnp.exp(own - top)
            total = (r[:, HEAD_DIM : HEAD_DIM + 1] if h == 0 else r[:, 0:1]) + own_p
            results.append((r + own_p * v_own) * (1.0 / total))
            other = lane - (HEAD_DIM if h == 0 else 0)
            a, b, c = three_parts(top + jnp.log(total))
            aug = jnp.where(other == 5, -a, jnp.where(other == 6, -b, jnp.where(other == 7, -c, mq.astype(F32))))
            (qa0_s, qa1_s)[p][h, at, :] = jnp.where(own_lanes, qf, aug).astype(BF16)
        o = jnp.where(lane < HEAD_DIM, results[0], results[1])
        (o0_s, o1_s)[p][at, :] = o
        ob_s[p, at, :] = o.astype(BF16)

    o_moves = []
    for p in range(2):
        to = o_s.at[pl.ds(0, mine), lanes_at(4 * p + member, 128)]
        o_moves.append(
            [Copy(ob_s.at[p, pl.ds(b * mine, mine)], to, target) for b, target in ((1, over_z), (3, across), (2, sibling))]
        )
    for p in range(2):
        cols = slice(128 * p, 128 * p + 128)
        for h in range(2):
            own_lanes = (klane < HEAD_DIM) if h == 0 else (klane >= HEAD_DIM)
            ka_s[h] = jnp.where(own_lanes, k_s[:, cols], mk_s[...])
            va_s[h] = jnp.where(own_lanes, v_s[:, cols], jnp.ones_like(v_s[:, cols]))

        @pl.loop(0, steps)
        def _(j, p=p):
            attend(p, j)

        for made in o_moves[p]:
            made.start()
        o_s[0:mine, lanes_at(4 * p + member, 128)] = ob_s[p, 0:mine, :]
        stores[3 + p].start()
        stores[5 + p].start()
        if p == 0:

            @pl.when(moved)
            def _():
                dy_trade.wait_recv()

            @pl.when(stays)
            def _():
                dy_local.wait()

            dy_core.start()

    for load in wo_loads:
        load.wait()
    o_core = Copy(o_s.at[pl.ds(0, mine)], o_s.at[pl.ds(mine, mine)], sibling)
    n2_core = Copy(n2_s.at[pl.ds(0, mine)], n2_s.at[pl.ds(mine, mine)], sibling)
    half = dim // 2
    for made in o_moves[0]:
        made.wait_recv()
    h_s[...] = x_s[...].astype(F32) + dot_nn(o_s[0:mine, 0:half], wo_s[0:half, :])
    for made in o_moves[1]:
        made.wait_recv()
    o_core.start()
    for at in pieces:
        hh = h_s[at, :] + dot_nn(o_s[at, half:dim], wo_s[half:dim, :])
        h_s[at, :] = hh
        n2_s[at, :] = (hh * lax.rsqrt(jnp.mean(hh * hh, axis=1, keepdims=True) + EPS) * gain_two_ref[...]).astype(BF16)
    n2_core.start()
    stores[8].start()
    dy_core.wait_recv()
    stores[11].start()
    o_core.wait_recv()
    stores[10].start()
    n2_core.wait_recv()
    stores[9].start()
    for made in to_z + to_core + on_core + [code_z, code_core, code_on, dy_core, o_core, n2_core] + o_moves[0] + o_moves[1]:
        made.wait_send()

    @pl.when(moved)
    def _():
        dy_trade.wait_send()

    for store in stores:
        store.wait()


def opening(tokens, live, lengths, gains, weights, dy):
    mine, dim = tokens.shape
    row = 4 * mine
    vmem = pl.BlockSpec(memory_space=pltpu.VMEM)
    anywhere = pl.BlockSpec(memory_space=pl.ANY)
    kept = [((row, dim), BF16), ((row, 256), BF16), ((row, 256), BF16)]
    kept += [((2, row, 128), BF16)] * 2 + [((row, 128), F32)] * 2 + [((row, 128), BF16)]
    kept += [((mine, dim), F32)] + [((2 * mine, dim), BF16)] * 3 + [((mine, dim), BF16)]
    scratch = [pltpu.VMEM(*v) for v in kept]
    scratch += [
        pltpu.VMEM((4, mine, dim), BF16),
        pltpu.VMEM((4, 16, mine), BF16),
        pltpu.VMEM((dim, 768), BF16),
        pltpu.VMEM((dim, dim), BF16),
        pltpu.VMEM((row, 256), BF16),
        pltpu.VMEM((row, 128), BF16),
        pltpu.VMEM((2, row, 128), BF16),
        pltpu.VMEM((2, row, 128), BF16),
        pltpu.VMEM((2, row, 128), BF16),
    ]
    remote, local = 12 + 4 + 2 + 6 + 2, 6 + 8 + 1 + OPENED
    semaphores = [pltpu.SemaphoreType.DMA((count,)) for count in (remote, remote, local)]
    return pl.pallas_call(
        opening_kernel,
        in_specs=[vmem, vmem, pl.BlockSpec(memory_space=pltpu.SMEM), vmem, vmem] + [anywhere] * 5,
        out_specs=[anywhere] * OPENED,
        out_shape=[jax.ShapeDtypeStruct(*v) for v in kept],
        scratch_shapes=scratch + semaphores,
        compiler_params=pltpu.CompilerParams(collective_id=1, has_side_effects=True, vmem_limit_bytes=VMEM_BYTES),
        cost_estimate=pl.CostEstimate(flops=16 * row * row * 256, bytes_accessed=30 << 20, transcendentals=4 * row * row),
        name="opening",
    )(tokens, live, lengths, *gains, *weights, dy)


def middle_kernel(gain_ref, *refs):
    refs = list(refs)

    def take(n):
        taken, refs[:n] = refs[:n], []
        return taken

    n2_ref, dy_ref, h_ref, o_ref, wg_ref, wu_ref, wd_ref, wo_ref = take(8)
    lo_o, dh_o, do_o, gate_o, up_o, out_o, da_o, db_o = take(8)
    n2_s, n2t_s, dy_s, h_s, wg_s, wu_s, wd_s, z_s, zc_s, dg_s, du_s = take(11)
    dn2_s, give_s, come_r, da_s, dap_s, dcr_s, dorow_s, own_s, far_s, stage_s, out_s, ra_s, rb_s, fr_s = take(14)
    send_sem, recv_sem, local_sem = take(3)

    d = lax.axis_index("dp")
    s = lax.axis_index("seq")
    core = d % 2
    xb = (d // 2) % 2
    yb = (d // 4) % 2
    low = s % 2
    sibling = (d + 1 - 2 * core, s)
    over_x = (d + 2 - 4 * xb, s)
    over_y = (d + 4 - 8 * yb, s)
    over_z = (d, s + 1 - 2 * low)

    barrier = pltpu.get_barrier_semaphore()
    for other in (sibling, over_x, over_y, over_z):
        pl.semaphore_signal(barrier, inc=1, device_id=other, device_id_type=MESH)

    counts = {"remote": 0, "local": 0}

    class Copy:
        def __init__(self, src, dst, target, like=None):
            self.parts = (src, dst, target, counts["remote"] if like is None else like.parts[3])
            counts["remote"] += like is None

        def made(self):
            src, dst, target, i = self.parts
            return pltpu.make_async_remote_copy(
                src_ref=src, dst_ref=dst, send_sem=send_sem.at[i], recv_sem=recv_sem.at[i], device_id=target, device_id_type=MESH
            )

        def start(self):
            self.made().start()

        def wait_recv(self):
            self.made().wait_recv()

        def wait_send(self):
            self.made().wait_send()

    class Fetch:
        def __init__(self, src, dst):
            self.parts = (src, dst, counts["local"])
            counts["local"] += 1

        def made(self):
            src, dst, i = self.parts
            return pltpu.make_async_copy(src, dst, local_sem.at[i])

        def start(self):
            self.made().start()

        def wait(self):
            self.made().wait()

    def at_of(start, size):
        return pl.ds(pl.multiple_of(start * size, size), size)

    mine, dim = h_s.shape
    both = 2 * mine
    units = wd_s.shape[0]
    tiles = [(i, min(256, units - i)) for i in range(0, units, 256)]
    n2_load = Fetch(n2_ref, n2_s)
    dy_load = Fetch(dy_ref, dy_s)
    h_load = Fetch(h_ref, h_s)
    w_loads = []
    for first, size in tiles:
        cols = pl.ds(pl.multiple_of(core * units + first, 128), size)
        w_loads.append(
            [
                Fetch(wg_ref.at[:, cols], wg_s.at[:, pl.ds(first, size)]),
                Fetch(wu_ref.at[:, cols], wu_s.at[:, pl.ds(first, size)]),
                Fetch(wd_ref.at[cols, :], wd_s.at[pl.ds(first, size), :]),
            ]
        )
    n2_load.start()
    for load in w_loads[0]:
        load.start()
    dy_load.start()
    for loads in w_loads[1:]:
        for load in loads:
            load.start()
    h_load.start()

    n2_load.wait()
    dy_load.wait()
    chunk = 256
    for (first, size), loads in zip(tiles, w_loads):
        for load in loads:
            load.wait()
        cols = slice(first, first + size)

        @pl.loop(0, both // chunk)
        def _(i, cols=cols):
            at = at_of(i, chunk)
            n2 = n2_s[at, :]
            g = dot_nn(n2, wg_s[:, cols])
            u = dot_nn(n2, wu_s[:, cols])
            dz = dot_nt(dy_s[at, :], wd_s[cols, :])
            act, slope = gelu_parts(g)
            z_s[at, cols] = (act * u).astype(BF16)
            dg_s[at, cols] = (dz * u * slope).astype(BF16)
            du_s[at, cols] = (dz * act).astype(BF16)

    pl.semaphore_wait(barrier, 4)
    top, end = pl.ds(0, mine), pl.ds(mine, mine)
    z_moves = [Copy(z_s.at[top], zc_s.at[end], sibling), Copy(z_s.at[end], zc_s.at[top], sibling)]
    for made in z_moves:
        made.start()

    quarter = dim // 4

    @pl.loop(0, 4)
    def _(i):
        at = at_of(i, quarter)
        dn2 = dot_nt(dg_s[...], wg_s[at, :]) + dot_nt(du_s[...], wu_s[at, :])
        dn2_s[:, at] = dn2[0:mine, :]
        give_s[:, at] = dn2[mine:both, :].astype(BF16)

    dn2_move = Copy(give_s, come_r, sibling)
    dn2_move.start()
    wo_s = wg_s.at[:, pl.ds(0, dim)]
    o_s = wu_s.at[pl.ds(0, both), pl.ds(0, dim)]
    wo_load, o_load = Fetch(wo_ref, wo_s), Fetch(o_ref, o_s)
    wo_load.start()
    o_load.start()

    half = dim // 2
    cut = half // 2

    def down_of(to, left):
        for first, size in tiles:
            to[first : first + size, :] = dot_tn(left[:, first : first + size], dy_s[:, at_of(core, half)]).astype(BF16)

    down_of(own_s, z_s)
    for made in z_moves:
        made.wait_recv()
    down_of(far_s, zc_s)
    rows = units // 2
    first_cols, last_cols = pl.ds(0, cut), pl.ds(cut, cut)
    a_far = Copy(far_s.at[:, first_cols], ra_s, over_y)
    a_own = Copy(own_s.at[:, first_cols], ra_s, over_y, like=a_far)
    b_own = Copy(own_s.at[at_of(1 - xb, rows), last_cols], rb_s.at[at_of(core, rows)], over_x)
    b_far = Copy(far_s.at[at_of(1 - xb, rows), last_cols], rb_s.at[at_of(1 - core, rows)], over_x)
    b_own.start()
    b_far.start()
    pl.when(yb == core)(a_far.start)
    pl.when(yb != core)(a_own.start)

    h_load.wait()
    dn2_move.wait_recv()
    third = mine // 3
    for i in range(3):
        at = pl.ds(i * third, third)
        dn2 = (dn2_s[at, :] + come_r[at, :].astype(F32)) * gain_ref[...]
        h = h_s[at, :]
        scale = lax.rsqrt(jnp.mean(h * h, axis=1, keepdims=True) + EPS)
        dh = dy_s[at, :].astype(F32) + scale * dn2 - h * (scale * scale * scale * jnp.mean(h * dn2, axis=1, keepdims=True))
        dn2_s[at, :] = dh
        da_s[at, :] = dh.astype(BF16)
    dh_store = Fetch(dn2_s, dh_o)
    dh_store.start()
    da_move = Copy(da_s.at[:, at_of(1 - core, half)], dap_s.at[end], sibling)
    da_move.start()
    dap_s[0:mine, :] = da_s[:, at_of(core, half)]
    wo_load.wait()
    do_s = come_r
    for i in range(3):
        at = pl.ds(i * third, third)
        do_s[at, :] = dot_nt(da_s[at, :], wo_s[...]).astype(BF16)
    do_core = Copy(do_s.at[:, at_of(1 - core, half)], dcr_s, sibling)
    do_core.start()
    do_z = []
    for p in range(2):
        do_z.append(Copy(do_s.at[:, at_of((2 * core + 1 - low) * 2 + p, 128)], dorow_s.at[p, pl.ds(mine, mine)], over_z))
    for made in do_z:
        made.start()

    n2t_s[...] = n2_s[...].T
    stores = []

    def unit_rows(to, right, turn, b, place):
        slot = turn % 2
        if turn >= 2:
            stores[turn - 2].wait()
        stage_s[slot] = dot_nn(n2t_s[b * quarter : (b + 1) * quarter, :], right[...]).astype(BF16)
        stores.append(Fetch(stage_s.at[slot], to.at[pl.ds(place * quarter, quarter)]))
        stores[-1].start()

    unit_rows(gate_o, dg_s, 0, 0, 0)
    do_core.wait_recv()
    for p in range(2):
        do_z.append(Copy(dcr_s.at[:, at_of(2 * (1 - low) + p, 128)], dorow_s.at[p, pl.ds(3 * mine, mine)], over_z))
        do_z[-1].start()
    for p in range(2):
        dorow_s[p, 0:mine, :] = do_s[:, at_of((2 * core + low) * 2 + p, 128)]
        dorow_s[p, 2 * mine : 3 * mine, :] = dcr_s[:, at_of(2 * low + p, 128)]
    for b in range(1, 4):
        unit_rows(gate_o, dg_s, b, b, b)
    for b in range(4):
        unit_rows(up_o, du_s, 4 + b, b, 2 * (b % 2) + b // 2)

    dn2_move.wait_send()

    @pl.loop(0, 4)
    def _(i):
        at = at_of(i, quarter)
        f = dot_nn(z_s[...], wd_s[:, at])
        h_s[:, at] = h_s[:, at] + f[0:mine, :]
        give_s[:, at] = f[mine:both, :].astype(BF16)

    f_move = Copy(give_s, fr_s, sibling)
    f_move.start()

    o_load.wait()
    da_move.wait_recv()
    da_move.wait_send()
    for xx in range(2):
        for yy in range(2):
            for p in range(2):
                to = pl.ds(((2 * xx + yy) * 2 + p) * 128, 128)
                m = 4 * p + 2 * yy + xx
                out_s[to, :] = dot_tn(o_s[:, m * 128 : (m + 1) * 128], dap_s[...]).astype(BF16)
    out_store = Fetch(out_s, out_o)
    out_store.start()
    f_move.wait_recv()
    for i in range(3):
        at = pl.ds(i * third, third)
        da_s[at, :] = (h_s[at, :] + fr_s[at, :].astype(F32)).astype(BF16)
    lo_store = Fetch(da_s, lo_o)
    lo_store.start()
    for made in do_z:
        made.wait_recv()
    do_store = Fetch(dorow_s, do_o)
    do_store.start()

    b_own.wait_recv()
    b_far.wait_recv()
    for part, y in ((own_s, core), (far_s, 1 - core)):
        at = at_of(y, rows)
        rb_s[at, :] = (rb_s[at, :].astype(F32) + part[at_of(xb, rows), last_cols].astype(F32)).astype(BF16)
    b_store = Fetch(rb_s, db_o)
    b_store.start()
    a_far.wait_recv()

    @pl.when(yb == core)
    def _():
        ra_s[...] = (ra_s[...].astype(F32) + own_s[:, first_cols].astype(F32)).astype(BF16)

    @pl.when(yb != core)
    def _():
        ra_s[...] = (ra_s[...].astype(F32) + far_s[:, first_cols].astype(F32)).astype(BF16)

    a_store = Fetch(ra_s, da_o)
    a_store.start()
    for made in z_moves + [do_core, f_move, a_far, b_own, b_far] + do_z:
        made.wait_send()
    for store in stores[-2:] + [dh_store, out_store, lo_store, do_store, b_store, a_store]:
        store.wait()


def middle(gain, n2_both, dy_both, h, o_both, gate_weight, up_weight, down_weight, out_weight):
    mine, dim = h.shape
    units = gate_weight.shape[1] // 2
    tiles = -(-units // 256)
    both = 2 * mine
    half, quarter = dim // 2, dim // 4
    vmem = pl.BlockSpec(memory_space=pltpu.VMEM)
    anywhere = pl.BlockSpec(memory_space=pl.ANY)
    outs = [((mine, dim), BF16), ((mine, dim), F32), ((2, 4 * mine, 128), BF16), ((dim, units), BF16), ((dim, units), BF16)]
    outs += [((dim, half), BF16), ((units, quarter), BF16), ((units, quarter), BF16)]
    scratch = [((both, dim), BF16), ((dim, both), BF16), ((both, dim), BF16), ((mine, dim), F32)]
    scratch += [((dim, units), BF16)] * 2 + [((units, dim), BF16)] + [((both, units), BF16)] * 4
    scratch += [((mine, dim), F32)] + [((mine, dim), BF16)] * 3 + [((both, half), BF16), ((mine, half), BF16)]
    scratch += [((2, 4 * mine, 128), BF16)] + [((units, half), BF16)] * 2 + [((2, quarter, units), BF16), ((dim, half), BF16)]
    scratch += [((units, quarter), BF16)] * 2 + [((mine, dim), BF16)]
    remote, local = 2 + 1 + 3 + 1 + 1 + 4 + 1, 3 + 3 * tiles + 2 + 1 + 8 + 5
    semaphores = [pltpu.SemaphoreType.DMA((count,)) for count in (remote, remote, local)]
    return pl.pallas_call(
        middle_kernel,
        in_specs=[vmem] + [anywhere] * 8,
        out_specs=[anywhere] * 8,
        out_shape=[jax.ShapeDtypeStruct(*v) for v in outs],
        scratch_shapes=[pltpu.VMEM(*v) for v in scratch] + semaphores,
        compiler_params=pltpu.CompilerParams(collective_id=2, has_side_effects=True, vmem_limit_bytes=VMEM_BYTES),
        cost_estimate=pl.CostEstimate(flops=18 * both * dim * units, bytes_accessed=40 << 20, transcendentals=both * units),
        name="middle",
    )(gain, n2_both, dy_both, h, o_both, gate_weight, up_weight, down_weight, out_weight)


def closing_kernel(mask_k_ref, gain_one_ref, *refs):
    refs = list(refs)

    def take(n):
        taken, refs[:n] = refs[:n], []
        return taken

    fetched = take(FETCHED)
    wq_ref, wk_ref, wv_ref, x_ref = take(4)
    da_ref, db_ref, gate_ref, up_ref, out_ref = take(5)
    (gt_o,) = take(1)
    finals = take(ITEMS)
    (heads_o,) = take(1)
    fetched_s = take(FETCHED)
    dorow_s, qa0_s, qa1_s, k_s, v_s, o0_s, o1_s, n1_s, dh_s = fetched_s
    firsts_r, seconds_s = take(ITEMS - 2), take(ITEMS - 2)
    seconds_r, cores_s, accs, lines = [take(ITEMS) for _ in range(4)]
    doa_s, dq_s, dqkv_s, hs_s, h1_r, h2_s, h2_r, hk_s, hc_s, hh_s, hh_r = take(11)
    w_s, x_s, dn_s = take(3)
    cs_s, cr_r, zr_r, send_sem, recv_sem, local_sem = take(6)

    d = lax.axis_index("dp")
    s = lax.axis_index("seq")
    core = d % 2
    xb = (d // 2) % 2
    yb = (d // 4) % 2
    low = s % 2
    high = s // 2
    sibling = (d + 1 - 2 * core, s)
    over_x = (d + 2 - 4 * xb, s)
    over_y = (d + 4 - 8 * yb, s)
    over_z = (d, s + 1 - 2 * low)
    over_high = (d, s + 2 - 4 * high)
    swapped = (d + 1 - 2 * core, s + 2 - 4 * high)
    third = (d, 3 - s)
    inner = (s == 1) | (s == 2)
    outer = (s == 0) | (s == 3)
    moved = core != high

    barrier = pltpu.get_barrier_semaphore()
    for other in (sibling, over_x, over_y, over_z, over_high, swapped, third):
        pl.semaphore_signal(barrier, inc=1, device_id=other, device_id_type=MESH)
    pl.semaphore_wait(barrier, 7)

    counts = {"remote": 0, "local": 0}

    class Copy:
        def __init__(self, src, dst, target):
            self.parts = (src, dst, target, counts["remote"])
            counts["remote"] += 1

        def made(self):
            src, dst, target, i = self.parts
            return pltpu.make_async_remote_copy(
                src_ref=src, dst_ref=dst, send_sem=send_sem.at[i], recv_sem=recv_sem.at[i], device_id=target, device_id_type=MESH
            )

        def start(self):
            self.made().start()

        def wait_recv(self):
            self.made().wait_recv()

        def wait_send(self):
            self.made().wait_send()

    copy = Copy

    class Fetch:
        def __init__(self, src, dst):
            self.parts = (src, dst, counts["local"])
            counts["local"] += 1

        def made(self):
            src, dst, i = self.parts
            return pltpu.make_async_copy(src, dst, local_sem.at[i])

        def start(self):
            self.made().start()

        def wait(self):
            self.made().wait()

    def rows_at(start, size):
        return pl.ds(pl.multiple_of(start * size, size), size)

    def lanes_at(start, size):
        return pl.ds(pl.multiple_of(start * size, size), size)

    class Item:
        pass

    items = []
    along_x, along_y = (over_x, xb), (over_y, yb)
    wide = accs[2].shape[2]
    every, left, right = [pl.ds(0, size) for size in (accs[0].shape[2], wide, accs[6].shape[2])]
    rest = pl.ds(wide, accs[4].shape[2])
    for i, (whole, cols, first, second) in enumerate(
        (
            (da_ref, every, None, along_x),
            (db_ref, every, None, along_y),
            (gate_ref, left, along_y, along_x),
            (up_ref, left, along_x, along_y),
            (gate_ref, rest, along_y, along_x),
            (up_ref, rest, along_x, along_y),
            (out_ref, right, along_x, along_y),
        )
    ):
        it = Item()
        it.r, it.c, it.a, it.z, it.o = [group[i] for group in (seconds_r, cores_s, accs, lines, finals)]
        n = it.n = it.c.shape[0]
        target, it.bit = second
        base = it.bit * (2 * n)
        it.late = first is not None
        if it.late:
            it.r1, it.t = firsts_r[i - 2], seconds_s[i - 2]
            it.first = copy(whole.at[rows_at(1 - first[1], 4 * n), cols], it.r1, first[0])
            kept = first[1] * (4 * n)
            it.far = Fetch(whole.at[pl.ds(pl.multiple_of(kept + (1 - it.bit) * (2 * n), 2 * n), 2 * n), cols], it.t)
            it.chip = copy(it.t, it.r, target)
            base = base + kept
        else:
            it.chip = copy(whole.at[rows_at(1 - it.bit, 2 * n), cols], it.r, target)
        it.parts = [
            Fetch(whole.at[pl.ds(pl.multiple_of(base + (1 - core) * n, n), n), cols], it.c),
            Fetch(whole.at[pl.ds(pl.multiple_of(base + core * n, n), n), cols], it.a.at[core]),
        ]
        it.core = copy(it.c, it.a.at[core], sibling)
        it.in1 = copy(it.a, it.z, (d, jnp.where(s == 0, 1, 2)))
        it.in2 = copy(it.a, it.o, third)
        it.out = copy(it.o, it.o, (d, jnp.where(s == 1, 0, 3)))
        items.append(it)

    def start(it):
        if it.late:
            it.first.start()
            it.far.start()
        else:
            it.chip.start()
        for part in it.parts:
            part.start()

    def step0(it):
        at = rows_at(1 - it.bit, 2 * it.n)
        it.far.wait()
        it.first.wait_recv()
        it.t[...] = (it.t[...].astype(F32) + it.r1[at, :].astype(F32)).astype(BF16)
        it.chip.start()

    def step1(it):
        n = it.n
        for part in it.parts:
            part.wait()
        it.chip.wait_recv()

        def come(which):
            value = it.r[rows_at(which, n), :].astype(F32)
            if it.late:
                at = pl.ds(pl.multiple_of(it.bit * (2 * n) + which * n, n), n)
                value = value + it.r1[at, :].astype(F32)
            return value

        it.c[...] = (it.c[...].astype(F32) + come(1 - core)).astype(BF16)
        it.core.start()
        it.a[core] = (it.a[core].astype(F32) + come(core)).astype(BF16)

    def step2(it):
        it.core.wait_recv()

        @pl.when(outer)
        def _():
            it.in1.start()

    def step3(it):
        @pl.when(inner)
        def _():
            it.in1.wait_recv()
            it.a[...] = (it.a[...].astype(F32) + it.z[...].astype(F32)).astype(BF16)
            it.in2.start()

    def step4(it):
        @pl.when(inner)
        def _():
            it.in2.wait_recv()
            it.o[...] = (it.a[...].astype(F32) + it.o[...].astype(F32)).astype(BF16)
            it.out.start()

    def step5(it):
        @pl.when(outer)
        def _():
            it.out.wait_recv()

    def finish(it):
        if it.late:
            it.first.wait_send()
        it.chip.wait_send()
        it.core.wait_send()

        @pl.when(outer)
        def _():
            it.in1.wait_send()

        @pl.when(inner)
        def _():
            it.in2.wait_send()
            it.out.wait_send()

    down_a, down_b, gate_a, up_a, gate_b, up_b, outp = items

    mine, dim = x_s.shape
    loads = [Fetch(src, dst) for src, dst in zip(fetched, fetched_s)]
    x_load = Fetch(x_ref, x_s)
    w_loads = []
    for p in range(2):
        for t, w in enumerate((wq_ref, wk_ref, wv_ref)):
            w_loads.append(Fetch(w.at[:, lanes_at((2 * core + low) * 2 + p, 128)], w_s.at[:, pl.ds((3 * p + t) * 128, 128)]))
    for load in loads[:7]:
        load.start()
    for it in (down_a, down_b, gate_a, up_a):
        start(it)
    for load in loads[7:] + [x_load] + w_loads:
        load.start()

    block = hk_s.shape[1]
    half = block // 2
    firsts = ((over_x, over_y), (over_y, over_x))
    heads = []
    for p in range(2):
        h = Item()
        h.p1 = [copy(hs_s.at[p, i], h1_r.at[p, i], firsts[p][0]) for i in range(2)]
        h.p2 = copy(h2_s.at[p], h2_r.at[p], firsts[p][1])
        h.core = copy(hk_s.at[p, rows_at(1 - core, half)], hc_s.at[p, core], sibling)
        h.high = copy(hh_s.at[p], hh_r.at[p], over_high)
        h.z = copy(heads_o.at[low, p], heads_o.at[low, p], over_z)
        heads.append(h)

    def product(p, yy, xx):
        return dot_tn(n1_s[:, lanes_at(2 * yy + xx, block)], dqkv_s[p])

    def heads0(p):
        h = heads[p]
        for turn in range(2):
            if p == 0:
                i = (1 - yb) if turn == 0 else yb
                hs_s[p, turn] = product(p, i, 1 - xb).astype(BF16)
            else:
                i = (1 - xb) if turn == 0 else xb
                hs_s[p, turn] = product(p, 1 - yb, i).astype(BF16)
            h.p1[turn].start()

    def heads1(p):
        h = heads[p]
        part = product(p, 1 - yb, xb) if p == 0 else product(p, yb, 1 - xb)
        h.p1[0].wait_recv()
        h2_s[p] = (part + h1_r[p, 0].astype(F32)).astype(BF16)
        h.p2.start()

    def heads2(p):
        h = heads[p]
        part = product(p, yb, xb)
        h.p1[1].wait_recv()
        part = part + h1_r[p, 1].astype(F32)
        h.p2.wait_recv()
        hk_s[p] = (part + h2_r[p].astype(F32)).astype(BF16)
        h.core.start()
        hc_s[p, core] = hk_s[p, rows_at(core, half), :]

    def heads3(p):
        h = heads[p]
        h.core.wait_recv()
        hh_s[p] = hc_s[p]
        h.high.start()

    def heads4(p):
        h = heads[p]
        h.high.wait_recv()
        heads_o[low, p] = (hh_s[p].astype(F32) + hh_r[p].astype(F32)).astype(BF16)
        h.z.start()

    def heads5(p):
        heads[p].z.wait_recv()

    def finish_heads(p):
        h = heads[p]
        for made in h.p1 + [h.p2, h.core, h.high, h.z]:
            made.wait_send()

    tokens = k_s.shape[0]
    rows = 256
    steps = tokens // rows
    lane = lax.broadcasted_iota(jnp.int32, (tokens, 128), 1)
    klane = lax.broadcasted_iota(jnp.int32, (rows, 128), 1)

    def prepare(p):
        do = dorow_s[p].astype(F32)
        prod = do * (o0_s, o1_s)[p][...]
        for h in range(2):
            mine = (lane < HEAD_DIM) if h == 0 else (lane >= HEAD_DIM)
            other = lane - (HEAD_DIM if h == 0 else 0)
            delta = jnp.sum(jnp.where(mine, prod, 0.0), axis=1, keepdims=True)
            a, b, c = three_parts(delta)
            aug = jnp.where(other == 5, -a, jnp.where(other == 6, -b, jnp.where(other == 7, -c, 0.0)))
            doa_s[h] = jnp.where(mine, do, aug).astype(BF16)
        dq_s[...] = jnp.zeros_like(dq_s)

    def attend(p, j):
        qa_s = (qa0_s, qa1_s)[p]
        cols = slice(128 * p, 128 * p + 128)
        here = pl.ds(pl.multiple_of(j * rows, rows), rows)
        k = k_s[here, cols]
        v = v_s[here, cols]
        kf = k.astype(F32)
        vf = v.astype(F32)
        mk = mask_k_ref[here, :]
        dead = jnp.where(mk[:, 4:5].astype(F32) < 0, 1.0, 0.0)
        dks, dvs = [], []
        for h in range(2):
            kmine = (klane < HEAD_DIM) if h == 0 else (klane >= HEAD_DIM)
            other = klane - (HEAD_DIM if h == 0 else 0)
            one = (other >= 5) & (other < 8)
            ka = jnp.where(kmine, k, mk)
            va = jnp.where(kmine, v, jnp.where(one, jnp.ones_like(v), jnp.zeros_like(v)))
            pr = jnp.exp(dot_nt(ka, qa_s[h]))
            ds = (pr * dot_nt(va, doa_s[h])).astype(BF16)
            dk = dot_nn(ds, qa_s[h])
            dv = dot_nn(pr.astype(BF16), doa_s[h])
            dq_s[h] += dot_tn(ds, ka)
            qd = qa_s[h, here, :].astype(F32)
            dod = doa_s[h, here, :].astype(F32)
            own = jnp.sum(jnp.where(kmine | one, qd * jnp.where(kmine, kf, 1.0), 0.0), axis=1, keepdims=True)
            own_p = jnp.where(dead > 0, jnp.exp(jnp.where(dead > 0, own, 0.0)), 0.0)
            own_d = jnp.sum(jnp.where(kmine | one, dod * jnp.where(kmine, vf, 1.0), 0.0), axis=1, keepdims=True)
            own_ds = own_p * own_d
            dks.append(dk + own_ds * qd)
            dvs.append(dv + own_p * dod)
            dq_s[h, here, :] += jnp.where(kmine, own_ds * kf, 0.0)
        dqkv_s[p, here, 128:256] = jnp.where(klane < HEAD_DIM, dks[0], dks[1]).astype(BF16)
        dqkv_s[p, here, 256:384] = jnp.where(klane < HEAD_DIM, dvs[0], dvs[1]).astype(BF16)

    after = (
        {
            3: lambda: (step1(down_a), step1(down_b)),
            4: lambda: (step2(down_a), step2(down_b), start(gate_b), start(up_b)),
        },
        {
            0: lambda: (step0(gate_a), step0(up_a), step3(down_a)),
            2: lambda: step3(down_b),
            3: lambda: step4(down_a),
            4: lambda: (step1(gate_a), step1(up_a)),
            5: lambda: (step2(gate_a), step2(up_a), step4(down_b), step0(gate_b), step0(up_b), start(outp)),
        },
    )
    for load in loads[:7]:
        load.wait()
    for p in range(2):
        prepare(p)

        @pl.loop(0, steps)
        def _(j, p=p):
            attend(p, j)
            for i, work in after[p].items():

                @pl.when(j == i)
                def _(work=work):
                    work()

        dqkv_s[p, :, 0:128] = jnp.where(lane < HEAD_DIM, dq_s[0], dq_s[1]).astype(BF16)
        if p == 0:
            loads[7].wait()
        heads0(p)

    cut = mine // 3
    width = dqkv_s.shape[2]
    for load in w_loads + [x_load, loads[8]]:
        load.wait()

    def dn1_of(i):
        at = pl.ds(i * mine, mine)
        return dot_nt(dqkv_s[0, at, :], w_s[:, 0:width]) + dot_nt(dqkv_s[1, at, :], w_s[:, width : 2 * width])

    to_core = [copy(cs_s.at[i], cr_r.at[i], sibling) for i in range(2)]
    to_z = [copy(cs_s.at[1, pl.ds(i * cut, cut)], zr_r.at[pl.ds(i * cut, cut)], over_z) for i in range(3)]
    to_home = [copy(cs_s.at[0, pl.ds(i * cut, cut)], gt_o.at[pl.ds(i * cut, cut)], swapped) for i in range(3)]
    for i in (1, 0):
        cs_s[i] = dn1_of(2 + i).astype(BF16)
        to_core[i].start()
    dn = dn1_of(1)
    to_core[1].wait_recv()
    to_core[1].wait_send()
    cs_s[1] = (dn + cr_r[1].astype(F32)).astype(BF16)
    for made in to_z:
        made.start()
    heads1(0)
    step3(gate_a)
    dn_s[...] = dn1_of(0)
    heads2(0)
    to_core[0].wait_recv()
    to_core[0].wait_send()
    heads1(1)
    heads3(0)
    step3(up_a)
    heads2(1)
    step4(gate_a)
    heads4(0)
    heads3(1)
    for i in range(3):
        at = pl.ds(i * cut, cut)
        to_z[i].wait_recv()
        dn = dn_s[at, :] + cr_r[0, at, :].astype(F32) + zr_r[at, :].astype(F32)
        x = x_s[at, :].astype(F32)
        scale = lax.rsqrt(jnp.mean(x * x, axis=1, keepdims=True) + EPS)
        dn = dn * gain_one_ref[...]
        grad = dh_s[at, :] + scale * dn - x * (scale * scale * scale * jnp.mean(x * dn, axis=1, keepdims=True))
        cs_s[0, at, :] = grad.astype(BF16)

        @pl.when(moved)
        def _():
            to_home[i].start()

        @pl.when(jnp.logical_not(moved))
        def _():
            gt_o[at, :] = cs_s[0, at, :]

    step1(gate_b)
    step1(up_b)
    step4(up_a)
    step2(gate_b)
    step2(up_b)
    step0(outp)
    heads4(1)
    step3(gate_b)
    step3(up_b)
    step1(outp)
    step2(outp)
    step4(gate_b)
    step4(up_b)
    step3(outp)
    step4(outp)
    for it in items:
        step5(it)
    heads5(0)
    heads5(1)
    for it in items:
        finish(it)
    for p in range(2):
        finish_heads(p)
    for made in to_z:
        made.wait_send()

    @pl.when(moved)
    def _():
        for made in to_home:
            made.wait_recv()
            made.wait_send()


def closing(mask_key, gain, fetched, weights, x, grads):
    tokens = mask_key.shape[0]
    mine, dim = x.shape
    vmem = pl.BlockSpec(memory_space=pltpu.VMEM)
    anywhere = pl.BlockSpec(memory_space=pl.ANY)
    down, _, gate, _, outp = [w.shape for w in grads]
    wide = 128 * -(-(gate[1] // 2) // 128)
    shards = [(down[0] // 4, down[1])] * 2 + [(gate[0] // 8, wide)] * 2 + [(gate[0] // 8, gate[1] - wide)] * 2
    shards.append((outp[0] // 8, outp[1]))
    lates = shards[2:]
    block = dim // 4
    three = 3 * 128
    scratch = [pltpu.VMEM(v.shape, v.dtype) for v in fetched]
    scratch += [pltpu.VMEM((4 * rows, cols), BF16) for rows, cols in lates]
    scratch += [pltpu.VMEM((2 * rows, cols), BF16) for rows, cols in lates]
    scratch += [pltpu.VMEM((2 * rows, cols), BF16) for rows, cols in shards]
    scratch += [pltpu.VMEM(w, BF16) for w in shards]
    scratch += [pltpu.VMEM((2,) + w, BF16) for w in shards] * 2
    scratch += [
        pltpu.VMEM((2, tokens, 128), BF16),
        pltpu.VMEM((2, tokens, 128), F32),
        pltpu.VMEM((2, tokens, three), BF16),
        pltpu.VMEM((2, 2, block, three), BF16),
        pltpu.VMEM((2, 2, block, three), BF16),
        pltpu.VMEM((2, block, three), BF16),
        pltpu.VMEM((2, block, three), BF16),
        pltpu.VMEM((2, block, three), BF16),
        pltpu.VMEM((2, 2, block // 2, three), BF16),
        pltpu.VMEM((2, 2, block // 2, three), BF16),
        pltpu.VMEM((2, 2, block // 2, three), BF16),
        pltpu.VMEM((dim, 2 * three), BF16),
        pltpu.VMEM((mine, dim), BF16),
        pltpu.VMEM((mine, dim), F32),
        pltpu.VMEM((2, mine, dim), BF16),
        pltpu.VMEM((2, mine, dim), BF16),
        pltpu.VMEM((mine, dim), BF16),
    ]
    remote = 6 * ITEMS - 2 + 2 * 6 + 2 + 3 + 3
    local = FETCHED + 7 + 3 * ITEMS - 2
    semaphores = [pltpu.SemaphoreType.DMA((count,)) for count in (remote, remote, local)]
    return pl.pallas_call(
        closing_kernel,
        in_specs=[vmem] * 2 + [anywhere] * (FETCHED + 4 + 5),
        out_specs=[vmem] * (2 + ITEMS),
        out_shape=[jax.ShapeDtypeStruct((mine, dim), BF16)]
        + [jax.ShapeDtypeStruct((2,) + w, BF16) for w in shards]
        + [jax.ShapeDtypeStruct((2, 2, 2, block // 2, three), BF16)],
        scratch_shapes=scratch + semaphores,
        compiler_params=pltpu.CompilerParams(collective_id=0, has_side_effects=True, vmem_limit_bytes=VMEM_BYTES),
        cost_estimate=pl.CostEstimate(
            flops=40 * tokens * tokens * 256, bytes_accessed=40 << 20, transcendentals=4 * tokens * tokens
        ),
        name="closing",
    )(mask_key, gain, *fetched, *weights, x, *grads)


def placing_kernel(gt, da, db, ga, ua, gb, ub, out, heads, wq, wk, wv, wg, wu, g1, g2, *outs):
    gt_o, q_o, k_o, v_o, out_o, gate_o, up_o, down_o, g1_o, g2_o = outs
    gt_o[...] = gt[...].astype(F32)
    wide = ga.shape[2]
    size = wide + gb.shape[2]
    cut = da.shape[2]
    for c in range(2):
        for to, one, two in ((gate_o, ga, gb), (up_o, ua, ub)):
            to[:, c * size : c * size + wide] = one[c].astype(F32)
            to[:, c * size + wide : (c + 1) * size] = two[c].astype(F32)
        down_o[:, 2 * c * cut : (2 * c + 1) * cut] = da[c].astype(F32)
        down_o[:, (2 * c + 1) * cut : (2 * c + 2) * cut] = db[c].astype(F32)
        out_o[:, 2 * c * cut : (2 * c + 2) * cut] = out[c].astype(F32)
    for m in range(4):
        for p in range(2):
            at = slice((2 * m + p) * 128, (2 * m + p + 1) * 128)
            for t, to in enumerate((q_o, k_o, v_o)):
                to[:, at] = heads[m % 2, p, m // 2, :, t * 128 : (t + 1) * 128].astype(F32)

    def along(pairs):
        return sum(jnp.sum(grad[...] * w[...].astype(F32), axis=1, keepdims=True) for grad, w in pairs)

    g1_o[...] = along(((q_o, wq), (k_o, wk), (v_o, wv))) / g1[...]
    g2_o[...] = along(((gate_o, wg), (up_o, wu))) / g2[...]


def placing(grads, heads, shards):
    gt, da, _, ga, _, gb, _, out = grads
    n, dim = out.shape[1], 2 * out.shape[2]
    units = 2 * (ga.shape[2] + gb.shape[2])
    shapes = [gt.shape] + [(n, dim)] * 4 + [(n, units)] * 2 + [(da.shape[1], dim)] + [(n, 1)] * 2
    vmem = pl.BlockSpec(memory_space=pltpu.VMEM)
    return pl.pallas_call(
        placing_kernel,
        in_specs=[vmem] * 16,
        out_specs=[vmem] * 10,
        out_shape=[jax.ShapeDtypeStruct(v, F32) for v in shapes],
        compiler_params=pltpu.CompilerParams(vmem_limit_bytes=40 << 20),
        cost_estimate=pl.CostEstimate(flops=1 << 22, bytes_accessed=14 << 20, transcendentals=0),
        name="placing",
    )(*grads, heads, *shards)


def local_fused(
    dps,
    seqs,
    tokens,
    query_weight,
    key_weight,
    value_weight,
    out_weight,
    gate_weight,
    up_weight,
    down_weight,
    attention_gain,
    feedforward_gain,
    pair_lengths,
    live_mask,
    out_grad,
):
    mine, dim = tokens.shape
    d = lax.axis_index("dp")
    s = lax.axis_index("seq")
    core = d % 2
    x_bit = (d // 2) % 2
    y_bit = (d // 4) % 2
    moved = core != s // 2

    def move(value, target):
        pairs = []
        for i in range(dps * seqs):
            to = target(i // seqs, i % seqs)
            if to is not None:
                pairs.append((i, to[0] * seqs + to[1]))
        return lax.ppermute(value, AXES, pairs)

    def trade(value):
        return move(value, lambda dd, ss: (dd ^ 1, ss ^ 2) if dd % 2 != ss // 2 else None)

    def with_core(value):
        return move(value, lambda dd, ss: (dd ^ 1, ss))

    def half_of(value, which, axis):
        size = value.shape[axis] // 2
        return lax.dynamic_slice_in_dim(value, which * size, size, axis=axis)

    projections = (query_weight, key_weight, value_weight)
    n1_row, k, v, qa_0, qa_1, o_0, o_1, mask_key, h, n2_both, o_both, dy_both, x_low = opening(
        tokens, live_mask[None, :], pair_lengths, (attention_gain[None, :], feedforward_gain[None, :]),
        (*projections, out_weight), out_grad,
    )

    layer_out, dh, do, gate, up, outp, down_a, down_b = middle(
        feedforward_gain[None, :], n2_both, dy_both, h, o_both, gate_weight, up_weight, down_weight, out_weight
    )
    layer_out = jnp.where(moved, trade(layer_out), layer_out)

    *grads, heads_grads = closing(
        mask_key, attention_gain[None, :], (do, qa_0, qa_1, k, v, o_0, o_1, n1_row, dh), projections, x_low,
        (down_a, down_b, gate, up, outp),
    )

    def shard(weight):
        size = weight.shape[0] // dps
        return lax.dynamic_slice_in_dim(weight, d * size, size, axis=0)

    shards = [shard(w) for w in (query_weight, key_weight, value_weight, gate_weight, up_weight)]
    shards += [shard(w)[:, None] for w in (attention_gain, feedforward_gain)]
    *results, gain_one, gain_two = placing(grads, heads_grads, shards)
    return (layer_out, *results, gain_one[:, 0], gain_two[:, 0])


def solution(mesh):
    both = P(("dp", "seq"), None)
    rows = P("dp", None)
    dps, seqs = mesh.shape["dp"], mesh.shape["seq"]
    local = local_fused if (dps, seqs) == (8, 4) else local_plain
    return jax.shard_map(
        functools.partial(local, dps, seqs),
        mesh=mesh,
        in_specs=(both, P(), P(), P(), P(), P(), P(), P(), P(), P(), rows, P(("dp", "seq")), both),
        out_specs=(both, both, rows, rows, rows, rows, rows, rows, rows, P("dp"), P("dp")),
        check_vma=False,
    )
```

```python
import functools

import jax
import jax.numpy as jnp
from jax import lax
from jax.experimental import pallas as pl
from jax.experimental.pallas import tpu as pltpu
from jax.sharding import PartitionSpec as P

HEADS = 16
HEAD_DIM = 64
EPS = 1e-06
BIG = float(2.0**40)
F32 = jnp.float32
BF16 = jnp.bfloat16
AXES = ("dp", "seq")
MESH = pl.DeviceIdType.MESH
VMEM_BYTES = 62 << 20
ITEMS, FETCHED, OPENED = 9, 9, 13


def dot_nn(a, b):
    return lax.dot_general(a, b, (((1,), (0,)), ((), ())), preferred_element_type=F32)


def dot_nt(a, b):
    return lax.dot_general(a, b, (((1,), (1,)), ((), ())), preferred_element_type=F32)


def dot_tn(a, b):
    return lax.dot_general(a, b, (((0,), (0,)), ((), ())), preferred_element_type=F32)


def three_parts(v):
    high = v.astype(BF16).astype(F32)
    mid = (v - high).astype(BF16).astype(F32)
    low = (v - high - mid).astype(BF16).astype(F32)
    return high, mid, low


def forward_kernel(keep_queries, q_ref, k_ref, v_ref, mq_ref, mk_ref, dead_ref, kd_ref, vd_ref, o_ref, l_ref):
    lane = lax.broadcasted_iota(jnp.int32, q_ref.shape, 1)
    klane = lax.broadcasted_iota(jnp.int32, k_ref.shape, 1)
    q = q_ref[...]
    dead = dead_ref[...]
    qk = q.astype(F32) * kd_ref[...].astype(F32)
    outs, logs = [], []
    for h in range(2):
        mine = (lane < HEAD_DIM) if h == 0 else (lane >= HEAD_DIM)
        kmine = (klane < HEAD_DIM) if h == 0 else (klane >= HEAD_DIM)
        qa = jnp.where(mine, q, mq_ref[...])
        ka = jnp.where(kmine, k_ref[...], mk_ref[...])
        s = dot_nt(qa, ka)
        own = jnp.sum(jnp.where(mine, qk, 0.0), axis=1, keepdims=True)
        own = jnp.where(dead > 0, own, -BIG)
        top = jnp.maximum(jnp.max(s, axis=1, keepdims=True), own)
        p = jnp.exp(s - top).astype(BF16)
        va = jnp.where(kmine, v_ref[...], jnp.ones_like(v_ref[...]))
        r = dot_nn(p, va)
        own_p = jnp.exp(own - top)
        total = (r[:, HEAD_DIM : HEAD_DIM + 1] if h == 0 else r[:, 0:1]) + own_p
        outs.append((r + own_p * vd_ref[...].astype(F32)) * (1.0 / total))
        log = top + jnp.log(total)
        if keep_queries:
            other = lane - (HEAD_DIM if h == 0 else 0)
            a, b, c = three_parts(log)
            aug = mq_ref[...].astype(F32)
            aug = jnp.where(other == 5, -a, jnp.where(other == 6, -b, jnp.where(other == 7, -c, aug)))
            l_ref[h] = jnp.where(mine, q.astype(F32), aug).astype(BF16)
        logs.append(log)
    o_ref[...] = jnp.where(lane < HEAD_DIM, outs[0], outs[1])
    if not keep_queries:
        l_ref[...] = jnp.where(lane < HEAD_DIM, logs[0], logs[1])


def rows_per_step(tokens):
    for rows in (512, 384, 256, 128):
        if tokens % rows == 0 and rows * tokens <= 800000:
            return rows
    return 128


def attention_forward(q, k, v, mq, mk, dead, group=None):
    tokens, width = q.shape
    rows = rows_per_step(tokens)
    first, count = (0, width // 128) if group is None else (group, 1)
    part = pl.BlockSpec((rows, 128), lambda h, i: (i, h + first))
    full = pl.BlockSpec((tokens, 128), lambda h, i: (0, h + first))
    out = pl.BlockSpec((rows, 128), lambda h, i: (i, h))
    keep = group is not None
    log_out, log_shape = out, jax.ShapeDtypeStruct((tokens, 128 * count), F32)
    if keep:
        log_out = pl.BlockSpec((2, rows, 128), lambda h, i: (0, i, 0))
        log_shape = jax.ShapeDtypeStruct((2, tokens, 128), BF16)
    return pl.pallas_call(
        functools.partial(forward_kernel, keep),
        grid=(count, tokens // rows),
        in_specs=[
            part,
            full,
            full,
            pl.BlockSpec((rows, 128), lambda h, i: (i, 0)),
            pl.BlockSpec((tokens, 128), lambda h, i: (0, 0)),
            pl.BlockSpec((rows, 1), lambda h, i: (i, 0)),
            part,
            part,
        ],
        out_specs=[out, log_out],
        out_shape=[jax.ShapeDtypeStruct((tokens, 128 * count), F32), log_shape],
        compiler_params=pltpu.CompilerParams(vmem_limit_bytes=56 << 20),
        cost_estimate=pl.CostEstimate(
            flops=16 * tokens * tokens * 128 * count, bytes_accessed=16 * tokens * width, transcendentals=2 * tokens * tokens * count
        ),
        name="attention_forward",
    )(q, k, v, mq, mk, dead, k, v)


def backward_kernel(
    q_ref, k_ref, v_ref, do_ref, o_ref, l_ref, mq_ref, mk_ref, dead_ref, dq_ref, dk_ref, dv_ref, qa_s, doa_s, dq_s
):
    j = pl.program_id(1)
    tokens = q_ref.shape[0]
    rows = k_ref.shape[0]
    lane = lax.broadcasted_iota(jnp.int32, (tokens, 128), 1)
    klane = lax.broadcasted_iota(jnp.int32, (rows, 128), 1)

    @pl.when(j == 0)
    def _():
        do = do_ref[...].astype(F32)
        prod = do * o_ref[...]
        q = q_ref[...].astype(F32)
        logs = l_ref[...]
        for h in range(2):
            mine = (lane < HEAD_DIM) if h == 0 else (lane >= HEAD_DIM)
            other = lane - (HEAD_DIM if h == 0 else 0)
            delta = jnp.sum(jnp.where(mine, prod, 0.0), axis=1, keepdims=True)
            log = logs[:, 0:1] if h == 0 else logs[:, HEAD_DIM : HEAD_DIM + 1]
            a, b, c = three_parts(log)
            aug = mq_ref[...].astype(F32)
            aug = jnp.where(other == 5, -a, jnp.where(other == 6, -b, jnp.where(other == 7, -c, aug)))
            qa_s[h] = jnp.where(mine, q, aug).astype(BF16)
            a, b, c = three_parts(delta)
            aug = jnp.where(other == 5, -a, jnp.where(other == 6, -b, jnp.where(other == 7, -c, 0.0)))
            doa_s[h] = jnp.where(mine, do, aug).astype(BF16)
        dq_s[...] = jnp.zeros_like(dq_s)

    k = k_ref[...]
    v = v_ref[...]
    here = pl.ds(pl.multiple_of(j * rows, rows), rows)
    kf = k.astype(F32)
    vf = v.astype(F32)
    dead = dead_ref[...]
    dks, dvs = [], []
    for h in range(2):
        kmine = (klane < HEAD_DIM) if h == 0 else (klane >= HEAD_DIM)
        other = klane - (HEAD_DIM if h == 0 else 0)
        one = (other >= 5) & (other < 8)
        ka = jnp.where(kmine, k, mk_ref[...])
        va = jnp.where(kmine, v, jnp.where(one, jnp.ones_like(v), jnp.zeros_like(v)))
        p = jnp.exp(dot_nt(ka, qa_s[h]))
        ds = (p * dot_nt(va, doa_s[h])).astype(BF16)
        dk = dot_nn(ds, qa_s[h])
        dv = dot_nn(p.astype(BF16), doa_s[h])
        dq_s[h] += dot_tn(ds, ka)
        qd = qa_s[h, here, :].astype(F32)
        dod = doa_s[h, here, :].astype(F32)
        own = jnp.sum(jnp.where(kmine | one, qd * jnp.where(kmine, kf, 1.0), 0.0), axis=1, keepdims=True)
        own_p = jnp.where(dead > 0, jnp.exp(jnp.where(dead > 0, own, 0.0)), 0.0)
        own_d = jnp.sum(jnp.where(kmine | one, dod * jnp.where(kmine, vf, 1.0), 0.0), axis=1, keepdims=True)
        own_ds = own_p * own_d
        dks.append(dk + own_ds * qd)
        dvs.append(dv + own_p * dod)
        dq_s[h, here, :] += jnp.where(kmine, own_ds * kf, 0.0)
    dk_ref[...] = jnp.where(klane < HEAD_DIM, dks[0], dks[1]).astype(BF16)
    dv_ref[...] = jnp.where(klane < HEAD_DIM, dvs[0], dvs[1]).astype(BF16)

    @pl.when(j == pl.num_programs(1) - 1)
    def _():
        dq_ref[...] = jnp.where(lane < HEAD_DIM, dq_s[0], dq_s[1]).astype(BF16)


def attention_backward(q, k, v, do, o, logs, mq, mk, dead):
    tokens, width = q.shape
    rows = rows_per_step(tokens)
    part = pl.BlockSpec((rows, 128), lambda h, i: (i, h))
    full = pl.BlockSpec((tokens, 128), lambda h, i: (0, h))
    return pl.pallas_call(
        backward_kernel,
        grid=(width // 128, tokens // rows),
        in_specs=[
            full,
            part,
            part,
            full,
            full,
            full,
            pl.BlockSpec((tokens, 128), lambda h, i: (0, 0)),
            pl.BlockSpec((rows, 128), lambda h, i: (i, 0)),
            pl.BlockSpec((rows, 1), lambda h, i: (i, 0)),
        ],
        out_specs=[full, part, part],
        out_shape=[jax.ShapeDtypeStruct((tokens, width), BF16)] * 3,
        scratch_shapes=[
            pltpu.VMEM((2, tokens, 128), BF16),
            pltpu.VMEM((2, tokens, 128), BF16),
            pltpu.VMEM((2, tokens, 128), F32),
        ],
        compiler_params=pltpu.CompilerParams(vmem_limit_bytes=56 << 20),
        cost_estimate=pl.CostEstimate(
            flops=40 * tokens * tokens * width, bytes_accessed=24 * tokens * width, transcendentals=tokens * tokens * width // HEAD_DIM
        ),
        name="attention_backward",
    )(q, k, v, do, o, logs, mq, mk, dead)


def mask_terms(pair, live):
    lane = jnp.arange(128, dtype=jnp.int32)[None, :] % HEAD_DIM
    same = lane == pair[:, None]
    query = jnp.where(lane < 4, same, lane == 4).astype(BF16)
    key = jnp.where(
        lane < 4,
        jnp.where(same, 0.0, -BIG),
        jnp.where(lane == 4, jnp.where(live[:, None], 0.0, -BIG), ((lane >= 5) & (lane < 8)).astype(F32)),
    ).astype(BF16)
    return query, key, 1.0 - live.astype(F32)[:, None]


def gelu_parts(g):
    c = 0.7978845608028654
    t = jnp.tanh(c * (g + 0.044715 * g * g * g))
    act = 0.5 * g * (1.0 + t)
    slope = 0.5 * (1.0 + t) + 0.5 * g * (1.0 - t * t) * c * (1.0 + 3 * 0.044715 * g * g)
    return act, slope


def local_plain(
    dps,
    seqs,
    tokens,
    query_weight,
    key_weight,
    value_weight,
    out_weight,
    gate_weight,
    up_weight,
    down_weight,
    attention_gain,
    feedforward_gain,
    pair_lengths,
    live_mask,
    out_grad,
):
    mine, dim = tokens.shape
    units = gate_weight.shape[1]
    half = seqs // 2
    width = dim // seqs
    chips = dps // 2
    d = lax.axis_index("dp")
    s = lax.axis_index("seq")
    core = d % 2
    high = (s >= half).astype(jnp.int32)
    low = s % half
    member = core * half + low
    moved = core != high

    def move(value, target):
        pairs = []
        for i in range(dps * seqs):
            to = target(i // seqs, i % seqs)
            if to is not None:
                pairs.append((i, to[0] * seqs + to[1]))
        return lax.ppermute(value, AXES, pairs)

    def trade(value):
        def target(dd, ss):
            return (dd ^ 1, (ss + half) % seqs) if dd % 2 != ss // half else None

        return move(value, target)

    def with_core(value):
        return move(value, lambda dd, ss: (dd ^ 1, ss))

    def with_chip(value, bit):
        return move(value, lambda dd, ss: (dd ^ bit, ss))

    def with_seq(value, bit):
        return move(value, lambda dd, ss: (dd, ss ^ bit))

    def with_member(value, bit):
        return with_core(value) if bit == half else with_seq(value, bit)

    bits = []
    while (1 << len(bits)) < seqs:
        bits.append(1 << len(bits))
    chip_bits = []
    while (2 << len(chip_bits)) < dps:
        chip_bits.append(2 << len(chip_bits))

    def gather_row(value):
        value = value[None]
        for bit in bits:
            value = jnp.concatenate([value, with_member(value, bit)], axis=0)
        return value

    def to_tokens(value):
        value = value.reshape(seqs, mine, width)
        for bit in bits:
            value = value.reshape(value.shape[0] // 2, 2, mine, value.shape[2])
            keep, come = value[:, 0], with_member(value[:, 1], bit)
            upper = (member & bit) != 0
            value = jnp.concatenate([jnp.where(upper, come, keep), jnp.where(upper, keep, come)], axis=2)
        return value[0]

    def to_heads(value):
        value = value[None]
        for bit in reversed(bits):
            first, second = jnp.split(value, 2, axis=2)
            upper = (member & bit) != 0
            come = with_member(jnp.where(upper, first, second), bit)
            value = jnp.stack([jnp.where(upper, second, first), come], axis=1)
            value = value.reshape(-1, mine, value.shape[3])
        return value.reshape(seqs * mine, width)

    def row_sum(value):
        value = value.reshape(seqs, mine, dim)
        for bit in reversed(bits):
            keep, give = value[: value.shape[0] // 2], value[value.shape[0] // 2 :]
            value = keep + with_member(give.astype(BF16), bit).astype(F32)
        return value[0]

    def over_chips(value, order):
        cols = value.shape[1]
        rows = value.shape[0] // chips
        value = value.reshape((2,) * len(chip_bits) + (rows, cols))
        left = list(reversed(chip_bits))
        for bit in order:
            axis = left.index(bit)
            left.pop(axis)
            upper = ((d & bit) != 0).astype(jnp.int32)
            give = lax.dynamic_index_in_dim(value, 1 - upper, axis, keepdims=False)
            keep = lax.dynamic_index_in_dim(value, upper, axis, keepdims=False)
            come = with_chip(give, bit)
            value = (keep.astype(F32) + come.astype(F32)).astype(BF16)
        return value.reshape(rows, cols)

    def over_seq(value):
        for i in range(half - 1):
            come = move(
                value,
                lambda dd, ss: (dd, i + 1) if ss == i else ((dd, seqs - 2 - i) if ss == seqs - 1 - i else None),
            )
            value = (value.astype(F32) + come.astype(F32)).astype(BF16)
        come = move(value, lambda dd, ss: (dd, seqs - 1 - ss) if ss in (half - 1, half) else None)
        value = (value.astype(F32) + come.astype(F32)).astype(BF16)
        for i in reversed(range(half - 1)):
            come = move(
                value,
                lambda dd, ss: (dd, i) if ss == i + 1 else ((dd, seqs - 1 - i) if ss == seqs - 2 - i else None),
            )
            value = jnp.where((s == i) | (s == seqs - 1 - i), come, value)
        return value

    def my_core(value, axis, other=False):
        shape = value.shape
        size = shape[axis] // dps
        value = value.reshape(shape[:axis] + (chips, 2, size) + shape[axis + 1 :])
        value = lax.dynamic_index_in_dim(value, (1 - core) if other else core, axis + 1, keepdims=False)
        return value.reshape(shape[:axis] + (chips * size,) + shape[axis + 1 :])

    bounds = jnp.cumsum(pair_lengths[0])[:-1]
    place = s * mine + jnp.arange(mine, dtype=jnp.int32)
    pair = jnp.sum((place[:, None] >= bounds[None, :]).astype(jnp.int32), axis=1)
    code = (2 * pair + (live_mask > 0)).astype(BF16)
    lines = -(-mine // dim)
    code = jnp.pad(code, (0, 16 * dim * (-(-lines // 16)) - mine)).reshape(-1, dim)
    packed = jnp.concatenate([tokens, code], axis=0)
    packed = jnp.where(moved, trade(packed), packed)
    row = gather_row(packed)
    x_row = row[:, :mine].reshape(seqs * mine, dim)
    code_row = row[:, mine:].reshape(seqs, -1)[:, :mine].reshape(-1).astype(jnp.int32)
    mask_query, mask_key, dead = mask_terms(code_row // 2, code_row % 2 == 1)
    x = packed[:mine].astype(F32)
    dy = jnp.where(moved, trade(out_grad), out_grad)

    def scaled(v, gain):
        return v * lax.rsqrt(jnp.mean(v * v, axis=1, keepdims=True) + EPS) * gain[None, :]

    def heads_of(weight):
        return lax.dynamic_slice_in_dim(weight, member * width, width, axis=1)

    n1_row = scaled(x_row.astype(F32), attention_gain).astype(BF16)
    wq, wk, wv = heads_of(query_weight), heads_of(key_weight), heads_of(value_weight)
    lanes = -(-width // 128) * 128
    widen = (lambda v: jnp.pad(v, ((0, 0), (0, lanes - width)))) if lanes != width else (lambda v: v)
    q, k, v = [widen(dot_nn(n1_row, w).astype(BF16)) for w in (wq, wk, wv)]
    o_heads, logs = attention_forward(q, k, v, mask_query, mask_key, dead)
    o = to_tokens(o_heads[:, :width].astype(BF16))

    h = x + dot_nn(o, out_weight)
    h_scale = lax.rsqrt(jnp.mean(h * h, axis=1, keepdims=True) + EPS)
    n2 = (h * h_scale * feedforward_gain[None, :]).astype(BF16)
    n2_both = jnp.concatenate([n2, with_core(n2)], axis=0)
    dy_both = jnp.concatenate([dy, with_core(dy)], axis=0)
    wg, wu, wd = my_core(gate_weight, 1), my_core(up_weight, 1), my_core(down_weight, 0)
    g = dot_nn(n2_both, wg)
    u = dot_nn(n2_both, wu)
    act, slope = gelu_parts(g)
    z = (act * u).astype(BF16)
    f = dot_nn(z, wd)
    layer_out = (h + f[:mine] + with_core(f[mine:].astype(BF16)).astype(F32)).astype(BF16)
    layer_out = jnp.where(moved, trade(layer_out), layer_out)

    grad_down = dot_tn(z, dy_both).astype(BF16)
    dz = dot_nt(dy_both, wd)
    dg = (dz * u * slope).astype(BF16)
    du = (dz * act).astype(BF16)
    grad_gate = dot_tn(n2_both, dg).astype(BF16)
    grad_upward = dot_tn(n2_both, du).astype(BF16)
    dn2_both = dot_nt(dg, wg) + dot_nt(du, wu)
    dn2 = dn2_both[:mine] + with_core(dn2_both[mine:].astype(BF16)).astype(F32)

    ghd = dn2 * feedforward_gain[None, :]
    dh = dy.astype(F32) + h_scale * ghd - h * (h_scale**3 * jnp.mean(h * ghd, axis=1, keepdims=True))
    gain_two = jnp.sum(dn2 * h * h_scale, axis=0)
    da = dh.astype(BF16)
    do = to_heads(dot_nt(da, out_weight).astype(BF16))
    o_both = jnp.concatenate([my_core(o, 1), with_core(my_core(o, 1, other=True))], axis=0)
    da_both = jnp.concatenate([da, with_core(da)], axis=0)
    grad_output = dot_tn(o_both, da_both).astype(BF16)

    dq, dk, dv = attention_backward(q, k, v, widen(do), o_heads, logs, mask_query, mask_key, dead)
    dq, dk, dv = dq[:, :width], dk[:, :width], dv[:, :width]
    dn1_row = dot_nt(dq, wq) + dot_nt(dk, wk) + dot_nt(dv, wv)
    x_row_scale = lax.rsqrt(jnp.mean(jnp.square(x_row.astype(F32)), axis=1, keepdims=True) + EPS)
    gain_one = jnp.sum(dn1_row * (x_row.astype(F32) * x_row_scale), axis=0)
    grad_heads = dot_tn(n1_row, jnp.concatenate([dq, dk, dv], axis=1)).astype(BF16)
    gains = jnp.pad(jnp.stack([gain_one, gain_two], axis=1), ((0, 0), (0, 126))).astype(BF16)
    dn1 = row_sum(dn1_row)

    x_scale = lax.rsqrt(jnp.mean(x * x, axis=1, keepdims=True) + EPS)
    gxd = dn1 * attention_gain[None, :]
    grad_tokens = dh + x_scale * gxd - x * (x_scale**3 * jnp.mean(x * gxd, axis=1, keepdims=True))
    grad_tokens = jnp.where(moved, trade(grad_tokens.astype(BF16)).astype(F32), grad_tokens)

    ahead, back = chip_bits, chip_bits[::-1]
    down_out = over_seq(over_chips(grad_down, ahead)).astype(F32)

    def both_cores(value):
        n = value.shape[0] // 2
        first, second = value[:n], value[n:]
        upper = core == 1
        come = with_core(jnp.where(upper, first, second))
        keep = jnp.where(upper, second, first)
        return jnp.stack([jnp.where(upper, come, keep), jnp.where(upper, keep, come)], axis=1)

    def unit_columns(value):
        n = value.shape[0]
        return value.reshape(n, 2, chips, units // dps).transpose(0, 2, 1, 3).reshape(n, units)

    gate_out = unit_columns(over_seq(both_cores(over_chips(grad_gate, back)))).astype(F32)
    upward_out = unit_columns(over_seq(both_cores(over_chips(grad_upward, ahead)))).astype(F32)
    output_out = over_seq(over_chips(grad_output, back)).astype(F32)

    heads_part = over_chips(jnp.concatenate([grad_heads, gains], axis=1), back)
    heads_part = both_cores(heads_part)
    heads_part = (heads_part.astype(F32) + with_seq(heads_part, half).astype(F32)).astype(BF16)
    heads_part = heads_part[None]
    for bit in bits[:-1]:
        come = with_seq(heads_part, bit)
        upper = (member & bit) != 0
        heads_part = jnp.concatenate([jnp.where(upper, come, heads_part), jnp.where(upper, heads_part, come)], axis=0)
    heads_part = heads_part.transpose(1, 2, 0, 3).reshape(-1, seqs, 3 * width + 128)
    query_out, key_out, value_out = [
        heads_part[:, :, i * width : (i + 1) * width].reshape(-1, dim).astype(F32) for i in range(3)
    ]
    gains_out = jnp.sum(heads_part[:, :, 3 * width : 3 * width + 2].astype(F32), axis=1)
    return (
        layer_out,
        grad_tokens,
        query_out,
        key_out,
        value_out,
        output_out,
        gate_out,
        upward_out,
        down_out,
        gains_out[:, 0],
        gains_out[:, 1],
    )


def opening_kernel(tokens_ref, live_ref, lengths_ref, gain_one_ref, gain_two_ref, *refs):
    refs = list(refs)

    def take(n):
        taken, refs[:n] = refs[:n], []
        return taken

    wq_ref, wk_ref, wv_ref, wo_ref, dy_ref = take(5)
    outs = take(OPENED)
    kept = take(OPENED)
    n1_s, k_s, v_s, qa0_s, qa1_s, o0_s, o1_s, mk_s, h_s, n2_s, o_s, dy_s, x_s = kept
    xs, codes, w_s, wo_s, q_s, mq_s, ka_s, va_s, ob_s, send_sem, recv_sem, local_sem = take(12)

    d = lax.axis_index("dp")
    s = lax.axis_index("seq")
    core = d % 2
    low = s % 2
    high = s // 2
    member = 2 * core + low
    sibling = (d + 1 - 2 * core, s)
    over_z = (d, s + 1 - 2 * low)
    across = (d + 1 - 2 * core, s + 1 - 2 * low)
    swapped = (d + 1 - 2 * core, s + 2 - 4 * high)
    moved = core != high
    stays = core == high

    barrier = pltpu.get_barrier_semaphore()
    for other in (sibling, over_z, across, swapped):
        pl.semaphore_signal(barrier, inc=1, device_id=other, device_id_type=MESH)

    counts = {"remote": 0, "local": 0}

    class Copy:
        def __init__(self, src, dst, target):
            self.parts = (src, dst, target, counts["remote"])
            counts["remote"] += 1

        def made(self):
            src, dst, target, i = self.parts
            return pltpu.make_async_remote_copy(
                src_ref=src, dst_ref=dst, send_sem=send_sem.at[i], recv_sem=recv_sem.at[i], device_id=target, device_id_type=MESH
            )

        def start(self):
            self.made().start()

        def wait_recv(self):
            self.made().wait_recv()

        def wait_send(self):
            self.made().wait_send()

    class Fetch:
        def __init__(self, src, dst):
            self.parts = (src, dst, counts["local"])
            counts["local"] += 1

        def made(self):
            src, dst, i = self.parts
            return pltpu.make_async_copy(src, dst, local_sem.at[i])

        def start(self):
            self.made().start()

        def wait(self):
            self.made().wait()

    def lanes_at(start, size):
        return pl.ds(pl.multiple_of(start * size, size), size)

    mine, dim = tokens_ref.shape
    third = mine // 3
    pieces = [pl.ds(i * third, third) for i in range(3)]
    place = s * mine + lax.broadcasted_iota(jnp.int32, codes.shape[1:], 1)
    ends = [lengths_ref[0, 0]]
    for i in (1, 2):
        ends.append(ends[-1] + lengths_ref[0, i])
    pair = sum([jnp.where(place >= end, 1.0, 0.0) for end in ends])
    code = (2.0 * pair + jnp.where(live_ref[...] > 0, 1.0, 0.0)).astype(BF16)

    w_loads = []
    for p in range(2):
        for t, w in enumerate((wq_ref, wk_ref, wv_ref)):
            w_loads.append(Fetch(w.at[:, lanes_at(2 * member + p, 128)], w_s.at[:, pl.ds((3 * p + t) * 128, 128)]))
    wo_loads = [
        Fetch(wo_ref.at[pl.ds((2 * m + p) * 128, 128)], wo_s.at[pl.ds((4 * p + m) * 128, 128)]) for m in range(4) for p in range(2)
    ]

    trade = [Copy(tokens_ref.at[at], xs.at[0, at], swapped) for at in pieces]
    to_z = [Copy(xs.at[0, at], xs.at[1, at], over_z) for at in pieces]
    to_core = [Copy(xs.at[0, at], xs.at[2, at], sibling) for at in pieces]
    on_core = [Copy(xs.at[1, at], xs.at[3, at], sibling) for at in pieces]
    code_s = x_s.at[pl.ds(0, 16), pl.ds(0, mine)]
    code_trade = Copy(code_s, codes.at[0], swapped)
    code_z = Copy(codes.at[0], codes.at[1], over_z)
    code_core = Copy(codes.at[0], codes.at[2], sibling)
    code_on = Copy(codes.at[1], codes.at[3], sibling)
    dy_trade = Copy(dy_ref, dy_s.at[pl.ds(0, mine)], swapped)
    dy_local = Fetch(dy_ref, dy_s.at[pl.ds(0, mine)])
    dy_core = Copy(dy_s.at[pl.ds(0, mine)], dy_s.at[pl.ds(mine, mine)], sibling)

    code_s[...] = code
    pl.semaphore_wait(barrier, 4)

    @pl.when(moved)
    def _():
        code_trade.start()
        for made in trade:
            made.start()

    @pl.when(stays)
    def _():
        xs[0] = tokens_ref[...]
        codes[0] = code
        code_z.start()
        code_core.start()
        for a, b in zip(to_z, to_core):
            a.start()
            b.start()

    for load in w_loads + wo_loads:
        load.start()

    tokens = k_s.shape[0]
    lane = lax.broadcasted_iota(jnp.int32, (third, 128), 1)
    inside = lane % HEAD_DIM
    for load in w_loads:
        load.wait()

    def project(b):
        for i in range(3):
            at = pl.ds(i * third, third)
            x = xs[b, at, :].astype(F32)
            n1 = (x * lax.rsqrt(jnp.mean(x * x, axis=1, keepdims=True) + EPS) * gain_one_ref[...]).astype(BF16)
            to = pl.ds(pl.multiple_of(b * mine + i * third, 128), third)
            n1_s[to, :] = n1
            qkv = dot_nn(n1, w_s[...]).astype(BF16)
            for p in range(2):
                for t, out in enumerate((q_s, k_s, v_s)):
                    out[to, 128 * p : 128 * p + 128] = qkv[:, (3 * p + t) * 128 : (3 * p + t + 1) * 128]
            number = codes[b, 0:8, i * third : (i + 1) * third].astype(F32).T[:, 0:1]
            whose = jnp.floor(number * 0.5)
            dead = number - 2.0 * whose < 0.5
            same = inside.astype(F32) == whose
            mq_s[to, :] = jnp.where(inside < 4, jnp.where(same, 1.0, 0.0), jnp.where(inside == 4, 1.0, 0.0)).astype(BF16)
            key = jnp.where(inside == 4, jnp.where(dead, -BIG, 0.0), jnp.where((inside >= 5) & (inside < 8), 1.0, 0.0))
            mk_s[to, :] = jnp.where(inside < 4, jnp.where(same, 0.0, -BIG), key).astype(BF16)

    def block(i):
        return (i + 2 * moved.astype(jnp.int32)) % 4

    def relay():
        code_z.wait_recv()
        code_on.start()
        for a, b in zip(to_z, on_core):
            a.wait_recv()
            b.start()

    def from_core():
        code_core.wait_recv()
        for made in to_core:
            made.wait_recv()

    def from_core_on():
        code_on.wait_recv()
        for made in on_core:
            made.wait_recv()

    pl.when(moved)(from_core)
    project(block(0))

    @pl.when(moved)
    def _():
        code_trade.wait_recv()
        code_z.start()
        code_core.start()
        for made, a, b in zip(trade, to_z, to_core):
            made.wait_recv()
            a.start()
            b.start()
        dy_trade.start()
        from_core_on()

    pl.when(stays)(relay)
    project(block(1))
    pl.when(stays)(from_core)
    project(block(2))
    pl.when(moved)(relay)

    @pl.when(stays)
    def _():
        dy_local.start()
        from_core_on()

    project(block(3))
    code_trade_done = [code_trade] + trade

    @pl.when(moved)
    def _():
        for made in code_trade_done:
            made.wait_send()

    x_s[...] = xs[0]

    stores = [Fetch(src, dst) for src, dst in zip(kept, outs)]
    for i in (0, 1, 2, 7, 12):
        stores[i].start()

    rows = 256
    steps = tokens // rows
    lane = lax.broadcasted_iota(jnp.int32, (rows, 128), 1)
    klane = lax.broadcasted_iota(jnp.int32, (tokens, 128), 1)

    def attend(p, j):
        cols = slice(128 * p, 128 * p + 128)
        at = pl.ds(pl.multiple_of(j * rows, rows), rows)
        q = q_s[at, cols]
        mq = mq_s[at, :]
        qf = q.astype(F32)
        dead = mk_s[at, 4:5].astype(F32) < 0
        qk = qf * k_s[at, cols].astype(F32)
        v_own = v_s[at, cols].astype(F32)
        results = []
        for h in range(2):
            own_lanes = (lane < HEAD_DIM) if h == 0 else (lane >= HEAD_DIM)
            sc = dot_nt(jnp.where(own_lanes, q, mq), ka_s[h])
            own = jnp.sum(jnp.where(own_lanes, qk, 0.0), axis=1, keepdims=True)
            own = jnp.where(dead, own, -BIG)
            top = jnp.maximum(jnp.max(sc, axis=1, keepdims=True), own)
            pr = jnp.exp(sc - top).astype(BF16)
            r = dot_nn(pr, va_s[h])
            own_p = jnp.exp(own - top)
            total = (r[:, HEAD_DIM : HEAD_DIM + 1] if h == 0 else r[:, 0:1]) + own_p
            results.append((r + own_p * v_own) * (1.0 / total))
            other = lane - (HEAD_DIM if h == 0 else 0)
            a, b, c = three_parts(top + jnp.log(total))
            aug = jnp.where(other == 5, -a, jnp.where(other == 6, -b, jnp.where(other == 7, -c, mq.astype(F32))))
            (qa0_s, qa1_s)[p][h, at, :] = jnp.where(own_lanes, qf, aug).astype(BF16)
        o = jnp.where(lane < HEAD_DIM, results[0], results[1])
        (o0_s, o1_s)[p][at, :] = o
        ob_s[p, at, :] = o.astype(BF16)

    o_moves = []
    for p in range(2):
        to = o_s.at[pl.ds(0, mine), lanes_at(4 * p + member, 128)]
        o_moves.append(
            [Copy(ob_s.at[p, pl.ds(b * mine, mine)], to, target) for b, target in ((1, over_z), (3, across), (2, sibling))]
        )
    for p in range(2):
        cols = slice(128 * p, 128 * p + 128)
        for h in range(2):
            own_lanes = (klane < HEAD_DIM) if h == 0 else (klane >= HEAD_DIM)
            ka_s[h] = jnp.where(own_lanes, k_s[:, cols], mk_s[...])
            va_s[h] = jnp.where(own_lanes, v_s[:, cols], jnp.ones_like(v_s[:, cols]))

        @pl.loop(0, steps)
        def _(j, p=p):
            attend(p, j)

        for made in o_moves[p]:
            made.start()
        o_s[0:mine, lanes_at(4 * p + member, 128)] = ob_s[p, 0:mine, :]
        stores[3 + p].start()
        stores[5 + p].start()
        if p == 0:

            @pl.when(moved)
            def _():
                dy_trade.wait_recv()

            @pl.when(stays)
            def _():
                dy_local.wait()

            dy_core.start()

    for load in wo_loads:
        load.wait()
    o_core = Copy(o_s.at[pl.ds(0, mine)], o_s.at[pl.ds(mine, mine)], sibling)
    n2_core = Copy(n2_s.at[pl.ds(0, mine)], n2_s.at[pl.ds(mine, mine)], sibling)
    half = dim // 2
    for made in o_moves[0]:
        made.wait_recv()
    h_s[...] = x_s[...].astype(F32) + dot_nn(o_s[0:mine, 0:half], wo_s[0:half, :])
    for made in o_moves[1]:
        made.wait_recv()
    o_core.start()
    for at in pieces:
        hh = h_s[at, :] + dot_nn(o_s[at, half:dim], wo_s[half:dim, :])
        h_s[at, :] = hh
        n2_s[at, :] = (hh * lax.rsqrt(jnp.mean(hh * hh, axis=1, keepdims=True) + EPS) * gain_two_ref[...]).astype(BF16)
    n2_core.start()
    stores[8].start()
    dy_core.wait_recv()
    stores[11].start()
    o_core.wait_recv()
    stores[10].start()
    n2_core.wait_recv()
    stores[9].start()
    for made in to_z + to_core + on_core + [code_z, code_core, code_on, dy_core, o_core, n2_core] + o_moves[0] + o_moves[1]:
        made.wait_send()

    @pl.when(moved)
    def _():
        dy_trade.wait_send()

    for store in stores:
        store.wait()


def opening(tokens, live, lengths, gains, weights, dy):
    mine, dim = tokens.shape
    row = 4 * mine
    vmem = pl.BlockSpec(memory_space=pltpu.VMEM)
    anywhere = pl.BlockSpec(memory_space=pl.ANY)
    kept = [((row, dim), BF16), ((row, 256), BF16), ((row, 256), BF16)]
    kept += [((2, row, 128), BF16)] * 2 + [((row, 128), F32)] * 2 + [((row, 128), BF16)]
    kept += [((mine, dim), F32)] + [((2 * mine, dim), BF16)] * 3 + [((mine, dim), BF16)]
    scratch = [pltpu.VMEM(*v) for v in kept]
    scratch += [
        pltpu.VMEM((4, mine, dim), BF16),
        pltpu.VMEM((4, 16, mine), BF16),
        pltpu.VMEM((dim, 768), BF16),
        pltpu.VMEM((dim, dim), BF16),
        pltpu.VMEM((row, 256), BF16),
        pltpu.VMEM((row, 128), BF16),
        pltpu.VMEM((2, row, 128), BF16),
        pltpu.VMEM((2, row, 128), BF16),
        pltpu.VMEM((2, row, 128), BF16),
    ]
    remote, local = 12 + 4 + 2 + 6 + 2, 6 + 8 + 1 + OPENED
    semaphores = [pltpu.SemaphoreType.DMA((count,)) for count in (remote, remote, local)]
    return pl.pallas_call(
        opening_kernel,
        in_specs=[vmem, vmem, pl.BlockSpec(memory_space=pltpu.SMEM), vmem, vmem] + [anywhere] * 5,
        out_specs=[anywhere] * OPENED,
        out_shape=[jax.ShapeDtypeStruct(*v) for v in kept],
        scratch_shapes=scratch + semaphores,
        compiler_params=pltpu.CompilerParams(collective_id=1, has_side_effects=True, vmem_limit_bytes=VMEM_BYTES),
        cost_estimate=pl.CostEstimate(flops=16 * row * row * 256, bytes_accessed=30 << 20, transcendentals=4 * row * row),
        name="opening",
    )(tokens, live, lengths, *gains, *weights, dy)


def middle_kernel(gain_ref, *refs):
    refs = list(refs)

    def take(n):
        taken, refs[:n] = refs[:n], []
        return taken

    n2_ref, dy_ref, h_ref, o_ref, wg_ref, wu_ref, wd_ref, wo_ref = take(8)
    lo_o, dh_o, do_o, gate_o, up_o, out_o, da_o, db_o = take(8)
    n2_s, n2t_s, dy_s, h_s, wg_s, wu_s, wd_s, z_s, zc_s, dg_s, du_s = take(11)
    dn2_s, give_s, come_r, da_s, dap_s, dcr_s, dorow_s, own_s, far_s, stage_s, out_s, ra_s, rb_s, fr_s = take(14)
    f_s, lo_s = take(2)
    second_r, cores_s, accs = take(2), take(2), take(2)
    send_sem, recv_sem, local_sem = take(3)

    d = lax.axis_index("dp")
    s = lax.axis_index("seq")
    core = d % 2
    xb = (d // 2) % 2
    yb = (d // 4) % 2
    low = s % 2
    sibling = (d + 1 - 2 * core, s)
    over_x = (d + 2 - 4 * xb, s)
    over_y = (d + 4 - 8 * yb, s)
    over_z = (d, s + 1 - 2 * low)

    barrier = pltpu.get_barrier_semaphore()
    for other in (sibling, over_x, over_y, over_z):
        pl.semaphore_signal(barrier, inc=1, device_id=other, device_id_type=MESH)

    counts = {"remote": 0, "local": 0}

    class Copy:
        def __init__(self, src, dst, target, like=None):
            self.parts = (src, dst, target, counts["remote"] if like is None else like.parts[3])
            counts["remote"] += like is None

        def made(self):
            src, dst, target, i = self.parts
            return pltpu.make_async_remote_copy(
                src_ref=src, dst_ref=dst, send_sem=send_sem.at[i], recv_sem=recv_sem.at[i], device_id=target, device_id_type=MESH
            )

        def start(self):
            self.made().start()

        def wait_recv(self):
            self.made().wait_recv()

        def wait_send(self):
            self.made().wait_send()

    class Fetch:
        def __init__(self, src, dst):
            self.parts = (src, dst, counts["local"])
            counts["local"] += 1

        def made(self):
            src, dst, i = self.parts
            return pltpu.make_async_copy(src, dst, local_sem.at[i])

        def start(self):
            self.made().start()

        def wait(self):
            self.made().wait()

    def at_of(start, size):
        return pl.ds(pl.multiple_of(start * size, size), size)

    mine, dim = h_s.shape
    both = 2 * mine
    units = wd_s.shape[0]
    tiles = [(i, min(256, units - i)) for i in range(0, units, 256)]
    n2_load = Fetch(n2_ref, n2_s)
    dy_load = Fetch(dy_ref, dy_s)
    h_load = Fetch(h_ref, h_s)
    w_loads = []
    places = []
    for first, size in tiles:
        start = jnp.where(xb == 1, first, units - first - size)
        places.append(pl.ds(pl.multiple_of(start, 128), size))
        cols = pl.ds(pl.multiple_of(core * units + start, 128), size)
        w_loads.append(
            [
                Fetch(wg_ref.at[:, cols], wg_s.at[:, places[-1]]),
                Fetch(wu_ref.at[:, cols], wu_s.at[:, places[-1]]),
                Fetch(wd_ref.at[cols, :], wd_s.at[places[-1], :]),
            ]
        )
    n2_load.start()
    for load in w_loads[0]:
        load.start()
    dy_load.start()
    for loads in w_loads[1:]:
        for load in loads:
            load.start()
    h_load.start()

    half = dim // 2
    cut = half // 2
    rows = units // 2
    first_cols, last_cols = pl.ds(0, cut), pl.ds(cut, cut)
    top, end = pl.ds(0, mine), pl.ds(mine, mine)
    z_moves, a_far, a_own = [], [], []
    for cols in places:
        z_moves.append(Copy(z_s.at[top, cols], zc_s.at[end, cols], sibling))
        z_moves.append(Copy(z_s.at[end, cols], zc_s.at[top, cols], sibling))
        a_far.append(Copy(far_s.at[cols, first_cols], ra_s.at[cols], over_y))
        a_own.append(Copy(own_s.at[cols, first_cols], ra_s.at[cols], over_y, like=a_far[-1]))
    b_own = Copy(own_s.at[at_of(1 - xb, rows), last_cols], rb_s.at[at_of(core, rows)], over_x)
    b_far = Copy(far_s.at[at_of(1 - xb, rows), last_cols], rb_s.at[at_of(1 - core, rows)], over_x)

    def down_of(to, left, i):
        to[places[i], :] = dot_tn(left[:, places[i]], dy_s[:, at_of(core, half)]).astype(BF16)

    def far_of(i):
        z_moves[2 * i].wait_recv()
        z_moves[2 * i + 1].wait_recv()
        down_of(far_s, zc_s, i)
        pl.when(yb == core)(a_far[i].start)
        pl.when(yb != core)(a_own[i].start)
        done = tiles[i][0] + tiles[i][1]
        if done - tiles[i][1] < rows <= done:
            b_own.start()
            b_far.start()

    n2_load.wait()
    for i, (cols, loads) in enumerate(zip(places, w_loads)):
        loads[0].wait()
        loads[1].wait()
        g = dot_nn(n2_s[...], wg_s[:, cols])
        u = dot_nn(n2_s[...], wu_s[:, cols])
        act, slope = gelu_parts(g)
        z_s[:, cols] = (act * u).astype(BF16)
        if i == 0:
            pl.semaphore_wait(barrier, 4)
            dy_load.wait()
        z_moves[2 * i].start()
        z_moves[2 * i + 1].start()
        loads[2].wait()
        dz = dot_nt(dy_s[...], wd_s[cols, :])
        dg_s[:, cols] = (dz * u * slope).astype(BF16)
        du_s[:, cols] = (dz * act).astype(BF16)
        down_of(own_s, z_s, i)
        if i > 0:
            far_of(i - 1)
    far_of(len(tiles) - 1)

    size = rows // 2
    second = [
        Copy(ra_s.at[at_of(1 - xb, rows)], second_r[0], over_x),
        Copy(rb_s.at[at_of(1 - yb, rows)], second_r[1], over_y),
    ]
    on_core = [Copy(cores_s[i], accs[i].at[core], sibling) for i in range(2)]
    acc_stores = [Fetch(accs[i], (da_o, db_o)[i]) for i in range(2)]

    def add_first():
        for made in a_far:
            made.wait_recv()

        @pl.when(yb == core)
        def _():
            ra_s[...] = (ra_s[...].astype(F32) + own_s[:, first_cols].astype(F32)).astype(BF16)

        @pl.when(yb != core)
        def _():
            ra_s[...] = (ra_s[...].astype(F32) + far_s[:, first_cols].astype(F32)).astype(BF16)

        second[0].start()
        b_own.wait_recv()
        b_far.wait_recv()
        for part, y in ((own_s, core), (far_s, 1 - core)):
            at = at_of(y, rows)
            rb_s[at, :] = (rb_s[at, :].astype(F32) + part[at_of(xb, rows), last_cols].astype(F32)).astype(BF16)
        second[1].start()

    def add_second():
        for i, (whole, bit) in enumerate(((ra_s, xb), (rb_s, yb))):
            second[i].wait_recv()

            def summed(which):
                at = pl.ds(pl.multiple_of(bit * rows + which * size, size), size)
                return (whole[at, :].astype(F32) + second_r[i][at_of(which, size), :].astype(F32)).astype(BF16)

            cores_s[i][...] = summed(1 - core)
            on_core[i].start()
            accs[i][core] = summed(core)
        for i in range(2):
            on_core[i].wait_recv()
            acc_stores[i].start()

    quarter = dim // 4
    third = mine // 3
    h_load.wait()

    @pl.loop(0, 4)
    def _(i):
        at = at_of(i, quarter)
        dn2 = dot_nt(dg_s[...], wg_s[at, :]) + dot_nt(du_s[...], wu_s[at, :])
        dn2_s[:, at] = dn2[0:mine, :]
        give_s[:, at] = dn2[mine:both, :].astype(BF16)

    dn2_move = Copy(give_s, come_r, sibling)
    dn2_move.start()
    wo_s = wg_s.at[:, pl.ds(0, dim)]
    o_s = wu_s.at[pl.ds(0, both), pl.ds(0, dim)]
    wo_load, o_load = Fetch(wo_ref, wo_s), Fetch(o_ref, o_s)
    wo_load.start()
    o_load.start()

    dn2_move.wait_recv()
    for i in range(3):
        at = pl.ds(i * third, third)
        dn2 = (dn2_s[at, :] + come_r[at, :].astype(F32)) * gain_ref[...]
        h = h_s[at, :]
        scale = lax.rsqrt(jnp.mean(h * h, axis=1, keepdims=True) + EPS)
        dh = dy_s[at, :].astype(F32) + scale * dn2 - h * (scale * scale * scale * jnp.mean(h * dn2, axis=1, keepdims=True))
        dn2_s[at, :] = dh
        da_s[at, :] = dh.astype(BF16)
    dh_store = Fetch(dn2_s, dh_o)
    dh_store.start()
    da_move = Copy(da_s.at[:, at_of(1 - core, half)], dap_s.at[end], sibling)
    da_move.start()
    dap_s[0:mine, :] = da_s[:, at_of(core, half)]
    wo_load.wait()
    do_s = come_r
    for i in range(3):
        at = pl.ds(i * third, third)
        do_s[at, :] = dot_nt(da_s[at, :], wo_s[...]).astype(BF16)
    do_core = Copy(do_s.at[:, at_of(1 - core, half)], dcr_s, sibling)
    do_core.start()
    do_z = []
    for p in range(2):
        do_z.append(Copy(do_s.at[:, at_of((2 * core + 1 - low) * 2 + p, 128)], dorow_s.at[p, pl.ds(mine, mine)], over_z))
    for made in do_z:
        made.start()

    add_first()


    @pl.loop(0, 4)
    def _(i):
        at = at_of(i, quarter)
        f = dot_nn(z_s[...], wd_s[:, at])
        f_s[:, at] = f[0:mine, :].astype(BF16)
        lo_s[:, at] = f[mine:both, :].astype(BF16)

    f_move = Copy(lo_s, fr_s, sibling)
    f_move.start()

    n2t_s[...] = n2_s[...].T
    stores = []

    def unit_rows(to, right, turn, b, place):
        slot = turn % 2
        if turn >= 2:
            stores[turn - 2].wait()
        stage_s[slot] = dot_nn(n2t_s[b * quarter : (b + 1) * quarter, :], right[...]).astype(BF16)
        stores.append(Fetch(stage_s.at[slot], to.at[pl.ds(place * quarter, quarter)]))
        stores[-1].start()

    unit_rows(gate_o, dg_s, 0, 0, 0)
    do_core.wait_recv()
    for p in range(2):
        do_z.append(Copy(dcr_s.at[:, at_of(2 * (1 - low) + p, 128)], dorow_s.at[p, pl.ds(3 * mine, mine)], over_z))
        do_z[-1].start()
    for p in range(2):
        dorow_s[p, 0:mine, :] = do_s[:, at_of((2 * core + low) * 2 + p, 128)]
        dorow_s[p, 2 * mine : 3 * mine, :] = dcr_s[:, at_of(2 * low + p, 128)]
    for b in range(1, 4):
        unit_rows(gate_o, dg_s, b, b, b)
    for b in range(4):
        unit_rows(up_o, du_s, 4 + b, b, 2 * (b % 2) + b // 2)

    o_load.wait()
    da_move.wait_recv()
    da_move.wait_send()
    for xx in range(2):
        for yy in range(2):
            for p in range(2):
                to = pl.ds(((2 * xx + yy) * 2 + p) * 128, 128)
                m = 4 * p + 2 * yy + xx
                out_s[to, :] = dot_tn(o_s[:, m * 128 : (m + 1) * 128], dap_s[...]).astype(BF16)
    out_store = Fetch(out_s, out_o)
    out_store.start()
    f_move.wait_recv()
    f_move.wait_send()
    for i in range(3):
        at = pl.ds(i * third, third)
        lo_s[at, :] = (h_s[at, :] + f_s[at, :].astype(F32) + fr_s[at, :].astype(F32)).astype(BF16)
    lo_store = Fetch(lo_s, lo_o)
    lo_store.start()
    for made in do_z:
        made.wait_recv()
    do_store = Fetch(dorow_s, do_o)
    do_store.start()

    add_second()
    for made in z_moves + a_far + [do_core, dn2_move, b_own, b_far] + second + on_core + do_z:
        made.wait_send()
    for store in stores[-2:] + [dh_store, out_store, do_store] + acc_stores:
        store.wait()
    lo_store.wait()


def middle(gain, n2_both, dy_both, h, o_both, gate_weight, up_weight, down_weight, out_weight):
    mine, dim = h.shape
    units = gate_weight.shape[1] // 2
    tiles = -(-units // 256)
    both = 2 * mine
    half, quarter = dim // 2, dim // 4
    vmem = pl.BlockSpec(memory_space=pltpu.VMEM)
    anywhere = pl.BlockSpec(memory_space=pl.ANY)
    outs = [((mine, dim), BF16), ((mine, dim), F32), ((2, 4 * mine, 128), BF16), ((dim, units), BF16), ((dim, units), BF16)]
    outs += [((dim, half), BF16), ((2, units // 4, quarter), BF16), ((2, units // 4, quarter), BF16)]
    scratch = [((both, dim), BF16), ((dim, both), BF16), ((both, dim), BF16), ((mine, dim), F32)]
    scratch += [((dim, units), BF16)] * 2 + [((units, dim), BF16)] + [((both, units), BF16)] * 4
    scratch += [((mine, dim), F32)] + [((mine, dim), BF16)] * 3 + [((both, half), BF16), ((mine, half), BF16)]
    scratch += [((2, 4 * mine, 128), BF16)] + [((units, half), BF16)] * 2 + [((2, quarter, units), BF16), ((dim, half), BF16)]
    scratch += [((units, quarter), BF16)] * 2 + [((mine, dim), BF16)]
    scratch += [((mine, dim), BF16)] * 2
    scratch += [((units // 2, quarter), BF16)] * 2 + [((units // 4, quarter), BF16)] * 2 + [((2, units // 4, quarter), BF16)] * 2
    remote, local = 3 * tiles + 2 + 1 + 3 + 1 + 1 + 4 + 1 + 4, 3 + 3 * tiles + 2 + 1 + 8 + 5
    semaphores = [pltpu.SemaphoreType.DMA((count,)) for count in (remote, remote, local)]
    return pl.pallas_call(
        middle_kernel,
        in_specs=[vmem] + [anywhere] * 8,
        out_specs=[anywhere] * 8,
        out_shape=[jax.ShapeDtypeStruct(*v) for v in outs],
        scratch_shapes=[pltpu.VMEM(*v) for v in scratch] + semaphores,
        compiler_params=pltpu.CompilerParams(collective_id=2, has_side_effects=True, vmem_limit_bytes=VMEM_BYTES),
        cost_estimate=pl.CostEstimate(flops=18 * both * dim * units, bytes_accessed=40 << 20, transcendentals=both * units),
        name="middle",
    )(gain, n2_both, dy_both, h, o_both, gate_weight, up_weight, down_weight, out_weight)


ORDER = ((('start', 0), ('start', 1), ('start', 2), ('s2', 0), ('start', 3), ('s2', 1)),
 ((),
  ((), (), (('s3', 0), ('s0', 2), ('s0', 3), ('start', 5), ('start', 4)), (), (('s1', 3), ('s3', 1))),
  (('s2', 3), ('s1', 2))),
 ((('s4', 0), ('s2', 2)),
  ((),
   (('s0', 4), ('s0', 5), ('s3', 3)),
   (('start', 8), ('s3', 2), ('s4', 1)),
   (),
   (('s1', 4), ('s1', 5), ('s4', 3), ('s2', 4))),
  (('s5', 0),
   ('s4', 2),
   ('h0', 1),
   ('s2', 5),
   ('core', 1),
   ('start', 7),
   ('s3', 4),
   ('z', 0),
   ('start', 6),
   ('s3', 5),
   ('core', 0),
   ('h0', 0),
   ('s4', 5),
   ('h1', 0),
   ('s0', 7),
   ('own', 0),
   ('s0', 8),
   ('h1', 1),
   ('s4', 4),
   ('home', 0),
   ('h2', 0),
   ('s0', 6),
   ('h3', 0),
   ('s1', 7),
   ('s5', 5),
   ('s2', 7),
   ('s1', 6),
   ('s3', 7),
   ('s1', 8),
   ('s5', 4),
   ('s2', 6),
   ('h4', 0),
   ('s3', 6),
   ('s4', 7),
   ('s4', 6),
   ('h2', 1),
   ('h3', 1),
   ('s2', 8),
   ('h4', 1),
   ('s3', 8),
   ('s5', 3),
   ('s5', 1),
   ('home', 1),
   ('s5', 6),
   ('s5', 7),
   ('home', 2),
   ('s4', 8),
   ('h5', 1),
   ('s5', 8),
   ('s5', 2),
   ('h5', 0))))


def closing_kernel(mask_k_ref, gain_one_ref, *refs):
    refs = list(refs)

    def take(n):
        taken, refs[:n] = refs[:n], []
        return taken

    fetched = take(FETCHED)
    wq_ref, wk_ref, wv_ref, x_ref = take(4)
    da_ref, db_ref, gate_ref, up_ref, out_ref = take(5)
    (gt_o,) = take(1)
    finals = take(ITEMS)
    (heads_o,) = take(1)
    fetched_s = take(FETCHED)
    dorow_s, qa0_s, qa1_s, k_s, v_s, o0_s, o1_s, n1_s, dh_s = fetched_s
    firsts_r, seconds_s, seconds_r, cores_s = [take(ITEMS - 2) for _ in range(4)]
    accs, lines = take(ITEMS), take(ITEMS)
    doa_s, dq_s, dqkv_s, hs_s, h1_r, h2_s, h2_r, hk_s, hc_s, hh_s, hh_r = take(11)
    w_s, x_s, dn_s = take(3)
    cs_s, cr_r, zr_r, send_sem, recv_sem, local_sem = take(6)

    d = lax.axis_index("dp")
    s = lax.axis_index("seq")
    core = d % 2
    xb = (d // 2) % 2
    yb = (d // 4) % 2
    low = s % 2
    high = s // 2
    sibling = (d + 1 - 2 * core, s)
    over_x = (d + 2 - 4 * xb, s)
    over_y = (d + 4 - 8 * yb, s)
    over_z = (d, s + 1 - 2 * low)
    over_high = (d, s + 2 - 4 * high)
    swapped = (d + 1 - 2 * core, s + 2 - 4 * high)
    third = (d, 3 - s)
    inner = (s == 1) | (s == 2)
    outer = (s == 0) | (s == 3)
    moved = core != high

    barrier = pltpu.get_barrier_semaphore()
    for other in (sibling, over_x, over_y, over_z, over_high, swapped, third):
        pl.semaphore_signal(barrier, inc=1, device_id=other, device_id_type=MESH)
    pl.semaphore_wait(barrier, 7)

    counts = {"remote": 0, "local": 0}

    class Copy:
        def __init__(self, src, dst, target):
            self.parts = (src, dst, target, counts["remote"])
            counts["remote"] += 1

        def made(self):
            src, dst, target, i = self.parts
            return pltpu.make_async_remote_copy(
                src_ref=src, dst_ref=dst, send_sem=send_sem.at[i], recv_sem=recv_sem.at[i], device_id=target, device_id_type=MESH
            )

        def start(self):
            self.made().start()

        def wait_recv(self):
            self.made().wait_recv()

        def wait_send(self):
            self.made().wait_send()

    copy = Copy

    class Fetch:
        def __init__(self, src, dst):
            self.parts = (src, dst, counts["local"])
            counts["local"] += 1

        def made(self):
            src, dst, i = self.parts
            return pltpu.make_async_copy(src, dst, local_sem.at[i])

        def start(self):
            self.made().start()

        def wait(self):
            self.made().wait()

    def rows_at(start, size):
        return pl.ds(pl.multiple_of(start * size, size), size)

    def lanes_at(start, size):
        return pl.ds(pl.multiple_of(start * size, size), size)

    class Item:
        pass

    items = []
    along_x, along_y = (over_x, xb), (over_y, yb)
    windows, first_col = [], 0
    for acc in accs[2 : ITEMS - 1 : 2]:
        windows.append(pl.ds(first_col, acc.shape[2]))
        first_col += acc.shape[2]
    plans = [(gate_ref, cols, along_y, along_x) if turn == 0 else (up_ref, cols, along_x, along_y) for cols in windows for turn in (0, 1)]
    plans = [(da_ref, None, None, None), (db_ref, None, None, None)] + plans
    plans.append((out_ref, pl.ds(0, accs[-1].shape[2]), along_x, along_y))
    for i, (whole, cols, first, second) in enumerate(plans):
        it = Item()
        it.a, it.z, it.o = accs[i], lines[i], finals[i]
        it.late = first is not None
        if it.late:
            it.r1, it.t, it.r, it.c = [group[i - 2] for group in (firsts_r, seconds_s, seconds_r, cores_s)]
            n = it.n = it.c.shape[0]
            target, it.bit = second
            kept = first[1] * (4 * n)
            base = kept + it.bit * (2 * n)
            it.first = copy(whole.at[rows_at(1 - first[1], 4 * n), cols], it.r1, first[0])
            it.far = Fetch(whole.at[pl.ds(pl.multiple_of(kept + (1 - it.bit) * (2 * n), 2 * n), 2 * n), cols], it.t)
            it.chip = copy(it.t, it.r, target)
            it.parts = [
                Fetch(whole.at[pl.ds(pl.multiple_of(base + (1 - core) * n, n), n), cols], it.c),
                Fetch(whole.at[pl.ds(pl.multiple_of(base + core * n, n), n), cols], it.a.at[core]),
            ]
            it.core = copy(it.c, it.a.at[core], sibling)
        else:
            it.parts = [Fetch(whole, it.a)]
        it.in1 = copy(it.a, it.z, (d, jnp.where(s == 0, 1, 2)))
        it.in2 = copy(it.a, it.o, third)
        it.out = copy(it.o, it.o, (d, jnp.where(s == 1, 0, 3)))
        items.append(it)

    def start(it):
        if it.late:
            it.first.start()
            it.far.start()
        for part in it.parts:
            part.start()

    def step0(it):
        at = rows_at(1 - it.bit, 2 * it.n)
        it.far.wait()
        it.first.wait_recv()
        it.t[...] = (it.t[...].astype(F32) + it.r1[at, :].astype(F32)).astype(BF16)
        it.chip.start()

    def step1(it):
        n = it.n
        for part in it.parts:
            part.wait()
        it.chip.wait_recv()

        def come(which):
            at = pl.ds(pl.multiple_of(it.bit * (2 * n) + which * n, n), n)
            return it.r1[at, :].astype(F32) + it.r[rows_at(which, n), :].astype(F32)

        it.c[...] = (it.c[...].astype(F32) + come(1 - core)).astype(BF16)
        it.core.start()
        it.a[core] = (it.a[core].astype(F32) + come(core)).astype(BF16)

    def step2(it):
        if it.late:
            it.core.wait_recv()
        else:
            it.parts[0].wait()

        @pl.when(outer)
        def _():
            it.in1.start()

    def step3(it):
        @pl.when(inner)
        def _():
            it.in1.wait_recv()
            it.a[...] = (it.a[...].astype(F32) + it.z[...].astype(F32)).astype(BF16)
            it.in2.start()

    def step4(it):
        @pl.when(inner)
        def _():
            it.in2.wait_recv()
            it.o[...] = (it.a[...].astype(F32) + it.o[...].astype(F32)).astype(BF16)
            it.out.start()

    def step5(it):
        @pl.when(outer)
        def _():
            it.out.wait_recv()

    def finish(it):
        if it.late:
            it.first.wait_send()
            it.chip.wait_send()
            it.core.wait_send()

        @pl.when(outer)
        def _():
            it.in1.wait_send()

        @pl.when(inner)
        def _():
            it.in2.wait_send()
            it.out.wait_send()


    mine, dim = x_s.shape
    loads = [Fetch(src, dst) for src, dst in zip(fetched, fetched_s)]
    x_load = Fetch(x_ref, x_s)
    w_loads = []
    for p in range(2):
        for t, w in enumerate((wq_ref, wk_ref, wv_ref)):
            w_loads.append(Fetch(w.at[:, lanes_at((2 * core + low) * 2 + p, 128)], w_s.at[:, pl.ds((3 * p + t) * 128, 128)]))
    for load in loads[:7]:
        load.start()
    for load in loads[7:] + [x_load] + w_loads:
        load.start()

    block = hk_s.shape[1]
    half = block // 2
    firsts = ((over_x, over_y), (over_y, over_x))
    heads = []
    for p in range(2):
        h = Item()
        h.p1 = [copy(hs_s.at[p, i], h1_r.at[p, i], firsts[p][0]) for i in range(2)]
        h.p2 = copy(h2_s.at[p], h2_r.at[p], firsts[p][1])
        h.core = copy(hk_s.at[p, rows_at(1 - core, half)], hc_s.at[p, core], sibling)
        h.high = copy(hh_s.at[p], hh_r.at[p], over_high)
        h.z = copy(heads_o.at[low, p], heads_o.at[low, p], over_z)
        heads.append(h)

    def product(p, yy, xx):
        return dot_tn(n1_s[:, lanes_at(2 * yy + xx, block)], dqkv_s[p])

    def heads0(p):
        h = heads[p]
        for turn in range(2):
            if p == 0:
                i = (1 - yb) if turn == 0 else yb
                hs_s[p, turn] = product(p, i, 1 - xb).astype(BF16)
            else:
                i = (1 - xb) if turn == 0 else xb
                hs_s[p, turn] = product(p, 1 - yb, i).astype(BF16)
            h.p1[turn].start()

    def heads1(p):
        h = heads[p]
        part = product(p, 1 - yb, xb) if p == 0 else product(p, yb, 1 - xb)
        h.p1[0].wait_recv()
        h2_s[p] = (part + h1_r[p, 0].astype(F32)).astype(BF16)
        h.p2.start()

    def heads2(p):
        h = heads[p]
        part = product(p, yb, xb)
        h.p1[1].wait_recv()
        part = part + h1_r[p, 1].astype(F32)
        h.p2.wait_recv()
        hk_s[p] = (part + h2_r[p].astype(F32)).astype(BF16)
        h.core.start()
        hc_s[p, core] = hk_s[p, rows_at(core, half), :]

    def heads3(p):
        h = heads[p]
        h.core.wait_recv()
        hh_s[p] = hc_s[p]
        h.high.start()

    def heads4(p):
        h = heads[p]
        h.high.wait_recv()
        heads_o[low, p] = (hh_s[p].astype(F32) + hh_r[p].astype(F32)).astype(BF16)
        h.z.start()

    def heads5(p):
        heads[p].z.wait_recv()

    def finish_heads(p):
        h = heads[p]
        for made in h.p1 + [h.p2, h.core, h.high, h.z]:
            made.wait_send()

    tokens = k_s.shape[0]
    rows = 256
    steps = tokens // rows
    lane = lax.broadcasted_iota(jnp.int32, (tokens, 128), 1)
    klane = lax.broadcasted_iota(jnp.int32, (rows, 128), 1)

    def prepare(p):
        do = dorow_s[p].astype(F32)
        prod = do * (o0_s, o1_s)[p][...]
        for h in range(2):
            mine = (lane < HEAD_DIM) if h == 0 else (lane >= HEAD_DIM)
            other = lane - (HEAD_DIM if h == 0 else 0)
            delta = jnp.sum(jnp.where(mine, prod, 0.0), axis=1, keepdims=True)
            a, b, c = three_parts(delta)
            aug = jnp.where(other == 5, -a, jnp.where(other == 6, -b, jnp.where(other == 7, -c, 0.0)))
            doa_s[h] = jnp.where(mine, do, aug).astype(BF16)
        dq_s[...] = jnp.zeros_like(dq_s)

    def attend(p, j):
        qa_s = (qa0_s, qa1_s)[p]
        cols = slice(128 * p, 128 * p + 128)
        here = pl.ds(pl.multiple_of(j * rows, rows), rows)
        k = k_s[here, cols]
        v = v_s[here, cols]
        kf = k.astype(F32)
        vf = v.astype(F32)
        mk = mask_k_ref[here, :]
        dead = jnp.where(mk[:, 4:5].astype(F32) < 0, 1.0, 0.0)
        dks, dvs = [], []
        for h in range(2):
            kmine = (klane < HEAD_DIM) if h == 0 else (klane >= HEAD_DIM)
            other = klane - (HEAD_DIM if h == 0 else 0)
            one = (other >= 5) & (other < 8)
            ka = jnp.where(kmine, k, mk)
            va = jnp.where(kmine, v, jnp.where(one, jnp.ones_like(v), jnp.zeros_like(v)))
            pr = jnp.exp(dot_nt(ka, qa_s[h]))
            ds = (pr * dot_nt(va, doa_s[h])).astype(BF16)
            dk = dot_nn(ds, qa_s[h])
            dv = dot_nn(pr.astype(BF16), doa_s[h])
            dq_s[h] += dot_tn(ds, ka)
            qd = qa_s[h, here, :].astype(F32)
            dod = doa_s[h, here, :].astype(F32)
            own = jnp.sum(jnp.where(kmine | one, qd * jnp.where(kmine, kf, 1.0), 0.0), axis=1, keepdims=True)
            own_p = jnp.where(dead > 0, jnp.exp(jnp.where(dead > 0, own, 0.0)), 0.0)
            own_d = jnp.sum(jnp.where(kmine | one, dod * jnp.where(kmine, vf, 1.0), 0.0), axis=1, keepdims=True)
            own_ds = own_p * own_d
            dks.append(dk + own_ds * qd)
            dvs.append(dv + own_p * dod)
            dq_s[h, here, :] += jnp.where(kmine, own_ds * kf, 0.0)
        dqkv_s[p, here, 128:256] = jnp.where(klane < HEAD_DIM, dks[0], dks[1]).astype(BF16)
        dqkv_s[p, here, 256:384] = jnp.where(klane < HEAD_DIM, dvs[0], dvs[1]).astype(BF16)

    cut = mine // 3
    width = dqkv_s.shape[2]

    def dn1_of(i):
        at = pl.ds(i * mine, mine)
        return dot_nt(dqkv_s[0, at, :], w_s[:, 0:width]) + dot_nt(dqkv_s[1, at, :], w_s[:, width : 2 * width])

    to_core = [copy(cs_s.at[i], cr_r.at[i], sibling) for i in range(2)]
    to_z = [copy(cs_s.at[1, pl.ds(i * cut, cut)], zr_r.at[pl.ds(i * cut, cut)], over_z) for i in range(3)]
    to_home = [copy(cs_s.at[0, pl.ds(i * cut, cut)], gt_o.at[pl.ds(i * cut, cut)], swapped) for i in range(3)]

    late_loads = w_loads + [x_load, loads[8]]

    def give_core(i):
        while late_loads:
            late_loads.pop().wait()
        cs_s[i] = dn1_of(2 + i).astype(BF16)
        to_core[i].start()

    def give_z(_):
        dn = dn1_of(1)
        to_core[1].wait_recv()
        to_core[1].wait_send()
        cs_s[1] = (dn + cr_r[1].astype(F32)).astype(BF16)
        for made in to_z:
            made.start()

    def keep_own(_):
        dn_s[...] = dn1_of(0)
        to_core[0].wait_recv()
        to_core[0].wait_send()

    def give_home(i):
        at = pl.ds(i * cut, cut)
        to_z[i].wait_recv()
        dn = dn_s[at, :] + cr_r[0, at, :].astype(F32) + zr_r[at, :].astype(F32)
        x = x_s[at, :].astype(F32)
        scale = lax.rsqrt(jnp.mean(x * x, axis=1, keepdims=True) + EPS)
        dn = dn * gain_one_ref[...]
        grad = dh_s[at, :] + scale * dn - x * (scale * scale * scale * jnp.mean(x * dn, axis=1, keepdims=True))
        cs_s[0, at, :] = grad.astype(BF16)

        @pl.when(moved)
        def _():
            to_home[i].start()

        @pl.when(jnp.logical_not(moved))
        def _():
            gt_o[at, :] = cs_s[0, at, :]

    tasks = {
        "start": lambda i: start(items[i]),
        "s0": lambda i: step0(items[i]),
        "s1": lambda i: step1(items[i]),
        "s2": lambda i: step2(items[i]),
        "s3": lambda i: step3(items[i]),
        "s4": lambda i: step4(items[i]),
        "s5": lambda i: step5(items[i]),
        "h0": heads0,
        "h1": heads1,
        "h2": heads2,
        "h3": heads3,
        "h4": heads4,
        "h5": heads5,
        "core": give_core,
        "z": give_z,
        "own": keep_own,
        "home": give_home,
    }

    def run(todo):
        for name, i in todo:
            tasks[name](i)

    run(ORDER[0])
    for load in loads[:7]:
        load.wait()
    for p in range(2):
        before, slots, later = ORDER[1 + p]
        run(before)
        prepare(p)

        @pl.loop(0, steps)
        def _(j, p=p, slots=slots):
            attend(p, j)
            for i, todo in enumerate(slots):
                if todo:

                    @pl.when(j == i)
                    def _(todo=todo):
                        run(todo)

        dqkv_s[p, :, 0:128] = jnp.where(lane < HEAD_DIM, dq_s[0], dq_s[1]).astype(BF16)
        if p == 0:
            loads[7].wait()
        run(later)

    for it in items:
        finish(it)
    for p in range(2):
        finish_heads(p)
    for made in to_z:
        made.wait_send()

    @pl.when(moved)
    def _():
        for made in to_home:
            made.wait_recv()
            made.wait_send()


def closing(mask_key, gain, fetched, weights, x, grads):
    tokens = mask_key.shape[0]
    mine, dim = x.shape
    vmem = pl.BlockSpec(memory_space=pltpu.VMEM)
    anywhere = pl.BlockSpec(memory_space=pl.ANY)
    down, _, gate, _, outp = [w.shape for w in grads]
    third = 128 * (gate[1] // 128 // 3)
    widths = [third] + [128 * ((gate[1] - third) // 256)]
    widths.append(gate[1] - sum(widths))
    shards = [down[1:]] * 2 + [(gate[0] // 8, width) for width in widths for _ in range(2)]
    shards.append((outp[0] // 8, outp[1]))
    lates = shards[2:]
    block = dim // 4
    three = 3 * 128
    scratch = [pltpu.VMEM(v.shape, v.dtype) for v in fetched]
    scratch += [pltpu.VMEM((4 * rows, cols), BF16) for rows, cols in lates]
    scratch += [pltpu.VMEM((2 * rows, cols), BF16) for rows, cols in lates] * 2
    scratch += [pltpu.VMEM(w, BF16) for w in lates]
    scratch += [pltpu.VMEM((2,) + w, BF16) for w in shards] * 2
    scratch += [
        pltpu.VMEM((2, tokens, 128), BF16),
        pltpu.VMEM((2, tokens, 128), F32),
        pltpu.VMEM((2, tokens, three), BF16),
        pltpu.VMEM((2, 2, block, three), BF16),
        pltpu.VMEM((2, 2, block, three), BF16),
        pltpu.VMEM((2, block, three), BF16),
        pltpu.VMEM((2, block, three), BF16),
        pltpu.VMEM((2, block, three), BF16),
        pltpu.VMEM((2, 2, block // 2, three), BF16),
        pltpu.VMEM((2, 2, block // 2, three), BF16),
        pltpu.VMEM((2, 2, block // 2, three), BF16),
        pltpu.VMEM((dim, 2 * three), BF16),
        pltpu.VMEM((mine, dim), BF16),
        pltpu.VMEM((mine, dim), F32),
        pltpu.VMEM((2, mine, dim), BF16),
        pltpu.VMEM((2, mine, dim), BF16),
        pltpu.VMEM((mine, dim), BF16),
    ]
    remote = 6 * ITEMS - 6 + 2 * 6 + 2 + 3 + 3
    local = FETCHED + 7 + 3 * ITEMS - 4
    semaphores = [pltpu.SemaphoreType.DMA((count,)) for count in (remote, remote, local)]
    return pl.pallas_call(
        closing_kernel,
        in_specs=[vmem] * 2 + [anywhere] * (FETCHED + 4 + 5),
        out_specs=[vmem] * (2 + ITEMS),
        out_shape=[jax.ShapeDtypeStruct((mine, dim), BF16)]
        + [jax.ShapeDtypeStruct((2,) + w, BF16) for w in shards]
        + [jax.ShapeDtypeStruct((2, 2, 2, block // 2, three), BF16)],
        scratch_shapes=scratch + semaphores,
        compiler_params=pltpu.CompilerParams(collective_id=0, has_side_effects=True, vmem_limit_bytes=VMEM_BYTES),
        cost_estimate=pl.CostEstimate(
            flops=40 * tokens * tokens * 256, bytes_accessed=40 << 20, transcendentals=4 * tokens * tokens
        ),
        name="closing",
    )(mask_key, gain, *fetched, *weights, x, *grads)


def placing_kernel(count, g1, g2, *refs):
    weights, grads, outs, kept, sems = refs[:5], refs[5 : 9 + count], refs[9 + count : 19 + count], refs[19 + count : -1], refs[-1]
    loads = []
    sources = list(grads)
    for w, to in zip(weights, kept[len(grads) :]):
        n = to.shape[0]
        sources.append(w.at[pl.ds(pl.multiple_of(lax.axis_index("dp") * n, n), n)])
    for i, (src, to) in enumerate(zip(sources, kept)):
        loads.append(pltpu.make_async_copy(src, to, sems.at[i]))
        loads[-1].start()
    for load in loads:
        load.wait()
    gt, da, db, *units, out, heads = kept[: len(grads)]
    wq, wk, wv, wg, wu = kept[len(grads) :]
    gt_o, q_o, k_o, v_o, out_o, gate_o, up_o, down_o, g1_o, g2_o = outs
    gt_o[...] = gt[...].astype(F32)
    cut = da.shape[2]
    for c in range(2):
        first = [c * (gate_o.shape[1] // 2)] * 2
        for i, part in enumerate(units):
            to, size = (gate_o, up_o)[i % 2], part.shape[2]
            to[:, first[i % 2] : first[i % 2] + size] = part[c].astype(F32)
            first[i % 2] += size
        down_o[:, 2 * c * cut : (2 * c + 1) * cut] = da[c].astype(F32)
        down_o[:, (2 * c + 1) * cut : (2 * c + 2) * cut] = db[c].astype(F32)
        out_o[:, 2 * c * cut : (2 * c + 2) * cut] = out[c].astype(F32)
    for m in range(4):
        for p in range(2):
            at = slice((2 * m + p) * 128, (2 * m + p + 1) * 128)
            for t, to in enumerate((q_o, k_o, v_o)):
                to[:, at] = heads[m % 2, p, m // 2, :, t * 128 : (t + 1) * 128].astype(F32)

    def along(pairs, gain):
        total = sum([jnp.sum(grad[...] * w[...].astype(F32), axis=1, keepdims=True) for grad, w in pairs])
        n = total.shape[0]
        return jnp.broadcast_to(total, (n, n)).T[0:1, :] / gain[...]

    g1_o[...] = along(((q_o, wq), (k_o, wk), (v_o, wv)), g1)
    g2_o[...] = along(((gate_o, wg), (up_o, wu)), g2)


def placing(grads, heads, gains, weights):
    gt, da, out = grads[0], grads[1], grads[-1]
    n, dim = out.shape[1], 2 * out.shape[2]
    units = sum([part.shape[2] for part in grads[3:-1]])
    shapes = [gt.shape] + [(n, dim)] * 4 + [(n, units)] * 2 + [(da.shape[1], dim)] + [(1, n)] * 2
    vmem, anywhere = pl.BlockSpec(memory_space=pltpu.VMEM), pl.BlockSpec(memory_space=pl.ANY)
    kept = [v.shape for v in (*grads, heads)] + [(n, w.shape[1]) for w in weights]
    return pl.pallas_call(
        functools.partial(placing_kernel, len(grads) - 3),
        in_specs=[vmem] * 2 + [anywhere] * (6 + len(grads)),
        out_specs=[vmem] * 10,
        out_shape=[jax.ShapeDtypeStruct(v, F32) for v in shapes],
        scratch_shapes=[pltpu.VMEM(v, BF16) for v in kept] + [pltpu.SemaphoreType.DMA((len(kept),))],
        compiler_params=pltpu.CompilerParams(vmem_limit_bytes=VMEM_BYTES),
        cost_estimate=pl.CostEstimate(flops=1 << 22, bytes_accessed=14 << 20, transcendentals=0),
        name="placing",
    )(*gains, *weights, *grads, heads)


def local_fused(
    dps,
    seqs,
    tokens,
    query_weight,
    key_weight,
    value_weight,
    out_weight,
    gate_weight,
    up_weight,
    down_weight,
    attention_gain,
    feedforward_gain,
    pair_lengths,
    live_mask,
    out_grad,
):
    mine, dim = tokens.shape
    d = lax.axis_index("dp")
    s = lax.axis_index("seq")
    core = d % 2
    x_bit = (d // 2) % 2
    y_bit = (d // 4) % 2
    moved = core != s // 2

    def move(value, target):
        pairs = []
        for i in range(dps * seqs):
            to = target(i // seqs, i % seqs)
            if to is not None:
                pairs.append((i, to[0] * seqs + to[1]))
        return lax.ppermute(value, AXES, pairs)

    def trade(value):
        return move(value, lambda dd, ss: (dd ^ 1, ss ^ 2) if dd % 2 != ss // 2 else None)

    def with_core(value):
        return move(value, lambda dd, ss: (dd ^ 1, ss))

    def half_of(value, which, axis):
        size = value.shape[axis] // 2
        return lax.dynamic_slice_in_dim(value, which * size, size, axis=axis)

    projections = (query_weight, key_weight, value_weight)
    n1_row, k, v, qa_0, qa_1, o_0, o_1, mask_key, h, n2_both, o_both, dy_both, x_low = opening(
        tokens, live_mask[None, :], pair_lengths, (attention_gain[None, :], feedforward_gain[None, :]),
        (*projections, out_weight), out_grad,
    )

    layer_out, dh, do, gate, up, outp, down_a, down_b = middle(
        feedforward_gain[None, :], n2_both, dy_both, h, o_both, gate_weight, up_weight, down_weight, out_weight
    )

    layer_out = jnp.where(moved, trade(layer_out), layer_out)

    *grads, heads_grads = closing(
        mask_key, attention_gain[None, :], (do, qa_0, qa_1, k, v, o_0, o_1, n1_row, dh), projections, x_low,
        (down_a, down_b, gate, up, outp),
    )

    gains = [
        lax.dynamic_slice_in_dim(gain[None, :], lax.axis_index("dp") * (dim // dps), dim // dps, axis=1)
        for gain in (attention_gain, feedforward_gain)
    ]
    *results, gain_one, gain_two = placing(grads, heads_grads, gains, (*projections, gate_weight, up_weight))
    return (layer_out, *results, gain_one[0], gain_two[0])


def solution(mesh):
    both = P(("dp", "seq"), None)
    rows = P("dp", None)
    dps, seqs = mesh.shape["dp"], mesh.shape["seq"]
    local = local_fused if (dps, seqs) == (8, 4) else local_plain
    return jax.shard_map(
        functools.partial(local, dps, seqs),
        mesh=mesh,
        in_specs=(both, P(), P(), P(), P(), P(), P(), P(), P(), P(), rows, P(("dp", "seq")), both),
        out_specs=(both, both, rows, rows, rows, rows, rows, rows, rows, P("dp"), P("dp")),
        check_vma=False,
    )
```

```python
import functools

import jax
import jax.numpy as jnp
from jax import lax
from jax.experimental import pallas as pl
from jax.experimental.pallas import tpu as pltpu
from jax.sharding import PartitionSpec as P

HEADS = 16
HEAD_DIM = 64
EPS = 1e-06
BIG = float(2.0**40)
F32 = jnp.float32
BF16 = jnp.bfloat16
AXES = ("dp", "seq")
MESH = pl.DeviceIdType.MESH
VMEM_BYTES = 62 << 20
ITEMS, FETCHED, OPENED = 9, 9, 13


def dot_nn(a, b):
    return lax.dot_general(a, b, (((1,), (0,)), ((), ())), preferred_element_type=F32)


def dot_nt(a, b):
    return lax.dot_general(a, b, (((1,), (1,)), ((), ())), preferred_element_type=F32)


def dot_tn(a, b):
    return lax.dot_general(a, b, (((0,), (0,)), ((), ())), preferred_element_type=F32)


def three_parts(v):
    high = v.astype(BF16).astype(F32)
    mid = (v - high).astype(BF16).astype(F32)
    low = (v - high - mid).astype(BF16).astype(F32)
    return high, mid, low


def forward_kernel(keep_queries, q_ref, k_ref, v_ref, mq_ref, mk_ref, dead_ref, kd_ref, vd_ref, o_ref, l_ref):
    lane = lax.broadcasted_iota(jnp.int32, q_ref.shape, 1)
    klane = lax.broadcasted_iota(jnp.int32, k_ref.shape, 1)
    q = q_ref[...]
    dead = dead_ref[...]
    qk = q.astype(F32) * kd_ref[...].astype(F32)
    outs, logs = [], []
    for h in range(2):
        mine = (lane < HEAD_DIM) if h == 0 else (lane >= HEAD_DIM)
        kmine = (klane < HEAD_DIM) if h == 0 else (klane >= HEAD_DIM)
        qa = jnp.where(mine, q, mq_ref[...])
        ka = jnp.where(kmine, k_ref[...], mk_ref[...])
        s = dot_nt(qa, ka)
        own = jnp.sum(jnp.where(mine, qk, 0.0), axis=1, keepdims=True)
        own = jnp.where(dead > 0, own, -BIG)
        top = jnp.maximum(jnp.max(s, axis=1, keepdims=True), own)
        p = jnp.exp(s - top).astype(BF16)
        va = jnp.where(kmine, v_ref[...], jnp.ones_like(v_ref[...]))
        r = dot_nn(p, va)
        own_p = jnp.exp(own - top)
        total = (r[:, HEAD_DIM : HEAD_DIM + 1] if h == 0 else r[:, 0:1]) + own_p
        outs.append((r + own_p * vd_ref[...].astype(F32)) * (1.0 / total))
        log = top + jnp.log(total)
        if keep_queries:
            other = lane - (HEAD_DIM if h == 0 else 0)
            a, b, c = three_parts(log)
            aug = mq_ref[...].astype(F32)
            aug = jnp.where(other == 5, -a, jnp.where(other == 6, -b, jnp.where(other == 7, -c, aug)))
            l_ref[h] = jnp.where(mine, q.astype(F32), aug).astype(BF16)
        logs.append(log)
    o_ref[...] = jnp.where(lane < HEAD_DIM, outs[0], outs[1])
    if not keep_queries:
        l_ref[...] = jnp.where(lane < HEAD_DIM, logs[0], logs[1])


def rows_per_step(tokens):
    for rows in (512, 384, 256, 128):
        if tokens % rows == 0 and rows * tokens <= 800000:
            return rows
    return 128


def attention_forward(q, k, v, mq, mk, dead, group=None):
    tokens, width = q.shape
    rows = rows_per_step(tokens)
    first, count = (0, width // 128) if group is None else (group, 1)
    part = pl.BlockSpec((rows, 128), lambda h, i: (i, h + first))
    full = pl.BlockSpec((tokens, 128), lambda h, i: (0, h + first))
    out = pl.BlockSpec((rows, 128), lambda h, i: (i, h))
    keep = group is not None
    log_out, log_shape = out, jax.ShapeDtypeStruct((tokens, 128 * count), F32)
    if keep:
        log_out = pl.BlockSpec((2, rows, 128), lambda h, i: (0, i, 0))
        log_shape = jax.ShapeDtypeStruct((2, tokens, 128), BF16)
    return pl.pallas_call(
        functools.partial(forward_kernel, keep),
        grid=(count, tokens // rows),
        in_specs=[
            part,
            full,
            full,
            pl.BlockSpec((rows, 128), lambda h, i: (i, 0)),
            pl.BlockSpec((tokens, 128), lambda h, i: (0, 0)),
            pl.BlockSpec((rows, 1), lambda h, i: (i, 0)),
            part,
            part,
        ],
        out_specs=[out, log_out],
        out_shape=[jax.ShapeDtypeStruct((tokens, 128 * count), F32), log_shape],
        compiler_params=pltpu.CompilerParams(vmem_limit_bytes=56 << 20),
        cost_estimate=pl.CostEstimate(
            flops=16 * tokens * tokens * 128 * count, bytes_accessed=16 * tokens * width, transcendentals=2 * tokens * tokens * count
        ),
        name="attention_forward",
    )(q, k, v, mq, mk, dead, k, v)


def backward_kernel(
    q_ref, k_ref, v_ref, do_ref, o_ref, l_ref, mq_ref, mk_ref, dead_ref, dq_ref, dk_ref, dv_ref, qa_s, doa_s, dq_s
):
    j = pl.program_id(1)
    tokens = q_ref.shape[0]
    rows = k_ref.shape[0]
    lane = lax.broadcasted_iota(jnp.int32, (tokens, 128), 1)
    klane = lax.broadcasted_iota(jnp.int32, (rows, 128), 1)

    @pl.when(j == 0)
    def _():
        do = do_ref[...].astype(F32)
        prod = do * o_ref[...]
        q = q_ref[...].astype(F32)
        logs = l_ref[...]
        for h in range(2):
            mine = (lane < HEAD_DIM) if h == 0 else (lane >= HEAD_DIM)
            other = lane - (HEAD_DIM if h == 0 else 0)
            delta = jnp.sum(jnp.where(mine, prod, 0.0), axis=1, keepdims=True)
            log = logs[:, 0:1] if h == 0 else logs[:, HEAD_DIM : HEAD_DIM + 1]
            a, b, c = three_parts(log)
            aug = mq_ref[...].astype(F32)
            aug = jnp.where(other == 5, -a, jnp.where(other == 6, -b, jnp.where(other == 7, -c, aug)))
            qa_s[h] = jnp.where(mine, q, aug).astype(BF16)
            a, b, c = three_parts(delta)
            aug = jnp.where(other == 5, -a, jnp.where(other == 6, -b, jnp.where(other == 7, -c, 0.0)))
            doa_s[h] = jnp.where(mine, do, aug).astype(BF16)
        dq_s[...] = jnp.zeros_like(dq_s)

    k = k_ref[...]
    v = v_ref[...]
    here = pl.ds(pl.multiple_of(j * rows, rows), rows)
    kf = k.astype(F32)
    vf = v.astype(F32)
    dead = dead_ref[...]
    dks, dvs = [], []
    for h in range(2):
        kmine = (klane < HEAD_DIM) if h == 0 else (klane >= HEAD_DIM)
        other = klane - (HEAD_DIM if h == 0 else 0)
        one = (other >= 5) & (other < 8)
        ka = jnp.where(kmine, k, mk_ref[...])
        va = jnp.where(kmine, v, jnp.where(one, jnp.ones_like(v), jnp.zeros_like(v)))
        p = jnp.exp(dot_nt(ka, qa_s[h]))
        ds = (p * dot_nt(va, doa_s[h])).astype(BF16)
        dk = dot_nn(ds, qa_s[h])
        dv = dot_nn(p.astype(BF16), doa_s[h])
        dq_s[h] += dot_tn(ds, ka)
        qd = qa_s[h, here, :].astype(F32)
        dod = doa_s[h, here, :].astype(F32)
        own = jnp.sum(jnp.where(kmine | one, qd * jnp.where(kmine, kf, 1.0), 0.0), axis=1, keepdims=True)
        own_p = jnp.where(dead > 0, jnp.exp(jnp.where(dead > 0, own, 0.0)), 0.0)
        own_d = jnp.sum(jnp.where(kmine | one, dod * jnp.where(kmine, vf, 1.0), 0.0), axis=1, keepdims=True)
        own_ds = own_p * own_d
        dks.append(dk + own_ds * qd)
        dvs.append(dv + own_p * dod)
        dq_s[h, here, :] += jnp.where(kmine, own_ds * kf, 0.0)
    dk_ref[...] = jnp.where(klane < HEAD_DIM, dks[0], dks[1]).astype(BF16)
    dv_ref[...] = jnp.where(klane < HEAD_DIM, dvs[0], dvs[1]).astype(BF16)

    @pl.when(j == pl.num_programs(1) - 1)
    def _():
        dq_ref[...] = jnp.where(lane < HEAD_DIM, dq_s[0], dq_s[1]).astype(BF16)


def attention_backward(q, k, v, do, o, logs, mq, mk, dead):
    tokens, width = q.shape
    rows = rows_per_step(tokens)
    part = pl.BlockSpec((rows, 128), lambda h, i: (i, h))
    full = pl.BlockSpec((tokens, 128), lambda h, i: (0, h))
    return pl.pallas_call(
        backward_kernel,
        grid=(width // 128, tokens // rows),
        in_specs=[
            full,
            part,
            part,
            full,
            full,
            full,
            pl.BlockSpec((tokens, 128), lambda h, i: (0, 0)),
            pl.BlockSpec((rows, 128), lambda h, i: (i, 0)),
            pl.BlockSpec((rows, 1), lambda h, i: (i, 0)),
        ],
        out_specs=[full, part, part],
        out_shape=[jax.ShapeDtypeStruct((tokens, width), BF16)] * 3,
        scratch_shapes=[
            pltpu.VMEM((2, tokens, 128), BF16),
            pltpu.VMEM((2, tokens, 128), BF16),
            pltpu.VMEM((2, tokens, 128), F32),
        ],
        compiler_params=pltpu.CompilerParams(vmem_limit_bytes=56 << 20),
        cost_estimate=pl.CostEstimate(
            flops=40 * tokens * tokens * width, bytes_accessed=24 * tokens * width, transcendentals=tokens * tokens * width // HEAD_DIM
        ),
        name="attention_backward",
    )(q, k, v, do, o, logs, mq, mk, dead)


def mask_terms(pair, live):
    lane = jnp.arange(128, dtype=jnp.int32)[None, :] % HEAD_DIM
    same = lane == pair[:, None]
    query = jnp.where(lane < 4, same, lane == 4).astype(BF16)
    key = jnp.where(
        lane < 4,
        jnp.where(same, 0.0, -BIG),
        jnp.where(lane == 4, jnp.where(live[:, None], 0.0, -BIG), ((lane >= 5) & (lane < 8)).astype(F32)),
    ).astype(BF16)
    return query, key, 1.0 - live.astype(F32)[:, None]


def gelu_parts(g):
    c = 0.7978845608028654
    t = jnp.tanh(c * (g + 0.044715 * g * g * g))
    act = 0.5 * g * (1.0 + t)
    slope = 0.5 * (1.0 + t) + 0.5 * g * (1.0 - t * t) * c * (1.0 + 3 * 0.044715 * g * g)
    return act, slope


def local_plain(
    dps,
    seqs,
    tokens,
    query_weight,
    key_weight,
    value_weight,
    out_weight,
    gate_weight,
    up_weight,
    down_weight,
    attention_gain,
    feedforward_gain,
    pair_lengths,
    live_mask,
    out_grad,
):
    mine, dim = tokens.shape
    units = gate_weight.shape[1]
    half = seqs // 2
    width = dim // seqs
    chips = dps // 2
    d = lax.axis_index("dp")
    s = lax.axis_index("seq")
    core = d % 2
    high = (s >= half).astype(jnp.int32)
    low = s % half
    member = core * half + low
    moved = core != high

    def move(value, target):
        pairs = []
        for i in range(dps * seqs):
            to = target(i // seqs, i % seqs)
            if to is not None:
                pairs.append((i, to[0] * seqs + to[1]))
        return lax.ppermute(value, AXES, pairs)

    def trade(value):
        def target(dd, ss):
            return (dd ^ 1, (ss + half) % seqs) if dd % 2 != ss // half else None

        return move(value, target)

    def with_core(value):
        return move(value, lambda dd, ss: (dd ^ 1, ss))

    def with_chip(value, bit):
        return move(value, lambda dd, ss: (dd ^ bit, ss))

    def with_seq(value, bit):
        return move(value, lambda dd, ss: (dd, ss ^ bit))

    def with_member(value, bit):
        return with_core(value) if bit == half else with_seq(value, bit)

    bits = []
    while (1 << len(bits)) < seqs:
        bits.append(1 << len(bits))
    chip_bits = []
    while (2 << len(chip_bits)) < dps:
        chip_bits.append(2 << len(chip_bits))

    def gather_row(value):
        value = value[None]
        for bit in bits:
            value = jnp.concatenate([value, with_member(value, bit)], axis=0)
        return value

    def to_tokens(value):
        value = value.reshape(seqs, mine, width)
        for bit in bits:
            value = value.reshape(value.shape[0] // 2, 2, mine, value.shape[2])
            keep, come = value[:, 0], with_member(value[:, 1], bit)
            upper = (member & bit) != 0
            value = jnp.concatenate([jnp.where(upper, come, keep), jnp.where(upper, keep, come)], axis=2)
        return value[0]

    def to_heads(value):
        value = value[None]
        for bit in reversed(bits):
            first, second = jnp.split(value, 2, axis=2)
            upper = (member & bit) != 0
            come = with_member(jnp.where(upper, first, second), bit)
            value = jnp.stack([jnp.where(upper, second, first), come], axis=1)
            value = value.reshape(-1, mine, value.shape[3])
        return value.reshape(seqs * mine, width)

    def row_sum(value):
        value = value.reshape(seqs, mine, dim)
        for bit in reversed(bits):
            keep, give = value[: value.shape[0] // 2], value[value.shape[0] // 2 :]
            value = keep + with_member(give.astype(BF16), bit).astype(F32)
        return value[0]

    def over_chips(value, order):
        cols = value.shape[1]
        rows = value.shape[0] // chips
        value = value.reshape((2,) * len(chip_bits) + (rows, cols))
        left = list(reversed(chip_bits))
        for bit in order:
            axis = left.index(bit)
            left.pop(axis)
            upper = ((d & bit) != 0).astype(jnp.int32)
            give = lax.dynamic_index_in_dim(value, 1 - upper, axis, keepdims=False)
            keep = lax.dynamic_index_in_dim(value, upper, axis, keepdims=False)
            come = with_chip(give, bit)
            value = (keep.astype(F32) + come.astype(F32)).astype(BF16)
        return value.reshape(rows, cols)

    def over_seq(value):
        for i in range(half - 1):
            come = move(
                value,
                lambda dd, ss: (dd, i + 1) if ss == i else ((dd, seqs - 2 - i) if ss == seqs - 1 - i else None),
            )
            value = (value.astype(F32) + come.astype(F32)).astype(BF16)
        come = move(value, lambda dd, ss: (dd, seqs - 1 - ss) if ss in (half - 1, half) else None)
        value = (value.astype(F32) + come.astype(F32)).astype(BF16)
        for i in reversed(range(half - 1)):
            come = move(
                value,
                lambda dd, ss: (dd, i) if ss == i + 1 else ((dd, seqs - 1 - i) if ss == seqs - 2 - i else None),
            )
            value = jnp.where((s == i) | (s == seqs - 1 - i), come, value)
        return value

    def my_core(value, axis, other=False):
        shape = value.shape
        size = shape[axis] // dps
        value = value.reshape(shape[:axis] + (chips, 2, size) + shape[axis + 1 :])
        value = lax.dynamic_index_in_dim(value, (1 - core) if other else core, axis + 1, keepdims=False)
        return value.reshape(shape[:axis] + (chips * size,) + shape[axis + 1 :])

    bounds = jnp.cumsum(pair_lengths[0])[:-1]
    place = s * mine + jnp.arange(mine, dtype=jnp.int32)
    pair = jnp.sum((place[:, None] >= bounds[None, :]).astype(jnp.int32), axis=1)
    code = (2 * pair + (live_mask > 0)).astype(BF16)
    lines = -(-mine // dim)
    code = jnp.pad(code, (0, 16 * dim * (-(-lines // 16)) - mine)).reshape(-1, dim)
    packed = jnp.concatenate([tokens, code], axis=0)
    packed = jnp.where(moved, trade(packed), packed)
    row = gather_row(packed)
    x_row = row[:, :mine].reshape(seqs * mine, dim)
    code_row = row[:, mine:].reshape(seqs, -1)[:, :mine].reshape(-1).astype(jnp.int32)
    mask_query, mask_key, dead = mask_terms(code_row // 2, code_row % 2 == 1)
    x = packed[:mine].astype(F32)
    dy = jnp.where(moved, trade(out_grad), out_grad)

    def scaled(v, gain):
        return v * lax.rsqrt(jnp.mean(v * v, axis=1, keepdims=True) + EPS) * gain[None, :]

    def heads_of(weight):
        return lax.dynamic_slice_in_dim(weight, member * width, width, axis=1)

    n1_row = scaled(x_row.astype(F32), attention_gain).astype(BF16)
    wq, wk, wv = heads_of(query_weight), heads_of(key_weight), heads_of(value_weight)
    lanes = -(-width // 128) * 128
    widen = (lambda v: jnp.pad(v, ((0, 0), (0, lanes - width)))) if lanes != width else (lambda v: v)
    q, k, v = [widen(dot_nn(n1_row, w).astype(BF16)) for w in (wq, wk, wv)]
    o_heads, logs = attention_forward(q, k, v, mask_query, mask_key, dead)
    o = to_tokens(o_heads[:, :width].astype(BF16))

    h = x + dot_nn(o, out_weight)
    h_scale = lax.rsqrt(jnp.mean(h * h, axis=1, keepdims=True) + EPS)
    n2 = (h * h_scale * feedforward_gain[None, :]).astype(BF16)
    n2_both = jnp.concatenate([n2, with_core(n2)], axis=0)
    dy_both = jnp.concatenate([dy, with_core(dy)], axis=0)
    wg, wu, wd = my_core(gate_weight, 1), my_core(up_weight, 1), my_core(down_weight, 0)
    g = dot_nn(n2_both, wg)
    u = dot_nn(n2_both, wu)
    act, slope = gelu_parts(g)
    z = (act * u).astype(BF16)
    f = dot_nn(z, wd)
    layer_out = (h + f[:mine] + with_core(f[mine:].astype(BF16)).astype(F32)).astype(BF16)
    layer_out = jnp.where(moved, trade(layer_out), layer_out)

    grad_down = dot_tn(z, dy_both).astype(BF16)
    dz = dot_nt(dy_both, wd)
    dg = (dz * u * slope).astype(BF16)
    du = (dz * act).astype(BF16)
    grad_gate = dot_tn(n2_both, dg).astype(BF16)
    grad_upward = dot_tn(n2_both, du).astype(BF16)
    dn2_both = dot_nt(dg, wg) + dot_nt(du, wu)
    dn2 = dn2_both[:mine] + with_core(dn2_both[mine:].astype(BF16)).astype(F32)

    ghd = dn2 * feedforward_gain[None, :]
    dh = dy.astype(F32) + h_scale * ghd - h * (h_scale**3 * jnp.mean(h * ghd, axis=1, keepdims=True))
    gain_two = jnp.sum(dn2 * h * h_scale, axis=0)
    da = dh.astype(BF16)
    do = to_heads(dot_nt(da, out_weight).astype(BF16))
    o_both = jnp.concatenate([my_core(o, 1), with_core(my_core(o, 1, other=True))], axis=0)
    da_both = jnp.concatenate([da, with_core(da)], axis=0)
    grad_output = dot_tn(o_both, da_both).astype(BF16)

    dq, dk, dv = attention_backward(q, k, v, widen(do), o_heads, logs, mask_query, mask_key, dead)
    dq, dk, dv = dq[:, :width], dk[:, :width], dv[:, :width]
    dn1_row = dot_nt(dq, wq) + dot_nt(dk, wk) + dot_nt(dv, wv)
    x_row_scale = lax.rsqrt(jnp.mean(jnp.square(x_row.astype(F32)), axis=1, keepdims=True) + EPS)
    gain_one = jnp.sum(dn1_row * (x_row.astype(F32) * x_row_scale), axis=0)
    grad_heads = dot_tn(n1_row, jnp.concatenate([dq, dk, dv], axis=1)).astype(BF16)
    gains = jnp.pad(jnp.stack([gain_one, gain_two], axis=1), ((0, 0), (0, 126))).astype(BF16)
    dn1 = row_sum(dn1_row)

    x_scale = lax.rsqrt(jnp.mean(x * x, axis=1, keepdims=True) + EPS)
    gxd = dn1 * attention_gain[None, :]
    grad_tokens = dh + x_scale * gxd - x * (x_scale**3 * jnp.mean(x * gxd, axis=1, keepdims=True))
    grad_tokens = jnp.where(moved, trade(grad_tokens.astype(BF16)).astype(F32), grad_tokens)

    ahead, back = chip_bits, chip_bits[::-1]
    down_out = over_seq(over_chips(grad_down, ahead)).astype(F32)

    def both_cores(value):
        n = value.shape[0] // 2
        first, second = value[:n], value[n:]
        upper = core == 1
        come = with_core(jnp.where(upper, first, second))
        keep = jnp.where(upper, second, first)
        return jnp.stack([jnp.where(upper, come, keep), jnp.where(upper, keep, come)], axis=1)

    def unit_columns(value):
        n = value.shape[0]
        return value.reshape(n, 2, chips, units // dps).transpose(0, 2, 1, 3).reshape(n, units)

    gate_out = unit_columns(over_seq(both_cores(over_chips(grad_gate, back)))).astype(F32)
    upward_out = unit_columns(over_seq(both_cores(over_chips(grad_upward, ahead)))).astype(F32)
    output_out = over_seq(over_chips(grad_output, back)).astype(F32)

    heads_part = over_chips(jnp.concatenate([grad_heads, gains], axis=1), back)
    heads_part = both_cores(heads_part)
    heads_part = (heads_part.astype(F32) + with_seq(heads_part, half).astype(F32)).astype(BF16)
    heads_part = heads_part[None]
    for bit in bits[:-1]:
        come = with_seq(heads_part, bit)
        upper = (member & bit) != 0
        heads_part = jnp.concatenate([jnp.where(upper, come, heads_part), jnp.where(upper, heads_part, come)], axis=0)
    heads_part = heads_part.transpose(1, 2, 0, 3).reshape(-1, seqs, 3 * width + 128)
    query_out, key_out, value_out = [
        heads_part[:, :, i * width : (i + 1) * width].reshape(-1, dim).astype(F32) for i in range(3)
    ]
    gains_out = jnp.sum(heads_part[:, :, 3 * width : 3 * width + 2].astype(F32), axis=1)
    return (
        layer_out,
        grad_tokens,
        query_out,
        key_out,
        value_out,
        output_out,
        gate_out,
        upward_out,
        down_out,
        gains_out[:, 0],
        gains_out[:, 1],
    )


def opening_kernel(tokens_ref, live_ref, lengths_ref, gain_one_ref, gain_two_ref, *refs):
    refs = list(refs)

    def take(n):
        taken, refs[:n] = refs[:n], []
        return taken

    wq_ref, wk_ref, wv_ref, wo_ref, dy_ref = take(5)
    outs = take(OPENED)
    kept = take(OPENED)
    n1_s, k_s, v_s, qa0_s, qa1_s, o0_s, o1_s, mk_s, h_s, n2_s, o_s, dy_s, x_s = kept
    xs, codes, w_s, wo_s, q_s, mq_s, ka_s, va_s, ob_s, send_sem, recv_sem, local_sem = take(12)

    d = lax.axis_index("dp")
    s = lax.axis_index("seq")
    core = d % 2
    low = s % 2
    high = s // 2
    member = 2 * core + low
    sibling = (d + 1 - 2 * core, s)
    over_z = (d, s + 1 - 2 * low)
    across = (d + 1 - 2 * core, s + 1 - 2 * low)
    swapped = (d + 1 - 2 * core, s + 2 - 4 * high)
    moved = core != high
    stays = core == high

    barrier = pltpu.get_barrier_semaphore()
    for other in (sibling, over_z, across, swapped):
        pl.semaphore_signal(barrier, inc=1, device_id=other, device_id_type=MESH)

    counts = {"remote": 0, "local": 0}

    class Copy:
        def __init__(self, src, dst, target):
            self.parts = (src, dst, target, counts["remote"])
            counts["remote"] += 1

        def made(self):
            src, dst, target, i = self.parts
            return pltpu.make_async_remote_copy(
                src_ref=src, dst_ref=dst, send_sem=send_sem.at[i], recv_sem=recv_sem.at[i], device_id=target, device_id_type=MESH
            )

        def start(self):
            self.made().start()

        def wait_recv(self):
            self.made().wait_recv()

        def wait_send(self):
            self.made().wait_send()

    class Fetch:
        def __init__(self, src, dst):
            self.parts = (src, dst, counts["local"])
            counts["local"] += 1

        def made(self):
            src, dst, i = self.parts
            return pltpu.make_async_copy(src, dst, local_sem.at[i])

        def start(self):
            self.made().start()

        def wait(self):
            self.made().wait()

    def lanes_at(start, size):
        return pl.ds(pl.multiple_of(start * size, size), size)

    mine, dim = tokens_ref.shape
    third = mine // 3
    pieces = [pl.ds(i * third, third) for i in range(3)]
    place = s * mine + lax.broadcasted_iota(jnp.int32, codes.shape[1:], 1)
    ends = [lengths_ref[0, 0]]
    for i in (1, 2):
        ends.append(ends[-1] + lengths_ref[0, i])
    pair = sum([jnp.where(place >= end, 1.0, 0.0) for end in ends])
    code = (2.0 * pair + jnp.where(live_ref[...][None, :] > 0, 1.0, 0.0)).astype(BF16)

    w_loads = []
    for p in range(2):
        for t, w in enumerate((wq_ref, wk_ref, wv_ref)):
            w_loads.append(Fetch(w.at[:, lanes_at(2 * member + p, 128)], w_s.at[:, pl.ds((3 * p + t) * 128, 128)]))
    wo_loads = [
        Fetch(wo_ref.at[pl.ds((2 * m + p) * 128, 128)], wo_s.at[pl.ds((4 * p + m) * 128, 128)]) for m in range(4) for p in range(2)
    ]

    trade = [Copy(tokens_ref.at[at], xs.at[0, at], swapped) for at in pieces]
    to_z = [Copy(xs.at[0, at], xs.at[1, at], over_z) for at in pieces]
    to_core = [Copy(xs.at[0, at], xs.at[2, at], sibling) for at in pieces]
    on_core = [Copy(xs.at[1, at], xs.at[3, at], sibling) for at in pieces]
    code_s = x_s.at[pl.ds(0, 16), pl.ds(0, mine)]
    code_trade = Copy(code_s, codes.at[0], swapped)
    code_z = Copy(codes.at[0], codes.at[1], over_z)
    code_core = Copy(codes.at[0], codes.at[2], sibling)
    code_on = Copy(codes.at[1], codes.at[3], sibling)
    dy_trade = Copy(dy_ref, dy_s.at[pl.ds(0, mine)], swapped)
    dy_local = Fetch(dy_ref, dy_s.at[pl.ds(0, mine)])
    dy_core = Copy(dy_s.at[pl.ds(0, mine)], dy_s.at[pl.ds(mine, mine)], sibling)

    code_s[...] = code
    pl.semaphore_wait(barrier, 4)

    @pl.when(moved)
    def _():
        code_trade.start()
        for made in trade:
            made.start()

    @pl.when(stays)
    def _():
        xs[0] = tokens_ref[...]
        codes[0] = code
        code_z.start()
        code_core.start()
        for a, b in zip(to_z, to_core):
            a.start()
            b.start()

    for load in w_loads + wo_loads:
        load.start()

    tokens = k_s.shape[0]
    lane = lax.broadcasted_iota(jnp.int32, (third, 128), 1)
    inside = lane % HEAD_DIM
    for load in w_loads:
        load.wait()

    def project(b):
        for i in range(3):
            at = pl.ds(i * third, third)
            x = xs[b, at, :].astype(F32)
            n1 = (x * lax.rsqrt(jnp.mean(x * x, axis=1, keepdims=True) + EPS) * gain_one_ref[...]).astype(BF16)
            to = pl.ds(pl.multiple_of(b * mine + i * third, 128), third)
            n1_s[to, :] = n1
            qkv = dot_nn(n1, w_s[...]).astype(BF16)
            for p in range(2):
                for t, out in enumerate((q_s, k_s, v_s)):
                    out[to, 128 * p : 128 * p + 128] = qkv[:, (3 * p + t) * 128 : (3 * p + t + 1) * 128]
            number = codes[b, 0:8, i * third : (i + 1) * third].astype(F32).T[:, 0:1]
            whose = jnp.floor(number * 0.5)
            dead = number - 2.0 * whose < 0.5
            same = inside.astype(F32) == whose
            mq_s[to, :] = jnp.where(inside < 4, jnp.where(same, 1.0, 0.0), jnp.where(inside == 4, 1.0, 0.0)).astype(BF16)
            key = jnp.where(inside == 4, jnp.where(dead, -BIG, 0.0), jnp.where((inside >= 5) & (inside < 8), 1.0, 0.0))
            mk_s[to, :] = jnp.where(inside < 4, jnp.where(same, 0.0, -BIG), key).astype(BF16)

    def block(i):
        return (i + 2 * moved.astype(jnp.int32)) % 4

    def relay():
        code_z.wait_recv()
        code_on.start()
        for a, b in zip(to_z, on_core):
            a.wait_recv()
            b.start()

    def from_core():
        code_core.wait_recv()
        for made in to_core:
            made.wait_recv()

    def from_core_on():
        code_on.wait_recv()
        for made in on_core:
            made.wait_recv()

    pl.when(moved)(from_core)
    project(block(0))

    @pl.when(moved)
    def _():
        code_trade.wait_recv()
        code_z.start()
        code_core.start()
        for made, a, b in zip(trade, to_z, to_core):
            made.wait_recv()
            a.start()
            b.start()
        dy_trade.start()
        from_core_on()

    pl.when(stays)(relay)
    project(block(1))
    pl.when(stays)(from_core)
    project(block(2))
    pl.when(moved)(relay)

    @pl.when(stays)
    def _():
        dy_local.start()
        from_core_on()

    project(block(3))
    code_trade_done = [code_trade] + trade

    @pl.when(moved)
    def _():
        for made in code_trade_done:
            made.wait_send()

    x_s[...] = xs[0]

    stores = [Fetch(src, dst) for src, dst in zip(kept, outs)]
    for i in (0, 1, 2, 7, 12):
        stores[i].start()

    rows = 256
    steps = tokens // rows
    lane = lax.broadcasted_iota(jnp.int32, (rows, 128), 1)
    klane = lax.broadcasted_iota(jnp.int32, (tokens, 128), 1)

    def attend(p, j):
        cols = slice(128 * p, 128 * p + 128)
        at = pl.ds(pl.multiple_of(j * rows, rows), rows)
        q = q_s[at, cols]
        mq = mq_s[at, :]
        qf = q.astype(F32)
        dead = mk_s[at, 4:5].astype(F32) < 0
        qk = qf * k_s[at, cols].astype(F32)
        v_own = v_s[at, cols].astype(F32)
        results = []
        for h in range(2):
            own_lanes = (lane < HEAD_DIM) if h == 0 else (lane >= HEAD_DIM)
            sc = dot_nt(jnp.where(own_lanes, q, mq), ka_s[h])
            own = jnp.sum(jnp.where(own_lanes, qk, 0.0), axis=1, keepdims=True)
            own = jnp.where(dead, own, -BIG)
            top = jnp.maximum(jnp.max(sc, axis=1, keepdims=True), own)
            pr = jnp.exp(sc - top).astype(BF16)
            r = dot_nn(pr, va_s[h])
            own_p = jnp.exp(own - top)
            total = (r[:, HEAD_DIM : HEAD_DIM + 1] if h == 0 else r[:, 0:1]) + own_p
            results.append((r + own_p * v_own) * (1.0 / total))
            other = lane - (HEAD_DIM if h == 0 else 0)
            a, b, c = three_parts(top + jnp.log(total))
            aug = jnp.where(other == 5, -a, jnp.where(other == 6, -b, jnp.where(other == 7, -c, mq.astype(F32))))
            (qa0_s, qa1_s)[p][h, at, :] = jnp.where(own_lanes, qf, aug).astype(BF16)
        o = jnp.where(lane < HEAD_DIM, results[0], results[1])
        (o0_s, o1_s)[p][at, :] = o
        ob_s[p, at, :] = o.astype(BF16)

    o_moves = []
    for p in range(2):
        to = o_s.at[pl.ds(0, mine), lanes_at(4 * p + member, 128)]
        o_moves.append(
            [Copy(ob_s.at[p, pl.ds(b * mine, mine)], to, target) for b, target in ((1, over_z), (3, across), (2, sibling))]
        )
    for p in range(2):
        cols = slice(128 * p, 128 * p + 128)
        for h in range(2):
            own_lanes = (klane < HEAD_DIM) if h == 0 else (klane >= HEAD_DIM)
            ka_s[h] = jnp.where(own_lanes, k_s[:, cols], mk_s[...])
            va_s[h] = jnp.where(own_lanes, v_s[:, cols], jnp.ones_like(v_s[:, cols]))

        @pl.loop(0, steps)
        def _(j, p=p):
            attend(p, j)

        for made in o_moves[p]:
            made.start()
        o_s[0:mine, lanes_at(4 * p + member, 128)] = ob_s[p, 0:mine, :]
        stores[3 + p].start()
        stores[5 + p].start()
        if p == 0:

            @pl.when(moved)
            def _():
                dy_trade.wait_recv()

            @pl.when(stays)
            def _():
                dy_local.wait()

            dy_core.start()

    for load in wo_loads:
        load.wait()
    o_core = Copy(o_s.at[pl.ds(0, mine)], o_s.at[pl.ds(mine, mine)], sibling)
    n2_core = Copy(n2_s.at[pl.ds(0, mine)], n2_s.at[pl.ds(mine, mine)], sibling)
    half = dim // 2
    for made in o_moves[0]:
        made.wait_recv()
    h_s[...] = x_s[...].astype(F32) + dot_nn(o_s[0:mine, 0:half], wo_s[0:half, :])
    for made in o_moves[1]:
        made.wait_recv()
    o_core.start()
    for at in pieces:
        hh = h_s[at, :] + dot_nn(o_s[at, half:dim], wo_s[half:dim, :])
        h_s[at, :] = hh
        n2_s[at, :] = (hh * lax.rsqrt(jnp.mean(hh * hh, axis=1, keepdims=True) + EPS) * gain_two_ref[...]).astype(BF16)
    n2_core.start()
    stores[8].start()
    dy_core.wait_recv()
    stores[11].start()
    o_core.wait_recv()
    stores[10].start()
    n2_core.wait_recv()
    stores[9].start()
    for made in to_z + to_core + on_core + [code_z, code_core, code_on, dy_core, o_core, n2_core] + o_moves[0] + o_moves[1]:
        made.wait_send()

    @pl.when(moved)
    def _():
        dy_trade.wait_send()

    for store in stores:
        store.wait()


def opening(tokens, live, lengths, gains, weights, dy):
    mine, dim = tokens.shape
    row = 4 * mine
    vmem = pl.BlockSpec(memory_space=pltpu.VMEM)
    anywhere = pl.BlockSpec(memory_space=pl.ANY)
    kept = [((row, dim), BF16), ((row, 256), BF16), ((row, 256), BF16)]
    kept += [((2, row, 128), BF16)] * 2 + [((row, 128), F32)] * 2 + [((row, 128), BF16)]
    kept += [((mine, dim), F32)] + [((2 * mine, dim), BF16)] * 3 + [((mine, dim), BF16)]
    scratch = [pltpu.VMEM(*v) for v in kept]
    scratch += [
        pltpu.VMEM((4, mine, dim), BF16),
        pltpu.VMEM((4, 16, mine), BF16),
        pltpu.VMEM((dim, 768), BF16),
        pltpu.VMEM((dim, dim), BF16),
        pltpu.VMEM((row, 256), BF16),
        pltpu.VMEM((row, 128), BF16),
        pltpu.VMEM((2, row, 128), BF16),
        pltpu.VMEM((2, row, 128), BF16),
        pltpu.VMEM((2, row, 128), BF16),
    ]
    remote, local = 12 + 4 + 2 + 6 + 2, 6 + 8 + 1 + OPENED
    semaphores = [pltpu.SemaphoreType.DMA((count,)) for count in (remote, remote, local)]
    return pl.pallas_call(
        opening_kernel,
        in_specs=[vmem, vmem, pl.BlockSpec(memory_space=pltpu.SMEM), vmem, vmem] + [anywhere] * 5,
        out_specs=[anywhere] * OPENED,
        out_shape=[jax.ShapeDtypeStruct(*v) for v in kept],
        scratch_shapes=scratch + semaphores,
        compiler_params=pltpu.CompilerParams(collective_id=1, has_side_effects=True, vmem_limit_bytes=VMEM_BYTES),
        cost_estimate=pl.CostEstimate(flops=16 * row * row * 256, bytes_accessed=30 << 20, transcendentals=4 * row * row),
        name="opening",
    )(tokens, live, lengths, *gains, *weights, dy)


def middle_kernel(gain_ref, *refs):
    refs = list(refs)

    def take(n):
        taken, refs[:n] = refs[:n], []
        return taken

    n2_ref, dy_ref, h_ref, o_ref, wg_ref, wu_ref, wd_ref, wo_ref = take(8)
    lo_o, dh_o, do_o, gate_o, up_o, out_o, da_o, db_o = take(8)
    n2_s, n2t_s, dy_s, h_s, wg_s, wu_s, wd_s, z_s, zc_s, dg_s, du_s = take(11)
    dn2_s, give_s, come_r, da_s, dap_s, dcr_s, dorow_s, own_s, far_s, stage_s, out_s, ra_s, rb_s, fr_s = take(14)
    f_s, lo_s = take(2)
    second_r, cores_s, accs = take(2), take(2), take(2)
    send_sem, recv_sem, local_sem = take(3)

    d = lax.axis_index("dp")
    s = lax.axis_index("seq")
    core = d % 2
    xb = (d // 2) % 2
    yb = (d // 4) % 2
    low = s % 2
    sibling = (d + 1 - 2 * core, s)
    over_x = (d + 2 - 4 * xb, s)
    over_y = (d + 4 - 8 * yb, s)
    over_z = (d, s + 1 - 2 * low)

    barrier = pltpu.get_barrier_semaphore()
    for other in (sibling, over_x, over_y, over_z):
        pl.semaphore_signal(barrier, inc=1, device_id=other, device_id_type=MESH)

    counts = {"remote": 0, "local": 0}

    class Copy:
        def __init__(self, src, dst, target, like=None):
            self.parts = (src, dst, target, counts["remote"] if like is None else like.parts[3])
            counts["remote"] += like is None

        def made(self):
            src, dst, target, i = self.parts
            return pltpu.make_async_remote_copy(
                src_ref=src, dst_ref=dst, send_sem=send_sem.at[i], recv_sem=recv_sem.at[i], device_id=target, device_id_type=MESH
            )

        def start(self):
            self.made().start()

        def wait_recv(self):
            self.made().wait_recv()

        def wait_send(self):
            self.made().wait_send()

    class Fetch:
        def __init__(self, src, dst):
            self.parts = (src, dst, counts["local"])
            counts["local"] += 1

        def made(self):
            src, dst, i = self.parts
            return pltpu.make_async_copy(src, dst, local_sem.at[i])

        def start(self):
            self.made().start()

        def wait(self):
            self.made().wait()

    def at_of(start, size):
        return pl.ds(pl.multiple_of(start * size, size), size)

    mine, dim = h_s.shape
    both = 2 * mine
    units = wd_s.shape[0]
    tiles = [(i, min(256, units - i)) for i in range(0, units, 256)]
    n2_load = Fetch(n2_ref, n2_s)
    dy_load = Fetch(dy_ref, dy_s)
    h_load = Fetch(h_ref, h_s)
    w_loads = []
    places = []
    for first, size in tiles:
        start = jnp.where(xb == 1, first, units - first - size)
        places.append(pl.ds(pl.multiple_of(start, 128), size))
        cols = pl.ds(pl.multiple_of(core * units + start, 128), size)
        w_loads.append(
            [
                Fetch(wg_ref.at[:, cols], wg_s.at[:, places[-1]]),
                Fetch(wu_ref.at[:, cols], wu_s.at[:, places[-1]]),
                Fetch(wd_ref.at[cols, :], wd_s.at[places[-1], :]),
            ]
        )
    n2_load.start()
    for load in w_loads[0]:
        load.start()
    dy_load.start()
    for loads in w_loads[1:]:
        for load in loads:
            load.start()
    h_load.start()

    half = dim // 2
    cut = half // 2
    rows = units // 2
    first_cols, last_cols = pl.ds(0, cut), pl.ds(cut, cut)
    top, end = pl.ds(0, mine), pl.ds(mine, mine)
    z_moves, a_far, a_own = [], [], []
    for cols in places:
        z_moves.append(Copy(z_s.at[top, cols], zc_s.at[end, cols], sibling))
        z_moves.append(Copy(z_s.at[end, cols], zc_s.at[top, cols], sibling))
        a_far.append(Copy(far_s.at[cols, first_cols], ra_s.at[cols], over_y))
        a_own.append(Copy(own_s.at[cols, first_cols], ra_s.at[cols], over_y, like=a_far[-1]))
    b_own = Copy(own_s.at[at_of(1 - xb, rows), last_cols], rb_s.at[at_of(core, rows)], over_x)
    b_far = Copy(far_s.at[at_of(1 - xb, rows), last_cols], rb_s.at[at_of(1 - core, rows)], over_x)

    def down_of(to, left, i):
        to[places[i], :] = dot_tn(left[:, places[i]], dy_s[:, at_of(core, half)]).astype(BF16)

    def far_of(i):
        z_moves[2 * i].wait_recv()
        z_moves[2 * i + 1].wait_recv()
        down_of(far_s, zc_s, i)
        pl.when(yb == core)(a_far[i].start)
        pl.when(yb != core)(a_own[i].start)
        done = tiles[i][0] + tiles[i][1]
        if done - tiles[i][1] < rows <= done:
            b_own.start()
            b_far.start()

    n2_load.wait()
    for i, (cols, loads) in enumerate(zip(places, w_loads)):
        loads[0].wait()
        loads[1].wait()
        g = dot_nn(n2_s[...], wg_s[:, cols])
        u = dot_nn(n2_s[...], wu_s[:, cols])
        act, slope = gelu_parts(g)
        z_s[:, cols] = (act * u).astype(BF16)
        if i == 0:
            pl.semaphore_wait(barrier, 4)
            dy_load.wait()
        z_moves[2 * i].start()
        z_moves[2 * i + 1].start()
        loads[2].wait()
        dz = dot_nt(dy_s[...], wd_s[cols, :])
        dg_s[:, cols] = (dz * u * slope).astype(BF16)
        du_s[:, cols] = (dz * act).astype(BF16)
        down_of(own_s, z_s, i)
        if i > 0:
            far_of(i - 1)
    far_of(len(tiles) - 1)

    size = rows // 2
    second = [
        Copy(ra_s.at[at_of(1 - xb, rows)], second_r[0], over_x),
        Copy(rb_s.at[at_of(1 - yb, rows)], second_r[1], over_y),
    ]
    on_core = [Copy(cores_s[i], accs[i].at[core], sibling) for i in range(2)]
    acc_stores = [Fetch(accs[i], (da_o, db_o)[i]) for i in range(2)]

    def add_first():
        for made in a_far:
            made.wait_recv()

        @pl.when(yb == core)
        def _():
            ra_s[...] = (ra_s[...].astype(F32) + own_s[:, first_cols].astype(F32)).astype(BF16)

        @pl.when(yb != core)
        def _():
            ra_s[...] = (ra_s[...].astype(F32) + far_s[:, first_cols].astype(F32)).astype(BF16)

        second[0].start()
        b_own.wait_recv()
        b_far.wait_recv()
        for part, y in ((own_s, core), (far_s, 1 - core)):
            at = at_of(y, rows)
            rb_s[at, :] = (rb_s[at, :].astype(F32) + part[at_of(xb, rows), last_cols].astype(F32)).astype(BF16)
        second[1].start()

    def add_second():
        for i, (whole, bit) in enumerate(((ra_s, xb), (rb_s, yb))):
            second[i].wait_recv()

            def summed(which):
                at = pl.ds(pl.multiple_of(bit * rows + which * size, size), size)
                return (whole[at, :].astype(F32) + second_r[i][at_of(which, size), :].astype(F32)).astype(BF16)

            cores_s[i][...] = summed(1 - core)
            on_core[i].start()
            accs[i][core] = summed(core)
        for i in range(2):
            on_core[i].wait_recv()
            acc_stores[i].start()

    quarter = dim // 4
    third = mine // 3
    h_load.wait()

    @pl.loop(0, 4)
    def _(i):
        at = at_of(i, quarter)
        dn2 = dot_nt(dg_s[...], wg_s[at, :]) + dot_nt(du_s[...], wu_s[at, :])
        dn2_s[:, at] = dn2[0:mine, :]
        give_s[:, at] = dn2[mine:both, :].astype(BF16)

    dn2_move = Copy(give_s, come_r, sibling)
    dn2_move.start()
    wo_s = wg_s.at[:, pl.ds(0, dim)]
    o_s = wu_s.at[pl.ds(0, both), pl.ds(0, dim)]
    wo_load, o_load = Fetch(wo_ref, wo_s), Fetch(o_ref, o_s)
    wo_load.start()
    o_load.start()

    dn2_move.wait_recv()
    for i in range(3):
        at = pl.ds(i * third, third)
        dn2 = (dn2_s[at, :] + come_r[at, :].astype(F32)) * gain_ref[...]
        h = h_s[at, :]
        scale = lax.rsqrt(jnp.mean(h * h, axis=1, keepdims=True) + EPS)
        dh = dy_s[at, :].astype(F32) + scale * dn2 - h * (scale * scale * scale * jnp.mean(h * dn2, axis=1, keepdims=True))
        dn2_s[at, :] = dh
        da_s[at, :] = dh.astype(BF16)
    dh_store = Fetch(dn2_s, dh_o)
    dh_store.start()
    da_move = Copy(da_s.at[:, at_of(1 - core, half)], dap_s.at[end], sibling)
    da_move.start()
    dap_s[0:mine, :] = da_s[:, at_of(core, half)]
    wo_load.wait()
    do_s = come_r
    for i in range(3):
        at = pl.ds(i * third, third)
        do_s[at, :] = dot_nt(da_s[at, :], wo_s[...]).astype(BF16)
    do_core = Copy(do_s.at[:, at_of(1 - core, half)], dcr_s, sibling)
    do_core.start()
    do_z = []
    for p in range(2):
        do_z.append(Copy(do_s.at[:, at_of((2 * core + 1 - low) * 2 + p, 128)], dorow_s.at[p, pl.ds(mine, mine)], over_z))
    for made in do_z:
        made.start()

    add_first()


    @pl.loop(0, 4)
    def _(i):
        at = at_of(i, quarter)
        f = dot_nn(z_s[...], wd_s[:, at])
        f_s[:, at] = f[0:mine, :].astype(BF16)
        lo_s[:, at] = f[mine:both, :].astype(BF16)

    f_move = Copy(lo_s, fr_s, sibling)
    f_move.start()

    n2t_s[...] = n2_s[...].T
    stores = []

    def unit_rows(to, right, turn, b, place):
        slot = turn % 2
        if turn >= 2:
            stores[turn - 2].wait()
        stage_s[slot] = dot_nn(n2t_s[b * quarter : (b + 1) * quarter, :], right[...]).astype(BF16)
        stores.append(Fetch(stage_s.at[slot], to.at[pl.ds(place * quarter, quarter)]))
        stores[-1].start()

    unit_rows(gate_o, dg_s, 0, 0, 0)
    do_core.wait_recv()
    for p in range(2):
        do_z.append(Copy(dcr_s.at[:, at_of(2 * (1 - low) + p, 128)], dorow_s.at[p, pl.ds(3 * mine, mine)], over_z))
        do_z[-1].start()
    for p in range(2):
        dorow_s[p, 0:mine, :] = do_s[:, at_of((2 * core + low) * 2 + p, 128)]
        dorow_s[p, 2 * mine : 3 * mine, :] = dcr_s[:, at_of(2 * low + p, 128)]
    for b in range(1, 4):
        unit_rows(gate_o, dg_s, b, b, b)
    for b in range(4):
        unit_rows(up_o, du_s, 4 + b, b, 2 * (b % 2) + b // 2)

    o_load.wait()
    da_move.wait_recv()
    da_move.wait_send()
    for xx in range(2):
        for yy in range(2):
            for p in range(2):
                to = pl.ds(((2 * xx + yy) * 2 + p) * 128, 128)
                m = 4 * p + 2 * yy + xx
                out_s[to, :] = dot_tn(o_s[:, m * 128 : (m + 1) * 128], dap_s[...]).astype(BF16)
    out_store = Fetch(out_s, out_o)
    out_store.start()
    f_move.wait_recv()
    f_move.wait_send()
    for i in range(3):
        at = pl.ds(i * third, third)
        lo_s[at, :] = (h_s[at, :] + f_s[at, :].astype(F32) + fr_s[at, :].astype(F32)).astype(BF16)
    lo_store = Fetch(lo_s, lo_o)
    lo_store.start()
    for made in do_z:
        made.wait_recv()
    do_store = Fetch(dorow_s, do_o)
    do_store.start()

    add_second()
    for made in z_moves + a_far + [do_core, dn2_move, b_own, b_far] + second + on_core + do_z:
        made.wait_send()
    for store in stores[-2:] + [dh_store, out_store, do_store] + acc_stores:
        store.wait()
    lo_store.wait()


def middle(gain, n2_both, dy_both, h, o_both, gate_weight, up_weight, down_weight, out_weight):
    mine, dim = h.shape
    units = gate_weight.shape[1] // 2
    tiles = -(-units // 256)
    both = 2 * mine
    half, quarter = dim // 2, dim // 4
    vmem = pl.BlockSpec(memory_space=pltpu.VMEM)
    anywhere = pl.BlockSpec(memory_space=pl.ANY)
    outs = [((mine, dim), BF16), ((mine, dim), F32), ((2, 4 * mine, 128), BF16), ((dim, units), BF16), ((dim, units), BF16)]
    outs += [((dim, half), BF16), ((2, units // 4, quarter), BF16), ((2, units // 4, quarter), BF16)]
    scratch = [((both, dim), BF16), ((dim, both), BF16), ((both, dim), BF16), ((mine, dim), F32)]
    scratch += [((dim, units), BF16)] * 2 + [((units, dim), BF16)] + [((both, units), BF16)] * 4
    scratch += [((mine, dim), F32)] + [((mine, dim), BF16)] * 3 + [((both, half), BF16), ((mine, half), BF16)]
    scratch += [((2, 4 * mine, 128), BF16)] + [((units, half), BF16)] * 2 + [((2, quarter, units), BF16), ((dim, half), BF16)]
    scratch += [((units, quarter), BF16)] * 2 + [((mine, dim), BF16)]
    scratch += [((mine, dim), BF16)] * 2
    scratch += [((units // 2, quarter), BF16)] * 2 + [((units // 4, quarter), BF16)] * 2 + [((2, units // 4, quarter), BF16)] * 2
    remote, local = 3 * tiles + 2 + 1 + 3 + 1 + 1 + 4 + 1 + 4, 3 + 3 * tiles + 2 + 1 + 8 + 5
    semaphores = [pltpu.SemaphoreType.DMA((count,)) for count in (remote, remote, local)]
    return pl.pallas_call(
        middle_kernel,
        in_specs=[vmem] + [anywhere] * 8,
        out_specs=[anywhere] * 8,
        out_shape=[jax.ShapeDtypeStruct(*v) for v in outs],
        scratch_shapes=[pltpu.VMEM(*v) for v in scratch] + semaphores,
        compiler_params=pltpu.CompilerParams(collective_id=2, has_side_effects=True, vmem_limit_bytes=VMEM_BYTES),
        cost_estimate=pl.CostEstimate(flops=18 * both * dim * units, bytes_accessed=40 << 20, transcendentals=both * units),
        name="middle",
    )(gain, n2_both, dy_both, h, o_both, gate_weight, up_weight, down_weight, out_weight)


ORDER = ((('start', 1), ('start', 0), ('s2', 1), ('lo', 0), ('s2', 0), ('start', 2), ('start', 3)),
 ((), ((), (), (('s0', 2), ('s3', 1), ('s0', 3), ('start', 4), ('start', 5)), (), ()), ()),
 ((('s1', 3),),
  ((('s2', 3),),
   (('s1', 2), ('s0', 5), ('s3', 0)),
   (('s2', 2), ('s4', 1), ('s0', 4)),
   (),
   (('s1', 5), ('start', 6), ('s3', 2), ('s4', 0), ('s2', 5), ('start', 7))),
  (('s1', 4),
   ('h0', 1),
   ('s4', 2),
   ('s2', 4),
   ('s3', 3),
   ('core', 1),
   ('start', 8),
   ('z', 0),
   ('s3', 5),
   ('s0', 7),
   ('core', 0),
   ('s3', 4),
   ('s5', 1),
   ('own', 0),
   ('s4', 3),
   ('home', 0),
   ('s1', 7),
   ('h1', 1),
   ('s4', 5),
   ('s0', 8),
   ('s2', 7),
   ('h0', 0),
   ('s1', 8),
   ('s0', 6),
   ('h2', 1),
   ('s3', 7),
   ('s2', 8),
   ('s5', 5),
   ('s4', 4),
   ('s5', 3),
   ('h3', 1),
   ('s4', 7),
   ('s1', 6),
   ('s2', 6),
   ('s5', 7),
   ('s5', 4),
   ('h1', 0),
   ('s5', 2),
   ('s3', 8),
   ('h4', 1),
   ('s3', 6),
   ('s4', 8),
   ('h2', 0),
   ('h3', 0),
   ('s4', 6),
   ('home', 1),
   ('home', 2),
   ('s5', 0),
   ('h4', 0),
   ('h5', 0),
   ('h5', 1),
   ('s5', 8),
   ('s5', 6))))


def closing_kernel(mask_k_ref, gain_one_ref, *refs):
    refs = list(refs)

    def take(n):
        taken, refs[:n] = refs[:n], []
        return taken

    fetched = take(FETCHED)
    wq_ref, wk_ref, wv_ref, x_ref, lo_ref = take(5)
    da_ref, db_ref, gate_ref, up_ref, out_ref = take(5)
    (gt_o,) = take(1)
    finals = take(ITEMS)
    heads_o, lo_o = take(2)
    fetched_s = take(FETCHED)
    dorow_s, qa0_s, qa1_s, k_s, v_s, o0_s, o1_s, n1_s, dh_s = fetched_s
    firsts_r, seconds_s, seconds_r, cores_s = [take(ITEMS - 2) for _ in range(4)]
    accs, lines = take(ITEMS), take(ITEMS)
    doa_s, dq_s, dqkv_s, hs_s, h1_r, h2_s, h2_r, hk_s, hc_s, hh_s, hh_r = take(11)
    w_s, x_s, dn_s = take(3)
    cs_s, cr_r, zr_r, send_sem, recv_sem, local_sem = take(6)

    d = lax.axis_index("dp")
    s = lax.axis_index("seq")
    core = d % 2
    xb = (d // 2) % 2
    yb = (d // 4) % 2
    low = s % 2
    high = s // 2
    sibling = (d + 1 - 2 * core, s)
    over_x = (d + 2 - 4 * xb, s)
    over_y = (d + 4 - 8 * yb, s)
    over_z = (d, s + 1 - 2 * low)
    over_high = (d, s + 2 - 4 * high)
    swapped = (d + 1 - 2 * core, s + 2 - 4 * high)
    third = (d, 3 - s)
    inner = (s == 1) | (s == 2)
    outer = (s == 0) | (s == 3)
    moved = core != high

    barrier = pltpu.get_barrier_semaphore()
    for other in (sibling, over_x, over_y, over_z, over_high, swapped, third):
        pl.semaphore_signal(barrier, inc=1, device_id=other, device_id_type=MESH)
    pl.semaphore_wait(barrier, 7)

    counts = {"remote": 0, "local": 0}

    class Copy:
        def __init__(self, src, dst, target):
            self.parts = (src, dst, target, counts["remote"])
            counts["remote"] += 1

        def made(self):
            src, dst, target, i = self.parts
            return pltpu.make_async_remote_copy(
                src_ref=src, dst_ref=dst, send_sem=send_sem.at[i], recv_sem=recv_sem.at[i], device_id=target, device_id_type=MESH
            )

        def start(self):
            self.made().start()

        def wait_recv(self):
            self.made().wait_recv()

        def wait_send(self):
            self.made().wait_send()

    copy = Copy

    class Fetch:
        def __init__(self, src, dst):
            self.parts = (src, dst, counts["local"])
            counts["local"] += 1

        def made(self):
            src, dst, i = self.parts
            return pltpu.make_async_copy(src, dst, local_sem.at[i])

        def start(self):
            self.made().start()

        def wait(self):
            self.made().wait()

    def rows_at(start, size):
        return pl.ds(pl.multiple_of(start * size, size), size)

    def lanes_at(start, size):
        return pl.ds(pl.multiple_of(start * size, size), size)

    class Item:
        pass

    items = []
    along_x, along_y = (over_x, xb), (over_y, yb)
    windows, first_col = [], 0
    for acc in accs[2 : ITEMS - 1 : 2]:
        windows.append(pl.ds(first_col, acc.shape[2]))
        first_col += acc.shape[2]
    plans = [(gate_ref, cols, along_y, along_x) if turn == 0 else (up_ref, cols, along_x, along_y) for cols in windows for turn in (0, 1)]
    plans = [(da_ref, None, None, None), (db_ref, None, None, None)] + plans
    plans.append((out_ref, pl.ds(0, accs[-1].shape[2]), along_x, along_y))
    for i, (whole, cols, first, second) in enumerate(plans):
        it = Item()
        it.a, it.z, it.o = accs[i], lines[i], finals[i]
        it.late = first is not None
        if it.late:
            it.r1, it.t, it.r, it.c = [group[i - 2] for group in (firsts_r, seconds_s, seconds_r, cores_s)]
            n = it.n = it.c.shape[0]
            target, it.bit = second
            kept = first[1] * (4 * n)
            base = kept + it.bit * (2 * n)
            it.first = copy(whole.at[rows_at(1 - first[1], 4 * n), cols], it.r1, first[0])
            it.far = Fetch(whole.at[pl.ds(pl.multiple_of(kept + (1 - it.bit) * (2 * n), 2 * n), 2 * n), cols], it.t)
            it.chip = copy(it.t, it.r, target)
            it.parts = [
                Fetch(whole.at[pl.ds(pl.multiple_of(base + (1 - core) * n, n), n), cols], it.c),
                Fetch(whole.at[pl.ds(pl.multiple_of(base + core * n, n), n), cols], it.a.at[core]),
            ]
            it.core = copy(it.c, it.a.at[core], sibling)
        else:
            it.parts = [Fetch(whole, it.a)]
        it.in1 = copy(it.a, it.z, (d, jnp.where(s == 0, 1, 2)))
        it.in2 = copy(it.a, it.o, third)
        it.out = copy(it.o, it.o, (d, jnp.where(s == 1, 0, 3)))
        items.append(it)

    def start(it):
        if it.late:
            it.first.start()
            it.far.start()
        for part in it.parts:
            part.start()

    def step0(it):
        at = rows_at(1 - it.bit, 2 * it.n)
        it.far.wait()
        it.first.wait_recv()
        it.t[...] = (it.t[...].astype(F32) + it.r1[at, :].astype(F32)).astype(BF16)
        it.chip.start()

    def step1(it):
        n = it.n
        for part in it.parts:
            part.wait()
        it.chip.wait_recv()

        def come(which):
            at = pl.ds(pl.multiple_of(it.bit * (2 * n) + which * n, n), n)
            return it.r1[at, :].astype(F32) + it.r[rows_at(which, n), :].astype(F32)

        it.c[...] = (it.c[...].astype(F32) + come(1 - core)).astype(BF16)
        it.core.start()
        it.a[core] = (it.a[core].astype(F32) + come(core)).astype(BF16)

    def step2(it):
        if it.late:
            it.core.wait_recv()
        else:
            it.parts[0].wait()

        @pl.when(outer)
        def _():
            it.in1.start()

    def step3(it):
        @pl.when(inner)
        def _():
            it.in1.wait_recv()
            it.a[...] = (it.a[...].astype(F32) + it.z[...].astype(F32)).astype(BF16)
            it.in2.start()

    def step4(it):
        @pl.when(inner)
        def _():
            it.in2.wait_recv()
            it.o[...] = (it.a[...].astype(F32) + it.o[...].astype(F32)).astype(BF16)
            it.out.start()

    def step5(it):
        @pl.when(outer)
        def _():
            it.out.wait_recv()

    def finish(it):
        if it.late:
            it.first.wait_send()
            it.chip.wait_send()
            it.core.wait_send()

        @pl.when(outer)
        def _():
            it.in1.wait_send()

        @pl.when(inner)
        def _():
            it.in2.wait_send()
            it.out.wait_send()


    mine, dim = x_s.shape
    loads = [Fetch(src, dst) for src, dst in zip(fetched, fetched_s)]
    x_load = Fetch(x_ref, x_s)
    w_loads = []
    for p in range(2):
        for t, w in enumerate((wq_ref, wk_ref, wv_ref)):
            w_loads.append(Fetch(w.at[:, lanes_at((2 * core + low) * 2 + p, 128)], w_s.at[:, pl.ds((3 * p + t) * 128, 128)]))
    for load in loads[:7]:
        load.start()
    for load in loads[7:] + [x_load] + w_loads:
        load.start()

    block = hk_s.shape[1]
    half = block // 2
    firsts = ((over_x, over_y), (over_y, over_x))
    heads = []
    for p in range(2):
        h = Item()
        h.p1 = [copy(hs_s.at[p, i], h1_r.at[p, i], firsts[p][0]) for i in range(2)]
        h.p2 = copy(h2_s.at[p], h2_r.at[p], firsts[p][1])
        h.core = copy(hk_s.at[p, rows_at(1 - core, half)], hc_s.at[p, core], sibling)
        h.high = copy(hh_s.at[p], hh_r.at[p], over_high)
        h.z = copy(heads_o.at[low, p], heads_o.at[low, p], over_z)
        heads.append(h)

    def product(p, yy, xx):
        return dot_tn(n1_s[:, lanes_at(2 * yy + xx, block)], dqkv_s[p])

    def heads0(p):
        h = heads[p]
        for turn in range(2):
            if p == 0:
                i = (1 - yb) if turn == 0 else yb
                hs_s[p, turn] = product(p, i, 1 - xb).astype(BF16)
            else:
                i = (1 - xb) if turn == 0 else xb
                hs_s[p, turn] = product(p, 1 - yb, i).astype(BF16)
            h.p1[turn].start()

    def heads1(p):
        h = heads[p]
        part = product(p, 1 - yb, xb) if p == 0 else product(p, yb, 1 - xb)
        h.p1[0].wait_recv()
        h2_s[p] = (part + h1_r[p, 0].astype(F32)).astype(BF16)
        h.p2.start()

    def heads2(p):
        h = heads[p]
        part = product(p, yb, xb)
        h.p1[1].wait_recv()
        part = part + h1_r[p, 1].astype(F32)
        h.p2.wait_recv()
        hk_s[p] = (part + h2_r[p].astype(F32)).astype(BF16)
        h.core.start()
        hc_s[p, core] = hk_s[p, rows_at(core, half), :]

    def heads3(p):
        h = heads[p]
        h.core.wait_recv()
        hh_s[p] = hc_s[p]
        h.high.start()

    def heads4(p):
        h = heads[p]
        h.high.wait_recv()
        heads_o[low, p] = (hh_s[p].astype(F32) + hh_r[p].astype(F32)).astype(BF16)
        h.z.start()

    def heads5(p):
        heads[p].z.wait_recv()

    def finish_heads(p):
        h = heads[p]
        for made in h.p1 + [h.p2, h.core, h.high, h.z]:
            made.wait_send()

    tokens = k_s.shape[0]
    rows = 256
    steps = tokens // rows
    lane = lax.broadcasted_iota(jnp.int32, (tokens, 128), 1)
    klane = lax.broadcasted_iota(jnp.int32, (rows, 128), 1)

    def prepare(p):
        do = dorow_s[p].astype(F32)
        prod = do * (o0_s, o1_s)[p][...]
        for h in range(2):
            mine = (lane < HEAD_DIM) if h == 0 else (lane >= HEAD_DIM)
            other = lane - (HEAD_DIM if h == 0 else 0)
            delta = jnp.sum(jnp.where(mine, prod, 0.0), axis=1, keepdims=True)
            a, b, c = three_parts(delta)
            aug = jnp.where(other == 5, -a, jnp.where(other == 6, -b, jnp.where(other == 7, -c, 0.0)))
            doa_s[h] = jnp.where(mine, do, aug).astype(BF16)
        dq_s[...] = jnp.zeros_like(dq_s)

    def attend(p, j):
        qa_s = (qa0_s, qa1_s)[p]
        cols = slice(128 * p, 128 * p + 128)
        here = pl.ds(pl.multiple_of(j * rows, rows), rows)
        k = k_s[here, cols]
        v = v_s[here, cols]
        kf = k.astype(F32)
        vf = v.astype(F32)
        mk = mask_k_ref[here, :]
        dead = jnp.where(mk[:, 4:5].astype(F32) < 0, 1.0, 0.0)
        dks, dvs = [], []
        for h in range(2):
            kmine = (klane < HEAD_DIM) if h == 0 else (klane >= HEAD_DIM)
            other = klane - (HEAD_DIM if h == 0 else 0)
            one = (other >= 5) & (other < 8)
            ka = jnp.where(kmine, k, mk)
            va = jnp.where(kmine, v, jnp.where(one, jnp.ones_like(v), jnp.zeros_like(v)))
            pr = jnp.exp(dot_nt(ka, qa_s[h]))
            ds = (pr * dot_nt(va, doa_s[h])).astype(BF16)
            dk = dot_nn(ds, qa_s[h])
            dv = dot_nn(pr.astype(BF16), doa_s[h])
            dq_s[h] += dot_tn(ds, ka)
            qd = qa_s[h, here, :].astype(F32)
            dod = doa_s[h, here, :].astype(F32)
            own = jnp.sum(jnp.where(kmine | one, qd * jnp.where(kmine, kf, 1.0), 0.0), axis=1, keepdims=True)
            own_p = jnp.where(dead > 0, jnp.exp(jnp.where(dead > 0, own, 0.0)), 0.0)
            own_d = jnp.sum(jnp.where(kmine | one, dod * jnp.where(kmine, vf, 1.0), 0.0), axis=1, keepdims=True)
            own_ds = own_p * own_d
            dks.append(dk + own_ds * qd)
            dvs.append(dv + own_p * dod)
            dq_s[h, here, :] += jnp.where(kmine, own_ds * kf, 0.0)
        dqkv_s[p, here, 128:256] = jnp.where(klane < HEAD_DIM, dks[0], dks[1]).astype(BF16)
        dqkv_s[p, here, 256:384] = jnp.where(klane < HEAD_DIM, dvs[0], dvs[1]).astype(BF16)

    cut = mine // 3
    width = dqkv_s.shape[2]

    def dn1_of(i):
        at = pl.ds(i * mine, mine)
        return dot_nt(dqkv_s[0, at, :], w_s[:, 0:width]) + dot_nt(dqkv_s[1, at, :], w_s[:, width : 2 * width])

    to_core = [copy(cs_s.at[i], cr_r.at[i], sibling) for i in range(2)]
    to_z = [copy(cs_s.at[1, pl.ds(i * cut, cut)], zr_r.at[pl.ds(i * cut, cut)], over_z) for i in range(3)]
    to_home = [copy(cs_s.at[0, pl.ds(i * cut, cut)], gt_o.at[pl.ds(i * cut, cut)], swapped) for i in range(3)]

    late_loads = w_loads + [x_load, loads[8]]

    def give_core(i):
        while late_loads:
            late_loads.pop().wait()
        cs_s[i] = dn1_of(2 + i).astype(BF16)
        to_core[i].start()

    def give_z(_):
        dn = dn1_of(1)
        to_core[1].wait_recv()
        to_core[1].wait_send()
        cs_s[1] = (dn + cr_r[1].astype(F32)).astype(BF16)
        for made in to_z:
            made.start()

    def keep_own(_):
        dn_s[...] = dn1_of(0)
        to_core[0].wait_recv()
        to_core[0].wait_send()

    def give_home(i):
        at = pl.ds(i * cut, cut)
        to_z[i].wait_recv()
        dn = dn_s[at, :] + cr_r[0, at, :].astype(F32) + zr_r[at, :].astype(F32)
        x = x_s[at, :].astype(F32)
        scale = lax.rsqrt(jnp.mean(x * x, axis=1, keepdims=True) + EPS)
        dn = dn * gain_one_ref[...]
        grad = dh_s[at, :] + scale * dn - x * (scale * scale * scale * jnp.mean(x * dn, axis=1, keepdims=True))
        cs_s[0, at, :] = grad.astype(BF16)

        @pl.when(moved)
        def _():
            to_home[i].start()

        @pl.when(jnp.logical_not(moved))
        def _():
            gt_o[at, :] = cs_s[0, at, :]

    tasks = {
        "start": lambda i: start(items[i]),
        "s0": lambda i: step0(items[i]),
        "s1": lambda i: step1(items[i]),
        "s2": lambda i: step2(items[i]),
        "s3": lambda i: step3(items[i]),
        "s4": lambda i: step4(items[i]),
        "s5": lambda i: step5(items[i]),
        "h0": heads0,
        "h1": heads1,
        "h2": heads2,
        "h3": heads3,
        "h4": heads4,
        "h5": heads5,
        "core": give_core,
        "z": give_z,
        "own": keep_own,
        "home": give_home,
    }

    lo_move, lo_local = copy(lo_ref, lo_o, swapped), Fetch(lo_ref, lo_o)

    def give_layer(_):
        pl.when(moved)(lo_move.start)
        pl.when(jnp.logical_not(moved))(lo_local.start)

    tasks["lo"] = give_layer

    def run(todo):
        for name, i in todo:
            tasks[name](i)

    run(ORDER[0])
    for load in loads[:7]:
        load.wait()
    for p in range(2):
        before, slots, later = ORDER[1 + p]
        run(before)
        prepare(p)

        @pl.loop(0, steps)
        def _(j, p=p, slots=slots):
            attend(p, j)
            for i, todo in enumerate(slots):
                if todo:

                    @pl.when(j == i)
                    def _(todo=todo):
                        run(todo)

        dqkv_s[p, :, 0:128] = jnp.where(lane < HEAD_DIM, dq_s[0], dq_s[1]).astype(BF16)
        if p == 0:
            loads[7].wait()
        run(later)

    for it in items:
        finish(it)
    for p in range(2):
        finish_heads(p)
    for made in to_z:
        made.wait_send()

    @pl.when(moved)
    def _():
        for made in to_home + [lo_move]:
            made.wait_recv()
            made.wait_send()

    @pl.when(jnp.logical_not(moved))
    def _():
        lo_local.wait()


def closing(mask_key, gain, fetched, weights, x, layer_out, grads):
    tokens = mask_key.shape[0]
    mine, dim = x.shape
    vmem = pl.BlockSpec(memory_space=pltpu.VMEM)
    anywhere = pl.BlockSpec(memory_space=pl.ANY)
    down, _, gate, _, outp = [w.shape for w in grads]
    third = 128 * (gate[1] // 128 // 3)
    widths = [third] + [128 * ((gate[1] - third) // 256)]
    widths.append(gate[1] - sum(widths))
    shards = [down[1:]] * 2 + [(gate[0] // 8, width) for width in widths for _ in range(2)]
    shards.append((outp[0] // 8, outp[1]))
    lates = shards[2:]
    block = dim // 4
    three = 3 * 128
    scratch = [pltpu.VMEM(v.shape, v.dtype) for v in fetched]
    scratch += [pltpu.VMEM((4 * rows, cols), BF16) for rows, cols in lates]
    scratch += [pltpu.VMEM((2 * rows, cols), BF16) for rows, cols in lates] * 2
    scratch += [pltpu.VMEM(w, BF16) for w in lates]
    scratch += [pltpu.VMEM((2,) + w, BF16) for w in shards] * 2
    scratch += [
        pltpu.VMEM((2, tokens, 128), BF16),
        pltpu.VMEM((2, tokens, 128), F32),
        pltpu.VMEM((2, tokens, three), BF16),
        pltpu.VMEM((2, 2, block, three), BF16),
        pltpu.VMEM((2, 2, block, three), BF16),
        pltpu.VMEM((2, block, three), BF16),
        pltpu.VMEM((2, block, three), BF16),
        pltpu.VMEM((2, block, three), BF16),
        pltpu.VMEM((2, 2, block // 2, three), BF16),
        pltpu.VMEM((2, 2, block // 2, three), BF16),
        pltpu.VMEM((2, 2, block // 2, three), BF16),
        pltpu.VMEM((dim, 2 * three), BF16),
        pltpu.VMEM((mine, dim), BF16),
        pltpu.VMEM((mine, dim), F32),
        pltpu.VMEM((2, mine, dim), BF16),
        pltpu.VMEM((2, mine, dim), BF16),
        pltpu.VMEM((mine, dim), BF16),
    ]
    remote = 6 * ITEMS - 6 + 2 * 6 + 2 + 3 + 3 + 1
    local = FETCHED + 7 + 3 * ITEMS - 4 + 1
    semaphores = [pltpu.SemaphoreType.DMA((count,)) for count in (remote, remote, local)]
    return pl.pallas_call(
        closing_kernel,
        in_specs=[vmem] * 2 + [anywhere] * (FETCHED + 5 + 5),
        out_specs=[vmem] * (2 + ITEMS) + [anywhere],
        out_shape=[jax.ShapeDtypeStruct((mine, dim), BF16)]
        + [jax.ShapeDtypeStruct((2,) + w, BF16) for w in shards]
        + [jax.ShapeDtypeStruct((2, 2, 2, block // 2, three), BF16), jax.ShapeDtypeStruct((mine, dim), BF16)],
        scratch_shapes=scratch + semaphores,
        compiler_params=pltpu.CompilerParams(collective_id=0, has_side_effects=True, vmem_limit_bytes=VMEM_BYTES),
        cost_estimate=pl.CostEstimate(
            flops=40 * tokens * tokens * 256, bytes_accessed=40 << 20, transcendentals=4 * tokens * tokens
        ),
        name="closing",
    )(mask_key, gain, *fetched, *weights, x, layer_out, *grads)


def placing_kernel(count, g1, g2, *refs):
    weights, grads, outs, kept, sems = refs[:5], refs[5 : 9 + count], refs[9 + count : 19 + count], refs[19 + count : -1], refs[-1]
    loads = []
    sources = list(grads)
    for w, to in zip(weights, kept[len(grads) :]):
        n = to.shape[0]
        sources.append(w.at[pl.ds(pl.multiple_of(lax.axis_index("dp") * n, n), n)])
    for i, (src, to) in enumerate(zip(sources, kept)):
        loads.append(pltpu.make_async_copy(src, to, sems.at[i]))
        loads[-1].start()
    for load in loads:
        load.wait()
    gt, da, db, *units, out, heads = kept[: len(grads)]
    wq, wk, wv, wg, wu = kept[len(grads) :]
    gt_o, q_o, k_o, v_o, out_o, gate_o, up_o, down_o, g1_o, g2_o = outs
    gt_o[...] = gt[...].astype(F32)
    cut = da.shape[2]
    for c in range(2):
        first = [c * (gate_o.shape[1] // 2)] * 2
        for i, part in enumerate(units):
            to, size = (gate_o, up_o)[i % 2], part.shape[2]
            to[:, first[i % 2] : first[i % 2] + size] = part[c].astype(F32)
            first[i % 2] += size
        down_o[:, 2 * c * cut : (2 * c + 1) * cut] = da[c].astype(F32)
        down_o[:, (2 * c + 1) * cut : (2 * c + 2) * cut] = db[c].astype(F32)
        out_o[:, 2 * c * cut : (2 * c + 2) * cut] = out[c].astype(F32)
    for m in range(4):
        for p in range(2):
            at = slice((2 * m + p) * 128, (2 * m + p + 1) * 128)
            for t, to in enumerate((q_o, k_o, v_o)):
                to[:, at] = heads[m % 2, p, m // 2, :, t * 128 : (t + 1) * 128].astype(F32)

    def along(pairs, gain):
        total = sum([jnp.sum(grad[...] * w[...].astype(F32), axis=1, keepdims=True) for grad, w in pairs])
        n = total.shape[0]
        return jnp.broadcast_to(total, (n, n)).T[0:1, :] / gain[...]

    g1_o[...] = along(((q_o, wq), (k_o, wk), (v_o, wv)), g1)
    g2_o[...] = along(((gate_o, wg), (up_o, wu)), g2)


def placing(grads, heads, gains, weights):
    gt, da, out = grads[0], grads[1], grads[-1]
    n, dim = out.shape[1], 2 * out.shape[2]
    units = sum([part.shape[2] for part in grads[3:-1]])
    shapes = [gt.shape] + [(n, dim)] * 4 + [(n, units)] * 2 + [(da.shape[1], dim)] + [(1, n)] * 2
    vmem, anywhere = pl.BlockSpec(memory_space=pltpu.VMEM), pl.BlockSpec(memory_space=pl.ANY)
    kept = [v.shape for v in (*grads, heads)] + [(n, w.shape[1]) for w in weights]
    return pl.pallas_call(
        functools.partial(placing_kernel, len(grads) - 3),
        in_specs=[vmem] * 2 + [anywhere] * (6 + len(grads)),
        out_specs=[vmem] * 10,
        out_shape=[jax.ShapeDtypeStruct(v, F32) for v in shapes],
        scratch_shapes=[pltpu.VMEM(v, BF16) for v in kept] + [pltpu.SemaphoreType.DMA((len(kept),))],
        compiler_params=pltpu.CompilerParams(vmem_limit_bytes=VMEM_BYTES),
        cost_estimate=pl.CostEstimate(flops=1 << 22, bytes_accessed=14 << 20, transcendentals=0),
        name="placing",
    )(*gains, *weights, *grads, heads)


def local_fused(
    dps,
    seqs,
    tokens,
    query_weight,
    key_weight,
    value_weight,
    out_weight,
    gate_weight,
    up_weight,
    down_weight,
    attention_gain,
    feedforward_gain,
    pair_lengths,
    live_mask,
    out_grad,
):
    mine, dim = tokens.shape
    projections = (query_weight, key_weight, value_weight)
    n1_row, k, v, qa_0, qa_1, o_0, o_1, mask_key, h, n2_both, o_both, dy_both, x_low = opening(
        tokens, live_mask, pair_lengths, (attention_gain[None, :], feedforward_gain[None, :]),
        (*projections, out_weight), out_grad,
    )

    layer_out, dh, do, gate, up, outp, down_a, down_b = middle(
        feedforward_gain[None, :], n2_both, dy_both, h, o_both, gate_weight, up_weight, down_weight, out_weight
    )

    *grads, heads_grads, layer_out = closing(
        mask_key, attention_gain[None, :], (do, qa_0, qa_1, k, v, o_0, o_1, n1_row, dh), projections, x_low, layer_out,
        (down_a, down_b, gate, up, outp),
    )

    gains = [
        lax.dynamic_slice_in_dim(gain[None, :], lax.axis_index("dp") * (dim // dps), dim // dps, axis=1)
        for gain in (attention_gain, feedforward_gain)
    ]
    *results, gain_one, gain_two = placing(grads, heads_grads, gains, (*projections, gate_weight, up_weight))
    return (layer_out, *results, gain_one[0], gain_two[0])


def solution(mesh):
    both = P(("dp", "seq"), None)
    rows = P("dp", None)
    dps, seqs = mesh.shape["dp"], mesh.shape["seq"]
    local = local_fused if (dps, seqs) == (8, 4) else local_plain
    return jax.shard_map(
        functools.partial(local, dps, seqs),
        mesh=mesh,
        in_specs=(both, P(), P(), P(), P(), P(), P(), P(), P(), P(), rows, P(("dp", "seq")), both),
        out_specs=(both, both, rows, rows, rows, rows, rows, rows, rows, P("dp"), P("dp")),
        check_vma=False,
    )
```

```python
import functools

import jax
import jax.numpy as jnp
from jax import lax
from jax.experimental import pallas as pl
from jax.experimental.pallas import tpu as pltpu
from jax.sharding import PartitionSpec as P

HEADS = 16
HEAD_DIM = 64
EPS = 1e-06
BIG = float(2.0**40)
F32 = jnp.float32
BF16 = jnp.bfloat16
AXES = ("dp", "seq")
MESH = pl.DeviceIdType.MESH
VMEM_BYTES = 62 << 20
ITEMS, FETCHED, OPENED = 9, 9, 13


def dot_nn(a, b):
    return lax.dot_general(a, b, (((1,), (0,)), ((), ())), preferred_element_type=F32)


def dot_nt(a, b):
    return lax.dot_general(a, b, (((1,), (1,)), ((), ())), preferred_element_type=F32)


def dot_tn(a, b):
    return lax.dot_general(a, b, (((0,), (0,)), ((), ())), preferred_element_type=F32)


def three_parts(v):
    high = v.astype(BF16).astype(F32)
    mid = (v - high).astype(BF16).astype(F32)
    low = (v - high - mid).astype(BF16).astype(F32)
    return high, mid, low


def forward_kernel(keep_queries, q_ref, k_ref, v_ref, mq_ref, mk_ref, dead_ref, kd_ref, vd_ref, o_ref, l_ref):
    lane = lax.broadcasted_iota(jnp.int32, q_ref.shape, 1)
    klane = lax.broadcasted_iota(jnp.int32, k_ref.shape, 1)
    q = q_ref[...]
    dead = dead_ref[...]
    qk = q.astype(F32) * kd_ref[...].astype(F32)
    outs, logs = [], []
    for h in range(2):
        mine = (lane < HEAD_DIM) if h == 0 else (lane >= HEAD_DIM)
        kmine = (klane < HEAD_DIM) if h == 0 else (klane >= HEAD_DIM)
        qa = jnp.where(mine, q, mq_ref[...])
        ka = jnp.where(kmine, k_ref[...], mk_ref[...])
        s = dot_nt(qa, ka)
        own = jnp.sum(jnp.where(mine, qk, 0.0), axis=1, keepdims=True)
        own = jnp.where(dead > 0, own, -BIG)
        top = jnp.maximum(jnp.max(s, axis=1, keepdims=True), own)
        p = jnp.exp(s - top).astype(BF16)
        va = jnp.where(kmine, v_ref[...], jnp.ones_like(v_ref[...]))
        r = dot_nn(p, va)
        own_p = jnp.exp(own - top)
        total = (r[:, HEAD_DIM : HEAD_DIM + 1] if h == 0 else r[:, 0:1]) + own_p
        outs.append((r + own_p * vd_ref[...].astype(F32)) * (1.0 / total))
        log = top + jnp.log(total)
        if keep_queries:
            other = lane - (HEAD_DIM if h == 0 else 0)
            a, b, c = three_parts(log)
            aug = mq_ref[...].astype(F32)
            aug = jnp.where(other == 5, -a, jnp.where(other == 6, -b, jnp.where(other == 7, -c, aug)))
            l_ref[h] = jnp.where(mine, q.astype(F32), aug).astype(BF16)
        logs.append(log)
    o_ref[...] = jnp.where(lane < HEAD_DIM, outs[0], outs[1])
    if not keep_queries:
        l_ref[...] = jnp.where(lane < HEAD_DIM, logs[0], logs[1])


def rows_per_step(tokens):
    for rows in (512, 384, 256, 128):
        if tokens % rows == 0 and rows * tokens <= 800000:
            return rows
    return 128


def attention_forward(q, k, v, mq, mk, dead, group=None):
    tokens, width = q.shape
    rows = rows_per_step(tokens)
    first, count = (0, width // 128) if group is None else (group, 1)
    part = pl.BlockSpec((rows, 128), lambda h, i: (i, h + first))
    full = pl.BlockSpec((tokens, 128), lambda h, i: (0, h + first))
    out = pl.BlockSpec((rows, 128), lambda h, i: (i, h))
    keep = group is not None
    log_out, log_shape = out, jax.ShapeDtypeStruct((tokens, 128 * count), F32)
    if keep:
        log_out = pl.BlockSpec((2, rows, 128), lambda h, i: (0, i, 0))
        log_shape = jax.ShapeDtypeStruct((2, tokens, 128), BF16)
    return pl.pallas_call(
        functools.partial(forward_kernel, keep),
        grid=(count, tokens // rows),
        in_specs=[
            part,
            full,
            full,
            pl.BlockSpec((rows, 128), lambda h, i: (i, 0)),
            pl.BlockSpec((tokens, 128), lambda h, i: (0, 0)),
            pl.BlockSpec((rows, 1), lambda h, i: (i, 0)),
            part,
            part,
        ],
        out_specs=[out, log_out],
        out_shape=[jax.ShapeDtypeStruct((tokens, 128 * count), F32), log_shape],
        compiler_params=pltpu.CompilerParams(vmem_limit_bytes=56 << 20),
        cost_estimate=pl.CostEstimate(
            flops=16 * tokens * tokens * 128 * count, bytes_accessed=16 * tokens * width, transcendentals=2 * tokens * tokens * count
        ),
        name="attention_forward",
    )(q, k, v, mq, mk, dead, k, v)


def backward_kernel(
    q_ref, k_ref, v_ref, do_ref, o_ref, l_ref, mq_ref, mk_ref, dead_ref, dq_ref, dk_ref, dv_ref, qa_s, doa_s, dq_s
):
    j = pl.program_id(1)
    tokens = q_ref.shape[0]
    rows = k_ref.shape[0]
    lane = lax.broadcasted_iota(jnp.int32, (tokens, 128), 1)
    klane = lax.broadcasted_iota(jnp.int32, (rows, 128), 1)

    @pl.when(j == 0)
    def _():
        do = do_ref[...].astype(F32)
        prod = do * o_ref[...]
        q = q_ref[...].astype(F32)
        logs = l_ref[...]
        for h in range(2):
            mine = (lane < HEAD_DIM) if h == 0 else (lane >= HEAD_DIM)
            other = lane - (HEAD_DIM if h == 0 else 0)
            delta = jnp.sum(jnp.where(mine, prod, 0.0), axis=1, keepdims=True)
            log = logs[:, 0:1] if h == 0 else logs[:, HEAD_DIM : HEAD_DIM + 1]
            a, b, c = three_parts(log)
            aug = mq_ref[...].astype(F32)
            aug = jnp.where(other == 5, -a, jnp.where(other == 6, -b, jnp.where(other == 7, -c, aug)))
            qa_s[h] = jnp.where(mine, q, aug).astype(BF16)
            a, b, c = three_parts(delta)
            aug = jnp.where(other == 5, -a, jnp.where(other == 6, -b, jnp.where(other == 7, -c, 0.0)))
            doa_s[h] = jnp.where(mine, do, aug).astype(BF16)
        dq_s[...] = jnp.zeros_like(dq_s)

    k = k_ref[...]
    v = v_ref[...]
    here = pl.ds(pl.multiple_of(j * rows, rows), rows)
    kf = k.astype(F32)
    vf = v.astype(F32)
    dead = dead_ref[...]
    dks, dvs = [], []
    for h in range(2):
        kmine = (klane < HEAD_DIM) if h == 0 else (klane >= HEAD_DIM)
        other = klane - (HEAD_DIM if h == 0 else 0)
        one = (other >= 5) & (other < 8)
        ka = jnp.where(kmine, k, mk_ref[...])
        va = jnp.where(kmine, v, jnp.where(one, jnp.ones_like(v), jnp.zeros_like(v)))
        p = jnp.exp(dot_nt(ka, qa_s[h]))
        ds = (p * dot_nt(va, doa_s[h])).astype(BF16)
        dk = dot_nn(ds, qa_s[h])
        dv = dot_nn(p.astype(BF16), doa_s[h])
        dq_s[h] += dot_tn(ds, ka)
        qd = qa_s[h, here, :].astype(F32)
        dod = doa_s[h, here, :].astype(F32)
        own = jnp.sum(jnp.where(kmine | one, qd * jnp.where(kmine, kf, 1.0), 0.0), axis=1, keepdims=True)
        own_p = jnp.where(dead > 0, jnp.exp(jnp.where(dead > 0, own, 0.0)), 0.0)
        own_d = jnp.sum(jnp.where(kmine | one, dod * jnp.where(kmine, vf, 1.0), 0.0), axis=1, keepdims=True)
        own_ds = own_p * own_d
        dks.append(dk + own_ds * qd)
        dvs.append(dv + own_p * dod)
        dq_s[h, here, :] += jnp.where(kmine, own_ds * kf, 0.0)
    dk_ref[...] = jnp.where(klane < HEAD_DIM, dks[0], dks[1]).astype(BF16)
    dv_ref[...] = jnp.where(klane < HEAD_DIM, dvs[0], dvs[1]).astype(BF16)

    @pl.when(j == pl.num_programs(1) - 1)
    def _():
        dq_ref[...] = jnp.where(lane < HEAD_DIM, dq_s[0], dq_s[1]).astype(BF16)


def attention_backward(q, k, v, do, o, logs, mq, mk, dead):
    tokens, width = q.shape
    rows = rows_per_step(tokens)
    part = pl.BlockSpec((rows, 128), lambda h, i: (i, h))
    full = pl.BlockSpec((tokens, 128), lambda h, i: (0, h))
    return pl.pallas_call(
        backward_kernel,
        grid=(width // 128, tokens // rows),
        in_specs=[
            full,
            part,
            part,
            full,
            full,
            full,
            pl.BlockSpec((tokens, 128), lambda h, i: (0, 0)),
            pl.BlockSpec((rows, 128), lambda h, i: (i, 0)),
            pl.BlockSpec((rows, 1), lambda h, i: (i, 0)),
        ],
        out_specs=[full, part, part],
        out_shape=[jax.ShapeDtypeStruct((tokens, width), BF16)] * 3,
        scratch_shapes=[
            pltpu.VMEM((2, tokens, 128), BF16),
            pltpu.VMEM((2, tokens, 128), BF16),
            pltpu.VMEM((2, tokens, 128), F32),
        ],
        compiler_params=pltpu.CompilerParams(vmem_limit_bytes=56 << 20),
        cost_estimate=pl.CostEstimate(
            flops=40 * tokens * tokens * width, bytes_accessed=24 * tokens * width, transcendentals=tokens * tokens * width // HEAD_DIM
        ),
        name="attention_backward",
    )(q, k, v, do, o, logs, mq, mk, dead)


def mask_terms(pair, live):
    lane = jnp.arange(128, dtype=jnp.int32)[None, :] % HEAD_DIM
    same = lane == pair[:, None]
    query = jnp.where(lane < 4, same, lane == 4).astype(BF16)
    key = jnp.where(
        lane < 4,
        jnp.where(same, 0.0, -BIG),
        jnp.where(lane == 4, jnp.where(live[:, None], 0.0, -BIG), ((lane >= 5) & (lane < 8)).astype(F32)),
    ).astype(BF16)
    return query, key, 1.0 - live.astype(F32)[:, None]


def gelu_parts(g):
    c = 0.7978845608028654
    t = jnp.tanh(c * (g + 0.044715 * g * g * g))
    act = 0.5 * g * (1.0 + t)
    slope = 0.5 * (1.0 + t) + 0.5 * g * (1.0 - t * t) * c * (1.0 + 3 * 0.044715 * g * g)
    return act, slope


def local_plain(
    dps,
    seqs,
    tokens,
    query_weight,
    key_weight,
    value_weight,
    out_weight,
    gate_weight,
    up_weight,
    down_weight,
    attention_gain,
    feedforward_gain,
    pair_lengths,
    live_mask,
    out_grad,
):
    mine, dim = tokens.shape
    units = gate_weight.shape[1]
    half = seqs // 2
    width = dim // seqs
    chips = dps // 2
    d = lax.axis_index("dp")
    s = lax.axis_index("seq")
    core = d % 2
    high = (s >= half).astype(jnp.int32)
    low = s % half
    member = core * half + low
    moved = core != high

    def move(value, target):
        pairs = []
        for i in range(dps * seqs):
            to = target(i // seqs, i % seqs)
            if to is not None:
                pairs.append((i, to[0] * seqs + to[1]))
        return lax.ppermute(value, AXES, pairs)

    def trade(value):
        def target(dd, ss):
            return (dd ^ 1, (ss + half) % seqs) if dd % 2 != ss // half else None

        return move(value, target)

    def with_core(value):
        return move(value, lambda dd, ss: (dd ^ 1, ss))

    def with_chip(value, bit):
        return move(value, lambda dd, ss: (dd ^ bit, ss))

    def with_seq(value, bit):
        return move(value, lambda dd, ss: (dd, ss ^ bit))

    def with_member(value, bit):
        return with_core(value) if bit == half else with_seq(value, bit)

    bits = []
    while (1 << len(bits)) < seqs:
        bits.append(1 << len(bits))
    chip_bits = []
    while (2 << len(chip_bits)) < dps:
        chip_bits.append(2 << len(chip_bits))

    def gather_row(value):
        value = value[None]
        for bit in bits:
            value = jnp.concatenate([value, with_member(value, bit)], axis=0)
        return value

    def to_tokens(value):
        value = value.reshape(seqs, mine, width)
        for bit in bits:
            value = value.reshape(value.shape[0] // 2, 2, mine, value.shape[2])
            keep, come = value[:, 0], with_member(value[:, 1], bit)
            upper = (member & bit) != 0
            value = jnp.concatenate([jnp.where(upper, come, keep), jnp.where(upper, keep, come)], axis=2)
        return value[0]

    def to_heads(value):
        value = value[None]
        for bit in reversed(bits):
            first, second = jnp.split(value, 2, axis=2)
            upper = (member & bit) != 0
            come = with_member(jnp.where(upper, first, second), bit)
            value = jnp.stack([jnp.where(upper, second, first), come], axis=1)
            value = value.reshape(-1, mine, value.shape[3])
        return value.reshape(seqs * mine, width)

    def row_sum(value):
        value = value.reshape(seqs, mine, dim)
        for bit in reversed(bits):
            keep, give = value[: value.shape[0] // 2], value[value.shape[0] // 2 :]
            value = keep + with_member(give.astype(BF16), bit).astype(F32)
        return value[0]

    def over_chips(value, order):
        cols = value.shape[1]
        rows = value.shape[0] // chips
        value = value.reshape((2,) * len(chip_bits) + (rows, cols))
        left = list(reversed(chip_bits))
        for bit in order:
            axis = left.index(bit)
            left.pop(axis)
            upper = ((d & bit) != 0).astype(jnp.int32)
            give = lax.dynamic_index_in_dim(value, 1 - upper, axis, keepdims=False)
            keep = lax.dynamic_index_in_dim(value, upper, axis, keepdims=False)
            come = with_chip(give, bit)
            value = (keep.astype(F32) + come.astype(F32)).astype(BF16)
        return value.reshape(rows, cols)

    def over_seq(value):
        for i in range(half - 1):
            come = move(
                value,
                lambda dd, ss: (dd, i + 1) if ss == i else ((dd, seqs - 2 - i) if ss == seqs - 1 - i else None),
            )
            value = (value.astype(F32) + come.astype(F32)).astype(BF16)
        come = move(value, lambda dd, ss: (dd, seqs - 1 - ss) if ss in (half - 1, half) else None)
        value = (value.astype(F32) + come.astype(F32)).astype(BF16)
        for i in reversed(range(half - 1)):
            come = move(
                value,
                lambda dd, ss: (dd, i) if ss == i + 1 else ((dd, seqs - 1 - i) if ss == seqs - 2 - i else None),
            )
            value = jnp.where((s == i) | (s == seqs - 1 - i), come, value)
        return value

    def my_core(value, axis, other=False):
        shape = value.shape
        size = shape[axis] // dps
        value = value.reshape(shape[:axis] + (chips, 2, size) + shape[axis + 1 :])
        value = lax.dynamic_index_in_dim(value, (1 - core) if other else core, axis + 1, keepdims=False)
        return value.reshape(shape[:axis] + (chips * size,) + shape[axis + 1 :])

    bounds = jnp.cumsum(pair_lengths[0])[:-1]
    place = s * mine + jnp.arange(mine, dtype=jnp.int32)
    pair = jnp.sum((place[:, None] >= bounds[None, :]).astype(jnp.int32), axis=1)
    code = (2 * pair + (live_mask > 0)).astype(BF16)
    lines = -(-mine // dim)
    code = jnp.pad(code, (0, 16 * dim * (-(-lines // 16)) - mine)).reshape(-1, dim)
    packed = jnp.concatenate([tokens, code], axis=0)
    packed = jnp.where(moved, trade(packed), packed)
    row = gather_row(packed)
    x_row = row[:, :mine].reshape(seqs * mine, dim)
    code_row = row[:, mine:].reshape(seqs, -1)[:, :mine].reshape(-1).astype(jnp.int32)
    mask_query, mask_key, dead = mask_terms(code_row // 2, code_row % 2 == 1)
    x = packed[:mine].astype(F32)
    dy = jnp.where(moved, trade(out_grad), out_grad)

    def scaled(v, gain):
        return v * lax.rsqrt(jnp.mean(v * v, axis=1, keepdims=True) + EPS) * gain[None, :]

    def heads_of(weight):
        return lax.dynamic_slice_in_dim(weight, member * width, width, axis=1)

    n1_row = scaled(x_row.astype(F32), attention_gain).astype(BF16)
    wq, wk, wv = heads_of(query_weight), heads_of(key_weight), heads_of(value_weight)
    lanes = -(-width // 128) * 128
    widen = (lambda v: jnp.pad(v, ((0, 0), (0, lanes - width)))) if lanes != width else (lambda v: v)
    q, k, v = [widen(dot_nn(n1_row, w).astype(BF16)) for w in (wq, wk, wv)]
    o_heads, logs = attention_forward(q, k, v, mask_query, mask_key, dead)
    o = to_tokens(o_heads[:, :width].astype(BF16))

    h = x + dot_nn(o, out_weight)
    h_scale = lax.rsqrt(jnp.mean(h * h, axis=1, keepdims=True) + EPS)
    n2 = (h * h_scale * feedforward_gain[None, :]).astype(BF16)
    n2_both = jnp.concatenate([n2, with_core(n2)], axis=0)
    dy_both = jnp.concatenate([dy, with_core(dy)], axis=0)
    wg, wu, wd = my_core(gate_weight, 1), my_core(up_weight, 1), my_core(down_weight, 0)
    g = dot_nn(n2_both, wg)
    u = dot_nn(n2_both, wu)
    act, slope = gelu_parts(g)
    z = (act * u).astype(BF16)
    f = dot_nn(z, wd)
    layer_out = (h + f[:mine] + with_core(f[mine:].astype(BF16)).astype(F32)).astype(BF16)
    layer_out = jnp.where(moved, trade(layer_out), layer_out)

    grad_down = dot_tn(z, dy_both).astype(BF16)
    dz = dot_nt(dy_both, wd)
    dg = (dz * u * slope).astype(BF16)
    du = (dz * act).astype(BF16)
    grad_gate = dot_tn(n2_both, dg).astype(BF16)
    grad_upward = dot_tn(n2_both, du).astype(BF16)
    dn2_both = dot_nt(dg, wg) + dot_nt(du, wu)
    dn2 = dn2_both[:mine] + with_core(dn2_both[mine:].astype(BF16)).astype(F32)

    ghd = dn2 * feedforward_gain[None, :]
    dh = dy.astype(F32) + h_scale * ghd - h * (h_scale**3 * jnp.mean(h * ghd, axis=1, keepdims=True))
    gain_two = jnp.sum(dn2 * h * h_scale, axis=0)
    da = dh.astype(BF16)
    do = to_heads(dot_nt(da, out_weight).astype(BF16))
    o_both = jnp.concatenate([my_core(o, 1), with_core(my_core(o, 1, other=True))], axis=0)
    da_both = jnp.concatenate([da, with_core(da)], axis=0)
    grad_output = dot_tn(o_both, da_both).astype(BF16)

    dq, dk, dv = attention_backward(q, k, v, widen(do), o_heads, logs, mask_query, mask_key, dead)
    dq, dk, dv = dq[:, :width], dk[:, :width], dv[:, :width]
    dn1_row = dot_nt(dq, wq) + dot_nt(dk, wk) + dot_nt(dv, wv)
    x_row_scale = lax.rsqrt(jnp.mean(jnp.square(x_row.astype(F32)), axis=1, keepdims=True) + EPS)
    gain_one = jnp.sum(dn1_row * (x_row.astype(F32) * x_row_scale), axis=0)
    grad_heads = dot_tn(n1_row, jnp.concatenate([dq, dk, dv], axis=1)).astype(BF16)
    gains = jnp.pad(jnp.stack([gain_one, gain_two], axis=1), ((0, 0), (0, 126))).astype(BF16)
    dn1 = row_sum(dn1_row)

    x_scale = lax.rsqrt(jnp.mean(x * x, axis=1, keepdims=True) + EPS)
    gxd = dn1 * attention_gain[None, :]
    grad_tokens = dh + x_scale * gxd - x * (x_scale**3 * jnp.mean(x * gxd, axis=1, keepdims=True))
    grad_tokens = jnp.where(moved, trade(grad_tokens.astype(BF16)).astype(F32), grad_tokens)

    ahead, back = chip_bits, chip_bits[::-1]
    down_out = over_seq(over_chips(grad_down, ahead)).astype(F32)

    def both_cores(value):
        n = value.shape[0] // 2
        first, second = value[:n], value[n:]
        upper = core == 1
        come = with_core(jnp.where(upper, first, second))
        keep = jnp.where(upper, second, first)
        return jnp.stack([jnp.where(upper, come, keep), jnp.where(upper, keep, come)], axis=1)

    def unit_columns(value):
        n = value.shape[0]
        return value.reshape(n, 2, chips, units // dps).transpose(0, 2, 1, 3).reshape(n, units)

    gate_out = unit_columns(over_seq(both_cores(over_chips(grad_gate, back)))).astype(F32)
    upward_out = unit_columns(over_seq(both_cores(over_chips(grad_upward, ahead)))).astype(F32)
    output_out = over_seq(over_chips(grad_output, back)).astype(F32)

    heads_part = over_chips(jnp.concatenate([grad_heads, gains], axis=1), back)
    heads_part = both_cores(heads_part)
    heads_part = (heads_part.astype(F32) + with_seq(heads_part, half).astype(F32)).astype(BF16)
    heads_part = heads_part[None]
    for bit in bits[:-1]:
        come = with_seq(heads_part, bit)
        upper = (member & bit) != 0
        heads_part = jnp.concatenate([jnp.where(upper, come, heads_part), jnp.where(upper, heads_part, come)], axis=0)
    heads_part = heads_part.transpose(1, 2, 0, 3).reshape(-1, seqs, 3 * width + 128)
    query_out, key_out, value_out = [
        heads_part[:, :, i * width : (i + 1) * width].reshape(-1, dim).astype(F32) for i in range(3)
    ]
    gains_out = jnp.sum(heads_part[:, :, 3 * width : 3 * width + 2].astype(F32), axis=1)
    return (
        layer_out,
        grad_tokens,
        query_out,
        key_out,
        value_out,
        output_out,
        gate_out,
        upward_out,
        down_out,
        gains_out[:, 0],
        gains_out[:, 1],
    )


def opening_kernel(tokens_ref, live_ref, lengths_ref, gain_one_ref, gain_two_ref, *refs):
    refs = list(refs)

    def take(n):
        taken, refs[:n] = refs[:n], []
        return taken

    wq_ref, wk_ref, wv_ref, wo_ref, dy_ref = take(5)
    outs = take(OPENED)
    kept = take(OPENED)
    n1_s, k_s, v_s, qa0_s, qa1_s, o0_s, o1_s, mk_s, h_s, n2_s, o_s, dy_s, x_s = kept
    xs, codes, w_s, wo_s, q_s, mq_s, ka_s, va_s, ob_s, send_sem, recv_sem, local_sem = take(12)

    d = lax.axis_index("dp")
    s = lax.axis_index("seq")
    core = d % 2
    low = s % 2
    high = s // 2
    member = 2 * core + low
    sibling = (d + 1 - 2 * core, s)
    over_z = (d, s + 1 - 2 * low)
    across = (d + 1 - 2 * core, s + 1 - 2 * low)
    swapped = (d + 1 - 2 * core, s + 2 - 4 * high)
    moved = core != high
    stays = core == high

    barrier = pltpu.get_barrier_semaphore()
    for other in (sibling, over_z, across, swapped):
        pl.semaphore_signal(barrier, inc=1, device_id=other, device_id_type=MESH)

    counts = {"remote": 0, "local": 0}

    class Copy:
        def __init__(self, src, dst, target):
            self.parts = (src, dst, target, counts["remote"])
            counts["remote"] += 1

        def made(self):
            src, dst, target, i = self.parts
            return pltpu.make_async_remote_copy(
                src_ref=src, dst_ref=dst, send_sem=send_sem.at[i], recv_sem=recv_sem.at[i], device_id=target, device_id_type=MESH
            )

        def start(self):
            self.made().start()

        def wait_recv(self):
            self.made().wait_recv()

        def wait_send(self):
            self.made().wait_send()

    class Fetch:
        def __init__(self, src, dst):
            self.parts = (src, dst, counts["local"])
            counts["local"] += 1

        def made(self):
            src, dst, i = self.parts
            return pltpu.make_async_copy(src, dst, local_sem.at[i])

        def start(self):
            self.made().start()

        def wait(self):
            self.made().wait()

    def lanes_at(start, size):
        return pl.ds(pl.multiple_of(start * size, size), size)

    mine, dim = tokens_ref.shape
    third = mine // 3
    pieces = [pl.ds(i * third, third) for i in range(3)]
    place = s * mine + lax.broadcasted_iota(jnp.int32, codes.shape[1:], 1)
    ends = [lengths_ref[0, 0]]
    for i in (1, 2):
        ends.append(ends[-1] + lengths_ref[0, i])
    pair = sum([jnp.where(place >= end, 1.0, 0.0) for end in ends])
    code = (2.0 * pair + jnp.where(live_ref[...][None, :] > 0, 1.0, 0.0)).astype(BF16)

    w_loads = []
    for p in range(2):
        for t, w in enumerate((wq_ref, wk_ref, wv_ref)):
            w_loads.append(Fetch(w.at[:, lanes_at(2 * member + p, 128)], w_s.at[:, pl.ds((3 * p + t) * 128, 128)]))
    wo_loads = [
        Fetch(wo_ref.at[pl.ds((2 * m + p) * 128, 128)], wo_s.at[pl.ds((4 * p + m) * 128, 128)]) for m in range(4) for p in range(2)
    ]

    trade = [Copy(tokens_ref.at[at], xs.at[0, at], swapped) for at in pieces]
    to_z = [Copy(xs.at[0, at], xs.at[1, at], over_z) for at in pieces]
    to_core = [Copy(xs.at[0, at], xs.at[2, at], sibling) for at in pieces]
    on_core = [Copy(xs.at[1, at], xs.at[3, at], sibling) for at in pieces]
    code_s = x_s.at[pl.ds(0, 16), pl.ds(0, mine)]
    code_trade = Copy(code_s, codes.at[0], swapped)
    code_z = Copy(codes.at[0], codes.at[1], over_z)
    code_core = Copy(codes.at[0], codes.at[2], sibling)
    code_on = Copy(codes.at[1], codes.at[3], sibling)
    dy_trade = Copy(dy_ref, dy_s.at[pl.ds(0, mine)], swapped)
    dy_local = Fetch(dy_ref, dy_s.at[pl.ds(0, mine)])
    dy_core = Copy(dy_s.at[pl.ds(0, mine)], dy_s.at[pl.ds(mine, mine)], sibling)

    code_s[...] = code
    pl.semaphore_wait(barrier, 4)

    @pl.when(moved)
    def _():
        code_trade.start()
        for made in trade:
            made.start()

    @pl.when(stays)
    def _():
        xs[0] = tokens_ref[...]
        codes[0] = code
        code_z.start()
        code_core.start()
        for a, b in zip(to_z, to_core):
            a.start()
            b.start()

    for load in w_loads + wo_loads:
        load.start()

    tokens = k_s.shape[0]
    lane = lax.broadcasted_iota(jnp.int32, (third, 128), 1)
    inside = lane % HEAD_DIM
    for load in w_loads:
        load.wait()

    def project(b):
        for i in range(3):
            at = pl.ds(i * third, third)
            x = xs[b, at, :].astype(F32)
            n1 = (x * lax.rsqrt(jnp.mean(x * x, axis=1, keepdims=True) + EPS) * gain_one_ref[...]).astype(BF16)
            to = pl.ds(pl.multiple_of(b * mine + i * third, 128), third)
            n1_s[to, :] = n1
            qkv = dot_nn(n1, w_s[...]).astype(BF16)
            for p in range(2):
                for t, out in enumerate((q_s, k_s, v_s)):
                    out[to, 128 * p : 128 * p + 128] = qkv[:, (3 * p + t) * 128 : (3 * p + t + 1) * 128]
            number = codes[b, 0:8, i * third : (i + 1) * third].astype(F32).T[:, 0:1]
            whose = jnp.floor(number * 0.5)
            dead = number - 2.0 * whose < 0.5
            same = inside.astype(F32) == whose
            mq_s[to, :] = jnp.where(inside < 4, jnp.where(same, 1.0, 0.0), jnp.where(inside == 4, 1.0, 0.0)).astype(BF16)
            key = jnp.where(inside == 4, jnp.where(dead, -BIG, 0.0), jnp.where((inside >= 5) & (inside < 8), 1.0, 0.0))
            mk_s[to, :] = jnp.where(inside < 4, jnp.where(same, 0.0, -BIG), key).astype(BF16)

    def block(i):
        return (i + 2 * moved.astype(jnp.int32)) % 4

    def relay():
        code_z.wait_recv()
        code_on.start()
        for a, b in zip(to_z, on_core):
            a.wait_recv()
            b.start()

    def from_core():
        code_core.wait_recv()
        for made in to_core:
            made.wait_recv()

    def from_core_on():
        code_on.wait_recv()
        for made in on_core:
            made.wait_recv()

    pl.when(moved)(from_core)
    project(block(0))

    @pl.when(moved)
    def _():
        code_trade.wait_recv()
        code_z.start()
        code_core.start()
        for made, a, b in zip(trade, to_z, to_core):
            made.wait_recv()
            a.start()
            b.start()
        dy_trade.start()
        from_core_on()

    pl.when(stays)(relay)
    project(block(1))
    pl.when(stays)(from_core)
    project(block(2))
    pl.when(moved)(relay)

    @pl.when(stays)
    def _():
        dy_local.start()
        from_core_on()

    project(block(3))
    code_trade_done = [code_trade] + trade

    @pl.when(moved)
    def _():
        for made in code_trade_done:
            made.wait_send()

    x_s[...] = xs[0]

    stores = [Fetch(src, dst) for src, dst in zip(kept, outs)]
    for i in (0, 1, 2, 7, 12):
        stores[i].start()

    rows = 256
    steps = tokens // rows
    lane = lax.broadcasted_iota(jnp.int32, (rows, 128), 1)
    klane = lax.broadcasted_iota(jnp.int32, (tokens, 128), 1)

    def attend(p, j):
        cols = slice(128 * p, 128 * p + 128)
        at = pl.ds(pl.multiple_of(j * rows, rows), rows)
        q = q_s[at, cols]
        mq = mq_s[at, :]
        qf = q.astype(F32)
        dead = mk_s[at, 4:5].astype(F32) < 0
        qk = qf * k_s[at, cols].astype(F32)
        v_own = v_s[at, cols].astype(F32)
        results = []
        for h in range(2):
            own_lanes = (lane < HEAD_DIM) if h == 0 else (lane >= HEAD_DIM)
            sc = dot_nt(jnp.where(own_lanes, q, mq), ka_s[h])
            own = jnp.sum(jnp.where(own_lanes, qk, 0.0), axis=1, keepdims=True)
            own = jnp.where(dead, own, -BIG)
            top = jnp.maximum(jnp.max(sc, axis=1, keepdims=True), own)
            pr = jnp.exp(sc - top).astype(BF16)
            r = dot_nn(pr, va_s[h])
            own_p = jnp.exp(own - top)
            total = (r[:, HEAD_DIM : HEAD_DIM + 1] if h == 0 else r[:, 0:1]) + own_p
            results.append((r + own_p * v_own) * (1.0 / total))
            other = lane - (HEAD_DIM if h == 0 else 0)
            a, b, c = three_parts(top + jnp.log(total))
            aug = jnp.where(other == 5, -a, jnp.where(other == 6, -b, jnp.where(other == 7, -c, mq.astype(F32))))
            (qa0_s, qa1_s)[p][h, at, :] = jnp.where(own_lanes, qf, aug).astype(BF16)
        o = jnp.where(lane < HEAD_DIM, results[0], results[1])
        (o0_s, o1_s)[p][at, :] = o
        ob_s[p, at, :] = o.astype(BF16)

    o_moves = []
    for p in range(2):
        to = o_s.at[pl.ds(0, mine), lanes_at(4 * p + member, 128)]
        o_moves.append(
            [Copy(ob_s.at[p, pl.ds(b * mine, mine)], to, target) for b, target in ((1, over_z), (3, across), (2, sibling))]
        )
    for p in range(2):
        cols = slice(128 * p, 128 * p + 128)
        for h in range(2):
            own_lanes = (klane < HEAD_DIM) if h == 0 else (klane >= HEAD_DIM)
            ka_s[h] = jnp.where(own_lanes, k_s[:, cols], mk_s[...])
            va_s[h] = jnp.where(own_lanes, v_s[:, cols], jnp.ones_like(v_s[:, cols]))

        @pl.loop(0, steps)
        def _(j, p=p):
            attend(p, steps - 1 - j)
            for made, b in zip(o_moves[p], (1, 3, 2)):

                @pl.when(j == steps - 1 - b * mine // rows)
                def _(made=made):
                    made.start()

        o_s[0:mine, lanes_at(4 * p + member, 128)] = ob_s[p, 0:mine, :]
        stores[3 + p].start()
        stores[5 + p].start()
        if p == 0:

            @pl.when(moved)
            def _():
                dy_trade.wait_recv()

            @pl.when(stays)
            def _():
                dy_local.wait()

            dy_core.start()

    for load in wo_loads:
        load.wait()
    o_core = Copy(o_s.at[pl.ds(0, mine)], o_s.at[pl.ds(mine, mine)], sibling)
    n2_core = Copy(n2_s.at[pl.ds(0, mine)], n2_s.at[pl.ds(mine, mine)], sibling)
    half = dim // 2
    for made in o_moves[0]:
        made.wait_recv()
    h_s[...] = x_s[...].astype(F32) + dot_nn(o_s[0:mine, 0:half], wo_s[0:half, :])
    for made in o_moves[1]:
        made.wait_recv()
    o_core.start()
    for at in pieces:
        hh = h_s[at, :] + dot_nn(o_s[at, half:dim], wo_s[half:dim, :])
        h_s[at, :] = hh
        n2_s[at, :] = (hh * lax.rsqrt(jnp.mean(hh * hh, axis=1, keepdims=True) + EPS) * gain_two_ref[...]).astype(BF16)
    n2_core.start()
    stores[8].start()
    dy_core.wait_recv()
    stores[11].start()
    o_core.wait_recv()
    stores[10].start()
    n2_core.wait_recv()
    stores[9].start()
    for made in to_z + to_core + on_core + [code_z, code_core, code_on, dy_core, o_core, n2_core] + o_moves[0] + o_moves[1]:
        made.wait_send()

    @pl.when(moved)
    def _():
        dy_trade.wait_send()

    for store in stores:
        store.wait()


def opening(tokens, live, lengths, gains, weights, dy):
    mine, dim = tokens.shape
    row = 4 * mine
    vmem = pl.BlockSpec(memory_space=pltpu.VMEM)
    anywhere = pl.BlockSpec(memory_space=pl.ANY)
    kept = [((row, dim), BF16), ((row, 256), BF16), ((row, 256), BF16)]
    kept += [((2, row, 128), BF16)] * 2 + [((row, 128), F32)] * 2 + [((row, 128), BF16)]
    kept += [((mine, dim), F32)] + [((2 * mine, dim), BF16)] * 3 + [((mine, dim), BF16)]
    scratch = [pltpu.VMEM(*v) for v in kept]
    scratch += [
        pltpu.VMEM((4, mine, dim), BF16),
        pltpu.VMEM((4, 16, mine), BF16),
        pltpu.VMEM((dim, 768), BF16),
        pltpu.VMEM((dim, dim), BF16),
        pltpu.VMEM((row, 256), BF16),
        pltpu.VMEM((row, 128), BF16),
        pltpu.VMEM((2, row, 128), BF16),
        pltpu.VMEM((2, row, 128), BF16),
        pltpu.VMEM((2, row, 128), BF16),
    ]
    remote, local = 12 + 4 + 2 + 6 + 2, 6 + 8 + 1 + OPENED
    semaphores = [pltpu.SemaphoreType.DMA((count,)) for count in (remote, remote, local)]
    return pl.pallas_call(
        opening_kernel,
        in_specs=[vmem, vmem, pl.BlockSpec(memory_space=pltpu.SMEM), vmem, vmem] + [anywhere] * 5,
        out_specs=[anywhere] * OPENED,
        out_shape=[jax.ShapeDtypeStruct(*v) for v in kept],
        scratch_shapes=scratch + semaphores,
        compiler_params=pltpu.CompilerParams(collective_id=1, has_side_effects=True, vmem_limit_bytes=VMEM_BYTES),
        cost_estimate=pl.CostEstimate(flops=16 * row * row * 256, bytes_accessed=30 << 20, transcendentals=4 * row * row),
        name="opening",
    )(tokens, live, lengths, *gains, *weights, dy)


def middle_kernel(gain_ref, *refs):
    refs = list(refs)

    def take(n):
        taken, refs[:n] = refs[:n], []
        return taken

    n2_ref, dy_ref, h_ref, o_ref, wg_ref, wu_ref, wd_ref, wo_ref = take(8)
    lo_o, dh_o, do_o, gate_o, up_o, out_o, da_o, db_o = take(8)
    n2_s, n2t_s, dy_s, h_s, wg_s, wu_s, wd_s, z_s, zc_s, dg_s, du_s = take(11)
    dn2_s, give_s, come_r, da_s, dap_s, dcr_s, dorow_s, own_s, far_s, stage_s, out_s, ra_s, rb_s, fr_s = take(14)
    f_s, lo_s = take(2)
    second_r, cores_s, accs = take(2), take(2), take(2)
    send_sem, recv_sem, local_sem = take(3)

    d = lax.axis_index("dp")
    s = lax.axis_index("seq")
    core = d % 2
    xb = (d // 2) % 2
    yb = (d // 4) % 2
    low = s % 2
    sibling = (d + 1 - 2 * core, s)
    over_x = (d + 2 - 4 * xb, s)
    over_y = (d + 4 - 8 * yb, s)
    over_z = (d, s + 1 - 2 * low)

    barrier = pltpu.get_barrier_semaphore()
    for other in (sibling, over_x, over_y, over_z):
        pl.semaphore_signal(barrier, inc=1, device_id=other, device_id_type=MESH)

    counts = {"remote": 0, "local": 0}

    class Copy:
        def __init__(self, src, dst, target, like=None):
            self.parts = (src, dst, target, counts["remote"] if like is None else like.parts[3])
            counts["remote"] += like is None

        def made(self):
            src, dst, target, i = self.parts
            return pltpu.make_async_remote_copy(
                src_ref=src, dst_ref=dst, send_sem=send_sem.at[i], recv_sem=recv_sem.at[i], device_id=target, device_id_type=MESH
            )

        def start(self):
            self.made().start()

        def wait_recv(self):
            self.made().wait_recv()

        def wait_send(self):
            self.made().wait_send()

    class Fetch:
        def __init__(self, src, dst):
            self.parts = (src, dst, counts["local"])
            counts["local"] += 1

        def made(self):
            src, dst, i = self.parts
            return pltpu.make_async_copy(src, dst, local_sem.at[i])

        def start(self):
            self.made().start()

        def wait(self):
            self.made().wait()

    def at_of(start, size):
        return pl.ds(pl.multiple_of(start * size, size), size)

    mine, dim = h_s.shape
    both = 2 * mine
    units = wd_s.shape[0]
    tiles = [(i, min(256, units - i)) for i in range(0, units, 256)]
    n2_load = Fetch(n2_ref, n2_s)
    dy_load = Fetch(dy_ref, dy_s)
    h_load = Fetch(h_ref, h_s)
    w_loads = []
    places = []
    for first, size in tiles:
        start = jnp.where(xb == 1, first, units - first - size)
        places.append(pl.ds(pl.multiple_of(start, 128), size))
        cols = pl.ds(pl.multiple_of(core * units + start, 128), size)
        w_loads.append(
            [
                Fetch(wg_ref.at[:, cols], wg_s.at[:, places[-1]]),
                Fetch(wu_ref.at[:, cols], wu_s.at[:, places[-1]]),
                Fetch(wd_ref.at[cols, :], wd_s.at[places[-1], :]),
            ]
        )
    n2_load.start()
    for load in w_loads[0]:
        load.start()
    dy_load.start()
    for loads in w_loads[1:]:
        for load in loads:
            load.start()
    h_load.start()

    half = dim // 2
    cut = half // 2
    rows = units // 2
    first_cols, last_cols = pl.ds(0, cut), pl.ds(cut, cut)
    top, end = pl.ds(0, mine), pl.ds(mine, mine)
    z_moves, a_far, a_own = [], [], []
    for cols in places:
        z_moves.append(Copy(z_s.at[top, cols], zc_s.at[end, cols], sibling))
        z_moves.append(Copy(z_s.at[end, cols], zc_s.at[top, cols], sibling))
        a_far.append(Copy(far_s.at[cols, first_cols], ra_s.at[cols], over_y))
        a_own.append(Copy(own_s.at[cols, first_cols], ra_s.at[cols], over_y, like=a_far[-1]))
    b_own = Copy(own_s.at[at_of(1 - xb, rows), last_cols], rb_s.at[at_of(core, rows)], over_x)
    b_far = Copy(far_s.at[at_of(1 - xb, rows), last_cols], rb_s.at[at_of(1 - core, rows)], over_x)

    def down_of(to, left, i):
        to[places[i], :] = dot_tn(left[:, places[i]], dy_s[:, at_of(core, half)]).astype(BF16)

    def far_of(i):
        z_moves[2 * i].wait_recv()
        z_moves[2 * i + 1].wait_recv()
        down_of(far_s, zc_s, i)
        pl.when(yb == core)(a_far[i].start)
        pl.when(yb != core)(a_own[i].start)
        done = tiles[i][0] + tiles[i][1]
        if done - tiles[i][1] < rows <= done:
            b_own.start()
            b_far.start()

    n2_load.wait()
    for i, (cols, loads) in enumerate(zip(places, w_loads)):
        loads[0].wait()
        loads[1].wait()
        g = dot_nn(n2_s[...], wg_s[:, cols])
        u = dot_nn(n2_s[...], wu_s[:, cols])
        act, slope = gelu_parts(g)
        z_s[:, cols] = (act * u).astype(BF16)
        if i == 0:
            pl.semaphore_wait(barrier, 4)
            dy_load.wait()
        z_moves[2 * i].start()
        z_moves[2 * i + 1].start()
        loads[2].wait()
        dz = dot_nt(dy_s[...], wd_s[cols, :])
        dg_s[:, cols] = (dz * u * slope).astype(BF16)
        du_s[:, cols] = (dz * act).astype(BF16)
        down_of(own_s, z_s, i)
        if i > 0:
            far_of(i - 1)
    far_of(len(tiles) - 1)

    size = rows // 2
    second = [
        Copy(ra_s.at[at_of(1 - xb, rows)], second_r[0], over_x),
        Copy(rb_s.at[at_of(1 - yb, rows)], second_r[1], over_y),
    ]
    on_core = [Copy(cores_s[i], accs[i].at[core], sibling) for i in range(2)]
    acc_stores = [Fetch(accs[i], (da_o, db_o)[i]) for i in range(2)]

    def add_first():
        for made in a_far:
            made.wait_recv()

        @pl.when(yb == core)
        def _():
            ra_s[...] = (ra_s[...].astype(F32) + own_s[:, first_cols].astype(F32)).astype(BF16)

        @pl.when(yb != core)
        def _():
            ra_s[...] = (ra_s[...].astype(F32) + far_s[:, first_cols].astype(F32)).astype(BF16)

        second[0].start()
        b_own.wait_recv()
        b_far.wait_recv()
        for part, y in ((own_s, core), (far_s, 1 - core)):
            at = at_of(y, rows)
            rb_s[at, :] = (rb_s[at, :].astype(F32) + part[at_of(xb, rows), last_cols].astype(F32)).astype(BF16)
        second[1].start()

    def add_second():
        for i, (whole, bit) in enumerate(((ra_s, xb), (rb_s, yb))):
            second[i].wait_recv()

            def summed(which):
                at = pl.ds(pl.multiple_of(bit * rows + which * size, size), size)
                return (whole[at, :].astype(F32) + second_r[i][at_of(which, size), :].astype(F32)).astype(BF16)

            cores_s[i][...] = summed(1 - core)
            on_core[i].start()
            accs[i][core] = summed(core)
        for i in range(2):
            on_core[i].wait_recv()
            acc_stores[i].start()

    quarter = dim // 4
    third = mine // 3
    h_load.wait()

    @pl.loop(0, 4)
    def _(i):
        at = at_of(i, quarter)
        dn2 = dot_nt(dg_s[...], wg_s[at, :]) + dot_nt(du_s[...], wu_s[at, :])
        dn2_s[:, at] = dn2[0:mine, :]
        give_s[:, at] = dn2[mine:both, :].astype(BF16)

    dn2_move = Copy(give_s, come_r, sibling)
    dn2_move.start()
    wo_s = wg_s.at[:, pl.ds(0, dim)]
    o_s = wu_s.at[pl.ds(0, both), pl.ds(0, dim)]
    wo_load, o_load = Fetch(wo_ref, wo_s), Fetch(o_ref, o_s)
    wo_load.start()
    o_load.start()

    dn2_move.wait_recv()
    for i in range(3):
        at = pl.ds(i * third, third)
        dn2 = (dn2_s[at, :] + come_r[at, :].astype(F32)) * gain_ref[...]
        h = h_s[at, :]
        scale = lax.rsqrt(jnp.mean(h * h, axis=1, keepdims=True) + EPS)
        dh = dy_s[at, :].astype(F32) + scale * dn2 - h * (scale * scale * scale * jnp.mean(h * dn2, axis=1, keepdims=True))
        dn2_s[at, :] = dh
        da_s[at, :] = dh.astype(BF16)
    dh_store = Fetch(dn2_s, dh_o)
    dh_store.start()
    da_move = Copy(da_s.at[:, at_of(1 - core, half)], dap_s.at[end], sibling)
    da_move.start()
    dap_s[0:mine, :] = da_s[:, at_of(core, half)]
    wo_load.wait()
    do_s = come_r
    for i in range(3):
        at = pl.ds(i * third, third)
        do_s[at, :] = dot_nt(da_s[at, :], wo_s[...]).astype(BF16)
    do_core = Copy(do_s.at[:, at_of(1 - core, half)], dcr_s, sibling)
    do_core.start()
    do_z = []
    for p in range(2):
        do_z.append(Copy(do_s.at[:, at_of((2 * core + 1 - low) * 2 + p, 128)], dorow_s.at[p, pl.ds(mine, mine)], over_z))
    for made in do_z:
        made.start()

    add_first()


    @pl.loop(0, 4)
    def _(i):
        at = at_of(i, quarter)
        f = dot_nn(z_s[...], wd_s[:, at])
        f_s[:, at] = f[0:mine, :].astype(BF16)
        lo_s[:, at] = f[mine:both, :].astype(BF16)

    f_move = Copy(lo_s, fr_s, sibling)
    f_move.start()

    n2t_s[...] = n2_s[...].T
    stores = []

    def unit_rows(to, right, turn, b, place):
        slot = turn % 2
        if turn >= 2:
            stores[turn - 2].wait()
        stage_s[slot] = dot_nn(n2t_s[b * quarter : (b + 1) * quarter, :], right[...]).astype(BF16)
        stores.append(Fetch(stage_s.at[slot], to.at[pl.ds(place * quarter, quarter)]))
        stores[-1].start()

    unit_rows(gate_o, dg_s, 0, 0, 0)
    do_core.wait_recv()
    for p in range(2):
        do_z.append(Copy(dcr_s.at[:, at_of(2 * (1 - low) + p, 128)], dorow_s.at[p, pl.ds(3 * mine, mine)], over_z))
        do_z[-1].start()
    for p in range(2):
        dorow_s[p, 0:mine, :] = do_s[:, at_of((2 * core + low) * 2 + p, 128)]
        dorow_s[p, 2 * mine : 3 * mine, :] = dcr_s[:, at_of(2 * low + p, 128)]
    for b in range(1, 4):
        unit_rows(gate_o, dg_s, b, b, b)
    for b in range(4):
        unit_rows(up_o, du_s, 4 + b, b, 2 * (b % 2) + b // 2)

    o_load.wait()
    da_move.wait_recv()
    da_move.wait_send()
    for xx in range(2):
        for yy in range(2):
            for p in range(2):
                to = pl.ds(((2 * xx + yy) * 2 + p) * 128, 128)
                m = 4 * p + 2 * yy + xx
                out_s[to, :] = dot_tn(o_s[:, m * 128 : (m + 1) * 128], dap_s[...]).astype(BF16)
    out_store = Fetch(out_s, out_o)
    out_store.start()
    f_move.wait_recv()
    f_move.wait_send()
    for i in range(3):
        at = pl.ds(i * third, third)
        lo_s[at, :] = (h_s[at, :] + f_s[at, :].astype(F32) + fr_s[at, :].astype(F32)).astype(BF16)
    lo_store = Fetch(lo_s, lo_o)
    lo_store.start()
    for made in do_z:
        made.wait_recv()
    do_store = Fetch(dorow_s, do_o)
    do_store.start()

    add_second()
    for made in z_moves + a_far + [do_core, dn2_move, b_own, b_far] + second + on_core + do_z:
        made.wait_send()
    for store in stores[-2:] + [dh_store, out_store, do_store] + acc_stores:
        store.wait()
    lo_store.wait()


def middle(gain, n2_both, dy_both, h, o_both, gate_weight, up_weight, down_weight, out_weight):
    mine, dim = h.shape
    units = gate_weight.shape[1] // 2
    tiles = -(-units // 256)
    both = 2 * mine
    half, quarter = dim // 2, dim // 4
    vmem = pl.BlockSpec(memory_space=pltpu.VMEM)
    anywhere = pl.BlockSpec(memory_space=pl.ANY)
    outs = [((mine, dim), BF16), ((mine, dim), F32), ((2, 4 * mine, 128), BF16), ((dim, units), BF16), ((dim, units), BF16)]
    outs += [((dim, half), BF16), ((2, units // 4, quarter), BF16), ((2, units // 4, quarter), BF16)]
    scratch = [((both, dim), BF16), ((dim, both), BF16), ((both, dim), BF16), ((mine, dim), F32)]
    scratch += [((dim, units), BF16)] * 2 + [((units, dim), BF16)] + [((both, units), BF16)] * 4
    scratch += [((mine, dim), F32)] + [((mine, dim), BF16)] * 3 + [((both, half), BF16), ((mine, half), BF16)]
    scratch += [((2, 4 * mine, 128), BF16)] + [((units, half), BF16)] * 2 + [((2, quarter, units), BF16), ((dim, half), BF16)]
    scratch += [((units, quarter), BF16)] * 2 + [((mine, dim), BF16)]
    scratch += [((mine, dim), BF16)] * 2
    scratch += [((units // 2, quarter), BF16)] * 2 + [((units // 4, quarter), BF16)] * 2 + [((2, units // 4, quarter), BF16)] * 2
    remote, local = 3 * tiles + 2 + 1 + 3 + 1 + 1 + 4 + 1 + 4, 3 + 3 * tiles + 2 + 1 + 8 + 5
    semaphores = [pltpu.SemaphoreType.DMA((count,)) for count in (remote, remote, local)]
    return pl.pallas_call(
        middle_kernel,
        in_specs=[vmem] + [anywhere] * 8,
        out_specs=[anywhere] * 8,
        out_shape=[jax.ShapeDtypeStruct(*v) for v in outs],
        scratch_shapes=[pltpu.VMEM(*v) for v in scratch] + semaphores,
        compiler_params=pltpu.CompilerParams(collective_id=2, has_side_effects=True, vmem_limit_bytes=VMEM_BYTES),
        cost_estimate=pl.CostEstimate(flops=18 * both * dim * units, bytes_accessed=40 << 20, transcendentals=both * units),
        name="middle",
    )(gain, n2_both, dy_both, h, o_both, gate_weight, up_weight, down_weight, out_weight)


ORDER = ((('start', 0), ('start', 1), ('s2', 1), ('lo', 0), ('s2', 0), ('start', 3), ('start', 2)),
 ((), ((), (), (('s0', 3), ('s0', 2), ('start', 5), ('start', 4), ('s3', 1)), (), (('s1', 2),)), (('s1', 3),)),
 ((),
  ((),
   (('s0', 5), ('s3', 0), ('s4', 1), ('s0', 4), ('start', 7), ('s2', 3)),
   (('s3', 3), ('start', 8), ('s2', 2)),
   (('s4', 0),),
   (('s1', 5), ('start', 6), ('s4', 3), ('s1', 4), ('s3', 2), ('s2', 5))),
  (('h0', 1),
   ('s4', 2),
   ('s2', 4),
   ('core', 1),
   ('s0', 7),
   ('core', 0),
   ('z', 0),
   ('s3', 5),
   ('h1', 1),
   ('s5', 3),
   ('own', 0),
   ('h0', 0),
   ('s3', 4),
   ('s0', 6),
   ('s4', 4),
   ('s0', 8),
   ('s5', 1),
   ('s1', 7),
   ('home', 0),
   ('h2', 1),
   ('h3', 1),
   ('s2', 7),
   ('h1', 0),
   ('s4', 5),
   ('s1', 8),
   ('s5', 0),
   ('s3', 7),
   ('s2', 8),
   ('h4', 1),
   ('h2', 0),
   ('s5', 4),
   ('s1', 6),
   ('s3', 8),
   ('s2', 6),
   ('h5', 1),
   ('s4', 7),
   ('s5', 7),
   ('h3', 0),
   ('s4', 8),
   ('s3', 6),
   ('s4', 6),
   ('s5', 8),
   ('s5', 5),
   ('home', 1),
   ('s5', 2),
   ('h4', 0),
   ('home', 2),
   ('h5', 0),
   ('s5', 6))))


def closing_kernel(mask_k_ref, gain_one_ref, *refs):
    refs = list(refs)

    def take(n):
        taken, refs[:n] = refs[:n], []
        return taken

    fetched = take(FETCHED)
    wq_ref, wk_ref, wv_ref, x_ref, lo_ref = take(5)
    da_ref, db_ref, gate_ref, up_ref, out_ref = take(5)
    (gt_o,) = take(1)
    finals = take(ITEMS)
    heads_o, lo_o = take(2)
    fetched_s = take(FETCHED)
    dorow_s, qa0_s, qa1_s, k_s, v_s, o0_s, o1_s, n1_s, dh_s = fetched_s
    firsts_r, seconds_s, seconds_r, cores_s = [take(ITEMS - 2) for _ in range(4)]
    accs, lines = take(ITEMS), take(ITEMS)
    doa_s, dq_s, dqkv_s, hs_s, h1_r, h2_s, h2_r, hk_s, hc_s, hh_s, hh_r = take(11)
    w_s, x_s, dn_s = take(3)
    cs_s, cr_r, zr_r, send_sem, recv_sem, local_sem = take(6)

    d = lax.axis_index("dp")
    s = lax.axis_index("seq")
    core = d % 2
    xb = (d // 2) % 2
    yb = (d // 4) % 2
    low = s % 2
    high = s // 2
    sibling = (d + 1 - 2 * core, s)
    over_x = (d + 2 - 4 * xb, s)
    over_y = (d + 4 - 8 * yb, s)
    over_z = (d, s + 1 - 2 * low)
    over_high = (d, s + 2 - 4 * high)
    swapped = (d + 1 - 2 * core, s + 2 - 4 * high)
    third = (d, 3 - s)
    inner = (s == 1) | (s == 2)
    outer = (s == 0) | (s == 3)
    moved = core != high

    barrier = pltpu.get_barrier_semaphore()
    for other in (sibling, over_x, over_y, over_z, over_high, swapped, third):
        pl.semaphore_signal(barrier, inc=1, device_id=other, device_id_type=MESH)
    pl.semaphore_wait(barrier, 7)

    counts = {"remote": 0, "local": 0}

    class Copy:
        def __init__(self, src, dst, target):
            self.parts = (src, dst, target, counts["remote"])
            counts["remote"] += 1

        def made(self):
            src, dst, target, i = self.parts
            return pltpu.make_async_remote_copy(
                src_ref=src, dst_ref=dst, send_sem=send_sem.at[i], recv_sem=recv_sem.at[i], device_id=target, device_id_type=MESH
            )

        def start(self):
            self.made().start()

        def wait_recv(self):
            self.made().wait_recv()

        def wait_send(self):
            self.made().wait_send()

    copy = Copy

    class Fetch:
        def __init__(self, src, dst):
            self.parts = (src, dst, counts["local"])
            counts["local"] += 1

        def made(self):
            src, dst, i = self.parts
            return pltpu.make_async_copy(src, dst, local_sem.at[i])

        def start(self):
            self.made().start()

        def wait(self):
            self.made().wait()

    def rows_at(start, size):
        return pl.ds(pl.multiple_of(start * size, size), size)

    def lanes_at(start, size):
        return pl.ds(pl.multiple_of(start * size, size), size)

    class Item:
        pass

    items = []
    along_x, along_y = (over_x, xb), (over_y, yb)
    windows, first_col = [], 0
    for acc in accs[2 : ITEMS - 1 : 2]:
        windows.append(pl.ds(first_col, acc.shape[2]))
        first_col += acc.shape[2]
    plans = [(gate_ref, cols, along_y, along_x) if turn == 0 else (up_ref, cols, along_x, along_y) for cols in windows for turn in (0, 1)]
    plans = [(da_ref, None, None, None), (db_ref, None, None, None)] + plans
    plans.append((out_ref, pl.ds(0, accs[-1].shape[2]), along_x, along_y))
    for i, (whole, cols, first, second) in enumerate(plans):
        it = Item()
        it.a, it.z, it.o = accs[i], lines[i], finals[i]
        it.late = first is not None
        if it.late:
            it.r1, it.t, it.r, it.c = [group[i - 2] for group in (firsts_r, seconds_s, seconds_r, cores_s)]
            n = it.n = it.c.shape[0]
            target, it.bit = second
            kept = first[1] * (4 * n)
            base = kept + it.bit * (2 * n)
            it.first = copy(whole.at[rows_at(1 - first[1], 4 * n), cols], it.r1, first[0])
            it.far = Fetch(whole.at[pl.ds(pl.multiple_of(kept + (1 - it.bit) * (2 * n), 2 * n), 2 * n), cols], it.t)
            it.chip = copy(it.t, it.r, target)
            it.parts = [
                Fetch(whole.at[pl.ds(pl.multiple_of(base + (1 - core) * n, n), n), cols], it.c),
                Fetch(whole.at[pl.ds(pl.multiple_of(base + core * n, n), n), cols], it.a.at[core]),
            ]
            it.core = copy(it.c, it.a.at[core], sibling)
        else:
            it.parts = [Fetch(whole, it.a)]
        it.in1 = copy(it.a, it.z, (d, jnp.where(s == 0, 1, 2)))
        it.in2 = copy(it.a, it.o, third)
        it.out = copy(it.o, it.o, (d, jnp.where(s == 1, 0, 3)))
        items.append(it)

    def start(it):
        if it.late:
            it.first.start()
            it.far.start()
        for part in it.parts:
            part.start()

    def step0(it):
        at = rows_at(1 - it.bit, 2 * it.n)
        it.far.wait()
        it.first.wait_recv()
        it.t[...] = (it.t[...].astype(F32) + it.r1[at, :].astype(F32)).astype(BF16)
        it.chip.start()

    def step1(it):
        n = it.n
        for part in it.parts:
            part.wait()
        it.chip.wait_recv()

        def come(which):
            at = pl.ds(pl.multiple_of(it.bit * (2 * n) + which * n, n), n)
            return it.r1[at, :].astype(F32) + it.r[rows_at(which, n), :].astype(F32)

        it.c[...] = (it.c[...].astype(F32) + come(1 - core)).astype(BF16)
        it.core.start()
        it.a[core] = (it.a[core].astype(F32) + come(core)).astype(BF16)

    def step2(it):
        if it.late:
            it.core.wait_recv()
        else:
            it.parts[0].wait()

        @pl.when(outer)
        def _():
            it.in1.start()

    def step3(it):
        @pl.when(inner)
        def _():
            it.in1.wait_recv()
            it.a[...] = (it.a[...].astype(F32) + it.z[...].astype(F32)).astype(BF16)
            it.in2.start()

    def step4(it):
        @pl.when(inner)
        def _():
            it.in2.wait_recv()
            it.o[...] = (it.a[...].astype(F32) + it.o[...].astype(F32)).astype(BF16)
            it.out.start()

    def step5(it):
        @pl.when(outer)
        def _():
            it.out.wait_recv()

    def finish(it):
        if it.late:
            it.first.wait_send()
            it.chip.wait_send()
            it.core.wait_send()

        @pl.when(outer)
        def _():
            it.in1.wait_send()

        @pl.when(inner)
        def _():
            it.in2.wait_send()
            it.out.wait_send()


    mine, dim = x_s.shape
    loads = [Fetch(src, dst) for src, dst in zip(fetched, fetched_s)]
    x_load = Fetch(x_ref, x_s)
    w_loads = []
    for p in range(2):
        for t, w in enumerate((wq_ref, wk_ref, wv_ref)):
            w_loads.append(Fetch(w.at[:, lanes_at((2 * core + low) * 2 + p, 128)], w_s.at[:, pl.ds((3 * p + t) * 128, 128)]))
    for load in loads[:7]:
        load.start()
    for load in loads[7:] + [x_load] + w_loads:
        load.start()

    block = hk_s.shape[1]
    half = block // 2
    firsts = ((over_x, over_y), (over_y, over_x))
    heads = []
    for p in range(2):
        h = Item()
        h.p1 = [copy(hs_s.at[p, i], h1_r.at[p, i], firsts[p][0]) for i in range(2)]
        h.p2 = copy(h2_s.at[p], h2_r.at[p], firsts[p][1])
        h.core = copy(hk_s.at[p, rows_at(1 - core, half)], hc_s.at[p, core], sibling)
        h.high = copy(hh_s.at[p], hh_r.at[p], over_high)
        h.z = copy(heads_o.at[low, p], heads_o.at[low, p], over_z)
        heads.append(h)

    def product(p, yy, xx):
        return dot_tn(n1_s[:, lanes_at(2 * yy + xx, block)], dqkv_s[p])

    def heads0(p):
        h = heads[p]
        for turn in range(2):
            if p == 0:
                i = (1 - yb) if turn == 0 else yb
                hs_s[p, turn] = product(p, i, 1 - xb).astype(BF16)
            else:
                i = (1 - xb) if turn == 0 else xb
                hs_s[p, turn] = product(p, 1 - yb, i).astype(BF16)
            h.p1[turn].start()

    def heads1(p):
        h = heads[p]
        part = product(p, 1 - yb, xb) if p == 0 else product(p, yb, 1 - xb)
        h.p1[0].wait_recv()
        h2_s[p] = (part + h1_r[p, 0].astype(F32)).astype(BF16)
        h.p2.start()

    def heads2(p):
        h = heads[p]
        part = product(p, yb, xb)
        h.p1[1].wait_recv()
        part = part + h1_r[p, 1].astype(F32)
        h.p2.wait_recv()
        hk_s[p] = (part + h2_r[p].astype(F32)).astype(BF16)
        h.core.start()
        hc_s[p, core] = hk_s[p, rows_at(core, half), :]

    def heads3(p):
        h = heads[p]
        h.core.wait_recv()
        hh_s[p] = hc_s[p]
        h.high.start()

    def heads4(p):
        h = heads[p]
        h.high.wait_recv()
        heads_o[low, p] = (hh_s[p].astype(F32) + hh_r[p].astype(F32)).astype(BF16)
        h.z.start()

    def heads5(p):
        heads[p].z.wait_recv()

    def finish_heads(p):
        h = heads[p]
        for made in h.p1 + [h.p2, h.core, h.high, h.z]:
            made.wait_send()

    tokens = k_s.shape[0]
    rows = 256
    steps = tokens // rows
    lane = lax.broadcasted_iota(jnp.int32, (tokens, 128), 1)
    klane = lax.broadcasted_iota(jnp.int32, (rows, 128), 1)

    def prepare(p):
        do = dorow_s[p].astype(F32)
        prod = do * (o0_s, o1_s)[p][...]
        for h in range(2):
            mine = (lane < HEAD_DIM) if h == 0 else (lane >= HEAD_DIM)
            other = lane - (HEAD_DIM if h == 0 else 0)
            delta = jnp.sum(jnp.where(mine, prod, 0.0), axis=1, keepdims=True)
            a, b, c = three_parts(delta)
            aug = jnp.where(other == 5, -a, jnp.where(other == 6, -b, jnp.where(other == 7, -c, 0.0)))
            doa_s[h] = jnp.where(mine, do, aug).astype(BF16)
        dq_s[...] = jnp.zeros_like(dq_s)

    def attend(p, j):
        qa_s = (qa0_s, qa1_s)[p]
        cols = slice(128 * p, 128 * p + 128)
        here = pl.ds(pl.multiple_of(j * rows, rows), rows)
        k = k_s[here, cols]
        v = v_s[here, cols]
        kf = k.astype(F32)
        vf = v.astype(F32)
        mk = mask_k_ref[here, :]
        dead = jnp.where(mk[:, 4:5].astype(F32) < 0, 1.0, 0.0)
        dks, dvs = [], []
        for h in range(2):
            kmine = (klane < HEAD_DIM) if h == 0 else (klane >= HEAD_DIM)
            other = klane - (HEAD_DIM if h == 0 else 0)
            one = (other >= 5) & (other < 8)
            ka = jnp.where(kmine, k, mk)
            va = jnp.where(kmine, v, jnp.where(one, jnp.ones_like(v), jnp.zeros_like(v)))
            pr = jnp.exp(dot_nt(ka, qa_s[h]))
            ds = (pr * dot_nt(va, doa_s[h])).astype(BF16)
            dk = dot_nn(ds, qa_s[h])
            dv = dot_nn(pr.astype(BF16), doa_s[h])
            dq_s[h] += dot_tn(ds, ka)
            qd = qa_s[h, here, :].astype(F32)
            dod = doa_s[h, here, :].astype(F32)
            own = jnp.sum(jnp.where(kmine | one, qd * jnp.where(kmine, kf, 1.0), 0.0), axis=1, keepdims=True)
            own_p = jnp.where(dead > 0, jnp.exp(jnp.where(dead > 0, own, 0.0)), 0.0)
            own_d = jnp.sum(jnp.where(kmine | one, dod * jnp.where(kmine, vf, 1.0), 0.0), axis=1, keepdims=True)
            own_ds = own_p * own_d
            dks.append(dk + own_ds * qd)
            dvs.append(dv + own_p * dod)
            dq_s[h, here, :] += jnp.where(kmine, own_ds * kf, 0.0)
        dqkv_s[p, here, 128:256] = jnp.where(klane < HEAD_DIM, dks[0], dks[1]).astype(BF16)
        dqkv_s[p, here, 256:384] = jnp.where(klane < HEAD_DIM, dvs[0], dvs[1]).astype(BF16)

    cut = mine // 3
    width = dqkv_s.shape[2]

    def dn1_of(i):
        at = pl.ds(i * mine, mine)
        return dot_nt(dqkv_s[0, at, :], w_s[:, 0:width]) + dot_nt(dqkv_s[1, at, :], w_s[:, width : 2 * width])

    to_core = [copy(cs_s.at[i], cr_r.at[i], sibling) for i in range(2)]
    to_z = [copy(cs_s.at[1, pl.ds(i * cut, cut)], zr_r.at[pl.ds(i * cut, cut)], over_z) for i in range(3)]
    to_home = [copy(cs_s.at[0, pl.ds(i * cut, cut)], gt_o.at[pl.ds(i * cut, cut)], swapped) for i in range(3)]

    late_loads = w_loads + [x_load, loads[8]]

    def give_core(i):
        while late_loads:
            late_loads.pop().wait()
        cs_s[i] = dn1_of(2 + i).astype(BF16)
        to_core[i].start()

    def give_z(_):
        dn = dn1_of(1)
        to_core[1].wait_recv()
        to_core[1].wait_send()
        cs_s[1] = (dn + cr_r[1].astype(F32)).astype(BF16)
        for made in to_z:
            made.start()

    def keep_own(_):
        dn_s[...] = dn1_of(0)
        to_core[0].wait_recv()
        to_core[0].wait_send()

    def give_home(i):
        at = pl.ds(i * cut, cut)
        to_z[i].wait_recv()
        dn = dn_s[at, :] + cr_r[0, at, :].astype(F32) + zr_r[at, :].astype(F32)
        x = x_s[at, :].astype(F32)
        scale = lax.rsqrt(jnp.mean(x * x, axis=1, keepdims=True) + EPS)
        dn = dn * gain_one_ref[...]
        grad = dh_s[at, :] + scale * dn - x * (scale * scale * scale * jnp.mean(x * dn, axis=1, keepdims=True))
        cs_s[0, at, :] = grad.astype(BF16)

        @pl.when(moved)
        def _():
            to_home[i].start()

        @pl.when(jnp.logical_not(moved))
        def _():
            gt_o[at, :] = cs_s[0, at, :]

    tasks = {
        "start": lambda i: start(items[i]),
        "s0": lambda i: step0(items[i]),
        "s1": lambda i: step1(items[i]),
        "s2": lambda i: step2(items[i]),
        "s3": lambda i: step3(items[i]),
        "s4": lambda i: step4(items[i]),
        "s5": lambda i: step5(items[i]),
        "h0": heads0,
        "h1": heads1,
        "h2": heads2,
        "h3": heads3,
        "h4": heads4,
        "h5": heads5,
        "core": give_core,
        "z": give_z,
        "own": keep_own,
        "home": give_home,
    }

    lo_move, lo_local = copy(lo_ref, lo_o, swapped), Fetch(lo_ref, lo_o)

    def give_layer(_):
        pl.when(moved)(lo_move.start)
        pl.when(jnp.logical_not(moved))(lo_local.start)

    tasks["lo"] = give_layer

    def run(todo):
        for name, i in todo:
            tasks[name](i)

    run(ORDER[0])
    for load in loads[:7]:
        load.wait()
    for p in range(2):
        before, slots, later = ORDER[1 + p]
        run(before)
        prepare(p)

        @pl.loop(0, steps)
        def _(j, p=p, slots=slots):
            attend(p, j)
            for i, todo in enumerate(slots):
                if todo:

                    @pl.when(j == i)
                    def _(todo=todo):
                        run(todo)

        dqkv_s[p, :, 0:128] = jnp.where(lane < HEAD_DIM, dq_s[0], dq_s[1]).astype(BF16)
        if p == 0:
            loads[7].wait()
        run(later)

    for it in items:
        finish(it)
    for p in range(2):
        finish_heads(p)
    for made in to_z:
        made.wait_send()

    @pl.when(moved)
    def _():
        for made in to_home + [lo_move]:
            made.wait_recv()
            made.wait_send()

    @pl.when(jnp.logical_not(moved))
    def _():
        lo_local.wait()


def closing(mask_key, gain, fetched, weights, x, layer_out, grads):
    tokens = mask_key.shape[0]
    mine, dim = x.shape
    vmem = pl.BlockSpec(memory_space=pltpu.VMEM)
    anywhere = pl.BlockSpec(memory_space=pl.ANY)
    down, _, gate, _, outp = [w.shape for w in grads]
    third = 128 * (gate[1] // 128 // 3)
    widths = [third] + [128 * ((gate[1] - third) // 256)]
    widths.append(gate[1] - sum(widths))
    shards = [down[1:]] * 2 + [(gate[0] // 8, width) for width in widths for _ in range(2)]
    shards.append((outp[0] // 8, outp[1]))
    lates = shards[2:]
    block = dim // 4
    three = 3 * 128
    scratch = [pltpu.VMEM(v.shape, v.dtype) for v in fetched]
    scratch += [pltpu.VMEM((4 * rows, cols), BF16) for rows, cols in lates]
    scratch += [pltpu.VMEM((2 * rows, cols), BF16) for rows, cols in lates] * 2
    scratch += [pltpu.VMEM(w, BF16) for w in lates]
    scratch += [pltpu.VMEM((2,) + w, BF16) for w in shards] * 2
    scratch += [
        pltpu.VMEM((2, tokens, 128), BF16),
        pltpu.VMEM((2, tokens, 128), F32),
        pltpu.VMEM((2, tokens, three), BF16),
        pltpu.VMEM((2, 2, block, three), BF16),
        pltpu.VMEM((2, 2, block, three), BF16),
        pltpu.VMEM((2, block, three), BF16),
        pltpu.VMEM((2, block, three), BF16),
        pltpu.VMEM((2, block, three), BF16),
        pltpu.VMEM((2, 2, block // 2, three), BF16),
        pltpu.VMEM((2, 2, block // 2, three), BF16),
        pltpu.VMEM((2, 2, block // 2, three), BF16),
        pltpu.VMEM((dim, 2 * three), BF16),
        pltpu.VMEM((mine, dim), BF16),
        pltpu.VMEM((mine, dim), F32),
        pltpu.VMEM((2, mine, dim), BF16),
        pltpu.VMEM((2, mine, dim), BF16),
        pltpu.VMEM((mine, dim), BF16),
    ]
    remote = 6 * ITEMS - 6 + 2 * 6 + 2 + 3 + 3 + 1
    local = FETCHED + 7 + 3 * ITEMS - 4 + 1
    semaphores = [pltpu.SemaphoreType.DMA((count,)) for count in (remote, remote, local)]
    return pl.pallas_call(
        closing_kernel,
        in_specs=[vmem] * 2 + [anywhere] * (FETCHED + 5 + 5),
        out_specs=[vmem] * (2 + ITEMS) + [anywhere],
        out_shape=[jax.ShapeDtypeStruct((mine, dim), BF16)]
        + [jax.ShapeDtypeStruct((2,) + w, BF16) for w in shards]
        + [jax.ShapeDtypeStruct((2, 2, 2, block // 2, three), BF16), jax.ShapeDtypeStruct((mine, dim), BF16)],
        scratch_shapes=scratch + semaphores,
        compiler_params=pltpu.CompilerParams(collective_id=0, has_side_effects=True, vmem_limit_bytes=VMEM_BYTES),
        cost_estimate=pl.CostEstimate(
            flops=40 * tokens * tokens * 256, bytes_accessed=40 << 20, transcendentals=4 * tokens * tokens
        ),
        name="closing",
    )(mask_key, gain, *fetched, *weights, x, layer_out, *grads)


def placing_kernel(count, g1, g2, *refs):
    weights, grads, results = refs[:5], refs[5 : 9 + count], refs[9 + count : 19 + count]
    outs, kept, sems = refs[19 + count : 27 + count], refs[27 + count : -1], refs[-1]
    outs = (*outs, *results[8:])
    loads = []
    sources = list(grads)
    for w, to in zip(weights, kept[len(grads) :]):
        n = to.shape[0]
        sources.append(w.at[pl.ds(pl.multiple_of(lax.axis_index("dp") * n, n), n)])
    for i, (src, to) in enumerate(zip(sources, kept)):
        loads.append(pltpu.make_async_copy(src, to, sems.at[i]))
        loads[-1].start()
    last = len(loads)
    stores = []

    def store(i):
        stores.append(pltpu.make_async_copy(outs[i], results[i], sems.at[last + i]))
        stores[-1].start()

    gt, da, db, *units, out, heads = kept[: len(grads)]
    wq, wk, wv, wg, wu = kept[len(grads) :]
    gt_o, q_o, k_o, v_o, out_o, gate_o, up_o, down_o, g1_o, g2_o = outs
    loads[0].wait()
    gt_o[...] = gt[...].astype(F32)
    store(0)
    for load in loads[1 : len(grads) - 1]:
        load.wait()
    cut = da.shape[2]
    for c in range(2):
        first = [c * (gate_o.shape[1] // 2)] * 2
        for i, part in enumerate(units):
            to, size = (gate_o, up_o)[i % 2], part.shape[2]
            to[:, first[i % 2] : first[i % 2] + size] = part[c].astype(F32)
            first[i % 2] += size
        down_o[:, 2 * c * cut : (2 * c + 1) * cut] = da[c].astype(F32)
        down_o[:, (2 * c + 1) * cut : (2 * c + 2) * cut] = db[c].astype(F32)
        out_o[:, 2 * c * cut : (2 * c + 2) * cut] = out[c].astype(F32)
    for i in (4, 5, 6, 7):
        store(i)
    loads[len(grads) - 1].wait()
    for m in range(4):
        for p in range(2):
            at = slice((2 * m + p) * 128, (2 * m + p + 1) * 128)
            for t, to in enumerate((q_o, k_o, v_o)):
                to[:, at] = heads[m % 2, p, m // 2, :, t * 128 : (t + 1) * 128].astype(F32)

    for i in (1, 2, 3):
        store(i)
    for load in loads[len(grads) :]:
        load.wait()

    def along(pairs, gain):
        total = sum([jnp.sum(grad[...] * w[...].astype(F32), axis=1, keepdims=True) for grad, w in pairs])
        n = total.shape[0]
        return jnp.broadcast_to(total, (n, n)).T[0:1, :] / gain[...]

    g1_o[...] = along(((q_o, wq), (k_o, wk), (v_o, wv)), g1)
    g2_o[...] = along(((gate_o, wg), (up_o, wu)), g2)
    for made in stores:
        made.wait()


def placing(grads, heads, gains, weights):
    gt, da, out = grads[0], grads[1], grads[-1]
    n, dim = out.shape[1], 2 * out.shape[2]
    units = sum([part.shape[2] for part in grads[3:-1]])
    shapes = [gt.shape] + [(n, dim)] * 4 + [(n, units)] * 2 + [(da.shape[1], dim)] + [(1, n)] * 2
    vmem, anywhere = pl.BlockSpec(memory_space=pltpu.VMEM), pl.BlockSpec(memory_space=pl.ANY)
    kept = [v.shape for v in (*grads, heads)] + [(n, w.shape[1]) for w in weights]
    return pl.pallas_call(
        functools.partial(placing_kernel, len(grads) - 3),
        in_specs=[vmem] * 2 + [anywhere] * (6 + len(grads)),
        out_specs=[anywhere] * 8 + [vmem] * 2,
        out_shape=[jax.ShapeDtypeStruct(v, F32) for v in shapes],
        scratch_shapes=[pltpu.VMEM(v, F32) for v in shapes[:8]]
        + [pltpu.VMEM(v, BF16) for v in kept]
        + [pltpu.SemaphoreType.DMA((len(kept) + 8,))],
        compiler_params=pltpu.CompilerParams(vmem_limit_bytes=VMEM_BYTES),
        cost_estimate=pl.CostEstimate(flops=1 << 22, bytes_accessed=14 << 20, transcendentals=0),
        name="placing",
    )(*gains, *weights, *grads, heads)


def local_fused(
    dps,
    seqs,
    tokens,
    query_weight,
    key_weight,
    value_weight,
    out_weight,
    gate_weight,
    up_weight,
    down_weight,
    attention_gain,
    feedforward_gain,
    pair_lengths,
    live_mask,
    out_grad,
):
    mine, dim = tokens.shape
    projections = (query_weight, key_weight, value_weight)
    n1_row, k, v, qa_0, qa_1, o_0, o_1, mask_key, h, n2_both, o_both, dy_both, x_low = opening(
        tokens, live_mask, pair_lengths, (attention_gain[None, :], feedforward_gain[None, :]),
        (*projections, out_weight), out_grad,
    )

    layer_out, dh, do, gate, up, outp, down_a, down_b = middle(
        feedforward_gain[None, :], n2_both, dy_both, h, o_both, gate_weight, up_weight, down_weight, out_weight
    )

    *grads, heads_grads, layer_out = closing(
        mask_key, attention_gain[None, :], (do, qa_0, qa_1, k, v, o_0, o_1, n1_row, dh), projections, x_low, layer_out,
        (down_a, down_b, gate, up, outp),
    )

    gains = [
        lax.dynamic_slice_in_dim(gain[None, :], lax.axis_index("dp") * (dim // dps), dim // dps, axis=1)
        for gain in (attention_gain, feedforward_gain)
    ]
    *results, gain_one, gain_two = placing(grads, heads_grads, gains, (*projections, gate_weight, up_weight))
    return (layer_out, *results, gain_one[0], gain_two[0])


def solution(mesh):
    both = P(("dp", "seq"), None)
    rows = P("dp", None)
    dps, seqs = mesh.shape["dp"], mesh.shape["seq"]
    local = local_fused if (dps, seqs) == (8, 4) else local_plain
    return jax.shard_map(
        functools.partial(local, dps, seqs),
        mesh=mesh,
        in_specs=(both, P(), P(), P(), P(), P(), P(), P(), P(), P(), rows, P(("dp", "seq")), both),
        out_specs=(both, both, rows, rows, rows, rows, rows, rows, rows, P("dp"), P("dp")),
        check_vma=False,
    )
```
